32 devices in a mesh: dp: 8 (over z, y), rep: 4 (over x, core).
Axes of the slice: x: 2, y: 2, z: 4, core: 2. Of those that a mesh axis runs over, the one named last changes fastest.
Arguments:
- slow_input: bfloat16 [256, 196, 1024], P(('dp', 'rep')), may hold values from -30 to 30
- fast_input: bfloat16 [1024, 196, 128], P(('dp', 'rep')), may hold values from -30 to 30
- clip_ids: int32 [32, 8], P(('dp', 'rep')), may hold values from 0 to 3, never falling along the last dimension, each value on 1 to 5 neighbouring positions
- fast_narrow: bfloat16 [3, 32, 128], replicated, may hold values from -0.3125 to 0.3125
- fast_spatial: bfloat16 [9, 32, 32], replicated, may hold values from -0.375 to 0.375
- fast_widen: bfloat16 [128, 32], replicated, may hold values from -1 to 1
- lateral_conv: bfloat16 [5, 256, 128], replicated, may hold values from -0.25 to 0.25
- slow_narrow: bfloat16 [3, 256, 1280], replicated, may hold values from -0.09375 to 0.09375
- slow_spatial: bfloat16 [9, 256, 256], replicated, may hold values from -0.125 to 0.125
- slow_widen: bfloat16 [1024, 256], replicated, may hold values from -0.375 to 0.375
- norm_gains: float32 [1984], replicated, may hold values from 0.5 to 1.5
- norm_biases: float32 [1984], replicated, may hold values from -2 to 2
- slow_cotangent: bfloat16 [256, 196, 1024], P(('dp', 'rep')), may hold values from -6 to 6
- fast_cotangent: bfloat16 [1024, 196, 128], P(('dp', 'rep')), may hold values from -6 to 6
Outputs:
- slow_output: bfloat16 [256, 196, 1024], P(('dp', 'rep'))
- fast_output: bfloat16 [1024, 196, 128], P(('dp', 'rep'))
- slow_ingrad: bfloat16 [256, 196, 1024], P(('dp', 'rep'))
- fast_ingrad: bfloat16 [1024, 196, 128], P(('dp', 'rep'))
- fnarrow_grad: float32 [3, 32, 128], replicated
- fspatial_grad: float32 [9, 32, 32], replicated
- fwiden_grad: float32 [128, 32], replicated
- lateral_grad: float32 [5, 256, 128], replicated
- snarrow_grad: float32 [3, 256, 1280], replicated
- sspatial_grad: float32 [9, 256, 256], replicated
- swiden_grad: float32 [1024, 256], replicated
- gains_grad: float32 [1984], replicated
- biases_grad: float32 [1984], replicated
The draws below stay inside these ranges and needn't reach their ends.
Inputs may be any that keep to these rules, and one draw needn't show every extreme that they name: `clip_ids`: row r holds the clip numbers of slow frames r * 8 to r * 8 + 7: never falling, starting at 0, each clip 1 to 5 frames.
All inputs are finite; a program needn't handle non-finite values.
Results may differ from the reference program's by a relative error of at most 0.006.
Values sent between devices are 32-bit elements; how exact they have to be, the bound alone decides.
A program may use at most 256 MiB of HBM per device.

```python
import math
import jax
import jax.numpy as jnp
import numpy as np
from jax import lax

CS = 1024
BS = 256
CF = 128
BF = 32
ALPHA = 4
SLOW_DEV = 8
CL = 256
PLANE = 196
SLOW_FR = 256
FAST_FR = 1024
SPOS = 50176
BN_ALL = 1984
N_DP = 8
N_REP = 4


def shape_field(noise, key, top, block):
    chan_key, shift_key, factor_key = jax.random.split(key, 3)
    channels = noise.shape[2]
    blocks = noise.shape[0] // block
    offset = 0.5 * jax.random.truncated_normal(chan_key, -2.0, 2.0, (1, 1, channels), jnp.float32)
    shift = jax.random.uniform(shift_key, (blocks, 1, channels), jnp.float32, -0.5, 0.5)
    factor = jnp.exp(jax.random.uniform(factor_key, (blocks, 1, 1), jnp.float32, -0.5, 0.5))
    shift = jnp.repeat(shift, block, axis=0)
    factor = jnp.repeat(factor, block, axis=0)
    ramp = jnp.arange(noise.shape[0], dtype=jnp.float32)[:, None, None] / max(noise.shape[0] - 1, 1)
    return (noise + offset + shift) * factor * (1.0 + (top - 1.0) * ramp)


def block_offsets(noise, key, block):
    blocks = noise.shape[0] // block
    offset = jax.random.uniform(key, (blocks, 1, noise.shape[2]), jnp.float32, -1.5, 1.5)
    return noise + jnp.repeat(offset, block, axis=0)


def draw_slow_input(key, part):
    key = jax.random.fold_in(key, 11)
    noise_key, field_key = jax.random.split(key)
    noise = jax.random.truncated_normal(noise_key, -4.0, 4.0, (SLOW_FR, PLANE, CS), jnp.float32)
    top = 3.0
    return shape_field(noise, field_key, top, SLOW_DEV).astype(jnp.bfloat16)


def draw_fast_input(key, part):
    key = jax.random.fold_in(key, 23)
    noise_key, field_key = jax.random.split(key)
    noise = jax.random.truncated_normal(noise_key, -4.0, 4.0, (FAST_FR, PLANE, CF), jnp.float32)
    top = 3.0
    return shape_field(noise, field_key, top, ALPHA * SLOW_DEV).astype(jnp.bfloat16)


def draw_slow_cotangent(key, part):
    key = jax.random.fold_in(key, 31)
    noise_key, offset_key = jax.random.split(key)
    noise = jax.random.truncated_normal(noise_key, -4.0, 4.0, (SLOW_FR, PLANE, CS), jnp.float32)
    return block_offsets(noise, offset_key, SLOW_DEV).astype(jnp.bfloat16)


def draw_fast_cotangent(key, part):
    key = jax.random.fold_in(key, 37)
    noise_key, offset_key = jax.random.split(key)
    noise = jax.random.truncated_normal(noise_key, -4.0, 4.0, (FAST_FR, PLANE, CF), jnp.float32)
    return block_offsets(noise, offset_key, ALPHA * SLOW_DEV).astype(jnp.bfloat16)


def profile(count, total, limit, lean):
    portions = [(1 << 20) // math.isqrt(rank ** lean) + 1 for rank in range(2, count + 1)]
    spare, holding = total - limit - (count - 1), [1] * (count - 1)
    while spare > 0:
        movable = [i for i in range(count - 1) if holding[i] < limit]
        pool, left = sum([portions[i] for i in movable]), spare
        for i in movable:
            more = min(limit - holding[i], max(1, left * portions[i] // pool), spare)
            holding[i] = holding[i] + more
            spare = spare - more
    return np.array([limit] + holding)


def uneven_parts(stream_key, count, total, most, slope):
    if count == 2:
        one = jax.random.randint(stream_key, (), max(1, total - most), min(most, total - 1) + 1)
        return jnp.stack([one, total - one])
    lengths = jnp.asarray(profile(count, total, most, slope), jnp.int32)
    couples = (count - 1) // 2
    giver, receiver = lengths[1:1 + 2 * couples:2], lengths[2:2 + 2 * couples:2]
    room = jnp.minimum(giver - 1, most - receiver)
    moved = jax.random.randint(jax.random.fold_in(stream_key, 1), (couples,), 0, 1 << 20) % (room + 1)
    lengths = lengths.at[1:1 + 2 * couples:2].set(giver - moved).at[2:2 + 2 * couples:2].set(receiver + moved)
    return lengths[jax.random.permutation(jax.random.fold_in(stream_key, 2), count)]


def gaussian(rng, dims, scale, bound, held_as=jnp.bfloat16):
    drawn = scale * jax.random.normal(rng, dims, jnp.float32)
    return jnp.clip(drawn, min=-bound, max=bound).astype(held_as)


def setup_inputs(seed: int = 0) -> dict:
    streams_of = jax.random.split(jax.random.key(seed), 15)
    return {
        "slow_input": draw_slow_input(jax.random.fold_in(streams_of[14], 71), 0),
        "fast_input": draw_fast_input(jax.random.fold_in(streams_of[14], 71), 0),
        "clip_ids": jax.vmap(lambda own: jnp.searchsorted(jnp.cumsum(uneven_parts(own, max(1, SLOW_DEV // 2), SLOW_DEV, SLOW_DEV // 2 + 1, 0)), jnp.arange(SLOW_DEV), side="right"))(jax.random.split(streams_of[2], (N_DP * N_REP))).reshape((N_DP * N_REP, SLOW_DEV)).astype(jnp.int32),
        "fast_narrow": gaussian(streams_of[3], (3, BF, CF), (3 * CF) ** -0.5, 0.3125),
        "fast_spatial": gaussian(streams_of[4], (9, BF, BF), (9 * BF) ** -0.5, 0.375),
        "fast_widen": gaussian(streams_of[5], (CF, BF), BF ** -0.5, 1.0),
        "lateral_conv": gaussian(streams_of[6], (5, CL, CF), (5 * CF) ** -0.5, 0.25),
        "slow_narrow": gaussian(streams_of[7], (3, BS, CS + CL), (3 * (CS + CL)) ** -0.5, 0.09375),
        "slow_spatial": gaussian(streams_of[8], (9, BS, BS), (9 * BS) ** -0.5, 0.125),
        "slow_widen": gaussian(streams_of[9], (CS, BS), BS ** -0.5, 0.375),
        "norm_gains": jnp.clip(jax.random.uniform(streams_of[10], (BN_ALL,), jnp.float32, 0.5, 1.5), 0.5, 1.5),
        "norm_biases": gaussian(streams_of[11], (BN_ALL,), 0.5, 2.0, jnp.float32),
        "slow_cotangent": draw_slow_cotangent(jax.random.fold_in(streams_of[14], 71), 0),
        "fast_cotangent": draw_fast_cotangent(jax.random.fold_in(streams_of[14], 71), 0),
    }


@jax.custom_vjp
def low(v):
    return lax.optimization_barrier(v.astype(jnp.bfloat16)).astype(jnp.float32)

@jax.custom_vjp
def low_back(v):
    return v

def low_keep(v):
    return (low(v), None)

def low_pass(kept, grad):
    return (grad,)

def back_keep(v):
    return (v, None)

def back_low(kept, grad):
    return (low(grad),)
low.defvjp(low_keep, low_pass)
low_back.defvjp(back_keep, back_low)
EPS = 1e-05
HIGH = lax.Precision.HIGHEST

def shifted(values, axis, offset):
    if offset == 0:
        return values
    size = values.shape[axis]
    widths = [(0, 0)] * values.ndim
    widths[axis] = (max(-offset, 0), max(offset, 0))
    padded = jnp.pad(values, widths)
    return lax.slice_in_dim(padded, max(offset, 0), max(offset, 0) + size, axis=axis)

def clip_mask(rows, offset):
    size = rows.shape[1]
    padded = jnp.pad(rows, ((0, 0), (max(-offset, 0), max(offset, 0))), constant_values=-1)
    moved = lax.slice_in_dim(padded, max(offset, 0), max(offset, 0) + size, axis=1)
    return (moved == rows).astype(jnp.float32)[:, :, None, None]

def column_mask(plane, side, step):
    column = jnp.arange(plane, dtype=jnp.int32) % side
    inside = (column + step >= 0) & (column + step < side)
    return inside.astype(jnp.float32)[None, None, :, None]

def temporal_taps(values, rows):
    return [shifted(values, 1, offset) * clip_mask(rows, offset) for offset in (-1, 0, 1)]

def spatial_taps(values):
    plane = values.shape[2]
    side = math.isqrt(plane)
    return [shifted(values, 2, row_step * side + col_step) * column_mask(plane, side, col_step) for row_step in (-1, 0, 1) for col_step in (-1, 0, 1)]

def lateral_taps(values, rows):
    frames = rows.shape[1]
    stride = values.shape[1] // frames
    split = values.reshape(values.shape[0], frames, stride, values.shape[2], values.shape[3])
    result = []
    for tap_index in range(5):
        relative = tap_index - 2
        step = relative // stride
        result.append(shifted(split[:, :, relative % stride], 1, step) * clip_mask(rows, step))
    return result

def tap_conv(weight, taps):
    total = jnp.einsum('oc,gtpc->gtpo', weight[0], taps[0], precision=HIGH)
    for tap_index in range(1, len(taps)):
        total = total + jnp.einsum('oc,gtpc->gtpo', weight[tap_index], taps[tap_index], precision=HIGH)
    return total

def grouped(function, values, rows):
    count = values.shape[0]
    group = math.gcd(count, 16)
    blocks = count // group
    moved_values = values.reshape(blocks, group, values.shape[1], values.shape[2], values.shape[3])
    moved_rows = rows.reshape(blocks, group, rows.shape[1])
    outputs = lax.map(jax.checkpoint(lambda pair: function(pair[0], pair[1])), (moved_values, moved_rows))
    return outputs.reshape(count, outputs.shape[2], outputs.shape[3], outputs.shape[4])

def batch_norm(values, gain, bias):
    average = lax.optimization_barrier(jnp.mean(values, axis=(0, 1, 2), keepdims=True))
    spread = lax.optimization_barrier(jnp.mean(values * values, axis=(0, 1, 2), keepdims=True)) - average * average
    return (values - average) * lax.rsqrt(spread + EPS) * gain[None, None, None, :] + bias[None, None, None, :]

def split_channels(vector, widths):
    pieces = []
    start = 0
    for width in widths:
        pieces.append(vector[start:start + width])
        start = start + width
    return pieces

def forward(slow_in, fast_in, fast_narrow, fast_spatial, fast_widen, lateral_conv, slow_narrow, slow_spatial, slow_widen, norm_gains, norm_biases, clip_rows):
    fast_rows = jnp.repeat(clip_rows, fast_in.shape[1] // clip_rows.shape[1], axis=1)
    widths = [fast_narrow.shape[1], fast_spatial.shape[1], fast_widen.shape[0], lateral_conv.shape[1], slow_narrow.shape[1], slow_spatial.shape[1], slow_widen.shape[0]]
    gains = split_channels(norm_gains, widths)
    biases = split_channels(norm_biases, widths)
    fast_low = low(fast_in)
    section = low_back(grouped(lambda part, rows: tap_conv(fast_narrow, temporal_taps(part, rows)), fast_low, fast_rows))
    hidden_fa = low(jax.nn.silu(batch_norm(section, gains[0], biases[0])))
    section = low_back(grouped(lambda part, rows: tap_conv(fast_spatial, spatial_taps(part)), hidden_fa, fast_rows))
    hidden_fb = low(jax.nn.silu(batch_norm(section, gains[1], biases[1])))
    section = low_back(jnp.einsum('oc,gtpc->gtpo', fast_widen, hidden_fb, precision=HIGH))
    fast_out = jax.nn.silu(fast_in + batch_norm(section, gains[2], biases[2]))
    section = low_back(grouped(lambda part, rows: tap_conv(lateral_conv, lateral_taps(part, rows)), fast_low, clip_rows))
    lateral_act = low(jax.nn.silu(batch_norm(section, gains[3], biases[3])))
    joined = jnp.concatenate([low(slow_in), lateral_act], axis=3)
    section = low_back(grouped(lambda part, rows: tap_conv(slow_narrow, temporal_taps(part, rows)), joined, clip_rows))
    hidden_sa = low(jax.nn.silu(batch_norm(section, gains[4], biases[4])))
    section = low_back(grouped(lambda part, rows: tap_conv(slow_spatial, spatial_taps(part)), hidden_sa, clip_rows))
    hidden_sb = low(jax.nn.silu(batch_norm(section, gains[5], biases[5])))
    section = low_back(jnp.einsum('oc,gtpc->gtpo', slow_widen, hidden_sb, precision=HIGH))
    slow_out = jax.nn.silu(slow_in + batch_norm(section, gains[6], biases[6]))
    return (slow_out, fast_out)

def reference(slow_input, fast_input, clip_ids, fast_narrow, fast_spatial, fast_widen, lateral_conv, slow_narrow, slow_spatial, slow_widen, norm_gains, norm_biases, slow_cotangent, fast_cotangent):
    devices = clip_ids.shape[0]

    def regroup(values):
        return values.astype(jnp.float32).reshape(devices, values.shape[0] // devices, values.shape[1], values.shape[2])

    def flatten(values):
        return values.reshape(values.shape[0] * values.shape[1], values.shape[2], values.shape[3])
    primals = (regroup(slow_input), regroup(fast_input), fast_narrow.astype(jnp.float32), fast_spatial.astype(jnp.float32), fast_widen.astype(jnp.float32), lateral_conv.astype(jnp.float32), slow_narrow.astype(jnp.float32), slow_spatial.astype(jnp.float32), slow_widen.astype(jnp.float32), norm_gains.astype(jnp.float32), norm_biases.astype(jnp.float32))
    outputs, pullback = jax.vjp(lambda *params: forward(*params, clip_ids), *primals)
    grads = pullback((regroup(slow_cotangent), regroup(fast_cotangent)))
    scale = 1.0 / math.sqrt(float(SPOS))
    return (flatten(outputs[0]).astype(jnp.bfloat16), flatten(outputs[1]).astype(jnp.bfloat16), flatten(grads[0]).astype(jnp.bfloat16), flatten(grads[1]).astype(jnp.bfloat16), grads[2] * scale, grads[3] * scale, grads[4] * scale, grads[5] * scale, grads[6] * scale, grads[7] * scale, grads[8] * scale, grads[9] * scale, grads[10] * scale)
```

```python
import functools
import math

import jax
import jax.numpy as jnp
from jax import lax
from jax.experimental import pallas as pl
from jax.experimental.pallas import tpu as pltpu
from jax.sharding import PartitionSpec as P

EPS = 1e-05
F32 = jnp.float32
BF16 = jnp.bfloat16
MESH = pl.DeviceIdType.MESH
NN = ((1,), (0,))
NT = ((1,), (1,))
TN = ((0,), (0,))
LANES = 128
ROWS = (8, 8, 8, 16, 24, 8, 8, 8)


def dot(left, right, dims):
    return lax.dot_general(left, right, (dims, ((), ())), preferred_element_type=F32)


def sigmoid(values):
    return 0.5 * jnp.tanh(0.5 * values) + 0.5


def column_sums(values):
    return jnp.sum(values.reshape(values.shape[0] // 8, 8, values.shape[1]), axis=0)


def squash(partial):
    return jnp.sum(partial, axis=0, keepdims=True)


def fold_lanes(values):
    half = values + pltpu.roll(values, 64, 1)
    return half + pltpu.roll(half, 32, 1)


def loop(count, body, init=None):
    if init is None:

        def plain(index, carry):
            body(index)
            return carry

        lax.fori_loop(0, count, plain, 0)
        return None
    return lax.fori_loop(0, count, body, init)


def rows_at(index, size):
    return pl.ds(pl.multiple_of(index * size, 16), size)


def kernel(
    dims,
    xs_h, xf_h, cs_h, cf_h, clip, wfa_h, wfb_h, wfc_h, wl_h, wsa_h, wsb_h, wsc_h, gains_in, biases_in,
    slow_h, fast_h, sgrad_h, fgrad_h, dsa_h, dsb, dsc, dl, dfa, dfb, dfc, dgains, dbiases,
    xs, cs, gsum, xf, cf, big, sec_fc, gsf, hcs, gcs, hcf, gcf,
    sec_lat, sec_sa, sec_sb, dbuf, sec_fa, sec_fb, dbuf_f, jl, hbs, hbf, vx, dsa2,
    wsa, wsb, wsc, wl, wfa_in, wfb_in, wfc_in, wlat, wfa, wfb, wfbk, wfc,
    stage_a, stage_b, gain_rows, bias_rows, near_s, near_l, far_s, far_l, near_send, near_recv, far_send, far_recv, io_sem,
):
    n_dp, n_rep, low, frames, side, slow_count, fast_count, factor = dims
    rows = xs.shape[0]
    half = rows // 2
    band = side * frames
    bands = side
    fband = 4 * band
    cs_n = xs.shape[1]
    bs = wsb.shape[1]

    dp_i, rep_i = lax.axis_index("dp"), lax.axis_index("rep")
    dp_lo, dp_hi = lax.rem(dp_i, low), lax.div(dp_i, low)
    high = n_dp // low
    near_rank = dp_lo * n_rep + rep_i
    near_peers = [
        (dp_hi * low + lax.rem(dp_lo + a, low), lax.rem(rep_i + b, n_rep))
        for a in range(low)
        for b in range(n_rep)
        if a or b
    ]
    far_rank = dp_hi
    far_peers = [(lax.rem(dp_hi + a, high) * low + dp_lo, rep_i) for a in range(1, high)]

    barrier = pltpu.get_barrier_semaphore()
    for peer in near_peers + far_peers:
        pl.semaphore_signal(barrier, inc=1, device_id=peer, device_id_type=MESH)

    loads = {}
    for slot, (name, src, dst) in enumerate([
        ("xf", xf_h, xf), ("wfa", wfa_h, wfa_in), ("wl", wl_h, wl), ("xs", xs_h, xs),
        ("wsa", wsa_h, wsa), ("wfb", wfb_h, wfb_in), ("wfc", wfc_h, wfc_in), ("wsb", wsb_h, wsb),
        ("wsc", wsc_h, wsc), ("cf", cf_h, cf), ("cs", cs_h, cs),
    ]):
        loads[name] = pltpu.make_async_copy(src, dst, io_sem.at[slot])
        loads[name].start()
    stores = []

    def store(src, dst, slot):
        copy = pltpu.make_async_copy(src, dst, io_sem.at[slot])
        copy.start()
        return copy

    slots, counts = [], {8: 0, 24: 0}
    for size in ROWS:
        wide = 8 if size == 8 else 24
        slots.append((near_s, far_s, counts[wide]) if wide == 8 else (near_l, far_l, counts[wide]))
        counts[wide] += 1

    def put(turn, at, vector):
        near, far, slot = slots[turn]
        for piece in range(vector.shape[1] // LANES):
            near[slot, near_rank, pl.ds(at + piece, 1), :] = vector[:, piece * LANES : (piece + 1) * LANES]

    def near_copy(turn, first, count, peer):
        near, far, slot = slots[turn]
        span = near.at[slot, pl.ds(first, count), pl.ds(0, ROWS[turn])]
        return pltpu.make_async_remote_copy(
            src_ref=span, dst_ref=span, send_sem=near_send.at[turn], recv_sem=near_recv.at[turn],
            device_id=peer, device_id_type=MESH,
        )

    def far_copy(turn, first, count, peer):
        near, far, slot = slots[turn]
        span = far.at[slot, pl.ds(first, count), pl.ds(0, ROWS[turn])]
        return pltpu.make_async_remote_copy(
            src_ref=span, dst_ref=span, send_sem=far_send.at[turn], recv_sem=far_recv.at[turn],
            device_id=peer, device_id_type=MESH,
        )

    def exchange_start(turn):
        for peer in near_peers:
            near_copy(turn, near_rank, 1, peer).start()

    def exchange_middle(turn):
        near, far, slot = slots[turn]
        size = ROWS[turn]
        near_copy(turn, 0, len(near_peers), near_peers[0]).wait_recv()
        far[slot, far_rank, pl.ds(0, size), :] = jnp.sum(near[slot, :, pl.ds(0, size), :], axis=0)
        for peer in far_peers:
            far_copy(turn, far_rank, 1, peer).start()

    def exchange_end(turn):
        near, far, slot = slots[turn]
        size = ROWS[turn]
        far_copy(turn, 0, len(far_peers), far_peers[0]).wait_recv()
        total = jnp.sum(far[slot, :, pl.ds(0, size), :], axis=0)
        near_copy(turn, 0, len(near_peers), near_peers[0]).wait_send()
        far_copy(turn, 0, len(far_peers), far_peers[0]).wait_send()
        return total

    def take(total, at, width):
        pieces = [total[at + piece : at + piece + 1, :] for piece in range(width // LANES)]
        return pieces[0] if len(pieces) == 1 else jnp.concatenate(pieces, axis=1)

    def repeat4(vector):
        return jnp.concatenate([vector] * 4, axis=1)

    spots = {"fc": 0, "lat": 1, "sa": 3, "sb": 5, "sc": 7, "fa": 16, "fb": 17}

    lane16 = lax.broadcasted_iota(jnp.int32, (16, LANES), 1)

    def unpack(packed):
        fa = fold_lanes(jnp.where(lane16 // 32 == 0, packed, 0.0))[0:1, :]
        fb = fold_lanes(jnp.where(lane16 // 32 == 1, packed, 0.0))[0:1, :]
        turned = pltpu.roll(packed, 64, 1)
        moved = jnp.where(lane16 < 64, turned, pltpu.roll(turned, 15, 0))
        vectors = {"fa": fa, "fb": fb}
        at = 0
        for name, count in (("fc", 1), ("lat", 2), ("sa", 2), ("sb", 2), ("sc", 8)):
            vectors[name] = take(moved, at, count * LANES)
            at += count
        return vectors

    gains, biases = unpack(gains_in[...]), unpack(biases_in[...])

    def gain(name):
        return gains[name]

    def bias(name):
        return biases[name]

    def moments(total, squares, count):
        mean = total * (1.0 / count)
        return mean, lax.rsqrt(squares * (1.0 / count) - mean * mean + EPS)

    def back_vectors(name, stats, bias_total, gain_total, count):
        mean, scale = stats
        lead = gain(name) * scale
        tilt = lead * scale * gain_total * (1.0 / count)
        level = lead * bias_total * (1.0 / count) - mean * tilt
        return lead, level, tilt

    def report(name, bias_total, gain_total):
        at = spots[name]
        for piece in range(bias_total.shape[1] // LANES):
            lanes = slice(piece * LANES, (piece + 1) * LANES)
            gain_rows[at + piece : at + piece + 1, :] = gain_total[:, lanes]
            bias_rows[at + piece : at + piece + 1, :] = bias_total[:, lanes]

    def before_act(values, stats, name):
        mean, scale = stats
        normed = (values - mean) * scale
        return normed, normed * gain(name) + bias(name)

    def clip_masks(width):
        frame = lax.broadcasted_iota(jnp.int32, (1, 8, width), 1)
        with_prev = jnp.zeros((1, 8, width), F32)
        with_next = jnp.zeros((1, 8, width), F32)
        for t in range(1, frames):
            same = jnp.where(clip[0, t] == clip[0, t - 1], 1.0, 0.0)
            with_prev = jnp.where(frame == t, same, with_prev)
            with_next = jnp.where(frame == t - 1, same, with_next)
        return with_prev, with_next

    def roll_frames(values, mask, step, mask_first):
        grouped = values.reshape(values.shape[0] // 8, 8, values.shape[1])
        if mask_first:
            grouped = grouped * mask
        grouped = pltpu.roll(grouped, step % 8, 1)
        if not mask_first:
            grouped = grouped * mask
        return grouped.reshape(values.shape)

    def spread_columns(target, index, values):
        width = values.shape[1]
        nothing = jnp.zeros((frames, width), F32)
        at = pl.ds(pl.multiple_of((index + 1) * band, 16), band)
        target[at, 0:width] = jnp.concatenate([nothing, values[: band - frames]], axis=0).astype(BF16)
        target[at, width : 2 * width] = values.astype(BF16)
        target[at, 2 * width :] = jnp.concatenate([values[frames:], nothing], axis=0).astype(BF16)

    gain_rows[...] = jnp.zeros(gain_rows.shape, F32)
    bias_rows[...] = jnp.zeros(bias_rows.shape, F32)
    for target in (hcs, gcs, hcf, gcf):
        edge = jnp.zeros((band, target.shape[1]), BF16)
        target[0:band, :] = edge
        target[band + rows : rows + 2 * band, :] = edge

    lane_group = lax.broadcasted_iota(jnp.int32, (LANES, LANES), 1) // 32
    row_group = lax.broadcasted_iota(jnp.int32, (LANES, LANES), 0) // 32
    block_mask = jnp.where(lane_group == row_group, 1.0, 0.0)
    repeat_lanes = jnp.where(
        lax.broadcasted_iota(jnp.int32, (32, LANES), 1) % 32 == lax.broadcasted_iota(jnp.int32, (32, LANES), 0),
        1.0, 0.0,
    ).astype(BF16)

    wfa[...] = jnp.zeros(wfa.shape, BF16)
    loads["wfa"].wait()
    for phase in range(4):
        for k in range(3):
            wfa[32 * phase : 32 * (phase + 1), LANES * (phase + k) : LANES * (phase + k + 1)] = wfa_in[
                32 * k : 32 * (k + 1), :
            ]
    prev128, next128 = clip_masks(128)
    loads["xf"].wait()

    def arrange(i):
        at = rows_at(i, band)
        stage_a[...] = xf[rows_at(i, fband), :].astype(F32)
        phases = [stage_a[pl.ds(phase, band, stride=4), :] for phase in range(4)]
        vx[at, 0:128] = roll_frames(phases[2], prev128, 1, False).astype(BF16)
        vx[at, 128:256] = roll_frames(phases[3], prev128, 1, False).astype(BF16)
        for phase in range(4):
            vx[at, 256 + 128 * phase : 384 + 128 * phase] = phases[phase].astype(BF16)
        vx[at, 768:896] = roll_frames(phases[0], next128, -1, False).astype(BF16)

    loop(bands, arrange)
    loads["wl"].wait()
    for k in range(5):
        wlat[:, LANES * k : LANES * (k + 1)] = wl[bs * k : bs * (k + 1), :]

    def zero2(width):
        return (jnp.zeros((8, width), F32), jnp.zeros((8, width), F32))

    def conv_fa(i, carry):
        at = rows_at(i, half)
        value = dot(vx[at, 128:896], wfa[...], NT)
        sec_fa[at, :] = value
        return carry[0] + column_sums(value), carry[1] + column_sums(value * value)

    def conv_lat(i, carry):
        at = rows_at(i, half)
        value = dot(vx[at, 0:640], wlat[...], NT)
        sec_lat[at, :] = value
        return carry[0] + column_sums(value), carry[1] + column_sums(value * value)

    sum_fa, sq_fa = loop(2, conv_fa, zero2(128))
    sum_lat, sq_lat = loop(2, conv_lat, zero2(256))
    put(0, 0, squash(sum_fa))
    put(0, 1, squash(sq_fa))
    put(0, 2, squash(sum_lat))
    put(0, 4, squash(sq_lat))
    pl.semaphore_wait(barrier, len(near_peers) + len(far_peers))
    exchange_start(0)

    loads["xs"].wait()
    loads["wsa"].wait()

    def narrow_main(i):
        at = rows_at(i, half)
        for k in range(3):
            big[at, bs * k : bs * (k + 1)] = dot(xs[at, :], wsa[bs * k : bs * (k + 1), 0:cs_n], NT)

    loop(2, narrow_main)
    exchange_middle(0)
    loads["wfb"].wait()
    loads["wfc"].wait()
    spread = dot(wfb_in[...], repeat_lanes, NN)
    for a in range(3):
        for b in range(3):
            piece = spread[32 * (3 * a + b) : 32 * (3 * a + b + 1), :]
            block = (jnp.concatenate([piece] * 4, axis=0) * block_mask).astype(BF16)
            wfb[a, :, LANES * b : LANES * (b + 1)] = block
            wfbk[a, LANES * (2 - b) : LANES * (3 - b), :] = block
    widen = dot(wfc_in[...], repeat_lanes, TN)
    for phase in range(4):
        wfc[LANES * phase : LANES * (phase + 1), :] = jnp.where(lane_group == phase, widen, 0.0).astype(BF16)
    total = exchange_end(0)

    fa_rows = fold_lanes(total[0:8, :])
    stats_fa = moments(fa_rows[0:1, :], fa_rows[1:2, :], fast_count)
    stats_lat = moments(take(total, 2, 256), take(total, 4, 256), slow_count)

    def act_fa(i):
        normed, pre = before_act(sec_fa[rows_at(i, band), :], stats_fa, "fa")
        spread_columns(hcf, i, pre * sigmoid(pre))

    def act_lat(i):
        at = rows_at(i, band)
        normed, pre = before_act(sec_lat[at, :], stats_lat, "lat")
        jl[at, :] = (pre * sigmoid(pre)).astype(BF16)

    loop(bands, act_fa)
    loop(bands, act_lat)

    def conv_fb(i, carry):
        value = None
        for a in range(3):
            at = pl.ds(pl.multiple_of(i * half + band * a, 16), half)
            term = dot(hcf[at, :], wfb[a], NT)
            value = term if value is None else value + term
        sec_fb[rows_at(i, half), :] = value
        return carry[0] + column_sums(value), carry[1] + column_sums(value * value)

    sum_fb, sq_fb = loop(2, conv_fb, zero2(128))

    def narrow_lateral(i):
        at = rows_at(i, half)
        for k in range(3):
            big[at, bs * k : bs * (k + 1)] += dot(jl[at, :], wsa[bs * k : bs * (k + 1), cs_n:], NT)

    loop(2, narrow_lateral)
    prev256, next256 = clip_masks(256)

    def combine_sa(i, carry):
        at = rows_at(i, band)
        value = (
            big[at, bs : 2 * bs]
            + roll_frames(big[at, 0:bs], prev256, 1, False)
            + roll_frames(big[at, 2 * bs : 3 * bs], next256, -1, False)
        )
        sec_sa[at, :] = value
        return carry[0] + column_sums(value), carry[1] + column_sums(value * value)

    sum_sa, sq_sa = loop(bands, combine_sa, zero2(256))
    put(1, 0, squash(sum_fb))
    put(1, 1, squash(sq_fb))
    put(1, 2, squash(sum_sa))
    put(1, 4, squash(sq_sa))
    exchange_start(1)
    exchange_middle(1)
    total = exchange_end(1)

    fb_rows = fold_lanes(total[0:8, :])
    stats_fb = moments(fb_rows[0:1, :], fb_rows[1:2, :], fast_count)
    stats_sa = moments(take(total, 2, 256), take(total, 4, 256), slow_count)

    def act_sa(i):
        normed, pre = before_act(sec_sa[rows_at(i, band), :], stats_sa, "sa")
        spread_columns(hcs, i, pre * sigmoid(pre))

    def act_fb(i):
        at = rows_at(i, band)
        normed, pre = before_act(sec_fb[at, :], stats_fb, "fb")
        hbf[at, :] = (pre * sigmoid(pre)).astype(BF16)

    loop(bands, act_sa)
    loads["wsb"].wait()

    def conv_sb(i, carry):
        value = None
        for a in range(3):
            at = pl.ds(pl.multiple_of(i * half + band * a, 16), half)
            for b in range(3):
                tap = 3 * a + b
                term = dot(hcs[at, bs * b : bs * (b + 1)], wsb[bs * tap : bs * (tap + 1), :], NT)
                value = term if value is None else value + term
        sec_sb[rows_at(i, half), :] = value
        return carry[0] + column_sums(value), carry[1] + column_sums(value * value)

    sum_sb, sq_sb = loop(2, conv_sb, zero2(256))
    loop(bands, act_fb)

    def widen_fast(i, carry):
        at = rows_at(i, half)
        value = dot(hbf[at, :], wfc[...], NT)
        sec_fc[at, :] = value
        return carry[0] + column_sums(value), carry[1] + column_sums(value * value)

    sum_fc, sq_fc = loop(2, widen_fast, zero2(512))

    def fold4(vector):
        return vector[:, 0:128] + vector[:, 128:256] + vector[:, 256:384] + vector[:, 384:512]

    put(2, 0, squash(fold4(sum_fc)))
    put(2, 1, squash(fold4(sq_fc)))
    put(2, 2, squash(sum_sb))
    put(2, 4, squash(sq_sb))
    exchange_start(2)
    exchange_middle(2)
    total = exchange_end(2)

    stats_fc = moments(take(total, 0, 128), take(total, 1, 128), fast_count)
    stats_sb = moments(take(total, 2, 256), take(total, 4, 256), slow_count)

    def act_sb(i):
        at = rows_at(i, band)
        normed, pre = before_act(sec_sb[at, :], stats_sb, "sb")
        hbs[at, :] = (pre * sigmoid(pre)).astype(BF16)

    loop(bands, act_sb)
    loads["wsc"].wait()

    def widen_slow(i, carry):
        at = rows_at(i, half)
        value = dot(hbs[at, :], wsc[...], NT)
        big[at, :] = value
        return carry[0] + column_sums(value), carry[1] + column_sums(value * value)

    sum_sc, sq_sc = loop(2, widen_slow, zero2(cs_n))
    put(3, 0, squash(sum_sc))
    put(3, 8, squash(sq_sc))
    exchange_start(3)

    loads["cf"].wait()

    def finish_fast(i, carry):
        at, fat = rows_at(i, band), rows_at(i, fband)
        bias_sum, gain_sum = carry
        stage_b[...] = cf[fat, :].astype(F32)
        for phase in range(4):
            lanes = slice(128 * phase, 128 * (phase + 1))
            mean, scale = stats_fc
            normed = (sec_fc[at, lanes] - mean) * scale
            total_in = vx[at, 256 + 128 * phase : 384 + 128 * phase].astype(F32)
            value = total_in + normed * gain("fc") + bias("fc")
            gate = sigmoid(value)
            stage_a[pl.ds(phase, band, stride=4), :] = value * gate
            grad = stage_b[pl.ds(phase, band, stride=4), :] * (gate * (1.0 + value * (1.0 - gate)))
            gsf[at, lanes] = grad
            bias_sum = bias_sum + column_sums(grad)
            gain_sum = gain_sum + column_sums(grad * normed)
        xf[fat, :] = stage_a[...].astype(BF16)
        return bias_sum, gain_sum

    bias_fc, gain_fc = loop(bands, finish_fast, zero2(128))
    fast_store = store(xf, fast_h, 11)
    exchange_middle(3)
    loads["cs"].wait()
    total = exchange_end(3)

    stats_sc = moments(take(total, 0, cs_n), take(total, 8, cs_n), slow_count)
    thin = 32

    def finish_slow(i, carry):
        at = rows_at(i, thin)
        normed, shift = before_act(big[at, :], stats_sc, "sc")
        value = xs[at, :].astype(F32) + shift
        gate = sigmoid(value)
        grad = cs[at, :].astype(F32) * (gate * (1.0 + value * (1.0 - gate)))
        cs[at, :] = (value * gate).astype(BF16)
        gsum[at, :] = normed.astype(BF16)
        big[at, :] = grad
        return carry[0] + column_sums(grad), carry[1] + column_sums(grad * normed)

    bias_sc, gain_sc = loop(rows // thin, finish_slow, zero2(cs_n))
    slow_store = store(cs, slow_h, 12)
    put(4, 0, squash(bias_sc))
    put(4, 8, squash(gain_sc))
    put(4, 16, squash(bias_fc))
    put(4, 17, squash(gain_fc))
    exchange_start(4)
    exchange_middle(4)
    total = exchange_end(4)

    bias_sc, gain_sc = take(total, 0, cs_n), take(total, 8, cs_n)
    bias_fc, gain_fc = take(total, 16, 128), take(total, 17, 128)
    report("sc", bias_sc, gain_sc)
    report("fc", bias_fc, gain_fc)
    lead_sc = gain("sc") * stats_sc[1]
    level_sc = lead_sc * bias_sc * (1.0 / slow_count)
    tilt_sc = lead_sc * gain_sc * (1.0 / slow_count)
    slow_store.wait()

    def low_sc(i):
        at = rows_at(i, thin)
        grad = big[at, :]
        cs[at, :] = (grad * lead_sc - level_sc - gsum[at, :].astype(F32) * tilt_sc).astype(BF16)
        gsum[at, :] = grad.astype(BF16)

    loop(rows // thin, low_sc)

    def back_sc(i):
        at = rows_at(i, half)
        dbuf[at, :] = dot(cs[at, :], wsc[...], NN)

    loop(2, back_sc)

    def slope_pass(section, stats, name, buffer):
        def step(i, carry):
            at = rows_at(i, band)
            normed, pre = before_act(section[at, :], stats, name)
            gate = sigmoid(pre)
            grad = buffer[at, :] * (gate * (1.0 + pre * (1.0 - gate)))
            buffer[at, :] = grad
            return carry[0] + column_sums(grad), carry[1] + column_sums(grad * normed)

        return loop(bands, step, zero2(section.shape[1]))

    bias_sb, gain_sb = slope_pass(sec_sb, stats_sb, "sb", dbuf)

    mean_fc, scale_fc = stats_fc
    lead_fc = gain("fc") * scale_fc
    tilt_fc = lead_fc * scale_fc * gain_fc * (1.0 / fast_count)
    level_fc = lead_fc * bias_fc * (1.0 / fast_count) - mean_fc * tilt_fc

    def low_fc(i):
        at = rows_at(i, band)
        for phase in range(4):
            lanes = slice(128 * phase, 128 * (phase + 1))
            value = gsf[at, lanes] * lead_fc - level_fc - sec_fc[at, lanes] * tilt_fc
            cf[pl.ds(pl.multiple_of(rows * phase + i * band, 16), band), :] = value.astype(BF16)

    loop(bands, low_fc)

    def back_fc(i):
        value = None
        for phase in range(4):
            at = pl.ds(pl.multiple_of(rows * phase + i * half, 16), half)
            term = dot(cf[at, :], wfc[128 * phase : 128 * (phase + 1), :], NN)
            value = term if value is None else value + term
        dbuf_f[rows_at(i, half), :] = value

    loop(2, back_fc)
    bias_fb, gain_fb = slope_pass(sec_fb, stats_fb, "fb", dbuf_f)
    put(5, 0, squash(bias_fb))
    put(5, 1, squash(gain_fb))
    put(5, 2, squash(bias_sb))
    put(5, 4, squash(gain_sb))
    exchange_start(5)

    dsc[...] = dot(cs[...], hbs[...], TN)
    exchange_middle(5)
    wide = None
    for phase in range(4):
        term = jnp.where(
            lane_group == phase, dot(cf[rows * phase : rows * (phase + 1), :], hbf[...], TN), 0.0
        )
        wide = term if wide is None else wide + term
    dfc[...] = fold_lanes(wide)
    total = exchange_end(5)

    fold_rows = fold_lanes(total[0:8, :])
    bias_fb, gain_fb = fold_rows[0:1, :], fold_rows[1:2, :]
    bias_sb, gain_sb = take(total, 2, 256), take(total, 4, 256)
    report("fb", bias_fb, gain_fb)
    report("sb", bias_sb, gain_sb)
    vec_sb = back_vectors("sb", stats_sb, bias_sb, gain_sb, slow_count)
    vec_fb = back_vectors("fb", stats_fb, bias_fb, gain_fb, fast_count)

    def norm_grad(buffer, section, at, vectors):
        lead, level, tilt = vectors
        return buffer[at, :] * lead - level - section[at, :] * tilt

    def low_sb(i):
        spread_columns(gcs, i, norm_grad(dbuf, sec_sb, rows_at(i, band), vec_sb))

    loop(bands, low_sb)

    def back_sb(i):
        value = None
        for a in range(3):
            at = pl.ds(pl.multiple_of(i * half + band * (2 - a), 16), half)
            for b in range(3):
                tap = 3 * a + b
                term = dot(gcs[at, bs * (2 - b) : bs * (3 - b)], wsb[bs * tap : bs * (tap + 1), :], NN)
                value = term if value is None else value + term
        dbuf[rows_at(i, half), :] = value

    loop(2, back_sb)
    bias_sa, gain_sa = slope_pass(sec_sa, stats_sa, "sa", dbuf)

    def low_fb(i):
        spread_columns(gcf, i, norm_grad(dbuf_f, sec_fb, rows_at(i, band), vec_fb))

    loop(bands, low_fb)

    def back_fb(i):
        value = None
        for a in range(3):
            at = pl.ds(pl.multiple_of(i * half + band * (2 - a), 16), half)
            term = dot(gcf[at, :], wfbk[a], NN)
            value = term if value is None else value + term
        dbuf_f[rows_at(i, half), :] = value

    loop(2, back_fb)
    bias_fa, gain_fa = slope_pass(sec_fa, stats_fa, "fa", dbuf_f)
    put(6, 0, squash(bias_fa))
    put(6, 1, squash(gain_fa))
    put(6, 2, squash(bias_sa))
    put(6, 4, squash(gain_sa))
    exchange_start(6)

    for a in range(3):
        value = dot(gcs[band : band + rows, bs : 2 * bs], hcs[band * a : band * a + rows, :], TN)
        for b in range(3):
            tap = 3 * a + b
            dsb[bs * tap : bs * (tap + 1), :] = value[:, bs * b : bs * (b + 1)]
    exchange_middle(6)
    for a in range(3):
        value = dot(gcf[band : band + rows, 128:256], hcf[band * a : band * a + rows, :], TN)
        for b in range(3):
            tap = 3 * a + b
            block = value[:, 128 * b : 128 * (b + 1)] * block_mask
            piece = block[0:32] + block[32:64] + block[64:96] + block[96:128]
            dfb[32 * tap : 32 * (tap + 1), :] = fold_lanes(piece)
    total = exchange_end(6)

    fold_rows = fold_lanes(total[0:8, :])
    bias_fa, gain_fa = fold_rows[0:1, :], fold_rows[1:2, :]
    bias_sa, gain_sa = take(total, 2, 256), take(total, 4, 256)
    report("fa", bias_fa, gain_fa)
    report("sa", bias_sa, gain_sa)
    vec_sa = back_vectors("sa", stats_sa, bias_sa, gain_sa, slow_count)
    vec_fa = back_vectors("fa", stats_fa, bias_fa, gain_fa, fast_count)

    def low_sa(i):
        at = rows_at(i, band)
        value = norm_grad(dbuf, sec_sa, at, vec_sa)
        gcs[at, 0:bs] = roll_frames(value, prev256, -1, True).astype(BF16)
        gcs[at, bs : 2 * bs] = value.astype(BF16)
        gcs[at, 2 * bs :] = roll_frames(value, next256, 1, True).astype(BF16)

    loop(bands, low_sa)

    def back_lateral(i):
        at = rows_at(i, half)
        dbuf[at, :] = dot(gcs[at, :], wsa[:, cs_n:], NN)

    loop(2, back_lateral)
    bias_lat, gain_lat = slope_pass(sec_lat, stats_lat, "lat", dbuf)
    put(7, 0, squash(bias_lat))
    put(7, 2, squash(gain_lat))
    exchange_start(7)

    for tile in range(cs_n // 256):
        lanes = slice(256 * tile, 256 * (tile + 1))
        big[0 : 3 * bs, lanes] = dot(gcs[0:rows, :], xs[:, lanes], TN)
    dsa2[...] = dot(gcs[0:rows, :], jl[...], TN)
    sa_store = store(big.at[pl.ds(0, 3 * bs)], dsa_h.at[:, pl.ds(0, cs_n)], 13)
    sa2_store = store(dsa2, dsa_h.at[:, pl.ds(cs_n, bs)], 14)
    exchange_middle(7)

    def slow_back(i):
        at = rows_at(i, half)
        for tile in range(cs_n // 256):
            lanes = slice(256 * tile, 256 * (tile + 1))
            value = gsum[at, lanes].astype(F32) + dot(gcs[at, :], wsa[:, lanes], NN)
            gsum[at, lanes] = value.astype(BF16)

    loop(2, slow_back)
    sgrad_store = store(gsum, sgrad_h, 15)

    def low_fa(i):
        at = rows_at(i, band)
        hbf[at, :] = norm_grad(dbuf_f, sec_fa, at, vec_fa).astype(BF16)

    loop(bands, low_fa)
    value = dot(hbf[...], vx[:, 128:896], TN)
    for k in range(3):
        piece = None
        for phase in range(4):
            term = value[32 * phase : 32 * (phase + 1), 128 * (phase + k) : 128 * (phase + k + 1)]
            piece = term if piece is None else piece + term
        dfa[32 * k : 32 * (k + 1), :] = piece
    total = exchange_end(7)

    bias_lat, gain_lat = take(total, 0, 256), take(total, 2, 256)
    report("lat", bias_lat, gain_lat)
    vec_lat = back_vectors("lat", stats_lat, bias_lat, gain_lat, slow_count)

    def low_lat(i):
        at = rows_at(i, band)
        hbs[at, :] = norm_grad(dbuf, sec_lat, at, vec_lat).astype(BF16)

    loop(bands, low_lat)
    value = dot(hbs[...], vx[:, 0:640], TN)
    for k in range(5):
        dl[bs * k : bs * (k + 1), :] = value[:, 128 * k : 128 * (k + 1)]
    fast_store.wait()

    def fast_back(i):
        at, fat = rows_at(i, 2 * band), rows_at(i, 2 * fband)
        conv = dot(hbf[at, :], wfa[...], NN)
        side_in = dot(hbs[at, :], wlat[...], NN)

        def lane(values, block):
            return values[:, 128 * block : 128 * (block + 1)]

        grads = [gsf[at, 128 * phase : 128 * (phase + 1)] + lane(conv, phase + 1) for phase in range(4)]
        grads[0] = grads[0] + roll_frames(lane(conv, 5), next128, 1, True) + lane(side_in, 2)
        grads[1] = grads[1] + lane(side_in, 3)
        grads[2] = grads[2] + lane(side_in, 4) + roll_frames(lane(side_in, 0), prev128, -1, True)
        grads[3] = grads[3] + roll_frames(lane(side_in, 1) + lane(conv, 0), prev128, -1, True)
        for part in range(2):
            for phase in range(4):
                stage_a[pl.ds(phase, band, stride=4), :] = grads[phase][part * band : (part + 1) * band]
            xf[rows_at(2 * i + part, fband), :] = stage_a[...].astype(BF16)

    loop(bands // 2, fast_back)
    fgrad_store = store(xf, fgrad_h, 16)

    def pack(rows_ref, target):
        lanes = lax.broadcasted_iota(jnp.int32, (24, LANES), 1)
        stacked = rows_ref[...]
        turned = pltpu.roll(stacked, 64, 1)
        moved = jnp.where(lanes >= 64, turned, pltpu.roll(turned, 1, 0))[0:16, :]
        first = jnp.where(lane16[0:1, :] < 32, stacked[16:17, :], stacked[17:18, :])
        first = jnp.where(lane16[0:1, :] < 64, first, moved[0:1, :])
        target[...] = moved * factor
        target[0:1, :] = first * factor

    pack(gain_rows, dgains)
    pack(bias_rows, dbiases)
    sa_store.wait()
    sa2_store.wait()
    sgrad_store.wait()
    fgrad_store.wait()


def body(
    slow_input,
    fast_input,
    clip_ids,
    fast_narrow,
    fast_spatial,
    fast_widen,
    lateral_conv,
    slow_narrow,
    slow_spatial,
    slow_widen,
    norm_gains,
    norm_biases,
    slow_cotangent,
    fast_cotangent,
):
    n_dp, n_rep = lax.axis_size("dp"), lax.axis_size("rep")
    low = 2 if n_dp % 2 == 0 else 1
    high = n_dp // low
    frames, plane, channels = slow_input.shape
    fast_frames, _, fast_channels = fast_input.shape
    side = math.isqrt(plane)
    rows = frames * plane
    slow_count = rows * n_dp * n_rep
    fast_count = slow_count * (fast_frames // frames)

    def flat(values):
        return values.transpose(1, 0, 2).reshape(values.shape[0] * values.shape[1], values.shape[2])

    def unflat(values, count):
        return values.reshape(plane, count, values.shape[1]).transpose(1, 0, 2)

    widths = [
        fast_narrow.shape[1], fast_spatial.shape[1], fast_widen.shape[0], lateral_conv.shape[1],
        slow_narrow.shape[1], slow_spatial.shape[1], slow_widen.shape[0],
    ]

    def lay_out(vector):
        return jnp.pad(vector, (0, 16 * LANES - vector.shape[0])).reshape(16, LANES)

    cf = fast_channels
    bs = slow_spatial.shape[1]
    band = side * frames
    any_spec = pl.BlockSpec(memory_space=pl.ANY)
    vmem_spec = pl.BlockSpec(memory_space=pltpu.VMEM)
    small = sum(1 for size in ROWS if size == 8)
    large = len(ROWS) - small
    pad = rows + 2 * band

    def shape(dims, dtype):
        return jax.ShapeDtypeStruct(dims, dtype)

    out_shape = [
        shape((rows, channels), BF16), shape((4 * rows, cf), BF16),
        shape((rows, channels), BF16), shape((4 * rows, cf), BF16),
        shape((3 * bs, channels + bs), F32), shape((9 * bs, bs), F32), shape((channels, bs), F32),
        shape((5 * bs, cf), F32), shape((96, cf), F32), shape((288, 128), F32), shape((cf, 128), F32),
        shape((16, LANES), F32), shape((16, LANES), F32),
    ]
    scratch = [
        pltpu.VMEM((rows, channels), BF16), pltpu.VMEM((rows, channels), BF16),
        pltpu.VMEM((rows, channels), BF16), pltpu.VMEM((4 * rows, cf), BF16),
        pltpu.VMEM((4 * rows, cf), BF16), pltpu.VMEM((rows, channels), F32),
        pltpu.VMEM((rows, 512), F32), pltpu.VMEM((rows, 512), F32),
        pltpu.VMEM((pad, 3 * bs), BF16), pltpu.VMEM((pad, 3 * bs), BF16),
        pltpu.VMEM((pad, 384), BF16), pltpu.VMEM((pad, 384), BF16),
        pltpu.VMEM((rows, bs), F32), pltpu.VMEM((rows, bs), F32), pltpu.VMEM((rows, bs), F32),
        pltpu.VMEM((rows, bs), F32),
        pltpu.VMEM((rows, 128), F32), pltpu.VMEM((rows, 128), F32), pltpu.VMEM((rows, 128), F32),
        pltpu.VMEM((rows, bs), BF16), pltpu.VMEM((rows, bs), BF16), pltpu.VMEM((rows, 128), BF16),
        pltpu.VMEM((rows, 896), BF16), pltpu.VMEM((3 * bs, bs), F32),
        pltpu.VMEM((3 * bs, channels + bs), BF16), pltpu.VMEM((9 * bs, bs), BF16),
        pltpu.VMEM((channels, bs), BF16), pltpu.VMEM((5 * bs, cf), BF16),
        pltpu.VMEM((96, cf), BF16), pltpu.VMEM((288, 32), BF16), pltpu.VMEM((32, cf), BF16),
        pltpu.VMEM((bs, 640), BF16), pltpu.VMEM((128, 768), BF16),
        pltpu.VMEM((3, 128, 384), BF16), pltpu.VMEM((3, 384, 128), BF16), pltpu.VMEM((512, 128), BF16),
        pltpu.VMEM((4 * band, cf), F32), pltpu.VMEM((4 * band, cf), F32),
        pltpu.VMEM((24, LANES), F32), pltpu.VMEM((24, LANES), F32),
        pltpu.VMEM((small, low * n_rep, 8, LANES), F32), pltpu.VMEM((large, low * n_rep, 24, LANES), F32),
        pltpu.VMEM((small, high, 8, LANES), F32), pltpu.VMEM((large, high, 24, LANES), F32),
        pltpu.SemaphoreType.DMA((len(ROWS),)), pltpu.SemaphoreType.DMA((len(ROWS),)),
        pltpu.SemaphoreType.DMA((len(ROWS),)), pltpu.SemaphoreType.DMA((len(ROWS),)),
        pltpu.SemaphoreType.DMA((17,)),
    ]
    factor = 1.0 / math.sqrt(float(slow_count))
    results = pl.pallas_call(
        functools.partial(kernel, (n_dp, n_rep, low, frames, side, float(slow_count), float(fast_count), factor)),
        out_shape=out_shape,
        in_specs=[any_spec] * 4 + [pl.BlockSpec(memory_space=pltpu.SMEM)] + [any_spec] * 7 + [vmem_spec] * 2,
        out_specs=[any_spec] * 5 + [vmem_spec] * 8,
        scratch_shapes=scratch,
        compiler_params=pltpu.CompilerParams(
            collective_id=0, has_side_effects=True, vmem_limit_bytes=63 * 2**20
        ),
    )(
        flat(slow_input), flat(fast_input), flat(slow_cotangent), flat(fast_cotangent), clip_ids,
        fast_narrow.reshape(-1, cf), fast_spatial.reshape(-1, 32), fast_widen.T,
        lateral_conv.reshape(-1, cf), slow_narrow.reshape(3 * bs, -1), slow_spatial.reshape(9 * bs, bs),
        slow_widen, lay_out(norm_gains), lay_out(norm_biases),
    )
    slow_out, fast_out, slow_grad, fast_grad, dsa, dsb, dsc, dl, dfa, dfb, dfc, dgains, dbiases = results
    dsa, dsb, dsc, dl, dfa, dfb, dfc = lax.psum(
        (dsa, dsb, dsc, dl, dfa, dfb[:, 0:32], dfc[:, 0:32]), ("dp", "rep")
    )

    def gather(packed):
        return packed.reshape(16 * LANES)[0 : sum(widths)]

    return (
        unflat(slow_out, frames),
        unflat(fast_out, fast_frames),
        unflat(slow_grad, frames),
        unflat(fast_grad, fast_frames),
        (dfa * factor).reshape(fast_narrow.shape),
        (dfb * factor).reshape(fast_spatial.shape),
        dfc * factor,
        (dl * factor).reshape(lateral_conv.shape),
        (dsa * factor).reshape(slow_narrow.shape),
        (dsb * factor).reshape(slow_spatial.shape),
        dsc * factor,
        gather(dgains),
        gather(dbiases),
    )


def solution(mesh):
    sharded = P(("dp", "rep"), None, None)
    return jax.shard_map(
        body,
        mesh=mesh,
        in_specs=(sharded, sharded, P(("dp", "rep"), None)) + (P(),) * 9 + (sharded, sharded),
        out_specs=(sharded,) * 4 + (P(),) * 9,
        check_vma=False,
    )
```

```python
import functools
import math

import jax
import jax.numpy as jnp
from jax import lax
from jax.experimental import pallas as pl
from jax.experimental.pallas import tpu as pltpu
from jax.sharding import PartitionSpec as P

EPS = 1e-05
F32 = jnp.float32
BF16 = jnp.bfloat16
MESH = pl.DeviceIdType.MESH
NN = ((1,), (0,))
NT = ((1,), (1,))
TN = ((0,), (0,))
LANES = 128
ROWS = (8, 8, 8, 16, 24, 8, 8, 8)


def dot(left, right, dims):
    return lax.dot_general(left, right, (dims, ((), ())), preferred_element_type=F32)


def sigmoid(values):
    return 0.5 * jnp.tanh(0.5 * values) + 0.5


def column_sums(values):
    return jnp.sum(values.reshape(values.shape[0] // 8, 8, values.shape[1]), axis=0)


def squash(partial):
    return jnp.sum(partial, axis=0, keepdims=True)


def fold_lanes(values):
    half = values + pltpu.roll(values, 64, 1)
    return half + pltpu.roll(half, 32, 1)


def loop(count, body, init=None):
    if init is None:

        def plain(index, carry):
            body(index)
            return carry

        lax.fori_loop(0, count, plain, 0)
        return None
    return lax.fori_loop(0, count, body, init)


def rows_at(index, size):
    return pl.ds(pl.multiple_of(index * size, 16), size)


def kernel(
    dims,
    xs_h, xf_h, cs_h, cf_h, clip, wfa_h, wfb_h, wfc_h, wl_h, wsa_h, wsb_h, wsc_h, gains_in, biases_in,
    slow_h, fast_h, sgrad_h, fgrad_h, dsa_h, dsb_h, dsc_h, dl_h, dfa, dfb, dfc, dgains, dbiases, extra_h,
    xs, cs, gsum, xf, cf, big, sec_fc, gsf, hcs, gcs, hcf, gcf,
    sec_lat, sec_sa, sec_sb, dbuf, sec_fa, sec_fb, dbuf_f, jl, hbs, hbf, vx, slab, slab_sc, summed, gathered,
    wsa, wsb, wsc, wfa_in, wfb_in, wfc_in, wlat, wfa, wfb, wfbk, wfc,
    stage_a, stage_b, gain_rows, bias_rows, near_s, near_l, far_s, far_l, near_send, near_recv, far_send, far_recv, io_sem, own_sem, big_send, big_recv,
):
    n_dp, n_rep, low, frames, side, slow_count, fast_count, factor = dims
    rows = xs.shape[0]
    half = rows // 2
    band = side * frames
    bands = side
    fband = 4 * band
    cs_n = xs.shape[1]
    bs = wsb.shape[1]

    dp_i, rep_i = lax.axis_index("dp"), lax.axis_index("rep")
    dp_lo, dp_hi = lax.rem(dp_i, low), lax.div(dp_i, low)
    high = n_dp // low
    near_rank = dp_lo * n_rep + rep_i
    near_peers = [
        (dp_hi * low + lax.rem(dp_lo + a, low), lax.rem(rep_i + b, n_rep))
        for a in range(low)
        for b in range(n_rep)
        if a or b
    ]
    far_rank = dp_hi
    far_peers = [(lax.rem(dp_hi + a, high) * low + dp_lo, rep_i) for a in range(1, high)]

    c, x = lax.rem(rep_i, 2), lax.div(rep_i, 2)
    y, z = dp_lo, lax.rem(dp_hi, 4)
    outer, outers = lax.div(dp_hi, 4), high // 4
    core_peer = (dp_i, 2 * x + 1 - c)
    x_peer = (dp_i, 2 * (1 - x) + c)
    y_peer = (dp_hi * low + 1 - y, rep_i)
    z_peers = [((outer * 4 + lax.rem(z + k, 4)) * low + y, rep_i) for k in range(1, 4)]
    outer_peers = [((lax.rem(outer + k, outers) * 4 + z) * low + y, rep_i) for k in range(1, outers)]

    barrier = pltpu.get_barrier_semaphore()
    for peer in near_peers + far_peers:
        pl.semaphore_signal(barrier, inc=1, device_id=peer, device_id_type=MESH)

    loads = {}
    for slot, (name, src, dst) in enumerate([
        ("xf", xf_h, xf), ("wfa", wfa_h, wfa_in), ("xs", xs_h, xs),
        ("wsa", wsa_h, wsa), ("wfb", wfb_h, wfb_in), ("wfc", wfc_h, wfc_in), ("wsb", wsb_h, wsb),
        ("wsc", wsc_h, wsc), ("cf", cf_h, cf), ("cs", cs_h, cs),
    ]):
        loads[name] = pltpu.make_async_copy(src, dst, io_sem.at[slot])
        loads[name].start()
        if name == "wfa":
            taps = [
                pltpu.make_async_copy(
                    wl_h.at[pl.ds(bs * k, bs)], wlat.at[:, pl.ds(LANES * k, LANES)], io_sem.at[27 + k]
                )
                for k in range(5)
            ]
            for tap in taps:
                tap.start()
    stores = []

    def store(src, dst, slot):
        copy = pltpu.make_async_copy(src, dst, io_sem.at[slot])
        copy.start()
        return copy

    slots, counts = [], {8: 0, 24: 0}
    for size in ROWS:
        wide = 8 if size == 8 else 24
        slots.append((near_s, far_s, counts[wide]) if wide == 8 else (near_l, far_l, counts[wide]))
        counts[wide] += 1

    def put(turn, at, vector):
        near, far, slot = slots[turn]
        for piece in range(vector.shape[1] // LANES):
            near[slot, near_rank, pl.ds(at + piece, 1), :] = vector[:, piece * LANES : (piece + 1) * LANES]

    def near_copy(turn, first, count, peer):
        near, far, slot = slots[turn]
        span = near.at[slot, pl.ds(first, count), pl.ds(0, ROWS[turn])]
        return pltpu.make_async_remote_copy(
            src_ref=span, dst_ref=span, send_sem=near_send.at[turn], recv_sem=near_recv.at[turn],
            device_id=peer, device_id_type=MESH,
        )

    def far_copy(turn, first, count, peer):
        near, far, slot = slots[turn]
        span = far.at[slot, pl.ds(first, count), pl.ds(0, ROWS[turn])]
        return pltpu.make_async_remote_copy(
            src_ref=span, dst_ref=span, send_sem=far_send.at[turn], recv_sem=far_recv.at[turn],
            device_id=peer, device_id_type=MESH,
        )

    def exchange_start(turn):
        for peer in near_peers:
            near_copy(turn, near_rank, 1, peer).start()

    def exchange_middle(turn):
        near, far, slot = slots[turn]
        size = ROWS[turn]
        near_copy(turn, 0, len(near_peers), near_peers[0]).wait_recv()
        far[slot, far_rank, pl.ds(0, size), :] = jnp.sum(near[slot, :, pl.ds(0, size), :], axis=0)
        for peer in far_peers:
            far_copy(turn, far_rank, 1, peer).start()

    def exchange_end(turn):
        near, far, slot = slots[turn]
        size = ROWS[turn]
        far_copy(turn, 0, len(far_peers), far_peers[0]).wait_recv()
        total = jnp.sum(far[slot, :, pl.ds(0, size), :], axis=0)
        near_copy(turn, 0, len(near_peers), near_peers[0]).wait_send()
        far_copy(turn, 0, len(far_peers), far_peers[0]).wait_send()
        return total

    def take(total, at, width):
        pieces = [total[at + piece : at + piece + 1, :] for piece in range(width // LANES)]
        return pieces[0] if len(pieces) == 1 else jnp.concatenate(pieces, axis=1)

    def repeat4(vector):
        return jnp.concatenate([vector] * 4, axis=1)

    pieces = {}

    def add_piece(name, ref, lane, size, index):
        pieces[name] = {"name": name, "ref": ref, "lane": lane, "size": size, "index": index, "step": 0}

    for k in range(2):
        add_piece("sb%d" % k, sec_fc, 256 * k, 768, k)
    for k in range(4):
        add_piece("sa%d" % k, big, 256 * k, 768, 2 + k)
    add_piece("sb2", slab.at[0], 0, 768, 6)
    add_piece("sa4", slab.at[1], 0, 768, 7)
    add_piece("lt", slab.at[2], 0, 768, 8)
    add_piece("sc", slab_sc, 0, 1024, 9)

    def span(piece, start, count, lane=0, width=256):
        return piece["ref"].at[pl.ds(pl.multiple_of(start, 8), count), pl.ds(piece["lane"] + lane, width)]

    def send(piece, step, src, dst, peer):
        pltpu.make_async_remote_copy(
            src_ref=src, dst_ref=dst, send_sem=big_send.at[piece["index"], step],
            recv_sem=big_recv.at[piece["index"], step], device_id=peer, device_id_type=MESH,
        ).start()

    def result(piece, start, count, lane=0, width=256):
        name = piece["name"]
        start = pl.multiple_of(start, 8)
        if name == "lt":
            return summed.at[pl.ds(start, count), pl.ds(lane, width)]
        if name == "sc":
            return dsc_h.at[pl.ds(start, count), pl.ds(lane, width)]
        k = int(name[2])
        if name[1] == "a":
            return dsa_h.at[pl.ds(start, count), pl.ds(256 * k + lane, width)]
        return dsb_h.at[pl.ds(768 * k + start, count), pl.ds(lane, width)]

    def own_copies(piece, a, b, t):
        sem = own_sem.at[piece["index"]]
        return (
            pltpu.make_async_copy(span(piece, a, t, 0, 128), result(piece, a, t, 0, 128), sem.at[0]),
            pltpu.make_async_copy(span(piece, b, t, 128, 128), result(piece, b, t, 128, 128), sem.at[1]),
        )

    def arrived(piece, step, rows_in):
        block = span(piece, 0, rows_in) if step < 4 else result(piece, 0, rows_in)
        copy = pltpu.make_async_remote_copy(
            src_ref=block, dst_ref=block, send_sem=big_send.at[piece["index"], step],
            recv_sem=big_recv.at[piece["index"], step], device_id=core_peer, device_id_type=MESH,
        )
        copy.wait_recv()
        copy.wait_send()

    def add_rows(piece, target, source, count, lane, width):
        lanes = pl.ds(piece["lane"] + lane, width)
        chunk = piece["size"] // 32
        ref = piece["ref"]

        def step(i):
            into = pl.ds(pl.multiple_of(target + i * chunk, 8), chunk)
            ref[into, lanes] = ref[into, lanes] + ref[pl.ds(pl.multiple_of(source + i * chunk, 8), chunk), lanes]

        loop(count // chunk, step)

    order = ["sc", "sb0", "sb1", "sb2", "sa0", "sa1", "sa2", "sa3", "sa4", "lt"]

    def unpack_small():
        stores.append(store(summed.at[:, pl.ds(0, 128)], dl_h.at[pl.ds(0, 768)], 16))
        stores.append(store(summed.at[pl.ds(0, 512), pl.ds(128, 128)], dl_h.at[pl.ds(768, 512)], 17))
        dfa[...] = summed[512:608, 128:256]
        for tap in range(9):
            at = 608 + 32 * (tap // 4)
            block = summed[at : at + 32, 128:256]
            dfb[32 * tap : 32 * (tap + 1), :] = block[:, 32 * (tap % 4) : 32 * (tap % 4 + 1)]
        dfc[...] = summed[704:736, 128:256]

    def advance(name):
        piece = pieces[name]
        size, step = piece["size"], piece["step"]
        piece["step"] = step + 1
        h, q, o, t = size // 2, size // 4, size // 8, size // 32
        mine = c * h
        a1, a1o = mine + x * q, mine + (1 - x) * q
        b1, b1o = mine + y * q, mine + (1 - y) * q
        a2, a2o = a1 + y * o, a1 + (1 - y) * o
        b2, b2o = b1 + x * o, b1 + (1 - x) * o
        from_core, from_one, from_two = size, size + h, size + h + q
        from_z = size + h + q + o
        if step == 0:
            send(piece, 0, span(piece, (1 - c) * h, h), span(piece, from_core, h), core_peer)
        elif step == 1:
            arrived(piece, 0, h)
            add_rows(piece, mine, from_core, h, 0, 256)
            send(piece, 1, span(piece, a1o, q, 0, 128), span(piece, from_one, q, 0, 128), x_peer)
            send(piece, 1, span(piece, b1o, q, 128, 128), span(piece, from_one, q, 128, 128), y_peer)
        elif step == 2:
            arrived(piece, 1, q)
            add_rows(piece, a1, from_one, q, 0, 128)
            add_rows(piece, b1, from_one, q, 128, 128)
            send(piece, 2, span(piece, a2o, o, 0, 128), span(piece, from_two, o, 0, 128), y_peer)
            send(piece, 2, span(piece, b2o, o, 128, 128), span(piece, from_two, o, 128, 128), x_peer)
        elif step == 3:
            arrived(piece, 2, o)
            add_rows(piece, a2, from_two, o, 0, 128)
            add_rows(piece, b2, from_two, o, 128, 128)
            for k, peer in enumerate(z_peers):
                at, into = lax.rem(z + k + 1, 4) * t, from_z + k * t
                send(piece, 3, span(piece, a2 + at, t, 0, 128), span(piece, into, t, 0, 128), peer)
                send(piece, 3, span(piece, b2 + at, t, 128, 128), span(piece, into, t, 128, 128), peer)
        elif step == 4:
            arrived(piece, 3, 3 * t)
            ref, lane = piece["ref"], piece["lane"]
            own_a = (pl.ds(pl.multiple_of(a2 + z * t, 8), t), pl.ds(lane, 128))
            own_b = (pl.ds(pl.multiple_of(b2 + z * t, 8), t), pl.ds(lane + 128, 128))
            both = jnp.concatenate([ref[own_a], ref[own_b]], axis=1)
            for k in range(3):
                both = both + ref[pl.ds(from_z + k * t, t), pl.ds(lane, 256)]
            if outers > 1:
                index = piece["index"]
                held = span(piece, from_z, t)
                ref[pl.ds(from_z, t), pl.ds(lane, 256)] = both
                for peer in outer_peers:
                    send(piece, 8, held, extra_h.at[index, outer, pl.ds(0, t)], peer)
                block = extra_h.at[index, pl.ds(0, outers - 1), pl.ds(0, t)]
                copy = pltpu.make_async_remote_copy(
                    src_ref=block, dst_ref=block, send_sem=big_send.at[index, 8], recv_sem=big_recv.at[index, 8],
                    device_id=core_peer, device_id_type=MESH,
                )
                copy.wait_recv()
                copy.wait_send()
                for src, dst in (
                    (held, extra_h.at[index, outer, pl.ds(0, t)]),
                    (extra_h.at[index], gathered),
                ):
                    copy = pltpu.make_async_copy(src, dst, own_sem.at[index, 0])
                    copy.start()
                    copy.wait()
                both = jnp.sum(gathered[:, pl.ds(0, t), :], axis=0)
            both = both * factor
            ref[own_a] = both[:, 0:128]
            ref[own_b] = both[:, 128:256]
            own = (a2 + z * t, 0), (b2 + z * t, 128)
            for peer in z_peers:
                for at, half_lanes in own:
                    send(piece, 4, span(piece, at, t, half_lanes, 128), result(piece, at, t, half_lanes, 128), peer)
            for copy in own_copies(piece, own[0][0], own[1][0], t):
                copy.start()
        elif step == 5:
            arrived(piece, 4, 3 * t)
            for copy in own_copies(piece, a2 + z * t, b2 + z * t, t):
                copy.wait()
            block = result(piece, a2, o, 0, 128)
            send(piece, 5, block, block, y_peer)
            block = result(piece, b2, o, 128, 128)
            send(piece, 5, block, block, x_peer)
        elif step == 6:
            arrived(piece, 5, o)
            block = result(piece, a1, q, 0, 128)
            send(piece, 6, block, block, x_peer)
            block = result(piece, b1, q, 128, 128)
            send(piece, 6, block, block, y_peer)
        elif step == 7:
            arrived(piece, 6, q)
            block = result(piece, mine, h)
            send(piece, 7, block, block, core_peer)
        elif step == 8:
            arrived(piece, 7, h)
            if name == "lt":
                unpack_small()

    spots = {"fc": 0, "lat": 1, "sa": 3, "sb": 5, "sc": 7, "fa": 16, "fb": 17}

    lane16 = lax.broadcasted_iota(jnp.int32, (16, LANES), 1)

    def unpack(packed):
        fa = fold_lanes(jnp.where(lane16 // 32 == 0, packed, 0.0))[0:1, :]
        fb = fold_lanes(jnp.where(lane16 // 32 == 1, packed, 0.0))[0:1, :]
        turned = pltpu.roll(packed, 64, 1)
        moved = jnp.where(lane16 < 64, turned, pltpu.roll(turned, 15, 0))
        vectors = {"fa": fa, "fb": fb}
        at = 0
        for name, count in (("fc", 1), ("lat", 2), ("sa", 2), ("sb", 2), ("sc", 8)):
            vectors[name] = take(moved, at, count * LANES)
            at += count
        return vectors

    gains, biases = unpack(gains_in[...]), unpack(biases_in[...])

    def gain(name):
        return gains[name]

    def bias(name):
        return biases[name]

    def moments(total, squares, count):
        mean = total * (1.0 / count)
        return mean, lax.rsqrt(squares * (1.0 / count) - mean * mean + EPS)

    def back_vectors(name, stats, bias_total, gain_total, count):
        mean, scale = stats
        lead = gain(name) * scale
        tilt = lead * scale * gain_total * (1.0 / count)
        level = lead * bias_total * (1.0 / count) - mean * tilt
        return lead, level, tilt

    def report(name, bias_total, gain_total):
        at = spots[name]
        for piece in range(bias_total.shape[1] // LANES):
            lanes = slice(piece * LANES, (piece + 1) * LANES)
            gain_rows[at + piece : at + piece + 1, :] = gain_total[:, lanes]
            bias_rows[at + piece : at + piece + 1, :] = bias_total[:, lanes]

    def before_act(values, stats, name):
        mean, scale = stats
        normed = (values - mean) * scale
        return normed, normed * gain(name) + bias(name)

    def clip_masks(width):
        frame = lax.broadcasted_iota(jnp.int32, (1, 8, width), 1)
        with_prev = jnp.zeros((1, 8, width), F32)
        with_next = jnp.zeros((1, 8, width), F32)
        for t in range(1, frames):
            same = jnp.where(clip[0, t] == clip[0, t - 1], 1.0, 0.0)
            with_prev = jnp.where(frame == t, same, with_prev)
            with_next = jnp.where(frame == t - 1, same, with_next)
        return with_prev, with_next

    def roll_frames(values, mask, step, mask_first):
        grouped = values.reshape(values.shape[0] // 8, 8, values.shape[1])
        if mask_first:
            grouped = grouped * mask
        grouped = pltpu.roll(grouped, step % 8, 1)
        if not mask_first:
            grouped = grouped * mask
        return grouped.reshape(values.shape)

    def spread_columns(target, index, values):
        width = values.shape[1]
        nothing = jnp.zeros((frames, width), F32)
        at = pl.ds(pl.multiple_of((index + 1) * band, 16), band)
        target[at, 0:width] = jnp.concatenate([nothing, values[: band - frames]], axis=0).astype(BF16)
        target[at, width : 2 * width] = values.astype(BF16)
        target[at, 2 * width :] = jnp.concatenate([values[frames:], nothing], axis=0).astype(BF16)

    gain_rows[...] = jnp.zeros(gain_rows.shape, F32)
    bias_rows[...] = jnp.zeros(bias_rows.shape, F32)
    for target in (hcs, gcs, hcf, gcf):
        edge = jnp.zeros((band, target.shape[1]), BF16)
        target[0:band, :] = edge
        target[band + rows : rows + 2 * band, :] = edge

    lane_group = lax.broadcasted_iota(jnp.int32, (LANES, LANES), 1) // 32
    row_group = lax.broadcasted_iota(jnp.int32, (LANES, LANES), 0) // 32
    block_mask = jnp.where(lane_group == row_group, 1.0, 0.0)
    repeat_lanes = jnp.where(
        lax.broadcasted_iota(jnp.int32, (32, LANES), 1) % 32 == lax.broadcasted_iota(jnp.int32, (32, LANES), 0),
        1.0, 0.0,
    ).astype(BF16)

    wfa[...] = jnp.zeros(wfa.shape, BF16)
    loads["wfa"].wait()
    for phase in range(4):
        for k in range(3):
            wfa[32 * phase : 32 * (phase + 1), LANES * (phase + k) : LANES * (phase + k + 1)] = wfa_in[
                32 * k : 32 * (k + 1), :
            ]
    prev128, next128 = clip_masks(128)
    loads["xf"].wait()

    def arrange(i):
        at = rows_at(i, band)
        stage_a[...] = xf[rows_at(i, fband), :].astype(F32)
        phases = [stage_a[pl.ds(phase, band, stride=4), :] for phase in range(4)]
        vx[at, 0:128] = roll_frames(phases[2], prev128, 1, False).astype(BF16)
        vx[at, 128:256] = roll_frames(phases[3], prev128, 1, False).astype(BF16)
        for phase in range(4):
            vx[at, 256 + 128 * phase : 384 + 128 * phase] = phases[phase].astype(BF16)
        vx[at, 768:896] = roll_frames(phases[0], next128, -1, False).astype(BF16)

    loop(bands, arrange)
    for tap in taps:
        tap.wait()

    def zero2(width):
        return (jnp.zeros((8, width), F32), jnp.zeros((8, width), F32))

    def conv_fa(i, carry):
        at = rows_at(i, half)
        value = dot(vx[at, 128:896], wfa[...], NT)
        sec_fa[at, :] = value
        return carry[0] + column_sums(value), carry[1] + column_sums(value * value)

    def conv_lat(i, carry):
        at = rows_at(i, half)
        value = dot(vx[at, 0:640], wlat[...], NT)
        sec_lat[at, :] = value
        return carry[0] + column_sums(value), carry[1] + column_sums(value * value)

    sum_fa, sq_fa = loop(2, conv_fa, zero2(128))
    sum_lat, sq_lat = loop(2, conv_lat, zero2(256))
    put(0, 0, squash(sum_fa))
    put(0, 1, squash(sq_fa))
    put(0, 2, squash(sum_lat))
    put(0, 4, squash(sq_lat))
    pl.semaphore_wait(barrier, len(near_peers) + len(far_peers))
    exchange_start(0)

    loads["xs"].wait()
    loads["wsa"].wait()

    def narrow_main(i):
        at = rows_at(i, half)
        for k in range(3):
            big[at, bs * k : bs * (k + 1)] = dot(xs[at, :], wsa[bs * k : bs * (k + 1), 0:cs_n], NT)

    loop(2, narrow_main)
    exchange_middle(0)
    loads["wfb"].wait()
    loads["wfc"].wait()
    spread = dot(wfb_in[...], repeat_lanes, NN)
    for a in range(3):
        for b in range(3):
            piece = spread[32 * (3 * a + b) : 32 * (3 * a + b + 1), :]
            block = (jnp.concatenate([piece] * 4, axis=0) * block_mask).astype(BF16)
            wfb[a, :, LANES * b : LANES * (b + 1)] = block
            wfbk[a, LANES * (2 - b) : LANES * (3 - b), :] = block
    widen = dot(wfc_in[...], repeat_lanes, TN)
    for phase in range(4):
        wfc[LANES * phase : LANES * (phase + 1), :] = jnp.where(lane_group == phase, widen, 0.0).astype(BF16)
    total = exchange_end(0)

    fa_rows = fold_lanes(total[0:8, :])
    stats_fa = moments(fa_rows[0:1, :], fa_rows[1:2, :], fast_count)
    stats_lat = moments(take(total, 2, 256), take(total, 4, 256), slow_count)

    def act_fa(i):
        normed, pre = before_act(sec_fa[rows_at(i, band), :], stats_fa, "fa")
        spread_columns(hcf, i, pre * sigmoid(pre))

    def act_lat(i):
        at = rows_at(i, band)
        normed, pre = before_act(sec_lat[at, :], stats_lat, "lat")
        jl[at, :] = (pre * sigmoid(pre)).astype(BF16)

    loop(bands, act_fa)
    loop(bands, act_lat)

    def conv_fb(i, carry):
        value = None
        for a in range(3):
            at = pl.ds(pl.multiple_of(i * half + band * a, 16), half)
            term = dot(hcf[at, :], wfb[a], NT)
            value = term if value is None else value + term
        sec_fb[rows_at(i, half), :] = value
        return carry[0] + column_sums(value), carry[1] + column_sums(value * value)

    sum_fb, sq_fb = loop(2, conv_fb, zero2(128))

    def narrow_lateral(i):
        at = rows_at(i, half)
        for k in range(3):
            big[at, bs * k : bs * (k + 1)] += dot(jl[at, :], wsa[bs * k : bs * (k + 1), cs_n:], NT)

    loop(2, narrow_lateral)
    prev256, next256 = clip_masks(256)

    def combine_sa(i, carry):
        at = rows_at(i, band)
        value = (
            big[at, bs : 2 * bs]
            + roll_frames(big[at, 0:bs], prev256, 1, False)
            + roll_frames(big[at, 2 * bs : 3 * bs], next256, -1, False)
        )
        sec_sa[at, :] = value
        return carry[0] + column_sums(value), carry[1] + column_sums(value * value)

    sum_sa, sq_sa = loop(bands, combine_sa, zero2(256))
    put(1, 0, squash(sum_fb))
    put(1, 1, squash(sq_fb))
    put(1, 2, squash(sum_sa))
    put(1, 4, squash(sq_sa))
    exchange_start(1)
    exchange_middle(1)
    total = exchange_end(1)

    fb_rows = fold_lanes(total[0:8, :])
    stats_fb = moments(fb_rows[0:1, :], fb_rows[1:2, :], fast_count)
    stats_sa = moments(take(total, 2, 256), take(total, 4, 256), slow_count)

    def act_sa(i):
        normed, pre = before_act(sec_sa[rows_at(i, band), :], stats_sa, "sa")
        spread_columns(hcs, i, pre * sigmoid(pre))

    def act_fb(i):
        at = rows_at(i, band)
        normed, pre = before_act(sec_fb[at, :], stats_fb, "fb")
        hbf[at, :] = (pre * sigmoid(pre)).astype(BF16)

    loop(bands, act_sa)
    loads["wsb"].wait()

    def conv_sb(i, carry):
        value = None
        for a in range(3):
            at = pl.ds(pl.multiple_of(i * half + band * a, 16), half)
            for b in range(3):
                tap = 3 * a + b
                term = dot(hcs[at, bs * b : bs * (b + 1)], wsb[bs * tap : bs * (tap + 1), :], NT)
                value = term if value is None else value + term
        sec_sb[rows_at(i, half), :] = value
        return carry[0] + column_sums(value), carry[1] + column_sums(value * value)

    sum_sb, sq_sb = loop(2, conv_sb, zero2(256))
    loop(bands, act_fb)

    def widen_fast(i, carry):
        at = rows_at(i, half)
        value = dot(hbf[at, :], wfc[...], NT)
        sec_fc[at, :] = value
        return carry[0] + column_sums(value), carry[1] + column_sums(value * value)

    sum_fc, sq_fc = loop(2, widen_fast, zero2(512))

    def fold4(vector):
        return vector[:, 0:128] + vector[:, 128:256] + vector[:, 256:384] + vector[:, 384:512]

    put(2, 0, squash(fold4(sum_fc)))
    put(2, 1, squash(fold4(sq_fc)))
    put(2, 2, squash(sum_sb))
    put(2, 4, squash(sq_sb))
    exchange_start(2)
    exchange_middle(2)
    total = exchange_end(2)

    stats_fc = moments(take(total, 0, 128), take(total, 1, 128), fast_count)
    stats_sb = moments(take(total, 2, 256), take(total, 4, 256), slow_count)

    def act_sb(i):
        at = rows_at(i, band)
        normed, pre = before_act(sec_sb[at, :], stats_sb, "sb")
        hbs[at, :] = (pre * sigmoid(pre)).astype(BF16)

    loop(bands, act_sb)
    loads["wsc"].wait()

    def widen_slow(i, carry):
        at = rows_at(i, half)
        value = dot(hbs[at, :], wsc[...], NT)
        big[at, :] = value
        return carry[0] + column_sums(value), carry[1] + column_sums(value * value)

    sum_sc, sq_sc = loop(2, widen_slow, zero2(cs_n))
    put(3, 0, squash(sum_sc))
    put(3, 8, squash(sq_sc))
    exchange_start(3)

    loads["cf"].wait()

    def finish_fast(i, carry):
        at, fat = rows_at(i, band), rows_at(i, fband)
        bias_sum, gain_sum = carry
        stage_b[...] = cf[fat, :].astype(F32)
        for phase in range(4):
            lanes = slice(128 * phase, 128 * (phase + 1))
            mean, scale = stats_fc
            normed = (sec_fc[at, lanes] - mean) * scale
            total_in = vx[at, 256 + 128 * phase : 384 + 128 * phase].astype(F32)
            value = total_in + normed * gain("fc") + bias("fc")
            gate = sigmoid(value)
            stage_a[pl.ds(phase, band, stride=4), :] = value * gate
            grad = stage_b[pl.ds(phase, band, stride=4), :] * (gate * (1.0 + value * (1.0 - gate)))
            gsf[at, lanes] = grad
            bias_sum = bias_sum + column_sums(grad)
            gain_sum = gain_sum + column_sums(grad * normed)
        xf[fat, :] = stage_a[...].astype(BF16)
        return bias_sum, gain_sum

    bias_fc, gain_fc = loop(bands, finish_fast, zero2(128))
    fast_store = store(xf, fast_h, 10)
    exchange_middle(3)
    loads["cs"].wait()
    total = exchange_end(3)

    stats_sc = moments(take(total, 0, cs_n), take(total, 8, cs_n), slow_count)
    thin = 32

    def finish_slow(i, carry):
        at = rows_at(i, thin)
        normed, shift = before_act(big[at, :], stats_sc, "sc")
        value = xs[at, :].astype(F32) + shift
        gate = sigmoid(value)
        grad = cs[at, :].astype(F32) * (gate * (1.0 + value * (1.0 - gate)))
        cs[at, :] = (value * gate).astype(BF16)
        gsum[at, :] = normed.astype(BF16)
        big[at, :] = grad
        return carry[0] + column_sums(grad), carry[1] + column_sums(grad * normed)

    bias_sc, gain_sc = loop(rows // thin, finish_slow, zero2(cs_n))
    slow_store = store(cs, slow_h, 11)
    put(4, 0, squash(bias_sc))
    put(4, 8, squash(gain_sc))
    put(4, 16, squash(bias_fc))
    put(4, 17, squash(gain_fc))
    exchange_start(4)
    exchange_middle(4)
    total = exchange_end(4)

    bias_sc, gain_sc = take(total, 0, cs_n), take(total, 8, cs_n)
    bias_fc, gain_fc = take(total, 16, 128), take(total, 17, 128)
    report("sc", bias_sc, gain_sc)
    report("fc", bias_fc, gain_fc)
    lead_sc = gain("sc") * stats_sc[1]
    level_sc = lead_sc * bias_sc * (1.0 / slow_count)
    tilt_sc = lead_sc * gain_sc * (1.0 / slow_count)
    slow_store.wait()

    def low_sc(i):
        at = rows_at(i, thin)
        grad = big[at, :]
        cs[at, :] = (grad * lead_sc - level_sc - gsum[at, :].astype(F32) * tilt_sc).astype(BF16)
        gsum[at, :] = grad.astype(BF16)

    loop(rows // thin, low_sc)

    def back_sc(i):
        at = rows_at(i, half)
        dbuf[at, :] = dot(cs[at, :], wsc[...], NN)

    loop(2, back_sc)

    def slope_pass(section, stats, name, buffer):
        def step(i, carry):
            at = rows_at(i, band)
            normed, pre = before_act(section[at, :], stats, name)
            gate = sigmoid(pre)
            grad = buffer[at, :] * (gate * (1.0 + pre * (1.0 - gate)))
            buffer[at, :] = grad
            return carry[0] + column_sums(grad), carry[1] + column_sums(grad * normed)

        return loop(bands, step, zero2(section.shape[1]))

    bias_sb, gain_sb = slope_pass(sec_sb, stats_sb, "sb", dbuf)

    mean_fc, scale_fc = stats_fc
    lead_fc = gain("fc") * scale_fc
    tilt_fc = lead_fc * scale_fc * gain_fc * (1.0 / fast_count)
    level_fc = lead_fc * bias_fc * (1.0 / fast_count) - mean_fc * tilt_fc

    def low_fc(i):
        at = rows_at(i, band)
        for phase in range(4):
            lanes = slice(128 * phase, 128 * (phase + 1))
            value = gsf[at, lanes] * lead_fc - level_fc - sec_fc[at, lanes] * tilt_fc
            cf[pl.ds(pl.multiple_of(rows * phase + i * band, 16), band), :] = value.astype(BF16)

    loop(bands, low_fc)

    def back_fc(i):
        value = None
        for phase in range(4):
            at = pl.ds(pl.multiple_of(rows * phase + i * half, 16), half)
            term = dot(cf[at, :], wfc[128 * phase : 128 * (phase + 1), :], NN)
            value = term if value is None else value + term
        dbuf_f[rows_at(i, half), :] = value

    loop(2, back_fc)
    bias_fb, gain_fb = slope_pass(sec_fb, stats_fb, "fb", dbuf_f)
    put(5, 0, squash(bias_fb))
    put(5, 1, squash(gain_fb))
    put(5, 2, squash(bias_sb))
    put(5, 4, squash(gain_sb))
    exchange_start(5)

    slab_sc[0:cs_n, :] = dot(cs[...], hbs[...], TN)
    advance("sc")
    exchange_middle(5)
    widening = None
    for phase in range(4):
        term = dot(hbf[...], cf[rows * phase : rows * (phase + 1), :], TN)[32 * phase : 32 * (phase + 1), :]
        widening = term if widening is None else widening + term
    slab[2, 704:736, 128:256] = widening
    slab[2, 736:768, 128:256] = jnp.zeros((32, LANES), F32)
    advance("sc")
    total = exchange_end(5)

    fold_rows = fold_lanes(total[0:8, :])
    bias_fb, gain_fb = fold_rows[0:1, :], fold_rows[1:2, :]
    bias_sb, gain_sb = take(total, 2, 256), take(total, 4, 256)
    report("fb", bias_fb, gain_fb)
    report("sb", bias_sb, gain_sb)
    vec_sb = back_vectors("sb", stats_sb, bias_sb, gain_sb, slow_count)
    vec_fb = back_vectors("fb", stats_fb, bias_fb, gain_fb, fast_count)

    def norm_grad(buffer, section, at, vectors):
        lead, level, tilt = vectors
        return buffer[at, :] * lead - level - section[at, :] * tilt

    def low_sb(i):
        spread_columns(gcs, i, norm_grad(dbuf, sec_sb, rows_at(i, band), vec_sb))

    loop(bands, low_sb)
    advance("sc")

    def back_sb(i):
        value = None
        for a in range(3):
            at = pl.ds(pl.multiple_of(i * half + band * (2 - a), 16), half)
            for b in range(3):
                tap = 3 * a + b
                term = dot(gcs[at, bs * (2 - b) : bs * (3 - b)], wsb[bs * tap : bs * (tap + 1), :], NN)
                value = term if value is None else value + term
        dbuf[rows_at(i, half), :] = value

    loop(2, back_sb)
    advance("sc")
    bias_sa, gain_sa = slope_pass(sec_sa, stats_sa, "sa", dbuf)

    def low_fb(i):
        spread_columns(gcf, i, norm_grad(dbuf_f, sec_fb, rows_at(i, band), vec_fb))

    loop(bands, low_fb)
    advance("sc")

    def back_fb(i):
        value = None
        for a in range(3):
            at = pl.ds(pl.multiple_of(i * half + band * (2 - a), 16), half)
            term = dot(gcf[at, :], wfbk[a], NN)
            value = term if value is None else value + term
        dbuf_f[rows_at(i, half), :] = value

    loop(2, back_fb)
    bias_fa, gain_fa = slope_pass(sec_fa, stats_fa, "fa", dbuf_f)
    put(6, 0, squash(bias_fa))
    put(6, 1, squash(gain_fa))
    put(6, 2, squash(bias_sa))
    put(6, 4, squash(gain_sa))
    exchange_start(6)

    for a in range(3):
        value = dot(gcs[band : band + rows, bs : 2 * bs], hcs[band * a : band * a + rows, :], TN)
        ref, lane = pieces["sb%d" % a]["ref"], pieces["sb%d" % a]["lane"]
        for b in range(3):
            ref[bs * b : bs * (b + 1), lane : lane + bs] = value[:, bs * b : bs * (b + 1)]
        advance("sb%d" % a)
    exchange_middle(6)
    advance("sc")
    advance("sb0")
    for a in range(3):
        value = dot(gcf[band : band + rows, 128:256], hcf[band * a : band * a + rows, :], TN)
        for b in range(3):
            tap = 3 * a + b
            block = value[:, 128 * b : 128 * (b + 1)] * block_mask
            folded = fold_lanes(block[0:32] + block[32:64] + block[64:96] + block[96:128])
            folded = jnp.where(lane_group[0:32] == tap % 4, folded, 0.0)
            at = slice(608 + 32 * (tap // 4), 640 + 32 * (tap // 4))
            slab[2, at, 128:256] = folded if tap % 4 == 0 else slab[2, at, 128:256] + folded
    advance("sb1")
    advance("sb2")
    total = exchange_end(6)

    fold_rows = fold_lanes(total[0:8, :])
    bias_fa, gain_fa = fold_rows[0:1, :], fold_rows[1:2, :]
    bias_sa, gain_sa = take(total, 2, 256), take(total, 4, 256)
    report("fa", bias_fa, gain_fa)
    report("sa", bias_sa, gain_sa)
    vec_sa = back_vectors("sa", stats_sa, bias_sa, gain_sa, slow_count)
    vec_fa = back_vectors("fa", stats_fa, bias_fa, gain_fa, fast_count)

    def low_sa(i):
        at = rows_at(i, band)
        value = norm_grad(dbuf, sec_sa, at, vec_sa)
        gcs[at, 0:bs] = roll_frames(value, prev256, -1, True).astype(BF16)
        gcs[at, bs : 2 * bs] = value.astype(BF16)
        gcs[at, 2 * bs :] = roll_frames(value, next256, 1, True).astype(BF16)

    loop(bands, low_sa)

    def narrow_gradient(k):
        ref, lane = pieces["sa%d" % k]["ref"], pieces["sa%d" % k]["lane"]
        source = xs[:, 256 * k : 256 * (k + 1)] if k < 4 else jl[...]
        ref[0 : 3 * bs, lane : lane + 256] = dot(gcs[0:rows, :], source, TN)
        advance("sa%d" % k)

    narrow_gradient(0)

    def back_lateral(i):
        at = rows_at(i, half)
        dbuf[at, :] = dot(gcs[at, :], wsa[:, cs_n:], NN)

    loop(2, back_lateral)
    bias_lat, gain_lat = slope_pass(sec_lat, stats_lat, "lat", dbuf)
    put(7, 0, squash(bias_lat))
    put(7, 2, squash(gain_lat))
    exchange_start(7)

    for name in ("sc", "sb0", "sb1", "sb2", "sa0"):
        advance(name)
    narrow_gradient(1)
    narrow_gradient(2)
    exchange_middle(7)
    for name in ("sb0", "sb1", "sb2", "sa0", "sa1", "sa2"):
        advance(name)
    narrow_gradient(3)
    narrow_gradient(4)
    for name in ("sc", "sb0", "sb1", "sb2", "sa0", "sa1", "sa2", "sa3", "sa4"):
        advance(name)

    def slow_back(i):
        at = rows_at(i, half)
        for tile in range(cs_n // 256):
            lanes = slice(256 * tile, 256 * (tile + 1))
            value = gsum[at, lanes].astype(F32) + dot(gcs[at, :], wsa[:, lanes], NN)
            gsum[at, lanes] = value.astype(BF16)

    loop(2, slow_back)
    sgrad_store = store(gsum, sgrad_h, 12)

    def low_fa(i):
        at = rows_at(i, band)
        hbf[at, :] = norm_grad(dbuf_f, sec_fa, at, vec_fa).astype(BF16)

    loop(bands, low_fa)
    value = dot(hbf[...], vx[:, 128:896], TN)
    for k in range(3):
        piece = None
        for phase in range(4):
            term = value[32 * phase : 32 * (phase + 1), 128 * (phase + k) : 128 * (phase + k + 1)]
            piece = term if piece is None else piece + term
        slab[2, 512 + 32 * k : 544 + 32 * k, 128:256] = piece
    total = exchange_end(7)

    bias_lat, gain_lat = take(total, 0, 256), take(total, 2, 256)
    report("lat", bias_lat, gain_lat)
    vec_lat = back_vectors("lat", stats_lat, bias_lat, gain_lat, slow_count)

    def low_lat(i):
        at = rows_at(i, band)
        hbs[at, :] = norm_grad(dbuf, sec_lat, at, vec_lat).astype(BF16)

    loop(bands, low_lat)
    value = dot(hbs[...], vx[:, 0:640], TN)
    for k in range(5):
        at, lane = 256 * (k % 3), 128 * (k // 3)
        slab[2, at : at + 256, lane : lane + 128] = value[:, 128 * k : 128 * (k + 1)]
    advance("lt")
    for name in ("sb0", "sb1", "sb2", "sa0", "sa1", "sa2", "sa3", "sa4", "lt"):
        advance(name)
    fast_store.wait()

    def fast_back(i):
        at, fat = rows_at(i, 2 * band), rows_at(i, 2 * fband)
        conv = dot(hbf[at, :], wfa[...], NN)
        side_in = dot(hbs[at, :], wlat[...], NN)

        def lane(values, block):
            return values[:, 128 * block : 128 * (block + 1)]

        grads = [gsf[at, 128 * phase : 128 * (phase + 1)] + lane(conv, phase + 1) for phase in range(4)]
        grads[0] = grads[0] + roll_frames(lane(conv, 5), next128, 1, True) + lane(side_in, 2)
        grads[1] = grads[1] + lane(side_in, 3)
        grads[2] = grads[2] + lane(side_in, 4) + roll_frames(lane(side_in, 0), prev128, -1, True)
        grads[3] = grads[3] + roll_frames(lane(side_in, 1) + lane(conv, 0), prev128, -1, True)
        for part in range(2):
            for phase in range(4):
                stage_a[pl.ds(phase, band, stride=4), :] = grads[phase][part * band : (part + 1) * band]
            xf[rows_at(2 * i + part, fband), :] = stage_a[...].astype(BF16)

    loop(bands // 2, fast_back)
    fgrad_store = store(xf, fgrad_h, 13)
    for name in ("sb0", "sb1", "sb2", "sa0", "sa1", "sa2", "sa3", "sa4", "lt"):
        advance(name)
    def pack(rows_ref, target):
        lanes = lax.broadcasted_iota(jnp.int32, (24, LANES), 1)
        stacked = rows_ref[...]
        turned = pltpu.roll(stacked, 64, 1)
        moved = jnp.where(lanes >= 64, turned, pltpu.roll(turned, 1, 0))[0:16, :]
        first = jnp.where(lane16[0:1, :] < 32, stacked[16:17, :], stacked[17:18, :])
        first = jnp.where(lane16[0:1, :] < 64, first, moved[0:1, :])
        target[...] = moved * factor
        target[0:1, :] = first * factor

    pack(gain_rows, dgains)
    pack(bias_rows, dbiases)
    while any(piece["step"] <= 8 for piece in pieces.values()):
        for name in order:
            if pieces[name]["step"] <= 8:
                advance(name)
    for slot, copy in enumerate(stores):
        copy.wait()
    sgrad_store.wait()
    fgrad_store.wait()


def body(
    slow_input,
    fast_input,
    clip_ids,
    fast_narrow,
    fast_spatial,
    fast_widen,
    lateral_conv,
    slow_narrow,
    slow_spatial,
    slow_widen,
    norm_gains,
    norm_biases,
    slow_cotangent,
    fast_cotangent,
):
    n_dp, n_rep = lax.axis_size("dp"), lax.axis_size("rep")
    low = 2 if n_dp % 2 == 0 else 1
    high = n_dp // low
    frames, plane, channels = slow_input.shape
    fast_frames, _, fast_channels = fast_input.shape
    side = math.isqrt(plane)
    rows = frames * plane
    slow_count = rows * n_dp * n_rep
    fast_count = slow_count * (fast_frames // frames)

    def flat(values):
        return values.transpose(1, 0, 2).reshape(values.shape[0] * values.shape[1], values.shape[2])

    def unflat(values, count):
        return values.reshape(plane, count, values.shape[1]).transpose(1, 0, 2)

    widths = [
        fast_narrow.shape[1], fast_spatial.shape[1], fast_widen.shape[0], lateral_conv.shape[1],
        slow_narrow.shape[1], slow_spatial.shape[1], slow_widen.shape[0],
    ]

    def lay_out(vector):
        return jnp.pad(vector, (0, 16 * LANES - vector.shape[0])).reshape(16, LANES)

    cf = fast_channels
    bs = slow_spatial.shape[1]
    band = side * frames
    any_spec = pl.BlockSpec(memory_space=pl.ANY)
    vmem_spec = pl.BlockSpec(memory_space=pltpu.VMEM)
    small = sum(1 for size in ROWS if size == 8)
    large = len(ROWS) - small
    pad = rows + 2 * band

    def shape(dims, dtype):
        return jax.ShapeDtypeStruct(dims, dtype)

    out_shape = [
        shape((rows, channels), BF16), shape((4 * rows, cf), BF16),
        shape((rows, channels), BF16), shape((4 * rows, cf), BF16),
        shape((3 * bs, channels + bs), F32), shape((9 * bs, bs), F32), shape((channels, bs), F32),
        shape((5 * bs, cf), F32), shape((96, cf), F32), shape((288, 32), F32), shape((32, cf), F32),
        shape((16, LANES), F32), shape((16, LANES), F32),
        shape((10, max(high // 4, 1), 32, 256), F32),
    ]
    scratch = [
        pltpu.VMEM((rows, channels), BF16), pltpu.VMEM((rows, channels), BF16),
        pltpu.VMEM((rows, channels), BF16), pltpu.VMEM((4 * rows, cf), BF16),
        pltpu.VMEM((4 * rows, cf), BF16), pltpu.VMEM((rows, channels), F32),
        pltpu.VMEM((rows, 512), F32), pltpu.VMEM((rows, 512), F32),
        pltpu.VMEM((pad, 3 * bs), BF16), pltpu.VMEM((pad, 3 * bs), BF16),
        pltpu.VMEM((pad, 384), BF16), pltpu.VMEM((pad, 384), BF16),
        pltpu.VMEM((rows, bs), F32), pltpu.VMEM((rows, bs), F32), pltpu.VMEM((rows, bs), F32),
        pltpu.VMEM((rows, bs), F32),
        pltpu.VMEM((rows, 128), F32), pltpu.VMEM((rows, 128), F32), pltpu.VMEM((rows, 128), F32),
        pltpu.VMEM((rows, bs), BF16), pltpu.VMEM((rows, bs), BF16), pltpu.VMEM((rows, 128), BF16),
        pltpu.VMEM((rows, 896), BF16), pltpu.VMEM((3, 1512, 256), F32), pltpu.VMEM((2016, 256), F32),
        pltpu.VMEM((768, 256), F32), pltpu.VMEM((max(high // 4, 1), 32, 256), F32),
        pltpu.VMEM((3 * bs, channels + bs), BF16), pltpu.VMEM((9 * bs, bs), BF16),
        pltpu.VMEM((channels, bs), BF16),
        pltpu.VMEM((96, cf), BF16), pltpu.VMEM((288, 32), BF16), pltpu.VMEM((32, cf), BF16),
        pltpu.VMEM((bs, 640), BF16), pltpu.VMEM((128, 768), BF16),
        pltpu.VMEM((3, 128, 384), BF16), pltpu.VMEM((3, 384, 128), BF16), pltpu.VMEM((512, 128), BF16),
        pltpu.VMEM((4 * band, cf), F32), pltpu.VMEM((4 * band, cf), F32),
        pltpu.VMEM((24, LANES), F32), pltpu.VMEM((24, LANES), F32),
        pltpu.VMEM((small, low * n_rep, 8, LANES), F32), pltpu.VMEM((large, low * n_rep, 24, LANES), F32),
        pltpu.VMEM((small, high, 8, LANES), F32), pltpu.VMEM((large, high, 24, LANES), F32),
        pltpu.SemaphoreType.DMA((len(ROWS),)), pltpu.SemaphoreType.DMA((len(ROWS),)),
        pltpu.SemaphoreType.DMA((len(ROWS),)), pltpu.SemaphoreType.DMA((len(ROWS),)),
        pltpu.SemaphoreType.DMA((32,)), pltpu.SemaphoreType.DMA((10, 2)),
        pltpu.SemaphoreType.DMA((10, 9)), pltpu.SemaphoreType.DMA((10, 9)),
    ]
    factor = 1.0 / math.sqrt(float(slow_count))
    results = pl.pallas_call(
        functools.partial(kernel, (n_dp, n_rep, low, frames, side, float(slow_count), float(fast_count), factor)),
        out_shape=out_shape,
        in_specs=[any_spec] * 4 + [pl.BlockSpec(memory_space=pltpu.SMEM)] + [any_spec] * 7 + [vmem_spec] * 2,
        out_specs=[any_spec] * 8 + [vmem_spec] * 5 + [any_spec],
        scratch_shapes=scratch,
        compiler_params=pltpu.CompilerParams(
            collective_id=0, has_side_effects=True, vmem_limit_bytes=65000 * 2**10
        ),
    )(
        flat(slow_input), flat(fast_input), flat(slow_cotangent), flat(fast_cotangent), clip_ids,
        fast_narrow.reshape(-1, cf), fast_spatial.reshape(-1, 32), fast_widen.T,
        lateral_conv.reshape(-1, cf), slow_narrow.reshape(3 * bs, -1), slow_spatial.reshape(9 * bs, bs),
        slow_widen, lay_out(norm_gains), lay_out(norm_biases),
    )
    slow_out, fast_out, slow_grad, fast_grad, dsa, dsb, dsc, dl, dfa, dfb, dfc, dgains, dbiases, _ = results
    def gather(packed):
        return packed.reshape(16 * LANES)[0 : sum(widths)]

    return (
        unflat(slow_out, frames),
        unflat(fast_out, fast_frames),
        unflat(slow_grad, frames),
        unflat(fast_grad, fast_frames),
        dfa.reshape(fast_narrow.shape),
        dfb.reshape(fast_spatial.shape),
        dfc.T,
        dl.reshape(lateral_conv.shape),
        dsa.reshape(slow_narrow.shape),
        dsb.reshape(slow_spatial.shape),
        dsc,
        gather(dgains),
        gather(dbiases),
    )


def solution(mesh):
    sharded = P(("dp", "rep"), None, None)
    return jax.shard_map(
        body,
        mesh=mesh,
        in_specs=(sharded, sharded, P(("dp", "rep"), None)) + (P(),) * 9 + (sharded, sharded),
        out_specs=(sharded,) * 4 + (P(),) * 9,
        check_vma=False,
    )
```

```python
import functools
import math

import jax
import jax.numpy as jnp
from jax import lax
from jax.experimental import pallas as pl
from jax.experimental.pallas import tpu as pltpu
from jax.sharding import PartitionSpec as P

EPS = 1e-05
F32 = jnp.float32
BF16 = jnp.bfloat16
MESH = pl.DeviceIdType.MESH
NN = ((1,), (0,))
NT = ((1,), (1,))
TN = ((0,), (0,))
LANES = 128
TURNS = {
    "lat": 512, "fa": 128, "sa": 512, "fb": 128, "sb": 512, "fc": 256, "sc0": 768, "sc1": 512,
    "sc0_back": 1024, "sc1_back": 1024, "fc_back": 256, "sb_back": 512, "fb_back": 128, "sa_back": 512,
    "fa_back": 128, "lat_back": 512,
}


LINES = ('sb2', )
POLLS = (
    '',
    'sc',
    '',
    '',
    'sb0 sc',
    'sb1',
    'sb2',
    '',
    '',
    'sb0 sc sa0',
    '',
    'sb2 sb1',
    'sb0 sa1',
    'sa0 sc sa2',
    'sb1 sa3 lt',
    'sa1',
    'sa0 sa4 sb2',
    'sb0 sa2',
    '',
    'sa3 sc lt sa1 sa4 sa0 sb1 sa2 sb0 sa3 sa1 sc sa4 lt sa0 sb2 sb0 sb1 sa2 sc sa0 sa3 sb2 sc sa1 sb0 sb1 sb2 sa4 sa1 sa0 lt sb1 sa0 sa2 sa1 sa3 sa2 sb1 sb2 sa1 sa4 lt sa3 sb0 sa4 lt sa2 sb2 sa3 sa3 sa4 sa2 sa4 lt sb2 lt sb2',
)


def dot(left, right, dims):
    return lax.dot_general(left, right, (dims, ((), ())), preferred_element_type=F32)


def sigmoid(values):
    return 0.5 * jnp.tanh(0.5 * values) + 0.5


def column_sums(values):
    return jnp.sum(values.reshape(values.shape[0] // 8, 8, values.shape[1]), axis=0)


def squash(partial):
    return jnp.sum(partial, axis=0, keepdims=True)


def fold_lanes(values):
    half = values + pltpu.roll(values, 64, 1)
    return half + pltpu.roll(half, 32, 1)


def loop(count, body, init=None):
    if init is None:

        def plain(index, carry):
            body(index)
            return carry

        lax.fori_loop(0, count, plain, 0)
        return None
    return lax.fori_loop(0, count, body, init)


def rows_at(index, size):
    return pl.ds(pl.multiple_of(index * size, 16), size)


def kernel(
    dims,
    xs_h, xf_h, cs_h, cf_h, clip, wfa_h, wfb_h, wfc_h, wl_h, wsa_h, wsb_h, wsc_h, gains_in, biases_in,
    slow_h, fast_h, sgrad_h, fgrad_h, dsa_h, dsb_h, dsc_h, dl_h, dfa, dfb, dfc, dgains, dbiases, extra_h,
    xs, cs, gsum, xf, cf, big, sec_fc, gsf, hcs, gcs, hcf, gcf,
    sec_lat, sec_sa, sec_sb, dbuf, sec_fa, sec_fb, dbuf_f, jl, hbs, hbf, vx, slab, slab_sc, summed, gathered,
    wsa, wsb, wsc, wfa_in, wfb_in, wfc_in, wlat, wfa, wfb, wfbk, wfc,
    stage_a, stage_b, gain_rows, bias_rows, near, far, sum_send, sum_recv, io_sem, own_sem, big_send, big_recv,
):
    n_dp, n_rep, low, frames, side, slow_count, fast_count, factor = dims
    rows = xs.shape[0]
    half = rows // 2
    band = side * frames
    bands = side
    fband = 4 * band
    cs_n = xs.shape[1]
    bs = wsb.shape[1]

    dp_i, rep_i = lax.axis_index("dp"), lax.axis_index("rep")
    dp_lo, dp_hi = lax.rem(dp_i, low), lax.div(dp_i, low)
    high = n_dp // low
    direct = n_dp * n_rep <= 32
    near_low = n_dp if direct else low
    near_dp, far_dp = lax.rem(dp_i, near_low), lax.div(dp_i, near_low)
    near_peers = [
        (far_dp * near_low + lax.rem(near_dp + a, near_low), lax.rem(rep_i + b, n_rep))
        for a in range(near_low)
        for b in range(n_rep)
        if a or b
    ]
    far_count = n_dp // near_low
    far_peers = [(lax.rem(far_dp + a, far_count) * near_low + near_dp, rep_i) for a in range(1, far_count)]
    stages = [(near, near_dp * n_rep + rep_i, near_peers)]
    if far_peers:
        stages.append((far, far_dp, far_peers))

    c, x = lax.rem(rep_i, 2), lax.div(rep_i, 2)
    y, z = dp_lo, lax.rem(dp_hi, 4)
    outer, outers = lax.div(dp_hi, 4), high // 4
    core_peer = (dp_i, 2 * x + 1 - c)
    x_peer = (dp_i, 2 * (1 - x) + c)
    y_peer = (dp_hi * low + 1 - y, rep_i)
    def z_peer(flip):
        return ((outer * 4 + z + flip - 2 * flip * lax.rem(lax.div(z, flip), 2)) * low + y, rep_i)

    z_peers = [((outer * 4 + lax.rem(z + k, 4)) * low + y, rep_i) for k in range(1, 4)]
    outer_peers = [((lax.rem(outer + k, outers) * 4 + z) * low + y, rep_i) for k in range(1, outers)]

    barrier = pltpu.get_barrier_semaphore()
    greeted = near_peers + far_peers
    for peer in greeted:
        pl.semaphore_signal(barrier, inc=1, device_id=peer, device_id_type=MESH)

    loads = {}
    for slot, (name, src, dst) in enumerate([
        ("xf", xf_h, xf), ("wfa", wfa_h, wfa_in), ("xs", xs_h, xs),
        ("wsa", wsa_h, wsa), ("wfb", wfb_h, wfb_in), ("wfc", wfc_h, wfc_in), ("wsb", wsb_h, wsb),
        ("wsc", wsc_h, wsc), ("cf", cf_h, cf), ("cs", cs_h, cs),
    ]):
        loads[name] = pltpu.make_async_copy(src, dst, io_sem.at[slot])
        loads[name].start()
        if name == "wfa":
            taps = [
                pltpu.make_async_copy(
                    wl_h.at[pl.ds(bs * k, bs)], wlat.at[:, pl.ds(LANES * k, LANES)], io_sem.at[27 + k]
                )
                for k in range(5)
            ]
            for tap in taps:
                tap.start()
    stores = []

    def store(src, dst, slot):
        copy = pltpu.make_async_copy(src, dst, io_sem.at[slot])
        copy.start()
        return copy

    turn_at, turn_index = {}, {}
    for index, (turn, width) in enumerate(TURNS.items()):
        turn_at[turn] = sum(list(TURNS.values())[:index])
        turn_index[turn] = index

    def put(turn, at, vector):
        near[stages[0][1], :, pl.ds(turn_at[turn] + at, vector.shape[1])] = vector

    def sum_copy(turn, stage, first, count, peer):
        buffer = stages[stage][0]
        block = buffer.at[pl.ds(first, count), :, pl.ds(turn_at[turn], TURNS[turn])]
        return pltpu.make_async_remote_copy(
            src_ref=block, dst_ref=block, send_sem=sum_send.at[turn_index[turn], stage],
            recv_sem=sum_recv.at[turn_index[turn], stage], device_id=peer, device_id_type=MESH,
        )

    def exchange_start(turn):
        for peer in near_peers:
            sum_copy(turn, 0, stages[0][1], 1, peer).start()

    def exchange_end(turn):
        lanes = pl.ds(turn_at[turn], TURNS[turn])
        for stage, (buffer, rank, peers) in enumerate(stages):
            if stage:
                buffer[rank, :, lanes] = total
                for peer in peers:
                    sum_copy(turn, stage, rank, 1, peer).start()
            copy = sum_copy(turn, stage, 0, len(peers), peers[0])
            copy.wait_recv()
            total = jnp.sum(buffer[:, :, lanes], axis=0)
            copy.wait_send()
        return total

    def take(total, at, width):
        return total[:, at : at + width]

    def pair32(first, second):
        group = lax.broadcasted_iota(jnp.int32, (8, LANES), 1) // 32
        rows8 = (8, LANES)
        first = fold_lanes(jnp.broadcast_to(first, rows8))
        second = fold_lanes(jnp.broadcast_to(second, rows8))
        return jnp.where(group == 0, first, jnp.where(group == 1, second, 0.0))[0:1, :]

    def unpair32(total):
        group = lax.broadcasted_iota(jnp.int32, (8, LANES), 1) // 32
        total = jnp.broadcast_to(total, (8, LANES))
        first = fold_lanes(jnp.where(group == 0, total, 0.0))
        second = fold_lanes(jnp.where(group == 1, total, 0.0))
        return first[0:1, :], second[0:1, :]

    pieces = {}

    bits = {"c": (c, core_peer), "x": (x, x_peer), "y": (y, y_peer),
            "z0": (lax.rem(z, 2), z_peer(1)), "z1": (lax.div(z, 2), z_peer(2))}
    PLANE_FIRST = (("c", "x", "y", "z"), ("c", "y", "x", "z"))
    LINE_FIRST = (("c", "z0", "z1", "x", "y"), ("c", "z0", "z1", "y", "x"))

    def add_piece(name, ref, lane, size, index):
        axes = LINE_FIRST if name in LINES else PLANE_FIRST
        piece = {"name": name, "ref": ref, "lane": lane, "size": size, "index": index, "step": 0, "axes": axes}
        starts, counts, arriving = [[0], [0]], [size], [size]
        for step, pair in enumerate(zip(*axes)):
            for side, axis in enumerate(pair):
                if axis == "z":
                    starts[side].append(starts[side][-1] + z * (counts[-1] // 4))
                else:
                    starts[side].append(starts[side][-1] + bits[axis][0] * (counts[-1] // 2))
            counts.append(counts[-1] // (4 if pair[0] == "z" else 2))
            arriving.append(arriving[-1] + (3 if pair[0] == "z" else 1) * counts[-1])
        piece.update(starts=starts, counts=counts, arriving=arriving, steps=len(axes[0]))
        pieces[name] = piece

    for k in range(2):
        add_piece("sb%d" % k, sec_fc, 256 * k, 768, k)
    for k in range(4):
        add_piece("sa%d" % k, big, 256 * k, 768, 2 + k)
    add_piece("sb2", slab.at[0], 0, 768, 6)
    add_piece("sa4", slab.at[1], 0, 768, 7)
    add_piece("lt", slab.at[2], 0, 768, 8)
    add_piece("sc", slab_sc, 0, 1024, 9)

    def span(piece, start, count, lane=0, width=256):
        return piece["ref"].at[pl.ds(pl.multiple_of(start, 8), count), pl.ds(piece["lane"] + lane, width)]

    def send(piece, step, src, dst, peer):
        pltpu.make_async_remote_copy(
            src_ref=src, dst_ref=dst, send_sem=big_send.at[piece["index"], step],
            recv_sem=big_recv.at[piece["index"], step], device_id=peer, device_id_type=MESH,
        ).start()

    def result(piece, start, count, lane=0, width=256):
        name = piece["name"]
        start = pl.multiple_of(start, 8)
        if name == "lt":
            return summed.at[pl.ds(start, count), pl.ds(lane, width)]
        if name == "sc":
            return dsc_h.at[pl.ds(start, count), pl.ds(lane, width)]
        k = int(name[2])
        if name[1] == "a":
            return dsa_h.at[pl.ds(start, count), pl.ds(256 * k + lane, width)]
        return dsb_h.at[pl.ds(768 * k + start, count), pl.ds(lane, width)]

    def own_copies(piece):
        count, sem = piece["counts"][-1], own_sem.at[piece["index"]]
        return [
            pltpu.make_async_copy(
                span(piece, start[-1], count, 128 * side, 128),
                result(piece, start[-1], count, 128 * side, 128),
                sem.at[side],
            )
            for side, start in enumerate(piece["starts"])
        ]

    def arrived(piece, step, rows_in):
        block = span(piece, 0, rows_in) if step < piece["steps"] else result(piece, 0, rows_in)
        copy = pltpu.make_async_remote_copy(
            src_ref=block, dst_ref=block, send_sem=big_send.at[piece["index"], step],
            recv_sem=big_recv.at[piece["index"], step], device_id=core_peer, device_id_type=MESH,
        )
        copy.wait_recv()
        copy.wait_send()

    def add_rows(piece, target, source, count, lane, width):
        lanes = pl.ds(piece["lane"] + lane, width)
        chunk = piece["size"] // 32
        ref = piece["ref"]

        def step(i):
            into = pl.ds(pl.multiple_of(target + i * chunk, 8), chunk)
            ref[into, lanes] = ref[into, lanes] + ref[pl.ds(pl.multiple_of(source + i * chunk, 8), chunk), lanes]

        loop(count // chunk, step)

    order = ["sc", "sb0", "sb1", "sb2", "sa0", "sa1", "sa2", "sa3", "sa4", "lt"]

    def unpack_small():
        stores.append(store(summed.at[:, pl.ds(0, 128)], dl_h.at[pl.ds(0, 768)], 16))
        stores.append(store(summed.at[pl.ds(0, 512), pl.ds(128, 128)], dl_h.at[pl.ds(768, 512)], 17))
        dfa[...] = summed[512:608, 128:256]
        for tap in range(9):
            at = 608 + 32 * (tap // 4)
            block = summed[at : at + 32, 128:256]
            dfb[32 * tap : 32 * (tap + 1), :] = block[:, 32 * (tap % 4) : 32 * (tap % 4 + 1)]
        dfc[...] = summed[704:736, 128:256]

    def poll(turn):
        for name in POLLS[turn].split():
            advance(name)

    def done(name):
        return pieces[name]["step"] > 2 * pieces[name]["steps"]

    def advance(name):
        piece = pieces[name]
        step, steps, index = piece["step"], piece["steps"], piece["index"]
        piece["step"] = step + 1
        starts, counts, arriving, axes = piece["starts"], piece["counts"], piece["arriving"], piece["axes"]
        ref, lane = piece["ref"], piece["lane"]

        def received(last):
            fan = 3 if axes[0][last] == "z" else 1
            return fan * counts[last + 1]

        if 0 < step < steps or (step == steps and axes[0][-1] != "z"):
            arrived(piece, step - 1, received(step - 1))
            if step == 1:
                add_rows(piece, starts[0][1], arriving[0], counts[1], 0, 256)
            else:
                for side in range(2):
                    add_rows(piece, starts[side][step], arriving[step - 1], counts[step], 128 * side, 128)
        elif step == steps:
            arrived(piece, step - 1, received(step - 1))
        elif step > steps:
            arrived(piece, step - 1, received(2 * steps - step))

        if step < steps:
            held, keep = counts[step], counts[step + 1]
            if step == 0:
                at = starts[0][0] + (1 - c) * keep
                send(piece, 0, span(piece, at, keep), span(piece, arriving[0], keep), core_peer)
                return
            for side in range(2):
                axis, start = axes[side][step], starts[side][step]
                if axis == "z":
                    for k, peer in enumerate(z_peers):
                        at, into = start + lax.rem(z + k + 1, 4) * keep, arriving[step] + k * keep
                        send(
                            piece, step, span(piece, at, keep, 128 * side, 128),
                            span(piece, into, keep, 128 * side, 128), peer,
                        )
                else:
                    bit, peer = bits[axis]
                    at = start + (1 - bit) * keep
                    send(
                        piece, step, span(piece, at, keep, 128 * side, 128),
                        span(piece, arriving[step], keep, 128 * side, 128), peer,
                    )
        elif step == steps:
            last = counts[-1]
            own = [
                (pl.ds(pl.multiple_of(starts[side][-1], 8), last), pl.ds(lane + 128 * side, 128))
                for side in range(2)
            ]
            both = jnp.concatenate([ref[own[0]], ref[own[1]]], axis=1)
            if axes[0][-1] == "z":
                for k in range(3):
                    both = both + ref[pl.ds(arriving[steps - 1] + k * last, last), pl.ds(lane, 256)]
            if outers > 1:
                held = span(piece, arriving[steps - 1], last)
                ref[pl.ds(arriving[steps - 1], last), pl.ds(lane, 256)] = both
                for peer in outer_peers:
                    send(piece, 10, held, extra_h.at[index, outer, pl.ds(0, last)], peer)
                block = extra_h.at[index, pl.ds(0, outers - 1), pl.ds(0, last)]
                copy = pltpu.make_async_remote_copy(
                    src_ref=block, dst_ref=block, send_sem=big_send.at[index, 10], recv_sem=big_recv.at[index, 10],
                    device_id=core_peer, device_id_type=MESH,
                )
                copy.wait_recv()
                copy.wait_send()
                for src, dst in (
                    (held, extra_h.at[index, outer, pl.ds(0, last)]),
                    (extra_h.at[index], gathered),
                ):
                    copy = pltpu.make_async_copy(src, dst, own_sem.at[index, 0])
                    copy.start()
                    copy.wait()
                both = jnp.sum(gathered[:, pl.ds(0, last), :], axis=0)
            both = both * factor
            for side in range(2):
                ref[own[side]] = both[:, 128 * side : 128 * (side + 1)]
        if steps <= step < 2 * steps:
            back = 2 * steps - 1 - step
            count = counts[back + 1]
            if step == steps + 1:
                for copy in own_copies(piece):
                    copy.wait()
            if back == 0:
                block = result(piece, starts[0][1], count)
                send(piece, step, block, block, core_peer)
                return
            for side in range(2):
                axis, start = axes[side][back], starts[side][back + 1]
                block = result(piece, start, count, 128 * side, 128)
                source = span(piece, start, count, 128 * side, 128) if step == steps else block
                for peer in z_peers if axis == "z" else [bits[axis][1]]:
                    send(piece, step, source, block, peer)
            if step == steps:
                for copy in own_copies(piece):
                    copy.start()
        elif step == 2 * steps and name == "lt":
            unpack_small()

    spots = {"fc": 0, "lat": 1, "sa": 3, "sb": 5, "sc": 7, "fa": 16, "fb": 17}

    lane16 = lax.broadcasted_iota(jnp.int32, (16, LANES), 1)

    def unpack(packed):
        fa = fold_lanes(jnp.where(lane16 // 32 == 0, packed, 0.0))[0:1, :]
        fb = fold_lanes(jnp.where(lane16 // 32 == 1, packed, 0.0))[0:1, :]
        turned = pltpu.roll(packed, 64, 1)
        moved = jnp.where(lane16 < 64, turned, pltpu.roll(turned, 15, 0))
        vectors = {"fa": fa, "fb": fb}
        at = 0
        for name, count in (("fc", 1), ("lat", 2), ("sa", 2), ("sb", 2), ("sc", 8)):
            vectors[name] = jnp.concatenate([moved[at + k : at + k + 1, :] for k in range(count)], axis=1)
            at += count
        return vectors

    gains, biases = unpack(gains_in[...]), unpack(biases_in[...])

    def gain(name):
        return gains[name]

    def bias(name):
        return biases[name]

    def moments(total, squares, count):
        mean = total * (1.0 / count)
        return mean, lax.rsqrt(squares * (1.0 / count) - mean * mean + EPS)

    def back_vectors(name, stats, bias_total, gain_total, count):
        mean, scale = stats
        lead = gain(name) * scale
        tilt = lead * scale * gain_total * (1.0 / count)
        level = lead * bias_total * (1.0 / count) - mean * tilt
        return lead, level, tilt

    def report(name, bias_total, gain_total):
        at = spots[name]
        for piece in range(bias_total.shape[1] // LANES):
            lanes = slice(piece * LANES, (piece + 1) * LANES)
            gain_rows[at + piece : at + piece + 1, :] = gain_total[:, lanes]
            bias_rows[at + piece : at + piece + 1, :] = bias_total[:, lanes]

    def before_act(values, stats, name):
        mean, scale = stats
        normed = (values - mean) * scale
        return normed, normed * gain(name) + bias(name)

    def clip_masks(width):
        frame = lax.broadcasted_iota(jnp.int32, (1, 8, width), 1)
        with_prev = jnp.zeros((1, 8, width), F32)
        with_next = jnp.zeros((1, 8, width), F32)
        for t in range(1, frames):
            same = jnp.where(clip[0, t] == clip[0, t - 1], 1.0, 0.0)
            with_prev = jnp.where(frame == t, same, with_prev)
            with_next = jnp.where(frame == t - 1, same, with_next)
        return with_prev, with_next

    def roll_frames(values, mask, step, mask_first):
        grouped = values.reshape(values.shape[0] // 8, 8, values.shape[1])
        if mask_first:
            grouped = grouped * mask
        grouped = pltpu.roll(grouped, step % 8, 1)
        if not mask_first:
            grouped = grouped * mask
        return grouped.reshape(values.shape)

    def spread_columns(target, index, values):
        width = values.shape[1]
        nothing = jnp.zeros((frames, width), F32)
        at = pl.ds(pl.multiple_of((index + 1) * band, 16), band)
        target[at, 0:width] = jnp.concatenate([nothing, values[: band - frames]], axis=0).astype(BF16)
        target[at, width : 2 * width] = values.astype(BF16)
        target[at, 2 * width :] = jnp.concatenate([values[frames:], nothing], axis=0).astype(BF16)

    gain_rows[...] = jnp.zeros(gain_rows.shape, F32)
    bias_rows[...] = jnp.zeros(bias_rows.shape, F32)
    for target in (hcs, gcs, hcf, gcf):
        edge = jnp.zeros((band, target.shape[1]), BF16)
        target[0:band, :] = edge
        target[band + rows : rows + 2 * band, :] = edge

    lane_group = lax.broadcasted_iota(jnp.int32, (LANES, LANES), 1) // 32
    row_group = lax.broadcasted_iota(jnp.int32, (LANES, LANES), 0) // 32
    block_mask = jnp.where(lane_group == row_group, 1.0, 0.0)
    repeat_lanes = jnp.where(
        lax.broadcasted_iota(jnp.int32, (32, LANES), 1) % 32 == lax.broadcasted_iota(jnp.int32, (32, LANES), 0),
        1.0, 0.0,
    ).astype(BF16)

    wfa[...] = jnp.zeros(wfa.shape, BF16)
    loads["wfa"].wait()
    for phase in range(4):
        for k in range(3):
            wfa[32 * phase : 32 * (phase + 1), LANES * (phase + k) : LANES * (phase + k + 1)] = wfa_in[
                32 * k : 32 * (k + 1), :
            ]
    prev128, next128 = clip_masks(128)
    loads["xf"].wait()

    def arrange(i):
        at = rows_at(i, band)
        stage_a[...] = xf[rows_at(i, fband), :].astype(F32)
        phases = [stage_a[pl.ds(phase, band, stride=4), :] for phase in range(4)]
        vx[at, 0:128] = roll_frames(phases[2], prev128, 1, False).astype(BF16)
        vx[at, 128:256] = roll_frames(phases[3], prev128, 1, False).astype(BF16)
        for phase in range(4):
            vx[at, 256 + 128 * phase : 384 + 128 * phase] = phases[phase].astype(BF16)
        vx[at, 768:896] = roll_frames(phases[0], next128, -1, False).astype(BF16)

    loop(bands, arrange)
    for tap in taps:
        tap.wait()

    def zero2(width):
        return (jnp.zeros((8, width), F32), jnp.zeros((8, width), F32))

    def conv_fa(i, carry):
        at = rows_at(i, half)
        value = dot(vx[at, 128:896], wfa[...], NT)
        sec_fa[at, :] = value
        return carry[0] + column_sums(value), carry[1] + column_sums(value * value)

    def conv_lat(i, carry):
        at = rows_at(i, half)
        value = dot(vx[at, 0:640], wlat[...], NT)
        sec_lat[at, :] = value
        return carry[0] + column_sums(value), carry[1] + column_sums(value * value)

    sum_lat, sq_lat = loop(2, conv_lat, zero2(256))
    put("lat", 0, squash(sum_lat))
    put("lat", 256, squash(sq_lat))
    pl.semaphore_wait(barrier, len(greeted))
    exchange_start("lat")

    sum_fa, sq_fa = loop(2, conv_fa, zero2(128))
    put("fa", 0, pair32(squash(sum_fa), squash(sq_fa)))
    exchange_start("fa")

    loads["xs"].wait()
    loads["wsa"].wait()

    def narrow_main(i):
        at = rows_at(i, half)
        for k in range(3):
            big[at, bs * k : bs * (k + 1)] = dot(xs[at, :], wsa[bs * k : bs * (k + 1), 0:cs_n], NT)

    loop(2, narrow_main)
    loads["wfb"].wait()
    loads["wfc"].wait()
    spread = dot(wfb_in[...], repeat_lanes, NN)
    for a in range(3):
        for b in range(3):
            piece = spread[32 * (3 * a + b) : 32 * (3 * a + b + 1), :]
            block = (jnp.concatenate([piece] * 4, axis=0) * block_mask).astype(BF16)
            wfb[a, :, LANES * b : LANES * (b + 1)] = block
            wfbk[a, LANES * (2 - b) : LANES * (3 - b), :] = block
    widen = dot(wfc_in[...], repeat_lanes, TN)
    for phase in range(4):
        wfc[LANES * phase : LANES * (phase + 1), :] = jnp.where(lane_group == phase, widen, 0.0).astype(BF16)
    total = exchange_end("lat")

    stats_lat = moments(take(total, 0, 256), take(total, 256, 256), slow_count)

    def act_fa(i):
        normed, pre = before_act(sec_fa[rows_at(i, band), :], stats_fa, "fa")
        spread_columns(hcf, i, pre * sigmoid(pre))

    def act_lat(i):
        at = rows_at(i, band)
        normed, pre = before_act(sec_lat[at, :], stats_lat, "lat")
        jl[at, :] = (pre * sigmoid(pre)).astype(BF16)

    loop(bands, act_lat)

    def conv_fb(i, carry):
        value = None
        for a in range(3):
            at = pl.ds(pl.multiple_of(i * half + band * a, 16), half)
            term = dot(hcf[at, :], wfb[a], NT)
            value = term if value is None else value + term
        sec_fb[rows_at(i, half), :] = value
        return carry[0] + column_sums(value), carry[1] + column_sums(value * value)

    def narrow_lateral(i):
        at = rows_at(i, half)
        for k in range(3):
            big[at, bs * k : bs * (k + 1)] += dot(jl[at, :], wsa[bs * k : bs * (k + 1), cs_n:], NT)

    loop(2, narrow_lateral)
    prev256, next256 = clip_masks(256)

    def combine_sa(i, carry):
        at = rows_at(i, band)
        value = (
            big[at, bs : 2 * bs]
            + roll_frames(big[at, 0:bs], prev256, 1, False)
            + roll_frames(big[at, 2 * bs : 3 * bs], next256, -1, False)
        )
        sec_sa[at, :] = value
        return carry[0] + column_sums(value), carry[1] + column_sums(value * value)

    sum_sa, sq_sa = loop(bands, combine_sa, zero2(256))
    put("sa", 0, squash(sum_sa))
    put("sa", 256, squash(sq_sa))
    exchange_start("sa")

    total = exchange_end("fa")
    stats_fa = moments(*unpair32(total), fast_count)
    loop(bands, act_fa)
    sum_fb, sq_fb = loop(2, conv_fb, zero2(128))
    put("fb", 0, pair32(squash(sum_fb), squash(sq_fb)))
    exchange_start("fb")
    total = exchange_end("sa")

    stats_sa = moments(take(total, 0, 256), take(total, 256, 256), slow_count)

    def act_sa(i):
        normed, pre = before_act(sec_sa[rows_at(i, band), :], stats_sa, "sa")
        spread_columns(hcs, i, pre * sigmoid(pre))

    def act_fb(i):
        at = rows_at(i, band)
        normed, pre = before_act(sec_fb[at, :], stats_fb, "fb")
        hbf[at, :] = (pre * sigmoid(pre)).astype(BF16)

    loop(bands, act_sa)
    loads["wsb"].wait()

    def conv_sb(i, carry):
        value = None
        for a in range(3):
            at = pl.ds(pl.multiple_of(i * half + band * a, 16), half)
            for b in range(3):
                tap = 3 * a + b
                term = dot(hcs[at, bs * b : bs * (b + 1)], wsb[bs * tap : bs * (tap + 1), :], NT)
                value = term if value is None else value + term
        sec_sb[rows_at(i, half), :] = value
        return carry[0] + column_sums(value), carry[1] + column_sums(value * value)

    sum_sb, sq_sb = loop(2, conv_sb, zero2(256))
    put("sb", 0, squash(sum_sb))
    put("sb", 256, squash(sq_sb))
    exchange_start("sb")

    total = exchange_end("fb")
    stats_fb = moments(*unpair32(total), fast_count)
    loop(bands, act_fb)

    def widen_fast(i, carry):
        at = rows_at(i, half)
        value = dot(hbf[at, :], wfc[...], NT)
        sec_fc[at, :] = value
        return carry[0] + column_sums(value), carry[1] + column_sums(value * value)

    sum_fc, sq_fc = loop(2, widen_fast, zero2(512))

    def fold4(vector):
        return vector[:, 0:128] + vector[:, 128:256] + vector[:, 256:384] + vector[:, 384:512]

    put("fc", 0, squash(fold4(sum_fc)))
    put("fc", 128, squash(fold4(sq_fc)))
    exchange_start("fc")
    total = exchange_end("sb")

    stats_sb = moments(take(total, 0, 256), take(total, 256, 256), slow_count)

    def act_sb(i, carry):
        at = rows_at(i, band)
        normed, pre = before_act(sec_sb[at, :], stats_sb, "sb")
        value = (pre * sigmoid(pre)).astype(BF16)
        hbs[at, :] = value
        return carry + column_sums(value.astype(F32))

    sum_hbs = loop(bands, act_sb, jnp.zeros((8, bs), F32))
    loads["wsc"].wait()
    mid = cs_n // 2

    def widen_slow(part):
        lanes = slice(part * mid, (part + 1) * mid)

        def step(i, carry):
            at = rows_at(i, half)
            value = dot(hbs[at, :], wsc[lanes, :], NT)
            big[at, lanes] = value
            return carry + column_sums(value * value)

        return loop(2, step, jnp.zeros((8, mid), F32))

    put("sc0", 0, squash(sum_hbs))
    put("sc0", 256, squash(widen_slow(0)))
    exchange_start("sc0")
    put("sc1", 0, squash(widen_slow(1)))
    exchange_start("sc1")
    total = exchange_end("fc")
    stats_fc = moments(take(total, 0, 128), take(total, 128, 128), fast_count)

    loads["cf"].wait()

    def finish_fast(i, carry):
        at, fat = rows_at(i, band), rows_at(i, fband)
        bias_sum, gain_sum = carry
        stage_b[...] = cf[fat, :].astype(F32)
        for phase in range(4):
            lanes = slice(128 * phase, 128 * (phase + 1))
            mean, scale = stats_fc
            normed = (sec_fc[at, lanes] - mean) * scale
            total_in = vx[at, 256 + 128 * phase : 384 + 128 * phase].astype(F32)
            value = total_in + normed * gain("fc") + bias("fc")
            gate = sigmoid(value)
            stage_a[pl.ds(phase, band, stride=4), :] = value * gate
            grad = stage_b[pl.ds(phase, band, stride=4), :] * (gate * (1.0 + value * (1.0 - gate)))
            gsf[at, lanes] = grad
            bias_sum = bias_sum + column_sums(grad)
            gain_sum = gain_sum + column_sums(grad * normed)
        xf[fat, :] = stage_a[...].astype(BF16)
        return bias_sum, gain_sum

    bias_fc, gain_fc = loop(bands, finish_fast, zero2(128))
    fast_store = store(xf, fast_h, 10)
    put("fc_back", 0, squash(bias_fc))
    put("fc_back", 128, squash(gain_fc))
    exchange_start("fc_back")
    loads["cs"].wait()
    total = exchange_end("sc0")
    squares = jnp.concatenate([take(total, 256, mid), exchange_end("sc1")], axis=1)
    whole = lax.dot_general(
        jnp.broadcast_to(take(total, 0, 256), (8, bs)), wsc[...].astype(F32), (NT, ((), ())),
        precision=lax.Precision.HIGHEST, preferred_element_type=F32,
    )[0:1, :]

    stats_sc = moments(whole, squares, slow_count)
    thin = 32
    mean_sc, scale_sc = stats_sc
    half_lead = 0.5 * gain("sc") * scale_sc
    half_level = 0.5 * bias("sc") - mean_sc * half_lead

    def finish_slow(part):
        lanes = slice(part * mid, (part + 1) * mid)
        lead, level = half_lead[:, lanes], half_level[:, lanes]
        mean, scale = mean_sc[:, lanes], scale_sc[:, lanes]

        def step(i, carry):
            at = rows_at(i, thin)
            section = big[at, lanes]
            h = 0.5 * xs[at, lanes].astype(F32) + (section * lead + level)
            t = jnp.tanh(h)
            out = h + h * t
            gate = 0.5 + 0.5 * t
            grad = cs[at, lanes].astype(F32) * (gate + out * (1.0 - gate))
            normed = (section - mean) * scale
            cs[at, lanes] = out.astype(BF16)
            gsum[at, lanes] = normed.astype(BF16)
            big[at, lanes] = grad
            return carry[0] + column_sums(grad), carry[1] + column_sums(grad * normed)

        return loop(rows // thin, step, zero2(mid))

    for part in range(2):
        bias_part, gain_part = finish_slow(part)
        put("sc%d_back" % part, 0, squash(bias_part))
        put("sc%d_back" % part, mid, squash(gain_part))
        exchange_start("sc%d_back" % part)
    slow_store = store(cs, slow_h, 11)

    total = exchange_end("fc_back")
    bias_fc, gain_fc = take(total, 0, 128), take(total, 128, 128)
    report("fc", bias_fc, gain_fc)
    def slope_pass(section, stats, name, buffer):
        def step(i, carry):
            at = rows_at(i, band)
            normed, pre = before_act(section[at, :], stats, name)
            gate = sigmoid(pre)
            grad = buffer[at, :] * (gate * (1.0 + pre * (1.0 - gate)))
            buffer[at, :] = grad
            return carry[0] + column_sums(grad), carry[1] + column_sums(grad * normed)

        return loop(bands, step, zero2(section.shape[1]))

    mean_fc, scale_fc = stats_fc
    lead_fc = gain("fc") * scale_fc
    tilt_fc = lead_fc * scale_fc * gain_fc * (1.0 / fast_count)
    level_fc = lead_fc * bias_fc * (1.0 / fast_count) - mean_fc * tilt_fc

    def low_fc(i):
        at = rows_at(i, band)
        for phase in range(4):
            lanes = slice(128 * phase, 128 * (phase + 1))
            value = gsf[at, lanes] * lead_fc - level_fc - sec_fc[at, lanes] * tilt_fc
            cf[pl.ds(pl.multiple_of(rows * phase + i * band, 16), band), :] = value.astype(BF16)

    loop(bands, low_fc)

    def back_fc(i):
        value = None
        for phase in range(4):
            at = pl.ds(pl.multiple_of(rows * phase + i * half, 16), half)
            term = dot(cf[at, :], wfc[128 * phase : 128 * (phase + 1), :], NN)
            value = term if value is None else value + term
        dbuf_f[rows_at(i, half), :] = value

    loop(2, back_fc)
    bias_fb, gain_fb = slope_pass(sec_fb, stats_fb, "fb", dbuf_f)
    put("fb_back", 0, pair32(squash(bias_fb), squash(gain_fb)))
    exchange_start("fb_back")
    slow_store.wait()
    sums = [exchange_end("sc%d_back" % part) for part in range(2)]

    bias_sc = jnp.concatenate([take(total, 0, mid) for total in sums], axis=1)
    gain_sc = jnp.concatenate([take(total, mid, mid) for total in sums], axis=1)
    report("sc", bias_sc, gain_sc)
    lead_sc = gain("sc") * stats_sc[1]
    level_sc = lead_sc * bias_sc * (1.0 / slow_count)
    tilt_sc = lead_sc * gain_sc * (1.0 / slow_count)

    def low_sc(i):
        at = rows_at(i, thin)
        grad = big[at, :]
        cs[at, :] = (grad * lead_sc - level_sc - gsum[at, :].astype(F32) * tilt_sc).astype(BF16)
        gsum[at, :] = grad.astype(BF16)

    loop(rows // thin, low_sc)

    def back_sc(i):
        at = rows_at(i, half)
        dbuf[at, :] = dot(cs[at, :], wsc[...], NN)

    loop(2, back_sc)

    bias_sb, gain_sb = slope_pass(sec_sb, stats_sb, "sb", dbuf)

    put("sb_back", 0, squash(bias_sb))
    put("sb_back", 256, squash(gain_sb))
    exchange_start("sb_back")

    slab_sc[0:cs_n, :] = dot(cs[...], hbs[...], TN)
    advance("sc")
    widening = None
    for phase in range(4):
        term = dot(hbf[...], cf[rows * phase : rows * (phase + 1), :], TN)[32 * phase : 32 * (phase + 1), :]
        widening = term if widening is None else widening + term
    slab[2, 704:736, 128:256] = widening
    slab[2, 736:768, 128:256] = jnp.zeros((32, LANES), F32)
    poll(0)

    bias_fb, gain_fb = unpair32(exchange_end("fb_back"))
    report("fb", bias_fb, gain_fb)
    vec_fb = back_vectors("fb", stats_fb, bias_fb, gain_fb, fast_count)

    def norm_grad(buffer, section, at, vectors):
        lead, level, tilt = vectors
        return buffer[at, :] * lead - level - section[at, :] * tilt

    def low_fb(i):
        spread_columns(gcf, i, norm_grad(dbuf_f, sec_fb, rows_at(i, band), vec_fb))

    loop(bands, low_fb)

    def back_fb(i):
        value = None
        for a in range(3):
            at = pl.ds(pl.multiple_of(i * half + band * (2 - a), 16), half)
            term = dot(gcf[at, :], wfbk[a], NN)
            value = term if value is None else value + term
        dbuf_f[rows_at(i, half), :] = value

    loop(2, back_fb)
    bias_fa, gain_fa = slope_pass(sec_fa, stats_fa, "fa", dbuf_f)
    put("fa_back", 0, pair32(squash(bias_fa), squash(gain_fa)))
    exchange_start("fa_back")
    poll(1)
    total = exchange_end("sb_back")

    bias_sb, gain_sb = take(total, 0, 256), take(total, 256, 256)
    report("sb", bias_sb, gain_sb)
    vec_sb = back_vectors("sb", stats_sb, bias_sb, gain_sb, slow_count)

    def low_sb(i):
        spread_columns(gcs, i, norm_grad(dbuf, sec_sb, rows_at(i, band), vec_sb))

    loop(bands, low_sb)

    def back_sb(i):
        value = None
        for a in range(3):
            at = pl.ds(pl.multiple_of(i * half + band * (2 - a), 16), half)
            for b in range(3):
                tap = 3 * a + b
                term = dot(gcs[at, bs * (2 - b) : bs * (3 - b)], wsb[bs * tap : bs * (tap + 1), :], NN)
                value = term if value is None else value + term
        dbuf[rows_at(i, half), :] = value

    loop(2, back_sb)
    poll(2)
    bias_sa, gain_sa = slope_pass(sec_sa, stats_sa, "sa", dbuf)

    put("sa_back", 0, squash(bias_sa))
    put("sa_back", 256, squash(gain_sa))
    exchange_start("sa_back")
    poll(3)

    for a in range(3):
        value = dot(gcs[band : band + rows, bs : 2 * bs], hcs[band * a : band * a + rows, :], TN)
        ref, lane = pieces["sb%d" % a]["ref"], pieces["sb%d" % a]["lane"]
        for b in range(3):
            ref[bs * b : bs * (b + 1), lane : lane + bs] = value[:, bs * b : bs * (b + 1)]
        advance("sb%d" % a)
    poll(4)
    for a in range(3):
        value = dot(gcf[band : band + rows, 128:256], hcf[band * a : band * a + rows, :], TN)
        for b in range(3):
            tap = 3 * a + b
            block = value[:, 128 * b : 128 * (b + 1)] * block_mask
            folded = fold_lanes(block[0:32] + block[32:64] + block[64:96] + block[96:128])
            folded = jnp.where(lane_group[0:32] == tap % 4, folded, 0.0)
            at = slice(608 + 32 * (tap // 4), 640 + 32 * (tap // 4))
            slab[2, at, 128:256] = folded if tap % 4 == 0 else slab[2, at, 128:256] + folded
    poll(5)
    bias_fa, gain_fa = unpair32(exchange_end("fa_back"))
    report("fa", bias_fa, gain_fa)
    vec_fa = back_vectors("fa", stats_fa, bias_fa, gain_fa, fast_count)

    def low_fa(i):
        at = rows_at(i, band)
        hbf[at, :] = norm_grad(dbuf_f, sec_fa, at, vec_fa).astype(BF16)

    loop(bands, low_fa)
    value = dot(hbf[...], vx[:, 128:896], TN)
    for k in range(3):
        piece = None
        for phase in range(4):
            term = value[32 * phase : 32 * (phase + 1), 128 * (phase + k) : 128 * (phase + k + 1)]
            piece = term if piece is None else piece + term
        slab[2, 512 + 32 * k : 544 + 32 * k, 128:256] = piece
    poll(6)
    total = exchange_end("sa_back")
    poll(7)

    bias_sa, gain_sa = take(total, 0, 256), take(total, 256, 256)
    report("sa", bias_sa, gain_sa)
    vec_sa = back_vectors("sa", stats_sa, bias_sa, gain_sa, slow_count)
    def low_sa(i):
        at = rows_at(i, band)
        value = norm_grad(dbuf, sec_sa, at, vec_sa)
        gcs[at, 0:bs] = roll_frames(value, prev256, -1, True).astype(BF16)
        gcs[at, bs : 2 * bs] = value.astype(BF16)
        gcs[at, 2 * bs :] = roll_frames(value, next256, 1, True).astype(BF16)

    loop(bands, low_sa)

    def narrow_gradient(k):
        ref, lane = pieces["sa%d" % k]["ref"], pieces["sa%d" % k]["lane"]
        source = xs[:, 256 * k : 256 * (k + 1)] if k < 4 else jl[...]
        ref[0 : 3 * bs, lane : lane + 256] = dot(gcs[0:rows, :], source, TN)
        advance("sa%d" % k)

    narrow_gradient(0)
    poll(8)

    def back_lateral(i):
        at = rows_at(i, half)
        dbuf[at, :] = dot(gcs[at, :], wsa[:, cs_n:], NN)

    loop(2, back_lateral)
    bias_lat, gain_lat = slope_pass(sec_lat, stats_lat, "lat", dbuf)
    put("lat_back", 0, squash(bias_lat))
    put("lat_back", 256, squash(gain_lat))
    exchange_start("lat_back")

    poll(9)

    for k in range(1, 4):
        narrow_gradient(k)
        poll(9 + k)
    total = exchange_end("lat_back")

    bias_lat, gain_lat = take(total, 0, 256), take(total, 256, 256)
    report("lat", bias_lat, gain_lat)
    vec_lat = back_vectors("lat", stats_lat, bias_lat, gain_lat, slow_count)

    def low_lat(i):
        at = rows_at(i, band)
        hbs[at, :] = norm_grad(dbuf, sec_lat, at, vec_lat).astype(BF16)

    loop(bands, low_lat)
    value = dot(hbs[...], vx[:, 0:640], TN)
    for k in range(5):
        at, lane = 256 * (k % 3), 128 * (k // 3)
        slab[2, at : at + 256, lane : lane + 128] = value[:, 128 * k : 128 * (k + 1)]
    advance("lt")
    poll(13)
    narrow_gradient(4)
    poll(14)

    def slow_back(i):
        at = rows_at(i, half)
        for tile in range(cs_n // 256):
            lanes = slice(256 * tile, 256 * (tile + 1))
            value = gsum[at, lanes].astype(F32) + dot(gcs[at, :], wsa[:, lanes], NN)
            gsum[at, lanes] = value.astype(BF16)

    for part in range(2):
        slow_back(part)
        poll(15 + part)
    sgrad_store = store(gsum, sgrad_h, 12)

    fast_store.wait()

    def fast_back(i):
        at, fat = rows_at(i, 2 * band), rows_at(i, 2 * fband)
        conv = dot(hbf[at, :], wfa[...], NN)
        side_in = dot(hbs[at, :], wlat[...], NN)

        def lane(values, block):
            return values[:, 128 * block : 128 * (block + 1)]

        grads = [gsf[at, 128 * phase : 128 * (phase + 1)] + lane(conv, phase + 1) for phase in range(4)]
        grads[0] = grads[0] + roll_frames(lane(conv, 5), next128, 1, True) + lane(side_in, 2)
        grads[1] = grads[1] + lane(side_in, 3)
        grads[2] = grads[2] + lane(side_in, 4) + roll_frames(lane(side_in, 0), prev128, -1, True)
        grads[3] = grads[3] + roll_frames(lane(side_in, 1) + lane(conv, 0), prev128, -1, True)
        for part in range(2):
            for phase in range(4):
                stage_a[pl.ds(phase, band, stride=4), :] = grads[phase][part * band : (part + 1) * band]
            xf[rows_at(2 * i + part, fband), :] = stage_a[...].astype(BF16)

    loop(bands // 4, fast_back)
    poll(17)
    loop(bands // 2 - bands // 4, lambda i: fast_back(i + bands // 4))
    fgrad_store = store(xf, fgrad_h, 13)
    poll(18)

    def pack(rows_ref, target):
        lanes = lax.broadcasted_iota(jnp.int32, (24, LANES), 1)
        stacked = rows_ref[...]
        turned = pltpu.roll(stacked, 64, 1)
        moved = jnp.where(lanes >= 64, turned, pltpu.roll(turned, 1, 0))[0:16, :]
        first = jnp.where(lane16[0:1, :] < 32, stacked[16:17, :], stacked[17:18, :])
        first = jnp.where(lane16[0:1, :] < 64, first, moved[0:1, :])
        target[...] = moved * factor
        target[0:1, :] = first * factor

    pack(gain_rows, dgains)
    pack(bias_rows, dbiases)
    poll(19)
    while not all(done(name) for name in order):
        for name in order:
            if not done(name):
                advance(name)
    for slot, copy in enumerate(stores):
        copy.wait()
    sgrad_store.wait()
    fgrad_store.wait()


def hand_on(*refs):
    sources, targets, held, sem = refs[0:13], refs[13:26], refs[26:34], refs[34]
    loads = [pltpu.make_async_copy(sources[k], held[k], sem.at[k]) for k in range(8)]
    stores = [pltpu.make_async_copy(held[k], targets[k], sem.at[8 + k]) for k in range(8)]
    for copy in loads:
        copy.start()
    for k in range(8, 13):
        targets[k][...] = sources[k][...]
    for load, copy in zip(loads, stores):
        load.wait()
        copy.start()
    for copy in stores:
        copy.wait()


def body(
    slow_input,
    fast_input,
    clip_ids,
    fast_narrow,
    fast_spatial,
    fast_widen,
    lateral_conv,
    slow_narrow,
    slow_spatial,
    slow_widen,
    norm_gains,
    norm_biases,
    slow_cotangent,
    fast_cotangent,
):
    n_dp, n_rep = lax.axis_size("dp"), lax.axis_size("rep")
    low = 2 if n_dp % 2 == 0 else 1
    high = n_dp // low
    frames, plane, channels = slow_input.shape
    fast_frames, _, fast_channels = fast_input.shape
    side = math.isqrt(plane)
    rows = frames * plane
    slow_count = rows * n_dp * n_rep
    fast_count = slow_count * (fast_frames // frames)

    def flat(values):
        return values.transpose(1, 0, 2).reshape(values.shape[0] * values.shape[1], values.shape[2])

    def unflat(values, count):
        return values.reshape(plane, count, values.shape[1]).transpose(1, 0, 2)

    widths = [
        fast_narrow.shape[1], fast_spatial.shape[1], fast_widen.shape[0], lateral_conv.shape[1],
        slow_narrow.shape[1], slow_spatial.shape[1], slow_widen.shape[0],
    ]

    def lay_out(vector):
        return jnp.pad(vector, (0, 16 * LANES - vector.shape[0])).reshape(16, LANES)

    cf = fast_channels
    bs = slow_spatial.shape[1]
    band = side * frames
    any_spec = pl.BlockSpec(memory_space=pl.ANY)
    vmem_spec = pl.BlockSpec(memory_space=pltpu.VMEM)
    near_low = n_dp if n_dp * n_rep <= 32 else low
    pad = rows + 2 * band

    def shape(dims, dtype):
        return jax.ShapeDtypeStruct(dims, dtype)

    out_shape = [
        shape((rows, channels), BF16), shape((4 * rows, cf), BF16),
        shape((rows, channels), BF16), shape((4 * rows, cf), BF16),
        shape((3 * bs, channels + bs), F32), shape((9 * bs, bs), F32), shape((channels, bs), F32),
        shape((5 * bs, cf), F32), shape((96, cf), F32), shape((288, 32), F32), shape((32, cf), F32),
        shape((16, LANES), F32), shape((16, LANES), F32),
        shape((10, max(high // 4, 1), 32, 256), F32),
    ]
    scratch = [
        pltpu.VMEM((rows, channels), BF16), pltpu.VMEM((rows, channels), BF16),
        pltpu.VMEM((rows, channels), BF16), pltpu.VMEM((4 * rows, cf), BF16),
        pltpu.VMEM((4 * rows, cf), BF16), pltpu.VMEM((rows, channels), F32),
        pltpu.VMEM((rows, 512), F32), pltpu.VMEM((rows, 512), F32),
        pltpu.VMEM((pad, 3 * bs), BF16), pltpu.VMEM((pad, 3 * bs), BF16),
        pltpu.VMEM((pad, 384), BF16), pltpu.VMEM((pad, 384), BF16),
        pltpu.VMEM((rows, bs), F32), pltpu.VMEM((rows, bs), F32), pltpu.VMEM((rows, bs), F32),
        pltpu.VMEM((rows, bs), F32),
        pltpu.VMEM((rows, 128), F32), pltpu.VMEM((rows, 128), F32), pltpu.VMEM((rows, 128), F32),
        pltpu.VMEM((rows, bs), BF16), pltpu.VMEM((rows, bs), BF16), pltpu.VMEM((rows, 128), BF16),
        pltpu.VMEM((rows, 896), BF16), pltpu.VMEM((3, 1512, 256), F32), pltpu.VMEM((2016, 256), F32),
        pltpu.VMEM((768, 256), F32), pltpu.VMEM((max(high // 4, 1), 32, 256), F32),
        pltpu.VMEM((3 * bs, channels + bs), BF16), pltpu.VMEM((9 * bs, bs), BF16),
        pltpu.VMEM((channels, bs), BF16),
        pltpu.VMEM((96, cf), BF16), pltpu.VMEM((288, 32), BF16), pltpu.VMEM((32, cf), BF16),
        pltpu.VMEM((bs, 640), BF16), pltpu.VMEM((128, 768), BF16),
        pltpu.VMEM((3, 128, 384), BF16), pltpu.VMEM((3, 384, 128), BF16), pltpu.VMEM((512, 128), BF16),
        pltpu.VMEM((4 * band, cf), F32), pltpu.VMEM((4 * band, cf), F32),
        pltpu.VMEM((24, LANES), F32), pltpu.VMEM((24, LANES), F32),
        pltpu.VMEM((near_low * n_rep, 1, sum(TURNS.values())), F32),
        pltpu.VMEM((max(n_dp // near_low, 1), 1, sum(TURNS.values())), F32),
        pltpu.SemaphoreType.DMA((len(TURNS), 2)), pltpu.SemaphoreType.DMA((len(TURNS), 2)),
        pltpu.SemaphoreType.DMA((32,)), pltpu.SemaphoreType.DMA((10, 2)),
        pltpu.SemaphoreType.DMA((10, 11)), pltpu.SemaphoreType.DMA((10, 11)),
    ]
    factor = 1.0 / math.sqrt(float(slow_count))
    results = pl.pallas_call(
        functools.partial(kernel, (n_dp, n_rep, low, frames, side, float(slow_count), float(fast_count), factor)),
        out_shape=out_shape,
        in_specs=[any_spec] * 4 + [pl.BlockSpec(memory_space=pltpu.SMEM)] + [any_spec] * 7 + [vmem_spec] * 2,
        out_specs=[any_spec] * 8 + [vmem_spec] * 5 + [any_spec],
        scratch_shapes=scratch,
        compiler_params=pltpu.CompilerParams(
            collective_id=0, has_side_effects=True, vmem_limit_bytes=65000 * 2**10
        ),
    )(
        flat(slow_input), flat(fast_input), flat(slow_cotangent), flat(fast_cotangent), clip_ids,
        fast_narrow.reshape(-1, cf), fast_spatial.reshape(-1, 32), fast_widen.T,
        lateral_conv.reshape(-1, cf), slow_narrow.reshape(3 * bs, -1), slow_spatial.reshape(9 * bs, bs),
        slow_widen, lay_out(norm_gains), lay_out(norm_biases),
    )
    results = list(results[0:13])
    handed = pl.pallas_call(
        hand_on,
        out_shape=out_shape[0:13],
        in_specs=[any_spec] * 8 + [vmem_spec] * 5,
        out_specs=[any_spec] * 8 + [vmem_spec] * 5,
        scratch_shapes=[pltpu.VMEM(item.shape, item.dtype) for item in out_shape[0:8]]
        + [pltpu.SemaphoreType.DMA((16,))],
        compiler_params=pltpu.CompilerParams(vmem_limit_bytes=64000 * 2**10),
    )(*results)
    slow_out, fast_out, slow_grad, fast_grad, dsa, dsb, dsc, dl, dfa, dfb, dfc, dgains, dbiases = handed

    def gather(packed):
        return packed.reshape(16 * LANES)[0 : sum(widths)]

    return (
        unflat(slow_out, frames),
        unflat(fast_out, fast_frames),
        unflat(slow_grad, frames),
        unflat(fast_grad, fast_frames),
        dfa.reshape(fast_narrow.shape),
        dfb.reshape(fast_spatial.shape),
        dfc.T,
        dl.reshape(lateral_conv.shape),
        dsa.reshape(slow_narrow.shape),
        dsb.reshape(slow_spatial.shape),
        dsc,
        gather(dgains),
        gather(dbiases),
    )


def solution(mesh):
    sharded = P(("dp", "rep"), None, None)
    return jax.shard_map(
        body,
        mesh=mesh,
        in_specs=(sharded, sharded, P(("dp", "rep"), None)) + (P(),) * 9 + (sharded, sharded),
        out_specs=(sharded,) * 4 + (P(),) * 9,
        check_vma=False,
    )
```

```python
import functools
import math

import jax
import jax.numpy as jnp
from jax import lax
from jax.experimental import pallas as pl
from jax.experimental.pallas import tpu as pltpu
from jax.sharding import PartitionSpec as P

EPS = 1e-05
F32 = jnp.float32
BF16 = jnp.bfloat16
MESH = pl.DeviceIdType.MESH
NN = ((1,), (0,))
NT = ((1,), (1,))
TN = ((0,), (0,))
LANES = 128
TURNS = {
    "lat": 512, "fa": 128, "sa": 512, "fb": 128, "sb": 512, "fc": 256, "sc0": 768, "sc1": 512,
    "sc0_back": 1024, "sc1_back": 1024, "fc_back": 256, "sb_back": 512, "fb_back": 128, "sa_back": 512,
    "fa_back": 128, "lat_back": 512,
}


ORDERS = {
    "plane": (("c", "x", "y", "z"), ("c", "y", "x", "z")),
    "halves": (("c", "x", "y", "z0", "z1"), ("c", "y", "x", "z0", "z1")),
    "between": (("c", "x", "z0", "z1", "y"), ("c", "y", "z0", "z1", "x")),
    "line": (("c", "z0", "z1", "x", "y"), ("c", "z0", "z1", "y", "x")),
}
ORDER_OF = {
    "sc": "halves",
    "sb0": "halves",
    "sb1": "line",
    "sb2": "plane",
    "sa0": "halves",
    "sa1": "between",
    "sa2": "plane",
    "sa3": "plane",
    "sa4": "halves",
    "lt": "halves",
}
POLLS = (
    (),
    ("sc",),
    (),
    (),
    ("sc", "sb0"),
    ("sb1",),
    ("sb2",),
    (),
    ("sc",),
    ("sb0", "sa0"),
    ("sb2", "sb1"),
    ("sc",),
    ("sb0", "sa1"),
    ("sa0", "sb2", "sa2", "sa3"),
    ("sb0", "sb1", "lt"),
    ("sa0", "sc", "sa1", "sa4"),
    ("sb2", "sa2"),
    ("sb0",),
    ("sa0", "sc", "sa3", "sb1"),
    (
        "lt", "sa1", "sa4", "sb0", "sa2", "sb2", "sa0", "lt", "sc", "sa4", "sa3", "sa1",
        "sb0", "sb2", "sa2", "lt", "sa0", "sc", "sa4", "sb1", "sb0", "sa3", "sb2", "sa1",
        "sa0", "sa2", "lt", "sc", "sb1", "sa4", "sb2", "sa1", "sb0", "sa3", "lt", "sa0",
        "sa2", "sa4", "sc", "sb1", "sa3", "sa1", "lt", "sb0", "sa0", "sa2", "sa4", "sb1",
        "sa1", "sa3", "sa2", "lt", "sa0", "sa4", "sa3", "sa1", "sb1", "lt", "sa4", "sb1",
        "sa1", "lt", "sa4",
    ),
)


def dot(left, right, dims):
    return lax.dot_general(left, right, (dims, ((), ())), preferred_element_type=F32)


def column_sums(values):
    return jnp.sum(values.reshape(values.shape[0] // 8, 8, values.shape[1]), axis=0)


def squash(partial):
    return jnp.sum(partial, axis=0, keepdims=True)


def fold_lanes(values):
    half = values + pltpu.roll(values, 64, 1)
    return half + pltpu.roll(half, 32, 1)


def loop(count, body, init=None, unroll=1):
    if init is None:

        def plain(index, carry):
            body(index)
            return carry

        lax.fori_loop(0, count, plain, 0, unroll=unroll)
        return None
    return lax.fori_loop(0, count, body, init, unroll=unroll)


def rows_at(index, size):
    return pl.ds(pl.multiple_of(index * size, 16), size)


def kernel(
    dims,
    xs_h, xf_h, cs_h, cf_h, clip, wfa_h, wfb_h, wfc_h, wl_h, wsa_h, wsb_h, wsc_h, gains_h, biases_h,
    slow_h, fast_h, sgrad_h, fgrad_h, dsa_h, dsb_h, dsc_h, dl_h, small_h, dgains_h, dbiases_h, extra_h,
    xs, cs, gsum, xf, cf, big, sec_fc, gsf, hcs, gcs, hcf, gcf,
    sec_lat, sec_sa, sec_sb, dbuf, sec_fa, sec_fb, dbuf_f, jl, hbs, hbf, vx, slab, slab_sc, summed, gathered,
    wsa, wsb, wsc, gains_in, biases_in, vectors, masks, wfa_in, wfb_in, wfc_in, wlat, wfa, wfb, wfbk, wfc,
    stage_a, stage_b, gain_rows, bias_rows, near, far, sum_send, sum_recv, io_sem, own_sem, big_send, big_recv,
):
    n_dp, n_rep, low, frames, side, slow_count, fast_count, factor = dims
    rows = xs.shape[0]
    half = rows // 2
    band = side * frames
    bands = side
    fband = 4 * band
    cs_n = xs.shape[1]
    bs = wsb.shape[1]

    dp_i, rep_i = lax.axis_index("dp"), lax.axis_index("rep")
    dp_lo, dp_hi = lax.rem(dp_i, low), lax.div(dp_i, low)
    high = n_dp // low
    direct = n_dp * n_rep <= 32
    near_low = n_dp if direct else low
    near_dp, far_dp = lax.rem(dp_i, near_low), lax.div(dp_i, near_low)
    near_peers = [
        (far_dp * near_low + lax.rem(near_dp + a, near_low), lax.rem(rep_i + b, n_rep))
        for a in range(near_low)
        for b in range(n_rep)
        if a or b
    ]
    far_count = n_dp // near_low
    far_peers = [(lax.rem(far_dp + a, far_count) * near_low + near_dp, rep_i) for a in range(1, far_count)]
    stages = [(near, near_dp * n_rep + rep_i, near_peers)]
    if far_peers:
        stages.append((far, far_dp, far_peers))

    c, x = lax.rem(rep_i, 2), lax.div(rep_i, 2)
    y, z = dp_lo, lax.rem(dp_hi, 4)
    outer, outers = lax.div(dp_hi, 4), high // 4
    core_peer = (dp_i, 2 * x + 1 - c)
    x_peer = (dp_i, 2 * (1 - x) + c)
    y_peer = (dp_hi * low + 1 - y, rep_i)
    def z_peer(flip):
        return ((outer * 4 + z + flip - 2 * flip * lax.rem(lax.div(z, flip), 2)) * low + y, rep_i)

    z_peers = [((outer * 4 + lax.rem(z + k, 4)) * low + y, rep_i) for k in range(1, 4)]
    outer_peers = [((lax.rem(outer + k, outers) * 4 + z) * low + y, rep_i) for k in range(1, outers)]

    barrier = pltpu.get_barrier_semaphore()
    greeted = near_peers + far_peers
    for peer in greeted:
        pl.semaphore_signal(barrier, inc=1, device_id=peer, device_id_type=MESH)

    loads = {}
    for slot, (name, src, dst) in enumerate([
        ("xf", xf_h, xf), ("wfa", wfa_h, wfa_in), ("xs", xs_h, xs),
        ("wsa", wsa_h, wsa), ("wfb", wfb_h, wfb_in), ("wfc", wfc_h, wfc_in), ("wsb", wsb_h, wsb),
        ("wsc", wsc_h, wsc), ("cf", cf_h, cf), ("cs", cs_h, cs), ("gains", gains_h, gains_in), ("biases", biases_h, biases_in),
    ]):
        loads[name] = pltpu.make_async_copy(src, dst, io_sem.at[slot])
        loads[name].start()
        if name == "wfa":
            taps = [
                pltpu.make_async_copy(
                    wl_h.at[pl.ds(bs * k, bs)], wlat.at[:, pl.ds(LANES * k, LANES)], io_sem.at[27 + k]
                )
                for k in range(5)
            ]
            for tap in taps:
                tap.start()
    stores = []

    def store(src, dst, slot):
        copy = pltpu.make_async_copy(src, dst, io_sem.at[slot])
        copy.start()
        return copy

    turn_at, turn_index = {}, {}
    for index, (turn, width) in enumerate(TURNS.items()):
        turn_at[turn] = sum(list(TURNS.values())[:index])
        turn_index[turn] = index

    def put(turn, at, vector):
        near[stages[0][1], :, pl.ds(turn_at[turn] + at, vector.shape[1])] = vector

    def sum_copy(turn, stage, first, count, peer):
        buffer = stages[stage][0]
        block = buffer.at[pl.ds(first, count), :, pl.ds(turn_at[turn], TURNS[turn])]
        return pltpu.make_async_remote_copy(
            src_ref=block, dst_ref=block, send_sem=sum_send.at[stage, turn_index[turn]],
            recv_sem=sum_recv.at[stage, turn_index[turn]], device_id=peer, device_id_type=MESH,
        )

    def exchange_start(turn):
        for peer in near_peers:
            sum_copy(turn, 0, stages[0][1], 1, peer).start()

    def exchange_end(turn):
        lanes = pl.ds(turn_at[turn], TURNS[turn])
        for stage, (buffer, rank, peers) in enumerate(stages):
            if stage:
                buffer[rank, :, lanes] = total
                for peer in peers:
                    sum_copy(turn, stage, rank, 1, peer).start()
            copy = sum_copy(turn, stage, 0, len(peers), peers[0])
            copy.wait_recv()
            total = jnp.sum(buffer[:, :, lanes], axis=0)
            copy.wait_send()
        return total

    def take(total, at, width):
        return total[:, at : at + width]

    def pair32(first, second):
        group = lax.broadcasted_iota(jnp.int32, (8, LANES), 1) // 32
        rows8 = (8, LANES)
        first = fold_lanes(jnp.broadcast_to(first, rows8))
        second = fold_lanes(jnp.broadcast_to(second, rows8))
        return jnp.where(group == 0, first, jnp.where(group == 1, second, 0.0))[0:1, :]

    def unpair32(total):
        group = lax.broadcasted_iota(jnp.int32, (8, LANES), 1) // 32
        total = jnp.broadcast_to(total, (8, LANES))
        first = fold_lanes(jnp.where(group == 0, total, 0.0))
        second = fold_lanes(jnp.where(group == 1, total, 0.0))
        return first[0:1, :], second[0:1, :]

    pieces = {}

    bits = {"c": (c, core_peer), "x": (x, x_peer), "y": (y, y_peer),
            "z0": (lax.rem(z, 2), z_peer(1)), "z1": (lax.div(z, 2), z_peer(2))}

    def add_piece(name, ref, lane, size, index):
        axes = ORDERS[ORDER_OF[name]]
        piece = {"name": name, "ref": ref, "lane": lane, "size": size, "index": index, "step": 0, "axes": axes}
        starts, counts, arriving = [[0], [0]], [size], [size]
        for step, pair in enumerate(zip(*axes)):
            for side, axis in enumerate(pair):
                if axis == "z":
                    starts[side].append(starts[side][-1] + z * (counts[-1] // 4))
                else:
                    starts[side].append(starts[side][-1] + bits[axis][0] * (counts[-1] // 2))
            counts.append(counts[-1] // (4 if pair[0] == "z" else 2))
            arriving.append(arriving[-1] + (3 if pair[0] == "z" else 1) * counts[-1])
        piece.update(starts=starts, counts=counts, arriving=arriving, steps=len(axes[0]))
        pieces[name] = piece

    for k in range(2):
        add_piece("sb%d" % k, sec_fc, 256 * k, 768, k)
    for k in range(4):
        add_piece("sa%d" % k, big, 256 * k, 768, 2 + k)
    add_piece("sb2", slab.at[0], 0, 768, 6)
    add_piece("sa4", slab.at[1], 0, 768, 7)
    add_piece("lt", slab.at[2], 0, 768, 8)
    add_piece("sc", slab_sc, 0, 1024, 9)

    def span(piece, start, count, lane=0, width=256):
        return piece["ref"].at[pl.ds(pl.multiple_of(start, 8), count), pl.ds(piece["lane"] + lane, width)]

    def send(piece, step, src, dst, peer):
        pltpu.make_async_remote_copy(
            src_ref=src, dst_ref=dst, send_sem=big_send.at[piece["index"]],
            recv_sem=big_recv.at[piece["index"], step], device_id=peer, device_id_type=MESH,
        ).start()

    def result(piece, start, count, lane=0, width=256):
        name = piece["name"]
        start = pl.multiple_of(start, 8)
        if name == "lt":
            return summed.at[pl.ds(start, count), pl.ds(lane, width)]
        if name == "sc":
            return dsc_h.at[pl.ds(start, count), pl.ds(lane, width)]
        k = int(name[2])
        if name[1] == "a":
            return dsa_h.at[pl.ds(start, count), pl.ds(256 * k + lane, width)]
        return dsb_h.at[pl.ds(768 * k + start, count), pl.ds(lane, width)]

    def own_copies(piece):
        count, sem = piece["counts"][-1], own_sem.at[piece["index"]]
        return [
            pltpu.make_async_copy(
                span(piece, start[-1], count, 128 * side, 128),
                result(piece, start[-1], count, 128 * side, 128),
                sem.at[side],
            )
            for side, start in enumerate(piece["starts"])
        ]

    def arrived(piece, step, rows_in):
        block = span(piece, 0, rows_in) if step < piece["steps"] else result(piece, 0, rows_in)
        copy = pltpu.make_async_remote_copy(
            src_ref=block, dst_ref=block, send_sem=big_send.at[piece["index"]],
            recv_sem=big_recv.at[piece["index"], step], device_id=core_peer, device_id_type=MESH,
        )
        copy.wait_recv()
        copy.wait_send()

    def add_rows(piece, target, source, count, lane, width):
        lanes = pl.ds(piece["lane"] + lane, width)
        chunk = piece["size"] // 32
        ref = piece["ref"]

        def step(i):
            into = pl.ds(pl.multiple_of(target + i * chunk, 8), chunk)
            ref[into, lanes] = ref[into, lanes] + ref[pl.ds(pl.multiple_of(source + i * chunk, 8), chunk), lanes]

        loop(count // chunk, step)

    order = ["sc", "sb0", "sb1", "sb2", "sa0", "sa1", "sa2", "sa3", "sa4", "lt"]

    def unpack_small():
        stores.append(store(summed.at[:, pl.ds(0, 128)], dl_h.at[pl.ds(0, 768)], 16))
        stores.append(store(summed.at[pl.ds(0, 512), pl.ds(128, 128)], dl_h.at[pl.ds(768, 512)], 17))
        stores.append(store(summed.at[pl.ds(512, 256), pl.ds(128, 128)], small_h, 18))

    def poll(turn):
        for name in POLLS[turn]:
            advance(name)

    def done(name):
        return pieces[name]["step"] > 2 * pieces[name]["steps"]

    def advance(name):
        piece = pieces[name]
        step, steps, index = piece["step"], piece["steps"], piece["index"]
        piece["step"] = step + 1
        starts, counts, arriving, axes = piece["starts"], piece["counts"], piece["arriving"], piece["axes"]
        ref, lane = piece["ref"], piece["lane"]

        def received(last):
            fan = 3 if axes[0][last] == "z" else 1
            return fan * counts[last + 1]

        if 0 < step < steps or (step == steps and axes[0][-1] != "z"):
            arrived(piece, step - 1, received(step - 1))
            if step == 1:
                add_rows(piece, starts[0][1], arriving[0], counts[1], 0, 256)
            else:
                for side in range(2):
                    add_rows(piece, starts[side][step], arriving[step - 1], counts[step], 128 * side, 128)
        elif step == steps:
            arrived(piece, step - 1, received(step - 1))
        elif step > steps:
            arrived(piece, step - 1, received(2 * steps - step))

        if step < steps:
            held, keep = counts[step], counts[step + 1]
            if step == 0:
                at = starts[0][0] + (1 - c) * keep
                send(piece, 0, span(piece, at, keep), span(piece, arriving[0], keep), core_peer)
                return
            for side in range(2):
                axis, start = axes[side][step], starts[side][step]
                if axis == "z":
                    for k, peer in enumerate(z_peers):
                        at, into = start + lax.rem(z + k + 1, 4) * keep, arriving[step] + k * keep
                        send(
                            piece, step, span(piece, at, keep, 128 * side, 128),
                            span(piece, into, keep, 128 * side, 128), peer,
                        )
                else:
                    bit, peer = bits[axis]
                    at = start + (1 - bit) * keep
                    send(
                        piece, step, span(piece, at, keep, 128 * side, 128),
                        span(piece, arriving[step], keep, 128 * side, 128), peer,
                    )
        elif step == steps:
            last = counts[-1]
            own = [
                (pl.ds(pl.multiple_of(starts[side][-1], 8), last), pl.ds(lane + 128 * side, 128))
                for side in range(2)
            ]
            both = jnp.concatenate([ref[own[0]], ref[own[1]]], axis=1)
            if axes[0][-1] == "z":
                for k in range(3):
                    both = both + ref[pl.ds(arriving[steps - 1] + k * last, last), pl.ds(lane, 256)]
            if outers > 1:
                held = span(piece, arriving[steps - 1], last)
                ref[pl.ds(arriving[steps - 1], last), pl.ds(lane, 256)] = both
                for peer in outer_peers:
                    send(piece, 10, held, extra_h.at[index, outer, pl.ds(0, last)], peer)
                block = extra_h.at[index, pl.ds(0, outers - 1), pl.ds(0, last)]
                copy = pltpu.make_async_remote_copy(
                    src_ref=block, dst_ref=block, send_sem=big_send.at[index], recv_sem=big_recv.at[index, 10],
                    device_id=core_peer, device_id_type=MESH,
                )
                copy.wait_recv()
                copy.wait_send()
                for src, dst in (
                    (held, extra_h.at[index, outer, pl.ds(0, last)]),
                    (extra_h.at[index], gathered),
                ):
                    copy = pltpu.make_async_copy(src, dst, own_sem.at[index, 0])
                    copy.start()
                    copy.wait()
                both = jnp.sum(gathered[:, pl.ds(0, last), :], axis=0)
            both = both * factor
            for side in range(2):
                ref[own[side]] = both[:, 128 * side : 128 * (side + 1)]
        if steps <= step < 2 * steps:
            back = 2 * steps - 1 - step
            count = counts[back + 1]
            if step == steps + 1:
                for copy in own_copies(piece):
                    copy.wait()
            if back == 0:
                block = result(piece, starts[0][1], count)
                send(piece, step, block, block, core_peer)
                return
            for side in range(2):
                axis, start = axes[side][back], starts[side][back + 1]
                block = result(piece, start, count, 128 * side, 128)
                source = span(piece, start, count, 128 * side, 128) if step == steps else block
                for peer in z_peers if axis == "z" else [bits[axis][1]]:
                    send(piece, step, source, block, peer)
            if step == steps:
                for copy in own_copies(piece):
                    copy.start()
        elif step == 2 * steps and name == "lt":
            unpack_small()

    spots = {"fc": 0, "lat": 1, "sa": 3, "sb": 5, "sc": 7, "fa": 16, "fb": 17}

    lane16 = lax.broadcasted_iota(jnp.int32, (16, LANES), 1)

    def unpack(packed):
        fa = fold_lanes(jnp.where(lane16 // 32 == 0, packed, 0.0))[0:1, :]
        fb = fold_lanes(jnp.where(lane16 // 32 == 1, packed, 0.0))[0:1, :]
        turned = pltpu.roll(packed, 64, 1)
        moved = jnp.where(lane16 < 64, turned, pltpu.roll(turned, 15, 0))
        found = {"fa": fa, "fb": fb}
        at = 0
        for name, count in (("fc", 1), ("lat", 2), ("sa", 2), ("sb", 2), ("sc", 8)):
            found[name] = jnp.concatenate([moved[at + k : at + k + 1, :] for k in range(count)], axis=1)
            at += count
        return found

    held = [0]

    def settle(vector):
        at, width = held[0], vector.shape[1]
        held[0] += 1
        vectors[at, 0:1, 0:width] = vector

        def read(lanes=slice(0, width)):
            return vectors[at, 0:1, lanes]

        return read

    gains, biases = {}, {}

    def read_parameters():
        for name, flat_in, target in (("gains", gains_in, gains), ("biases", biases_in, biases)):
            loads[name].wait()
            count = flat_in.shape[0]
            stage_a[0:16, :] = jnp.zeros((16, LANES), F32)
            for row in range(16):
                width = min(LANES, count - row * LANES)
                stage_a[row : row + 1, 0:width] = flat_in[pl.ds(row * LANES, width)].reshape(1, width)
            for key, vector in unpack(stage_a[0:16, :]).items():
                target[key] = settle(vector)

    def gain(name):
        return gains[name]()

    def bias(name):
        return biases[name]()

    def moments(name, total, squares, count):
        mean = total * (1.0 / count)
        scale = lax.rsqrt(squares * (1.0 / count) - mean * mean + EPS)
        return settle(mean), settle(scale), settle(0.5 * gain(name) * scale), settle(0.5 * bias(name))

    def back_vectors(name, stats, bias_total, gain_total, count):
        mean, scale = stats[0](), stats[1]()
        lead = gain(name) * scale
        tilt = lead * scale * gain_total * (1.0 / count)
        level = lead * bias_total * (1.0 / count) - mean * tilt
        return settle(lead), settle(level), settle(tilt)

    def report(name, bias_total, gain_total):
        at = spots[name]
        for piece in range(bias_total.shape[1] // LANES):
            lanes = slice(piece * LANES, (piece + 1) * LANES)
            gain_rows[at + piece : at + piece + 1, :] = gain_total[:, lanes]
            bias_rows[at + piece : at + piece + 1, :] = bias_total[:, lanes]

    def silu_of(values, stats):
        h = (values - stats[0]()) * stats[2]() + stats[3]()
        return h + h * jnp.tanh(h)

    def slope_of(h):
        t = jnp.tanh(h)
        out, gate = h + h * t, 0.5 + 0.5 * t
        return out, gate + out * (1.0 - gate)

    def clip_masks(width):
        frame = lax.broadcasted_iota(jnp.int32, (1, 8, width), 1)
        with_prev = jnp.zeros((1, 8, width), F32)
        with_next = jnp.zeros((1, 8, width), F32)
        for t in range(1, frames):
            same = jnp.where(clip[0, t] == clip[0, t - 1], 1.0, 0.0)
            with_prev = jnp.where(frame == t, same, with_prev)
            with_next = jnp.where(frame == t - 1, same, with_next)
        return with_prev, with_next

    masks[0:1], masks[1:2] = clip_masks(256)

    def prev(width):
        return masks[0:1, :, 0:width]

    def following(width):
        return masks[1:2, :, 0:width]

    def roll_frames(values, mask, step, mask_first):
        grouped = values.reshape(values.shape[0] // 8, 8, values.shape[1])
        if mask_first:
            grouped = grouped * mask
        grouped = pltpu.roll(grouped, step % 8, 1)
        if not mask_first:
            grouped = grouped * mask
        return grouped.reshape(values.shape)

    def spread_columns(target, index, values):
        width = values.shape[1]
        nothing = jnp.zeros((frames, width), F32)
        at = pl.ds(pl.multiple_of((index + 1) * band, 16), band)
        target[at, 0:width] = jnp.concatenate([nothing, values[: band - frames]], axis=0).astype(BF16)
        target[at, width : 2 * width] = values.astype(BF16)
        target[at, 2 * width :] = jnp.concatenate([values[frames:], nothing], axis=0).astype(BF16)

    gain_rows[...] = jnp.zeros(gain_rows.shape, F32)
    bias_rows[...] = jnp.zeros(bias_rows.shape, F32)
    for target in (hcs, gcs, hcf, gcf):
        edge = jnp.zeros((band, target.shape[1]), BF16)
        target[0:band, :] = edge
        target[band + rows : rows + 2 * band, :] = edge

    def lane_groups(count=LANES):
        return lax.broadcasted_iota(jnp.int32, (count, LANES), 1) // 32

    def block_mask():
        row_group = lax.broadcasted_iota(jnp.int32, (LANES, LANES), 0) // 32
        return jnp.where(lane_groups() == row_group, 1.0, 0.0)

    repeat_lanes = jnp.where(
        lax.broadcasted_iota(jnp.int32, (32, LANES), 1) % 32 == lax.broadcasted_iota(jnp.int32, (32, LANES), 0),
        1.0, 0.0,
    ).astype(BF16)

    wfa[...] = jnp.zeros(wfa.shape, BF16)
    loads["wfa"].wait()
    for phase in range(4):
        for k in range(3):
            wfa[32 * phase : 32 * (phase + 1), LANES * (phase + k) : LANES * (phase + k + 1)] = wfa_in[
                32 * k : 32 * (k + 1), :
            ]
    loads["xf"].wait()

    def arrange(i):
        at = rows_at(i, band)
        stage_a[...] = xf[rows_at(i, fband), :].astype(F32)
        phases = [stage_a[pl.ds(phase, band, stride=4), :] for phase in range(4)]
        vx[at, 0:128] = roll_frames(phases[2], prev(128), 1, False).astype(BF16)
        vx[at, 128:256] = roll_frames(phases[3], prev(128), 1, False).astype(BF16)
        for phase in range(4):
            vx[at, 256 + 128 * phase : 384 + 128 * phase] = phases[phase].astype(BF16)
        vx[at, 768:896] = roll_frames(phases[0], following(128), -1, False).astype(BF16)

    loop(bands, arrange, unroll=2)
    for tap in taps:
        tap.wait()

    def zero2(width):
        return (jnp.zeros((8, width), F32), jnp.zeros((8, width), F32))

    def conv_fa(i, carry):
        at = rows_at(i, half)
        value = dot(vx[at, 128:896], wfa[...], NT)
        sec_fa[at, :] = value
        return carry[0] + column_sums(value), carry[1] + column_sums(value * value)

    def conv_lat(i, carry):
        at = rows_at(i, half)
        value = dot(vx[at, 0:640], wlat[...], NT)
        sec_lat[at, :] = value
        return carry[0] + column_sums(value), carry[1] + column_sums(value * value)

    sum_lat, sq_lat = loop(2, conv_lat, zero2(256))
    put("lat", 0, squash(sum_lat))
    put("lat", 256, squash(sq_lat))
    pl.semaphore_wait(barrier, len(greeted))
    exchange_start("lat")

    sum_fa, sq_fa = loop(2, conv_fa, zero2(128))
    put("fa", 0, pair32(squash(sum_fa), squash(sq_fa)))
    exchange_start("fa")

    loads["xs"].wait()
    loads["wsa"].wait()

    def narrow_main(i):
        at = rows_at(i, half)
        for k in range(3):
            big[at, bs * k : bs * (k + 1)] = dot(xs[at, :], wsa[bs * k : bs * (k + 1), 0:cs_n], NT)

    loop(2, narrow_main)
    loads["wfb"].wait()
    loads["wfc"].wait()
    spread = dot(wfb_in[...], repeat_lanes, NN)
    for a in range(3):
        for b in range(3):
            piece = spread[32 * (3 * a + b) : 32 * (3 * a + b + 1), :]
            block = (jnp.concatenate([piece] * 4, axis=0) * block_mask()).astype(BF16)
            wfb[a, :, LANES * b : LANES * (b + 1)] = block
            wfbk[a, LANES * (2 - b) : LANES * (3 - b), :] = block
    widen = dot(wfc_in[...], repeat_lanes, TN)
    for phase in range(4):
        wfc[LANES * phase : LANES * (phase + 1), :] = jnp.where(lane_groups() == phase, widen, 0.0).astype(BF16)
    read_parameters()
    total = exchange_end("lat")

    stats_lat = moments("lat", take(total, 0, 256), take(total, 256, 256), slow_count)

    def act_fa(i):
        spread_columns(hcf, i, silu_of(sec_fa[rows_at(i, band), :], stats_fa))

    def act_lat(i):
        at = rows_at(i, 2 * band)
        jl[at, :] = silu_of(sec_lat[at, :], stats_lat).astype(BF16)

    loop(bands // 2, act_lat)

    def conv_fb(i, carry):
        value = None
        for a in range(3):
            at = pl.ds(pl.multiple_of(i * half + band * a, 16), half)
            term = dot(hcf[at, :], wfb[a], NT)
            value = term if value is None else value + term
        sec_fb[rows_at(i, half), :] = value
        return carry[0] + column_sums(value), carry[1] + column_sums(value * value)

    def narrow_lateral(i):
        at = rows_at(i, half)
        for k in range(3):
            big[at, bs * k : bs * (k + 1)] += dot(jl[at, :], wsa[bs * k : bs * (k + 1), cs_n:], NT)

    loop(2, narrow_lateral)

    def combine_sa(i, carry):
        at = rows_at(i, band)
        value = (
            big[at, bs : 2 * bs]
            + roll_frames(big[at, 0:bs], prev(256), 1, False)
            + roll_frames(big[at, 2 * bs : 3 * bs], following(256), -1, False)
        )
        sec_sa[at, :] = value
        return carry[0] + column_sums(value), carry[1] + column_sums(value * value)

    sum_sa, sq_sa = loop(bands, combine_sa, zero2(256))
    put("sa", 0, squash(sum_sa))
    put("sa", 256, squash(sq_sa))
    exchange_start("sa")

    total = exchange_end("fa")
    stats_fa = moments("fa", *unpair32(total), fast_count)
    loop(bands, act_fa, unroll=2)
    sum_fb, sq_fb = loop(2, conv_fb, zero2(128))
    put("fb", 0, pair32(squash(sum_fb), squash(sq_fb)))
    exchange_start("fb")
    total = exchange_end("sa")

    stats_sa = moments("sa", take(total, 0, 256), take(total, 256, 256), slow_count)

    def act_sa(i):
        spread_columns(hcs, i, silu_of(sec_sa[rows_at(i, band), :], stats_sa))

    def act_fb(i):
        at = rows_at(i, 2 * band)
        hbf[at, :] = silu_of(sec_fb[at, :], stats_fb).astype(BF16)

    loop(bands, act_sa, unroll=2)
    loads["wsb"].wait()

    def conv_sb(i, carry):
        value = None
        for a in range(3):
            at = pl.ds(pl.multiple_of(i * half + band * a, 16), half)
            for b in range(3):
                tap = 3 * a + b
                term = dot(hcs[at, bs * b : bs * (b + 1)], wsb[bs * tap : bs * (tap + 1), :], NT)
                value = term if value is None else value + term
        sec_sb[rows_at(i, half), :] = value
        return carry[0] + column_sums(value), carry[1] + column_sums(value * value)

    sum_sb, sq_sb = loop(2, conv_sb, zero2(256))
    put("sb", 0, squash(sum_sb))
    put("sb", 256, squash(sq_sb))
    exchange_start("sb")

    total = exchange_end("fb")
    stats_fb = moments("fb", *unpair32(total), fast_count)
    loop(bands // 2, act_fb)

    def widen_fast(i, carry):
        at = rows_at(i, half)
        value = dot(hbf[at, :], wfc[...], NT)
        sec_fc[at, :] = value
        return carry[0] + column_sums(value), carry[1] + column_sums(value * value)

    sum_fc, sq_fc = loop(2, widen_fast, zero2(512))

    def fold4(vector):
        return vector[:, 0:128] + vector[:, 128:256] + vector[:, 256:384] + vector[:, 384:512]

    put("fc", 0, squash(fold4(sum_fc)))
    put("fc", 128, squash(fold4(sq_fc)))
    exchange_start("fc")
    total = exchange_end("sb")

    stats_sb = moments("sb", take(total, 0, 256), take(total, 256, 256), slow_count)

    def act_sb(i, carry):
        at = rows_at(i, 2 * band)
        value = silu_of(sec_sb[at, :], stats_sb).astype(BF16)
        hbs[at, :] = value
        return carry + column_sums(value.astype(F32))

    sum_hbs = loop(bands // 2, act_sb, jnp.zeros((8, bs), F32))
    loads["wsc"].wait()
    mid = cs_n // 2

    def widen_slow(part):
        lanes = slice(part * mid, (part + 1) * mid)

        def step(i, carry):
            at = rows_at(i, half)
            value = dot(hbs[at, :], wsc[lanes, :], NT)
            big[at, lanes] = value
            return carry + column_sums(value * value)

        return loop(2, step, jnp.zeros((8, mid), F32))

    put("sc0", 0, squash(sum_hbs))
    put("sc0", 256, squash(widen_slow(0)))
    exchange_start("sc0")
    put("sc1", 0, squash(widen_slow(1)))
    exchange_start("sc1")
    total = exchange_end("fc")
    stats_fc = moments("fc", take(total, 0, 128), take(total, 128, 128), fast_count)

    loads["cf"].wait()

    def finish_fast(i, carry):
        at, fat = rows_at(i, band), rows_at(i, fband)
        bias_sum, gain_sum = carry
        stage_b[...] = cf[fat, :].astype(F32)
        for phase in range(4):
            lanes = slice(128 * phase, 128 * (phase + 1))
            centred = sec_fc[at, lanes] - stats_fc[0]()
            total_in = vx[at, 256 + 128 * phase : 384 + 128 * phase].astype(F32)
            out, slope = slope_of(0.5 * total_in + (centred * stats_fc[2]() + stats_fc[3]()))
            stage_a[pl.ds(phase, band, stride=4), :] = out
            grad = stage_b[pl.ds(phase, band, stride=4), :] * slope
            gsf[at, lanes] = grad
            bias_sum = bias_sum + column_sums(grad)
            gain_sum = gain_sum + column_sums(grad * centred)
        xf[fat, :] = stage_a[...].astype(BF16)
        return bias_sum, gain_sum

    bias_fc, gain_fc = loop(bands, finish_fast, zero2(128))
    fast_store = store(xf, fast_h, 10)
    put("fc_back", 0, squash(bias_fc))
    put("fc_back", 128, squash(gain_fc) * stats_fc[1]())
    exchange_start("fc_back")
    loads["cs"].wait()
    total = exchange_end("sc0")
    squares = take(total, 256, mid)
    whole = settle(
        lax.dot_general(
            jnp.broadcast_to(take(total, 0, 256), (8, bs)), wsc[...].astype(F32), (NT, ((), ())),
            precision=lax.Precision.HIGHEST, preferred_element_type=F32,
        )[0:1, :]
    )
    squares = jnp.concatenate([squares, exchange_end("sc1")], axis=1)
    stats_sc = moments("sc", whole(), squares, slow_count)

    def finish_slow(part):
        lanes = slice(part * mid, (part + 1) * mid)
        def step(i, carry):
            at = rows_at(i, band)
            mean, lead, level = [stats_sc[k](lanes) for k in (0, 2, 3)]
            centred = big[at, lanes] - mean
            out, slope = slope_of(0.5 * xs[at, lanes].astype(F32) + (centred * lead + level))
            grad = cs[at, lanes].astype(F32) * slope
            cs[at, lanes] = out.astype(BF16)
            gsum[at, lanes] = centred.astype(BF16)
            big[at, lanes] = grad
            return carry[0] + column_sums(grad), carry[1] + column_sums(grad * centred)

        bias_part, gain_part = loop(bands, step, zero2(mid))
        return squash(bias_part), squash(gain_part) * stats_sc[1](lanes)

    for part in range(2):
        bias_part, gain_part = finish_slow(part)
        put("sc%d_back" % part, 0, bias_part)
        put("sc%d_back" % part, mid, gain_part)
        exchange_start("sc%d_back" % part)
    slow_store = store(cs, slow_h, 11)

    total = exchange_end("fc_back")
    bias_fc, gain_fc = take(total, 0, 128), take(total, 128, 128)
    report("fc", bias_fc, gain_fc)
    def slope_pass(section, stats, buffer):
        def step(i, carry):
            at = rows_at(i, 2 * band)
            centred = section[at, :] - stats[0]()
            grad = buffer[at, :] * slope_of(centred * stats[2]() + stats[3]())[1]
            buffer[at, :] = grad
            return carry[0] + column_sums(grad), carry[1] + column_sums(grad * centred)

        bias_sum, gain_sum = loop(bands // 2, step, zero2(section.shape[1]))
        return squash(bias_sum), squash(gain_sum) * stats[1]()

    lead_fc, level_fc, tilt_fc = back_vectors("fc", stats_fc, bias_fc, gain_fc, fast_count)

    def low_fc(i):
        at = rows_at(i, band)
        for phase in range(4):
            lanes = slice(128 * phase, 128 * (phase + 1))
            value = gsf[at, lanes] * lead_fc() - level_fc() - sec_fc[at, lanes] * tilt_fc()
            cf[pl.ds(pl.multiple_of(rows * phase + i * band, 16), band), :] = value.astype(BF16)

    loop(bands, low_fc, unroll=2)

    def back_fc(i):
        value = None
        for phase in range(4):
            at = pl.ds(pl.multiple_of(rows * phase + i * half, 16), half)
            term = dot(cf[at, :], wfc[128 * phase : 128 * (phase + 1), :], NN)
            value = term if value is None else value + term
        dbuf_f[rows_at(i, half), :] = value

    loop(2, back_fc)
    bias_fb, gain_fb = slope_pass(sec_fb, stats_fb, dbuf_f)
    put("fb_back", 0, pair32(bias_fb, gain_fb))
    exchange_start("fb_back")
    slow_store.wait()
    sums = [exchange_end("sc%d_back" % part) for part in range(2)]

    bias_sc = jnp.concatenate([take(total, 0, mid) for total in sums], axis=1)
    gain_sc = jnp.concatenate([take(total, mid, mid) for total in sums], axis=1)
    report("sc", bias_sc, gain_sc)
    lead_sc = gain("sc") * stats_sc[1]()
    tilt_sc = settle(lead_sc * stats_sc[1]() * gain_sc * (1.0 / slow_count))
    level_sc = settle(lead_sc * bias_sc * (1.0 / slow_count))
    lead_sc = settle(lead_sc)

    def low_sc(i):
        at = rows_at(i, 32)
        grad = big[at, :]
        cs[at, :] = (grad * lead_sc() - level_sc() - gsum[at, :].astype(F32) * tilt_sc()).astype(BF16)
        gsum[at, :] = grad.astype(BF16)

    loop(rows // 32, low_sc, unroll=7)

    def back_sc(i):
        at = rows_at(i, half)
        dbuf[at, :] = dot(cs[at, :], wsc[...], NN)

    loop(2, back_sc)

    bias_sb, gain_sb = slope_pass(sec_sb, stats_sb, dbuf)

    put("sb_back", 0, bias_sb)
    put("sb_back", 256, gain_sb)
    exchange_start("sb_back")

    slab_sc[0:cs_n, :] = dot(cs[...], hbs[...], TN)
    advance("sc")
    widening = None
    for phase in range(4):
        term = dot(hbf[...], cf[rows * phase : rows * (phase + 1), :], TN)[32 * phase : 32 * (phase + 1), :]
        widening = term if widening is None else widening + term
    slab[2, 704:736, 128:256] = widening
    slab[2, 736:768, 128:256] = jnp.zeros((32, LANES), F32)
    poll(0)

    bias_fb, gain_fb = unpair32(exchange_end("fb_back"))
    report("fb", bias_fb, gain_fb)
    vec_fb = back_vectors("fb", stats_fb, bias_fb, gain_fb, fast_count)

    def norm_grad(buffer, section, at, vectors):
        lead, level, tilt = vectors
        return buffer[at, :] * lead() - level() - section[at, :] * tilt()

    def low_fb(i):
        spread_columns(gcf, i, norm_grad(dbuf_f, sec_fb, rows_at(i, band), vec_fb))

    loop(bands, low_fb, unroll=2)

    def back_fb(i):
        value = None
        for a in range(3):
            at = pl.ds(pl.multiple_of(i * half + band * (2 - a), 16), half)
            term = dot(gcf[at, :], wfbk[a], NN)
            value = term if value is None else value + term
        dbuf_f[rows_at(i, half), :] = value

    loop(2, back_fb)
    bias_fa, gain_fa = slope_pass(sec_fa, stats_fa, dbuf_f)
    put("fa_back", 0, pair32(bias_fa, gain_fa))
    exchange_start("fa_back")
    poll(1)
    total = exchange_end("sb_back")

    bias_sb, gain_sb = take(total, 0, 256), take(total, 256, 256)
    report("sb", bias_sb, gain_sb)
    vec_sb = back_vectors("sb", stats_sb, bias_sb, gain_sb, slow_count)

    def low_sb(i):
        spread_columns(gcs, i, norm_grad(dbuf, sec_sb, rows_at(i, band), vec_sb))

    loop(bands, low_sb, unroll=2)

    def back_sb(i):
        value = None
        for a in range(3):
            at = pl.ds(pl.multiple_of(i * half + band * (2 - a), 16), half)
            for b in range(3):
                tap = 3 * a + b
                term = dot(gcs[at, bs * (2 - b) : bs * (3 - b)], wsb[bs * tap : bs * (tap + 1), :], NN)
                value = term if value is None else value + term
        dbuf[rows_at(i, half), :] = value

    loop(2, back_sb)
    poll(2)
    bias_sa, gain_sa = slope_pass(sec_sa, stats_sa, dbuf)

    put("sa_back", 0, bias_sa)
    put("sa_back", 256, gain_sa)
    exchange_start("sa_back")
    poll(3)

    for a in range(3):
        value = dot(gcs[band : band + rows, bs : 2 * bs], hcs[band * a : band * a + rows, :], TN)
        ref, lane = pieces["sb%d" % a]["ref"], pieces["sb%d" % a]["lane"]
        for b in range(3):
            ref[bs * b : bs * (b + 1), lane : lane + bs] = value[:, bs * b : bs * (b + 1)]
        advance("sb%d" % a)
    poll(4)
    for a in range(3):
        value = dot(gcf[band : band + rows, 128:256], hcf[band * a : band * a + rows, :], TN)
        for b in range(3):
            tap = 3 * a + b
            block = value[:, 128 * b : 128 * (b + 1)] * block_mask()
            folded = fold_lanes(block[0:32] + block[32:64] + block[64:96] + block[96:128])
            folded = jnp.where(lane_groups(32) == tap % 4, folded, 0.0)
            at = slice(608 + 32 * (tap // 4), 640 + 32 * (tap // 4))
            slab[2, at, 128:256] = folded if tap % 4 == 0 else slab[2, at, 128:256] + folded
    poll(5)
    bias_fa, gain_fa = unpair32(exchange_end("fa_back"))
    report("fa", bias_fa, gain_fa)
    vec_fa = back_vectors("fa", stats_fa, bias_fa, gain_fa, fast_count)

    def low_fa(i):
        at = rows_at(i, band)
        hbf[at, :] = norm_grad(dbuf_f, sec_fa, at, vec_fa).astype(BF16)

    loop(bands, low_fa, unroll=2)
    value = dot(hbf[...], vx[:, 128:896], TN)
    for k in range(3):
        piece = None
        for phase in range(4):
            term = value[32 * phase : 32 * (phase + 1), 128 * (phase + k) : 128 * (phase + k + 1)]
            piece = term if piece is None else piece + term
        slab[2, 512 + 32 * k : 544 + 32 * k, 128:256] = piece
    poll(6)
    total = exchange_end("sa_back")
    poll(7)

    bias_sa, gain_sa = take(total, 0, 256), take(total, 256, 256)
    report("sa", bias_sa, gain_sa)
    vec_sa = back_vectors("sa", stats_sa, bias_sa, gain_sa, slow_count)
    def low_sa(i):
        at = rows_at(i, band)
        value = norm_grad(dbuf, sec_sa, at, vec_sa)
        gcs[at, 0:bs] = roll_frames(value, prev(256), -1, True).astype(BF16)
        gcs[at, bs : 2 * bs] = value.astype(BF16)
        gcs[at, 2 * bs :] = roll_frames(value, following(256), 1, True).astype(BF16)

    loop(bands, low_sa, unroll=2)

    def narrow_gradient(k):
        ref, lane = pieces["sa%d" % k]["ref"], pieces["sa%d" % k]["lane"]
        source = xs[:, 256 * k : 256 * (k + 1)] if k < 4 else jl[...]
        ref[0 : 3 * bs, lane : lane + 256] = dot(gcs[0:rows, :], source, TN)
        advance("sa%d" % k)

    narrow_gradient(0)
    poll(8)

    def back_lateral(i):
        at = rows_at(i, half)
        dbuf[at, :] = dot(gcs[at, :], wsa[:, cs_n:], NN)

    loop(2, back_lateral)
    bias_lat, gain_lat = slope_pass(sec_lat, stats_lat, dbuf)
    put("lat_back", 0, bias_lat)
    put("lat_back", 256, gain_lat)
    exchange_start("lat_back")

    poll(9)

    for k in range(1, 4):
        narrow_gradient(k)
        poll(9 + k)
    total = exchange_end("lat_back")

    bias_lat, gain_lat = take(total, 0, 256), take(total, 256, 256)
    report("lat", bias_lat, gain_lat)

    def pack(rows_ref, target):
        lanes = lax.broadcasted_iota(jnp.int32, (24, LANES), 1)
        stacked = rows_ref[...]
        turned = pltpu.roll(stacked, 64, 1)
        moved = jnp.where(lanes >= 64, turned, pltpu.roll(turned, 1, 0))[0:16, :]
        first = jnp.where(lane16[0:1, :] < 32, stacked[16:17, :], stacked[17:18, :])
        first = jnp.where(lane16[0:1, :] < 64, first, moved[0:1, :])
        target[...] = moved * factor
        target[0:1, :] = first * factor

    pack(gain_rows, stage_b.at[pl.ds(0, 16)])
    pack(bias_rows, stage_b.at[pl.ds(16, 16)])
    parameter_stores = [
        store(stage_b.at[pl.ds(0, 16)], dgains_h, 19), store(stage_b.at[pl.ds(16, 16)], dbiases_h, 20)
    ]
    vec_lat = back_vectors("lat", stats_lat, bias_lat, gain_lat, slow_count)

    def low_lat(i):
        at = rows_at(i, band)
        hbs[at, :] = norm_grad(dbuf, sec_lat, at, vec_lat).astype(BF16)

    loop(bands, low_lat, unroll=2)
    value = dot(hbs[...], vx[:, 0:640], TN)
    for k in range(5):
        at, lane = 256 * (k % 3), 128 * (k // 3)
        slab[2, at : at + 256, lane : lane + 128] = value[:, 128 * k : 128 * (k + 1)]
    advance("lt")
    poll(13)
    narrow_gradient(4)
    poll(14)

    def slow_back(i):
        at = rows_at(i, half)
        for tile in range(cs_n // 256):
            lanes = slice(256 * tile, 256 * (tile + 1))
            value = gsum[at, lanes].astype(F32) + dot(gcs[at, :], wsa[:, lanes], NN)
            gsum[at, lanes] = value.astype(BF16)

    for part in range(2):
        slow_back(part)
        poll(15 + part)
    sgrad_store = store(gsum, sgrad_h, 12)

    fast_store.wait()

    def fast_back(i):
        at, fat = rows_at(i, 2 * band), rows_at(i, 2 * fband)
        conv = dot(hbf[at, :], wfa[...], NN)
        side_in = dot(hbs[at, :], wlat[...], NN)

        def lane(values, block):
            return values[:, 128 * block : 128 * (block + 1)]

        grads = [gsf[at, 128 * phase : 128 * (phase + 1)] + lane(conv, phase + 1) for phase in range(4)]
        grads[0] = grads[0] + roll_frames(lane(conv, 5), following(128), 1, True) + lane(side_in, 2)
        grads[1] = grads[1] + lane(side_in, 3)
        grads[2] = grads[2] + lane(side_in, 4) + roll_frames(lane(side_in, 0), prev(128), -1, True)
        grads[3] = grads[3] + roll_frames(lane(side_in, 1) + lane(conv, 0), prev(128), -1, True)
        for part in range(2):
            for phase in range(4):
                stage_a[pl.ds(phase, band, stride=4), :] = grads[phase][part * band : (part + 1) * band]
            xf[rows_at(2 * i + part, fband), :] = stage_a[...].astype(BF16)

    loop(bands // 4, fast_back)
    poll(17)
    loop(bands // 2 - bands // 4, lambda i: fast_back(i + bands // 4))
    fgrad_store = store(xf, fgrad_h, 13)
    poll(18)

    poll(19)
    while not all(done(name) for name in order):
        for name in order:
            if not done(name):
                advance(name)
    for copy in stores + parameter_stores:
        copy.wait()
    sgrad_store.wait()
    fgrad_store.wait()


def hand_on(*refs):
    sources, targets, held, small, sem = refs[0:11], refs[11:24], refs[24:35], refs[35:40], refs[40]
    loads = [pltpu.make_async_copy(sources[k], held[k], sem.at[k]) for k in range(11)]
    stores = [pltpu.make_async_copy(held[k], targets[k], sem.at[11 + k]) for k in range(8)]
    stores += [pltpu.make_async_copy(small[k], targets[8 + k], sem.at[19 + k]) for k in range(5)]
    for k in (8, 9, 10, 0, 1, 2, 3, 4, 5, 6, 7):
        loads[k].start()
    for k in (8, 9, 10):
        loads[k].wait()
    small[0][...] = held[8][0:96, :]
    for tap in range(9):
        at = 96 + 32 * (tap // 4)
        small[1][32 * tap : 32 * (tap + 1), :] = held[8][at : at + 32, 32 * (tap % 4) : 32 * (tap % 4 + 1)]
    small[2][...] = held[8][192:224, :]
    for source, target in ((held[9], small[3]), (held[10], small[4])):
        count = target.shape[0]
        for row in range(16):
            width = min(LANES, count - row * LANES)
            target[pl.ds(row * LANES, width)] = source[row : row + 1, 0:width].reshape(width)
    for copy in stores[8:13]:
        copy.start()
    for load, copy in zip(loads[0:8], stores[0:8]):
        load.wait()
        copy.start()
    for copy in stores:
        copy.wait()


def body(
    slow_input,
    fast_input,
    clip_ids,
    fast_narrow,
    fast_spatial,
    fast_widen,
    lateral_conv,
    slow_narrow,
    slow_spatial,
    slow_widen,
    norm_gains,
    norm_biases,
    slow_cotangent,
    fast_cotangent,
):
    n_dp, n_rep = lax.axis_size("dp"), lax.axis_size("rep")
    low = 2 if n_dp % 2 == 0 else 1
    high = n_dp // low
    frames, plane, channels = slow_input.shape
    fast_frames, _, fast_channels = fast_input.shape
    side = math.isqrt(plane)
    rows = frames * plane
    slow_count = rows * n_dp * n_rep
    fast_count = slow_count * (fast_frames // frames)

    def flat(values):
        return values.transpose(1, 0, 2).reshape(values.shape[0] * values.shape[1], values.shape[2])

    def unflat(values, count):
        return values.reshape(plane, count, values.shape[1]).transpose(1, 0, 2)

    widths = [
        fast_narrow.shape[1], fast_spatial.shape[1], fast_widen.shape[0], lateral_conv.shape[1],
        slow_narrow.shape[1], slow_spatial.shape[1], slow_widen.shape[0],
    ]

    cf = fast_channels
    bs = slow_spatial.shape[1]
    band = side * frames
    any_spec = pl.BlockSpec(memory_space=pl.ANY)
    vmem_spec = pl.BlockSpec(memory_space=pltpu.VMEM)
    near_low = n_dp if n_dp * n_rep <= 32 else low
    stages = 1 if near_low == n_dp else 2
    pad = rows + 2 * band

    def shape(dims, dtype):
        return jax.ShapeDtypeStruct(dims, dtype)

    out_shape = [
        shape((rows, channels), BF16), shape((4 * rows, cf), BF16),
        shape((rows, channels), BF16), shape((4 * rows, cf), BF16),
        shape((3 * bs, channels + bs), F32), shape((9 * bs, bs), F32), shape((channels, bs), F32),
        shape((5 * bs, cf), F32), shape((256, cf), F32), shape((16, LANES), F32), shape((16, LANES), F32),
        shape((10, max(high // 4, 1), 32, 256), F32),
    ]
    scratch = [
        pltpu.VMEM((rows, channels), BF16), pltpu.VMEM((rows, channels), BF16),
        pltpu.VMEM((rows, channels), BF16), pltpu.VMEM((4 * rows, cf), BF16),
        pltpu.VMEM((4 * rows, cf), BF16), pltpu.VMEM((rows, channels), F32),
        pltpu.VMEM((rows, 512), F32), pltpu.VMEM((rows, 512), F32),
        pltpu.VMEM((pad, 3 * bs), BF16), pltpu.VMEM((pad, 3 * bs), BF16),
        pltpu.VMEM((pad, 384), BF16), pltpu.VMEM((pad, 384), BF16),
        pltpu.VMEM((rows, bs), F32), pltpu.VMEM((rows, bs), F32), pltpu.VMEM((rows, bs), F32),
        pltpu.VMEM((rows, bs), F32),
        pltpu.VMEM((rows, 128), F32), pltpu.VMEM((rows, 128), F32), pltpu.VMEM((rows, 128), F32),
        pltpu.VMEM((rows, bs), BF16), pltpu.VMEM((rows, bs), BF16), pltpu.VMEM((rows, 128), BF16),
        pltpu.VMEM((rows, 896), BF16), pltpu.VMEM((3, 1512, 256), F32), pltpu.VMEM((2016, 256), F32),
        pltpu.VMEM((768, 256), F32), pltpu.VMEM((max(high // 4, 1), 32, 256), F32),
        pltpu.VMEM((3 * bs, channels + bs), BF16), pltpu.VMEM((9 * bs, bs), BF16),
        pltpu.VMEM((channels, bs), BF16), pltpu.VMEM(norm_gains.shape, F32), pltpu.VMEM(norm_gains.shape, F32),
        pltpu.VMEM((72, 8, channels), F32), pltpu.VMEM((2, 8, 256), F32),
        pltpu.VMEM((96, cf), BF16), pltpu.VMEM((288, 32), BF16), pltpu.VMEM((32, cf), BF16),
        pltpu.VMEM((bs, 640), BF16), pltpu.VMEM((128, 768), BF16),
        pltpu.VMEM((3, 128, 384), BF16), pltpu.VMEM((3, 384, 128), BF16), pltpu.VMEM((512, 128), BF16),
        pltpu.VMEM((4 * band, cf), F32), pltpu.VMEM((4 * band, cf), F32),
        pltpu.VMEM((24, LANES), F32), pltpu.VMEM((24, LANES), F32),
        pltpu.VMEM((near_low * n_rep, 1, sum(TURNS.values())), F32),
        pltpu.VMEM((max(n_dp // near_low, 1), 1, sum(TURNS.values())), F32),
        pltpu.SemaphoreType.DMA((stages, len(TURNS))), pltpu.SemaphoreType.DMA((stages, len(TURNS))),
        pltpu.SemaphoreType.DMA((32,)), pltpu.SemaphoreType.DMA((10, 2)),
        pltpu.SemaphoreType.DMA((10,)), pltpu.SemaphoreType.DMA((10, 10 if high == 4 else 11)),
    ]
    factor = 1.0 / math.sqrt(float(slow_count))
    results = pl.pallas_call(
        functools.partial(kernel, (n_dp, n_rep, low, frames, side, float(slow_count), float(fast_count), factor)),
        out_shape=out_shape,
        in_specs=[any_spec] * 4 + [pl.BlockSpec(memory_space=pltpu.SMEM)] + [any_spec] * 9,
        out_specs=[any_spec] * 12,
        scratch_shapes=scratch,
        compiler_params=pltpu.CompilerParams(
            collective_id=0, has_side_effects=True, vmem_limit_bytes=65000 * 2**10
        ),
    )(
        flat(slow_input), flat(fast_input), flat(slow_cotangent), flat(fast_cotangent), clip_ids,
        fast_narrow.reshape(-1, cf), fast_spatial.reshape(-1, 32), fast_widen.T,
        lateral_conv.reshape(-1, cf), slow_narrow.reshape(3 * bs, -1), slow_spatial.reshape(9 * bs, bs),
        slow_widen, norm_gains, norm_biases,
    )
    final = out_shape[0:8] + [
        shape((96, cf), F32), shape((288, 32), F32), shape((32, cf), F32),
        shape(norm_gains.shape, F32), shape(norm_gains.shape, F32),
    ]
    handed = pl.pallas_call(
        hand_on,
        out_shape=final,
        in_specs=[any_spec] * 11,
        out_specs=[any_spec] * 13,
        scratch_shapes=[pltpu.VMEM(item.shape, item.dtype) for item in out_shape[0:11] + final[8:13]]
        + [pltpu.SemaphoreType.DMA((24,))],
        compiler_params=pltpu.CompilerParams(vmem_limit_bytes=64000 * 2**10),
    )(*results[0:11])
    slow_out, fast_out, slow_grad, fast_grad, dsa, dsb, dsc, dl, dfa, dfb, dfc, dgains, dbiases = handed

    return (
        unflat(slow_out, frames),
        unflat(fast_out, fast_frames),
        unflat(slow_grad, frames),
        unflat(fast_grad, fast_frames),
        dfa.reshape(fast_narrow.shape),
        dfb.reshape(fast_spatial.shape),
        dfc.T,
        dl.reshape(lateral_conv.shape),
        dsa.reshape(slow_narrow.shape),
        dsb.reshape(slow_spatial.shape),
        dsc,
        dgains,
        dbiases,
    )


def solution(mesh):
    sharded = P(("dp", "rep"), None, None)
    return jax.shard_map(
        body,
        mesh=mesh,
        in_specs=(sharded, sharded, P(("dp", "rep"), None)) + (P(),) * 9 + (sharded, sharded),
        out_specs=(sharded,) * 4 + (P(),) * 9,
        check_vma=False,
    )
```

```python
import functools
import math

import jax
import jax.numpy as jnp
from jax import lax
from jax.experimental import pallas as pl
from jax.experimental.pallas import tpu as pltpu
from jax.sharding import PartitionSpec as P

EPS = 1e-05
F32 = jnp.float32
BF16 = jnp.bfloat16
MESH = pl.DeviceIdType.MESH
NN = ((1,), (0,))
NT = ((1,), (1,))
TN = ((0,), (0,))
LANES = 128
FA, FB, FC, LAT, SLOW_A, SLOW_B, SLOW_C = range(7)
FORWARD = {LAT: 512, FA: 128, SLOW_A: 512, FB: 128, SLOW_B: 512, FC: 256, SLOW_C: 768, SLOW_C + 1: 512}
BACKWARD = {SLOW_C: 1024, SLOW_C + 1: 1024, FC: 256, SLOW_B: 512, FB: 128, SLOW_A: 512, FA: 128, LAT: 512}
BACK = 8
TURNS = {**FORWARD, **{BACK + norm: lanes for norm, lanes in BACKWARD.items()}}


class Piece:
    pass


SC, SB, SA, LT = 0, 1, 4, 9
C, X, Y, Z, Z0, Z1 = range(6)
PLANE = ((C, X, Y, Z), (C, Y, X, Z))
HALVES = ((C, X, Y, Z0, Z1), (C, Y, X, Z0, Z1))
BETWEEN = ((C, X, Z0, Z1, Y), (C, Y, Z0, Z1, X))
LINE = ((C, Z0, Z1, X, Y), (C, Z0, Z1, Y, X))
ORDER_OF = (PLANE, HALVES, HALVES, PLANE, LINE, HALVES, HALVES, BETWEEN, PLANE, PLANE)
POLLS = (
    (),
    (0,),
    (),
    (),
    (),
    (),
    (),
    (0,),
    (),
    (1,),
    (2,),
    (0, 3),
    (),
    (),
    (),
    (1,),
    (),
    (2, 4),
    (3, 0, 1, 5),
    (2, 6),
    (3, 7),
    (5, 4, 9),
    (),
    (6, 2, 0, 1, 8),
    (7,),
    (5,),
    (3,),
    (
        9, 4, 2, 7, 0, 8, 5, 6, 4, 1, 2, 9, 7, 3, 6, 5, 0, 1, 4, 2, 7, 3, 9, 5,
        4, 6, 0, 1, 7, 8, 2, 9, 6, 3, 5, 4, 1, 9, 7, 8, 6, 3, 2, 5, 2, 4, 9, 1,
        7, 8, 1, 6, 5, 8, 4, 5, 9, 4, 7, 6, 7, 8, 6, 8,
    ),
)


def dot(left, right, dims):
    return lax.dot_general(left, right, (dims, ((), ())), preferred_element_type=F32)


def column_sums(values):
    return jnp.sum(values.reshape(values.shape[0] // 8, 8, values.shape[1]), axis=0)


def squash(partial):
    return jnp.sum(partial, axis=0, keepdims=True)


def fold_lanes(values):
    half = values + pltpu.roll(values, 64, 1)
    return half + pltpu.roll(half, 32, 1)


def loop(count, body, init=None, unroll=1):
    if init is None:

        def plain(index, carry):
            body(index)
            return carry

        lax.fori_loop(0, count, plain, 0, unroll=unroll)
        return None
    return lax.fori_loop(0, count, body, init, unroll=unroll)


def rows_at(index, size):
    return pl.ds(pl.multiple_of(index * size, 16), size)


def kernel(
    dims,
    xs_h, xf_h, cs_h, cf_h, clip, wfa_h, wfb_h, wfc_h, wl_h, wsa_h, wsb_h, wsc_h, gains_h, biases_h,
    slow_h, fast_h, gsum, xf, dsa, dsb, dsc_h, dl_h, small_h, dgains_h, dbiases_h, extra_h,
    xs, cs, cf, big, sec_fc, gsf, hcs, gcs, hcf, gcf,
    sec_lat, dbuf, sec_fa, sec_fb, dbuf_f, jl, hbs, hbf, vx, slab, slab_sc, summed,
    wsa, wsb, wsc, gains_in, biases_in, vectors, masks, wfa_in, wfb_in, wfc_in, wlat, wfa, wfb, wfbk, wfc,
    stage_a, gain_rows, bias_rows, near, far, sum_send, sum_recv, io_sem, own_sem, big_send, big_recv,
):
    n_dp, n_rep, low, frames, side, slow_count, fast_count, factor = dims
    sec_sa, sec_sb = dsa, dsb
    rows = xs.shape[0]
    half = rows // 2
    band = side * frames
    bands = side
    fband = 4 * band
    cs_n = xs.shape[1]
    bs = wsb.shape[1]

    dp_i, rep_i = lax.axis_index("dp"), lax.axis_index("rep")
    dp_lo, dp_hi = lax.rem(dp_i, low), lax.div(dp_i, low)
    high = n_dp // low
    direct = n_dp * n_rep <= 32
    near_low = n_dp if direct else low
    near_dp, far_dp = lax.rem(dp_i, near_low), lax.div(dp_i, near_low)
    near_peers = [
        (far_dp * near_low + lax.rem(near_dp + a, near_low), lax.rem(rep_i + b, n_rep))
        for a in range(near_low)
        for b in range(n_rep)
        if a or b
    ]
    far_count = n_dp // near_low
    far_peers = [(lax.rem(far_dp + a, far_count) * near_low + near_dp, rep_i) for a in range(1, far_count)]
    stages = [(near, near_dp * n_rep + rep_i, near_peers)]
    if far_peers:
        stages.append((far, far_dp, far_peers))

    c, x = lax.rem(rep_i, 2), lax.div(rep_i, 2)
    y, z = dp_lo, lax.rem(dp_hi, 4)
    outer, outers = lax.div(dp_hi, 4), high // 4
    core_peer = (dp_i, 2 * x + 1 - c)
    x_peer = (dp_i, 2 * (1 - x) + c)
    y_peer = (dp_hi * low + 1 - y, rep_i)
    def z_peer(flip):
        return ((outer * 4 + z + flip - 2 * flip * lax.rem(lax.div(z, flip), 2)) * low + y, rep_i)

    z_peers = [((outer * 4 + lax.rem(z + k, 4)) * low + y, rep_i) for k in range(1, 4)]
    outer_peers = [((lax.rem(outer + k, outers) * 4 + z) * low + y, rep_i) for k in range(1, outers)]

    barrier = pltpu.get_barrier_semaphore()
    greeted = near_peers + far_peers
    for peer in greeted:
        pl.semaphore_signal(barrier, inc=1, device_id=peer, device_id_type=MESH)

    loads = {}
    for slot, (name, src, dst) in enumerate([
        ("xf", xf_h, xf), ("wfa", wfa_h, wfa_in), ("xs", xs_h, xs),
        ("wsa", wsa_h, wsa), ("wfb", wfb_h, wfb_in), ("wfc", wfc_h, wfc_in), ("wsb", wsb_h, wsb),
        ("wsc", wsc_h, wsc), ("cf", cf_h, cf), ("cs", cs_h, cs), ("gains", gains_h, gains_in), ("biases", biases_h, biases_in),
    ]):
        loads[name] = pltpu.make_async_copy(src, dst, io_sem.at[slot])
        loads[name].start()
        if name == "wfa":
            taps = [
                pltpu.make_async_copy(
                    wl_h.at[pl.ds(bs * k, bs)], wlat.at[:, pl.ds(LANES * k, LANES)], io_sem.at[27 + k]
                )
                for k in range(5)
            ]
            for tap in taps:
                tap.start()
    stores = []

    def store(src, dst, slot):
        copy = pltpu.make_async_copy(src, dst, io_sem.at[slot])
        copy.start()
        return copy

    turn_at, turn_index = {}, {}
    for index, (turn, width) in enumerate(TURNS.items()):
        turn_at[turn] = sum(list(TURNS.values())[:index])
        turn_index[turn] = index

    def put(turn, at, vector):
        near[stages[0][1], :, pl.ds(turn_at[turn] + at, vector.shape[1])] = vector

    def sum_copy(turn, stage, first, count, peer):
        buffer = stages[stage][0]
        block = buffer.at[pl.ds(first, count), :, pl.ds(turn_at[turn], TURNS[turn])]
        return pltpu.make_async_remote_copy(
            src_ref=block, dst_ref=block, send_sem=sum_send.at[stage, turn_index[turn]],
            recv_sem=sum_recv.at[stage, turn_index[turn]], device_id=peer, device_id_type=MESH,
        )

    def exchange_start(turn):
        for peer in near_peers:
            sum_copy(turn, 0, stages[0][1], 1, peer).start()

    def exchange_end(turn):
        lanes = pl.ds(turn_at[turn], TURNS[turn])
        for stage, (buffer, rank, peers) in enumerate(stages):
            if stage:
                buffer[rank, :, lanes] = total
                for peer in peers:
                    sum_copy(turn, stage, rank, 1, peer).start()
            copy = sum_copy(turn, stage, 0, len(peers), peers[0])
            copy.wait_recv()
            total = jnp.sum(buffer[:, :, lanes], axis=0)
            copy.wait_send()
        return total

    def take(total, at, width):
        return total[:, at : at + width]

    def pair32(first, second):
        group = lax.broadcasted_iota(jnp.int32, (8, LANES), 1) // 32
        rows8 = (8, LANES)
        first = fold_lanes(jnp.broadcast_to(first, rows8))
        second = fold_lanes(jnp.broadcast_to(second, rows8))
        return jnp.where(group == 0, first, jnp.where(group == 1, second, 0.0))[0:1, :]

    def unpair32(total):
        group = lax.broadcasted_iota(jnp.int32, (8, LANES), 1) // 32
        total = jnp.broadcast_to(total, (8, LANES))
        first = fold_lanes(jnp.where(group == 0, total, 0.0))
        second = fold_lanes(jnp.where(group == 1, total, 0.0))
        return first[0:1, :], second[0:1, :]

    pieces = {}

    bits = {C: (c, core_peer), X: (x, x_peer), Y: (y, y_peer),
            Z0: (lax.rem(z, 2), z_peer(1)), Z1: (lax.div(z, 2), z_peer(2))}

    def add_piece(name, ref, lane, size, index):
        axes = ORDER_OF[name]
        piece = Piece()
        piece.name, piece.ref, piece.lane, piece.size, piece.index = name, ref, lane, size, index
        piece.step, piece.axes, piece.steps = 0, axes, len(axes[0])
        starts, counts, arriving = [[0], [0]], [size], [size]
        for step, pair in enumerate(zip(*axes)):
            for side, axis in enumerate(pair):
                if axis == Z:
                    starts[side].append(starts[side][-1] + z * (counts[-1] // 4))
                else:
                    starts[side].append(starts[side][-1] + bits[axis][0] * (counts[-1] // 2))
            counts.append(counts[-1] // (4 if pair[0] == Z else 2))
            arriving.append(arriving[-1] + (3 if pair[0] == Z else 1) * counts[-1])
        piece.starts, piece.counts, piece.arriving = starts, counts, arriving
        pieces[name] = piece

    for k in range(2):
        add_piece(SB + k, sec_fc, 256 * k, 768, k)
    for k in range(4):
        add_piece(SA + k, big, 256 * k, 768, 2 + k)
    add_piece(SB + 2, slab.at[0], 0, 768, 6)
    add_piece(SA + 4, slab.at[1], 0, 768, 7)
    add_piece(LT, slab.at[2], 0, 768, 8)
    add_piece(SC, slab_sc, 0, 1024, 9)

    def span(piece, start, count, lane=0, width=256):
        return piece.ref.at[pl.ds(pl.multiple_of(start, 8), count), pl.ds(piece.lane + lane, width)]

    def send(piece, step, src, dst, peer):
        pltpu.make_async_remote_copy(
            src_ref=src, dst_ref=dst, send_sem=big_send.at[piece.index],
            recv_sem=big_recv.at[piece.index, step], device_id=peer, device_id_type=MESH,
        ).start()

    def result(piece, start, count, lane=0, width=256):
        name = piece.name
        start = pl.multiple_of(start, 8)
        if name == LT:
            return summed.at[pl.ds(start, count), pl.ds(lane, width)]
        if name == SC:
            return dsc_h.at[pl.ds(start, count), pl.ds(lane, width)]
        if name >= SA:
            return dsa.at[pl.ds(768 * (name - SA) + start, count), pl.ds(lane, width)]
        return dsb.at[pl.ds(768 * (name - SB) + start, count), pl.ds(lane, width)]

    def own_copies(piece):
        count, sem = piece.counts[-1], own_sem.at[piece.index]
        return [
            pltpu.make_async_copy(
                span(piece, start[-1], count, 128 * side, 128),
                result(piece, start[-1], count, 128 * side, 128),
                sem.at[side],
            )
            for side, start in enumerate(piece.starts)
        ]

    def arrived(piece, step, rows_in):
        block = span(piece, 0, rows_in) if step < piece.steps else result(piece, 0, rows_in)
        copy = pltpu.make_async_remote_copy(
            src_ref=block, dst_ref=block, send_sem=big_send.at[piece.index],
            recv_sem=big_recv.at[piece.index, step], device_id=core_peer, device_id_type=MESH,
        )
        copy.wait_recv()
        copy.wait_send()

    def add_rows(piece, target, source, count, lane, width):
        lanes = pl.ds(piece.lane + lane, width)
        chunk = piece.size // 32
        ref = piece.ref

        def step(i):
            into = pl.ds(pl.multiple_of(target + i * chunk, 8), chunk)
            ref[into, lanes] = ref[into, lanes] + ref[pl.ds(pl.multiple_of(source + i * chunk, 8), chunk), lanes]

        loop(count // chunk, step)

    order = range(10)

    def unpack_small():
        stores.append(store(summed.at[:, pl.ds(0, 128)], dl_h.at[pl.ds(0, 768)], 16))
        stores.append(store(summed.at[pl.ds(0, 512), pl.ds(128, 128)], dl_h.at[pl.ds(768, 512)], 17))
        stores.append(store(summed.at[pl.ds(512, 256), pl.ds(128, 128)], small_h, 18))

    polled = [0]

    def poll():
        polled[0] += 1
        for name in POLLS[polled[0] - 1]:
            advance(name)

    def done(name):
        return pieces[name].step > 2 * pieces[name].steps

    def advance(name):
        piece = pieces[name]
        step, steps, index = piece.step, piece.steps, piece.index
        piece.step = step + 1
        starts, counts, arriving, axes = piece.starts, piece.counts, piece.arriving, piece.axes
        ref, lane = piece.ref, piece.lane

        def received(last):
            fan = 3 if axes[0][last] == Z else 1
            return fan * counts[last + 1]

        if 0 < step < steps or (step == steps and axes[0][-1] != Z):
            arrived(piece, step - 1, received(step - 1))
            if step == 1:
                add_rows(piece, starts[0][1], arriving[0], counts[1], 0, 256)
            else:
                for side in range(2):
                    add_rows(piece, starts[side][step], arriving[step - 1], counts[step], 128 * side, 128)
        elif step == steps:
            arrived(piece, step - 1, received(step - 1))
        elif step > steps:
            arrived(piece, step - 1, received(2 * steps - step))

        if step < steps:
            held, keep = counts[step], counts[step + 1]
            if step == 0:
                at = starts[0][0] + (1 - c) * keep
                send(piece, 0, span(piece, at, keep), span(piece, arriving[0], keep), core_peer)
                return
            for side in range(2):
                axis, start = axes[side][step], starts[side][step]
                if axis == Z:
                    for k, peer in enumerate(z_peers):
                        at, into = start + lax.rem(z + k + 1, 4) * keep, arriving[step] + k * keep
                        send(
                            piece, step, span(piece, at, keep, 128 * side, 128),
                            span(piece, into, keep, 128 * side, 128), peer,
                        )
                else:
                    bit, peer = bits[axis]
                    at = start + (1 - bit) * keep
                    send(
                        piece, step, span(piece, at, keep, 128 * side, 128),
                        span(piece, arriving[step], keep, 128 * side, 128), peer,
                    )
        elif step == steps:
            last = counts[-1]
            own = [
                (pl.ds(pl.multiple_of(starts[side][-1], 8), last), pl.ds(lane + 128 * side, 128))
                for side in range(2)
            ]
            both = jnp.concatenate([ref[own[0]], ref[own[1]]], axis=1)
            if axes[0][-1] == Z:
                for k in range(3):
                    both = both + ref[pl.ds(arriving[steps - 1] + k * last, last), pl.ds(lane, 256)]
            if outers > 1:
                held = span(piece, arriving[steps - 1], last)
                ref[pl.ds(arriving[steps - 1], last), pl.ds(lane, 256)] = both
                for peer in outer_peers:
                    send(piece, 10, held, extra_h.at[index, outer, pl.ds(0, last)], peer)
                block = extra_h.at[index, pl.ds(0, outers - 1), pl.ds(0, last)]
                copy = pltpu.make_async_remote_copy(
                    src_ref=block, dst_ref=block, send_sem=big_send.at[index], recv_sem=big_recv.at[index, 10],
                    device_id=core_peer, device_id_type=MESH,
                )
                copy.wait_recv()
                copy.wait_send()
                local = [(held, extra_h.at[index, outer, pl.ds(0, last)])]
                for k in range(outers):
                    local.append((extra_h.at[index, k, pl.ds(0, last)], span(piece, arriving[0] + k * last, last)))
                for src, dst in local:
                    copy = pltpu.make_async_copy(src, dst, own_sem.at[index, 0])
                    copy.start()
                    copy.wait()
                both = ref[pl.ds(arriving[0], last), pl.ds(lane, 256)]
                for k in range(1, outers):
                    both = both + ref[pl.ds(arriving[0] + k * last, last), pl.ds(lane, 256)]
            both = both * factor
            for side in range(2):
                ref[own[side]] = both[:, 128 * side : 128 * (side + 1)]
        if steps <= step < 2 * steps:
            back = 2 * steps - 1 - step
            count = counts[back + 1]
            if step == steps + 1:
                for copy in own_copies(piece):
                    copy.wait()
            if back == 0:
                block = result(piece, starts[0][1], count)
                send(piece, step, block, block, core_peer)
                return
            for side in range(2):
                axis, start = axes[side][back], starts[side][back + 1]
                block = result(piece, start, count, 128 * side, 128)
                source = span(piece, start, count, 128 * side, 128) if step == steps else block
                for peer in z_peers if axis == Z else [bits[axis][1]]:
                    send(piece, step, source, block, peer)
            if step == steps:
                for copy in own_copies(piece):
                    copy.start()
        elif step == 2 * steps and name == LT:
            unpack_small()

    spots = {FC: 0, LAT: 1, SLOW_A: 3, SLOW_B: 5, SLOW_C: 7, FA: 16, FB: 17}

    lane16 = lax.broadcasted_iota(jnp.int32, (16, LANES), 1)

    def unpack(packed):
        fa = fold_lanes(jnp.where(lane16 // 32 == 0, packed, 0.0))[0:1, :]
        fb = fold_lanes(jnp.where(lane16 // 32 == 1, packed, 0.0))[0:1, :]
        turned = pltpu.roll(packed, 64, 1)
        moved = jnp.where(lane16 < 64, turned, pltpu.roll(turned, 15, 0))
        found = {FA: fa, FB: fb}
        at = 0
        for name, count in ((FC, 1), (LAT, 2), (SLOW_A, 2), (SLOW_B, 2), (SLOW_C, 8)):
            found[name] = jnp.concatenate([moved[at + k : at + k + 1, :] for k in range(count)], axis=1)
            at += count
        return found

    held = [0]

    def settle(vector):
        at, width = held[0], vector.shape[1]
        held[0] += 1
        line, row = at // 8, slice(at % 8, at % 8 + 1)
        vectors[line, row, 0:width] = vector

        def read(lanes=slice(0, width)):
            return vectors[line, row, lanes]

        return read

    gains, biases = {}, {}

    def read_parameters():
        for name, flat_in, target in (("gains", gains_in, gains), ("biases", biases_in, biases)):
            loads[name].wait()
            count = flat_in.shape[0]
            stage_a[0:16, :] = jnp.zeros((16, LANES), F32)
            for row in range(16):
                width = min(LANES, count - row * LANES)
                stage_a[row : row + 1, 0:width] = flat_in[pl.ds(row * LANES, width)].reshape(1, width)
            for key, vector in unpack(stage_a[0:16, :]).items():
                target[key] = settle(vector)

    def gain(name):
        return gains[name]()

    def bias(name):
        return biases[name]()

    def moments(name, total, squares, count):
        mean = total * (1.0 / count)
        scale = lax.rsqrt(squares * (1.0 / count) - mean * mean + EPS)
        return settle(mean), settle(scale), settle(0.5 * gain(name) * scale), settle(0.5 * bias(name))

    def back_vectors(name, stats, bias_total, gain_total, count):
        mean, scale = stats[0](), stats[1]()
        lead = gain(name) * scale
        tilt = lead * scale * gain_total * (1.0 / count)
        level = lead * bias_total * (1.0 / count) - mean * tilt
        return settle(lead), settle(level), settle(tilt)

    def report(name, bias_total, gain_total):
        at = spots[name]
        for piece in range(bias_total.shape[1] // LANES):
            lanes = slice(piece * LANES, (piece + 1) * LANES)
            gain_rows[at + piece : at + piece + 1, :] = gain_total[:, lanes]
            bias_rows[at + piece : at + piece + 1, :] = bias_total[:, lanes]

    def silu_of(values, stats):
        h = (values - stats[0]()) * stats[2]() + stats[3]()
        return h + h * jnp.tanh(h)

    def slope_of(h):
        t = jnp.tanh(h)
        out, gate = h + h * t, 0.5 + 0.5 * t
        return out, gate + out * (1.0 - gate)

    def clip_masks(width):
        frame = lax.broadcasted_iota(jnp.int32, (1, 8, width), 1)
        with_prev = jnp.zeros((1, 8, width), F32)
        with_next = jnp.zeros((1, 8, width), F32)
        for t in range(1, frames):
            same = jnp.where(clip[0, t] == clip[0, t - 1], 1.0, 0.0)
            with_prev = jnp.where(frame == t, same, with_prev)
            with_next = jnp.where(frame == t - 1, same, with_next)
        return with_prev, with_next

    masks[0:1], masks[1:2] = clip_masks(256)

    def prev(width):
        return masks[0:1, :, 0:width]

    def following(width):
        return masks[1:2, :, 0:width]

    def roll_frames(values, mask, step, mask_first):
        grouped = values.reshape(values.shape[0] // 8, 8, values.shape[1])
        if mask_first:
            grouped = grouped * mask
        grouped = pltpu.roll(grouped, step % 8, 1)
        if not mask_first:
            grouped = grouped * mask
        return grouped.reshape(values.shape)

    def spread_columns(target, index, values):
        width = values.shape[1]
        nothing = jnp.zeros((frames, width), F32)
        at = pl.ds(pl.multiple_of((index + 1) * band, 16), band)
        target[at, 0:width] = jnp.concatenate([nothing, values[: band - frames]], axis=0).astype(BF16)
        target[at, width : 2 * width] = values.astype(BF16)
        target[at, 2 * width :] = jnp.concatenate([values[frames:], nothing], axis=0).astype(BF16)

    gain_rows[...] = jnp.zeros(gain_rows.shape, F32)
    bias_rows[...] = jnp.zeros(bias_rows.shape, F32)
    for target in (hcs, gcs, hcf, gcf):
        edge = jnp.zeros((band, target.shape[1]), BF16)
        target[0:band, :] = edge
        target[band + rows : rows + 2 * band, :] = edge

    def lane_groups(count=LANES):
        return lax.broadcasted_iota(jnp.int32, (count, LANES), 1) // 32

    def block_mask():
        row_group = lax.broadcasted_iota(jnp.int32, (LANES, LANES), 0) // 32
        return jnp.where(lane_groups() == row_group, 1.0, 0.0)

    repeat_lanes = jnp.where(
        lax.broadcasted_iota(jnp.int32, (32, LANES), 1) % 32 == lax.broadcasted_iota(jnp.int32, (32, LANES), 0),
        1.0, 0.0,
    ).astype(BF16)

    wfa[...] = jnp.zeros(wfa.shape, BF16)
    loads["wfa"].wait()
    for phase in range(4):
        for k in range(3):
            wfa[32 * phase : 32 * (phase + 1), LANES * (phase + k) : LANES * (phase + k + 1)] = wfa_in[
                32 * k : 32 * (k + 1), :
            ]
    loads["xf"].wait()

    def arrange(i):
        at = rows_at(i, band)
        stage_a[...] = xf[rows_at(i, fband), :].astype(F32)
        phases = [stage_a[pl.ds(phase, band, stride=4), :] for phase in range(4)]
        vx[at, 0:128] = roll_frames(phases[2], prev(128), 1, False).astype(BF16)
        vx[at, 128:256] = roll_frames(phases[3], prev(128), 1, False).astype(BF16)
        for phase in range(4):
            vx[at, 256 + 128 * phase : 384 + 128 * phase] = phases[phase].astype(BF16)
        vx[at, 768:896] = roll_frames(phases[0], following(128), -1, False).astype(BF16)

    loop(bands, arrange, unroll=2)
    for tap in taps:
        tap.wait()

    def zero2(width):
        return (jnp.zeros((8, width), F32), jnp.zeros((8, width), F32))

    def conv_fa(i, carry):
        at = rows_at(i, half)
        value = dot(vx[at, 128:896], wfa[...], NT)
        sec_fa[at, :] = value
        return carry[0] + column_sums(value), carry[1] + column_sums(value * value)

    def conv_lat(i, carry):
        at = rows_at(i, half)
        value = dot(vx[at, 0:640], wlat[...], NT)
        sec_lat[at, :] = value
        return carry[0] + column_sums(value), carry[1] + column_sums(value * value)

    sum_lat, sq_lat = loop(2, conv_lat, zero2(256))
    put(LAT, 0, squash(sum_lat))
    put(LAT, 256, squash(sq_lat))
    pl.semaphore_wait(barrier, len(greeted))
    exchange_start(LAT)

    sum_fa, sq_fa = loop(2, conv_fa, zero2(128))
    put(FA, 0, pair32(squash(sum_fa), squash(sq_fa)))
    exchange_start(FA)

    loads["xs"].wait()
    loads["wsa"].wait()

    def narrow_main(i):
        at = rows_at(i, half)
        for k in range(3):
            big[at, bs * k : bs * (k + 1)] = dot(xs[at, :], wsa[bs * k : bs * (k + 1), 0:cs_n], NT)

    loop(2, narrow_main)
    loads["wfb"].wait()
    loads["wfc"].wait()
    spread = dot(wfb_in[...], repeat_lanes, NN)
    for a in range(3):
        for b in range(3):
            piece = spread[32 * (3 * a + b) : 32 * (3 * a + b + 1), :]
            block = (jnp.concatenate([piece] * 4, axis=0) * block_mask()).astype(BF16)
            wfb[a, :, LANES * b : LANES * (b + 1)] = block
            wfbk[a, LANES * (2 - b) : LANES * (3 - b), :] = block
    widen = dot(wfc_in[...], repeat_lanes, TN)
    for phase in range(4):
        wfc[LANES * phase : LANES * (phase + 1), :] = jnp.where(lane_groups() == phase, widen, 0.0).astype(BF16)
    read_parameters()
    total = exchange_end(LAT)

    stats_lat = moments(LAT, take(total, 0, 256), take(total, 256, 256), slow_count)

    def act_fa(i):
        spread_columns(hcf, i, silu_of(sec_fa[rows_at(i, band), :], stats_fa))

    def act_lat(i):
        at = rows_at(i, 2 * band)
        jl[at, :] = silu_of(sec_lat[at, :], stats_lat).astype(BF16)

    loop(bands // 2, act_lat)

    def conv_fb(i, carry):
        value = None
        for a in range(3):
            at = pl.ds(pl.multiple_of(i * half + band * a, 16), half)
            term = dot(hcf[at, :], wfb[a], NT)
            value = term if value is None else value + term
        sec_fb[rows_at(i, half), :] = value
        return carry[0] + column_sums(value), carry[1] + column_sums(value * value)

    def narrow_lateral(i):
        at = rows_at(i, half)
        for k in range(3):
            big[at, bs * k : bs * (k + 1)] += dot(jl[at, :], wsa[bs * k : bs * (k + 1), cs_n:], NT)

    loop(2, narrow_lateral)

    def combine_sa(i, carry):
        at = rows_at(i, band)
        value = (
            big[at, bs : 2 * bs]
            + roll_frames(big[at, 0:bs], prev(256), 1, False)
            + roll_frames(big[at, 2 * bs : 3 * bs], following(256), -1, False)
        )
        sec_sa[at, :] = value
        return carry[0] + column_sums(value), carry[1] + column_sums(value * value)

    sum_sa, sq_sa = loop(bands, combine_sa, zero2(256))
    put(SLOW_A, 0, squash(sum_sa))
    put(SLOW_A, 256, squash(sq_sa))
    exchange_start(SLOW_A)

    total = exchange_end(FA)
    stats_fa = moments(FA, *unpair32(total), fast_count)
    loop(bands, act_fa, unroll=2)
    sum_fb, sq_fb = loop(2, conv_fb, zero2(128))
    put(FB, 0, pair32(squash(sum_fb), squash(sq_fb)))
    exchange_start(FB)
    total = exchange_end(SLOW_A)

    stats_sa = moments(SLOW_A, take(total, 0, 256), take(total, 256, 256), slow_count)

    def act_sa(i):
        spread_columns(hcs, i, silu_of(sec_sa[rows_at(i, band), :], stats_sa))

    def act_fb(i):
        at = rows_at(i, 2 * band)
        hbf[at, :] = silu_of(sec_fb[at, :], stats_fb).astype(BF16)

    loop(bands, act_sa, unroll=2)
    loads["wsb"].wait()

    def conv_sb(i, carry):
        value = None
        for a in range(3):
            at = pl.ds(pl.multiple_of(i * half + band * a, 16), half)
            for b in range(3):
                tap = 3 * a + b
                term = dot(hcs[at, bs * b : bs * (b + 1)], wsb[bs * tap : bs * (tap + 1), :], NT)
                value = term if value is None else value + term
        sec_sb[rows_at(i, half), :] = value
        return carry[0] + column_sums(value), carry[1] + column_sums(value * value)

    sum_sb, sq_sb = loop(2, conv_sb, zero2(256))
    put(SLOW_B, 0, squash(sum_sb))
    put(SLOW_B, 256, squash(sq_sb))
    exchange_start(SLOW_B)

    total = exchange_end(FB)
    stats_fb = moments(FB, *unpair32(total), fast_count)
    loop(bands // 2, act_fb)

    def widen_fast(i, carry):
        at = rows_at(i, half)
        value = dot(hbf[at, :], wfc[...], NT)
        sec_fc[at, :] = value
        return carry[0] + column_sums(value), carry[1] + column_sums(value * value)

    sum_fc, sq_fc = loop(2, widen_fast, zero2(512))

    def fold4(vector):
        return vector[:, 0:128] + vector[:, 128:256] + vector[:, 256:384] + vector[:, 384:512]

    put(FC, 0, squash(fold4(sum_fc)))
    put(FC, 128, squash(fold4(sq_fc)))
    exchange_start(FC)
    total = exchange_end(SLOW_B)

    stats_sb = moments(SLOW_B, take(total, 0, 256), take(total, 256, 256), slow_count)

    def act_sb(i, carry):
        at = rows_at(i, 2 * band)
        value = silu_of(sec_sb[at, :], stats_sb).astype(BF16)
        hbs[at, :] = value
        return carry + column_sums(value.astype(F32))

    sum_hbs = loop(bands // 2, act_sb, jnp.zeros((8, bs), F32))
    loads["wsc"].wait()
    mid = cs_n // 2

    def widen_slow(part):
        lanes = slice(part * mid, (part + 1) * mid)

        def step(i, carry):
            at = rows_at(i, half)
            value = dot(hbs[at, :], wsc[lanes, :], NT)
            big[at, lanes] = value
            return carry + column_sums(value * value)

        return loop(2, step, jnp.zeros((8, mid), F32))

    put(SLOW_C, 0, squash(sum_hbs))
    put(SLOW_C, 256, squash(widen_slow(0)))
    exchange_start(SLOW_C)
    put(SLOW_C + 1, 0, squash(widen_slow(1)))
    exchange_start(SLOW_C + 1)
    total = exchange_end(FC)
    stats_fc = moments(FC, take(total, 0, 128), take(total, 128, 128), fast_count)

    loads["cf"].wait()

    def finish_fast(i, carry):
        at, fat = rows_at(i, band), rows_at(i, fband)
        bias_sum, gain_sum = carry
        dbuf_f[0:fband, :] = cf[fat, :].astype(F32)
        for phase in range(4):
            lanes = slice(128 * phase, 128 * (phase + 1))
            centred = sec_fc[at, lanes] - stats_fc[0]()
            total_in = vx[at, 256 + 128 * phase : 384 + 128 * phase].astype(F32)
            out, slope = slope_of(0.5 * total_in + (centred * stats_fc[2]() + stats_fc[3]()))
            stage_a[pl.ds(phase, band, stride=4), :] = out
            grad = dbuf_f[pl.ds(phase, band, stride=4), :] * slope
            gsf[at, lanes] = grad
            bias_sum = bias_sum + column_sums(grad)
            gain_sum = gain_sum + column_sums(grad * centred)
        xf[fat, :] = stage_a[...].astype(BF16)
        return bias_sum, gain_sum

    bias_fc, gain_fc = loop(bands, finish_fast, zero2(128))
    fast_store = store(xf, fast_h, 10)
    put(BACK + FC, 0, squash(bias_fc))
    put(BACK + FC, 128, squash(gain_fc) * stats_fc[1]())
    exchange_start(BACK + FC)
    loads["cs"].wait()
    total = exchange_end(SLOW_C)
    squares = take(total, 256, mid)
    whole = settle(
        lax.dot_general(
            jnp.broadcast_to(take(total, 0, 256), (8, bs)), wsc[...].astype(F32), (NT, ((), ())),
            precision=lax.Precision.HIGHEST, preferred_element_type=F32,
        )[0:1, :]
    )
    squares = jnp.concatenate([squares, exchange_end(SLOW_C + 1)], axis=1)
    stats_sc = moments(SLOW_C, whole(), squares, slow_count)

    def finish_slow(part):
        lanes = slice(part * mid, (part + 1) * mid)
        def step(i, carry):
            at = rows_at(i, band)
            mean, lead, level = [stats_sc[k](lanes) for k in (0, 2, 3)]
            centred = big[at, lanes] - mean
            out, slope = slope_of(0.5 * xs[at, lanes].astype(F32) + (centred * lead + level))
            grad = cs[at, lanes].astype(F32) * slope
            cs[at, lanes] = out.astype(BF16)
            gsum[at, lanes] = centred.astype(BF16)
            big[at, lanes] = grad
            return carry[0] + column_sums(grad), carry[1] + column_sums(grad * centred)

        bias_part, gain_part = loop(bands, step, zero2(mid))
        return squash(bias_part), squash(gain_part) * stats_sc[1](lanes)

    for part in range(2):
        bias_part, gain_part = finish_slow(part)
        put(BACK + SLOW_C + part, 0, bias_part)
        put(BACK + SLOW_C + part, mid, gain_part)
        exchange_start(BACK + SLOW_C + part)
    slow_store = store(cs, slow_h, 11)

    total = exchange_end(BACK + FC)
    bias_fc, gain_fc = take(total, 0, 128), take(total, 128, 128)
    report(FC, bias_fc, gain_fc)
    def slope_pass(section, stats, buffer):
        def step(i, carry):
            at = rows_at(i, 2 * band)
            centred = section[at, :] - stats[0]()
            grad = buffer[at, :] * slope_of(centred * stats[2]() + stats[3]())[1]
            buffer[at, :] = grad
            return carry[0] + column_sums(grad), carry[1] + column_sums(grad * centred)

        bias_sum, gain_sum = loop(bands // 2, step, zero2(section.shape[1]))
        return squash(bias_sum), squash(gain_sum) * stats[1]()

    lead_fc, level_fc, tilt_fc = back_vectors(FC, stats_fc, bias_fc, gain_fc, fast_count)

    def low_fc(i):
        at = rows_at(i, band)
        for phase in range(4):
            lanes = slice(128 * phase, 128 * (phase + 1))
            value = gsf[at, lanes] * lead_fc() - level_fc() - sec_fc[at, lanes] * tilt_fc()
            cf[pl.ds(pl.multiple_of(rows * phase + i * band, 16), band), :] = value.astype(BF16)

    loop(bands, low_fc, unroll=2)

    def back_fc(i):
        value = None
        for phase in range(4):
            at = pl.ds(pl.multiple_of(rows * phase + i * half, 16), half)
            term = dot(cf[at, :], wfc[128 * phase : 128 * (phase + 1), :], NN)
            value = term if value is None else value + term
        dbuf_f[rows_at(i, half), :] = value

    loop(2, back_fc)
    bias_fb, gain_fb = slope_pass(sec_fb, stats_fb, dbuf_f)
    put(BACK + FB, 0, pair32(bias_fb, gain_fb))
    exchange_start(BACK + FB)
    slow_store.wait()
    sums = [exchange_end(BACK + SLOW_C + part) for part in range(2)]

    bias_sc = jnp.concatenate([take(total, 0, mid) for total in sums], axis=1)
    gain_sc = jnp.concatenate([take(total, mid, mid) for total in sums], axis=1)
    report(SLOW_C, bias_sc, gain_sc)
    lead_sc = gain(SLOW_C) * stats_sc[1]()
    tilt_sc = settle(lead_sc * stats_sc[1]() * gain_sc * (1.0 / slow_count))
    level_sc = settle(lead_sc * bias_sc * (1.0 / slow_count))
    lead_sc = settle(lead_sc)

    def low_sc(i):
        at = rows_at(i, 32)
        grad = big[at, :]
        cs[at, :] = (grad * lead_sc() - level_sc() - gsum[at, :].astype(F32) * tilt_sc()).astype(BF16)
        gsum[at, :] = grad.astype(BF16)

    loop(rows // 32, low_sc, unroll=7)

    def back_sc(i):
        at = rows_at(i, half)
        dbuf[at, :] = dot(cs[at, :], wsc[...], NN)

    loop(2, back_sc)

    bias_sb, gain_sb = slope_pass(sec_sb, stats_sb, dbuf)

    put(BACK + SLOW_B, 0, bias_sb)
    put(BACK + SLOW_B, 256, gain_sb)
    exchange_start(BACK + SLOW_B)

    slab_sc[0:cs_n, :] = dot(cs[...], hbs[...], TN)
    advance(SC)
    widening = None
    for phase in range(4):
        term = dot(hbf[...], cf[rows * phase : rows * (phase + 1), :], TN)[32 * phase : 32 * (phase + 1), :]
        widening = term if widening is None else widening + term
    slab[2, 704:736, 128:256] = widening
    slab[2, 736:768, 128:256] = jnp.zeros((32, LANES), F32)
    poll()

    bias_fb, gain_fb = unpair32(exchange_end(BACK + FB))
    report(FB, bias_fb, gain_fb)
    vec_fb = back_vectors(FB, stats_fb, bias_fb, gain_fb, fast_count)

    def norm_grad(buffer, section, at, vectors):
        lead, level, tilt = vectors
        return buffer[at, :] * lead() - level() - section[at, :] * tilt()

    def low_fb(i):
        spread_columns(gcf, i, norm_grad(dbuf_f, sec_fb, rows_at(i, band), vec_fb))

    loop(bands, low_fb, unroll=2)

    def back_fb(i):
        value = None
        for a in range(3):
            at = pl.ds(pl.multiple_of(i * half + band * (2 - a), 16), half)
            term = dot(gcf[at, :], wfbk[a], NN)
            value = term if value is None else value + term
        dbuf_f[rows_at(i, half), :] = value

    loop(2, back_fb)
    poll()
    bias_fa, gain_fa = slope_pass(sec_fa, stats_fa, dbuf_f)
    put(BACK + FA, 0, pair32(bias_fa, gain_fa))
    exchange_start(BACK + FA)
    poll()
    total = exchange_end(BACK + SLOW_B)

    bias_sb, gain_sb = take(total, 0, 256), take(total, 256, 256)
    report(SLOW_B, bias_sb, gain_sb)
    vec_sb = back_vectors(SLOW_B, stats_sb, bias_sb, gain_sb, slow_count)

    def low_sb(i):
        spread_columns(gcs, i, norm_grad(dbuf, sec_sb, rows_at(i, band), vec_sb))

    loop(bands, low_sb, unroll=2)
    poll()

    def back_sb(i):
        value = None
        for a in range(3):
            at = pl.ds(pl.multiple_of(i * half + band * (2 - a), 16), half)
            for b in range(3):
                tap = 3 * a + b
                term = dot(gcs[at, bs * (2 - b) : bs * (3 - b)], wsb[bs * tap : bs * (tap + 1), :], NN)
                value = term if value is None else value + term
        dbuf[rows_at(i, half), :] = value

    for part in range(2):
        back_sb(part)
        poll()
    bias_sa, gain_sa = slope_pass(sec_sa, stats_sa, dbuf)

    put(BACK + SLOW_A, 0, bias_sa)
    put(BACK + SLOW_A, 256, gain_sa)
    exchange_start(BACK + SLOW_A)
    poll()

    for a in range(3):
        value = dot(gcs[band : band + rows, bs : 2 * bs], hcs[band * a : band * a + rows, :], TN)
        ref, lane = pieces[SB + a].ref, pieces[SB + a].lane
        for b in range(3):
            ref[bs * b : bs * (b + 1), lane : lane + bs] = value[:, bs * b : bs * (b + 1)]
        advance(SB + a)
        poll()
    for a in range(3):
        value = dot(gcf[band : band + rows, 128:256], hcf[band * a : band * a + rows, :], TN)
        for b in range(3):
            tap = 3 * a + b
            block = value[:, 128 * b : 128 * (b + 1)] * block_mask()
            folded = fold_lanes(block[0:32] + block[32:64] + block[64:96] + block[96:128])
            folded = jnp.where(lane_groups(32) == tap % 4, folded, 0.0)
            at = slice(608 + 32 * (tap // 4), 640 + 32 * (tap // 4))
            slab[2, at, 128:256] = folded if tap % 4 == 0 else slab[2, at, 128:256] + folded
    poll()
    bias_fa, gain_fa = unpair32(exchange_end(BACK + FA))
    report(FA, bias_fa, gain_fa)
    vec_fa = back_vectors(FA, stats_fa, bias_fa, gain_fa, fast_count)

    def low_fa(i):
        at = rows_at(i, band)
        hbf[at, :] = norm_grad(dbuf_f, sec_fa, at, vec_fa).astype(BF16)

    loop(bands, low_fa, unroll=2)
    value = dot(hbf[...], vx[:, 128:896], TN)
    for k in range(3):
        piece = None
        for phase in range(4):
            term = value[32 * phase : 32 * (phase + 1), 128 * (phase + k) : 128 * (phase + k + 1)]
            piece = term if piece is None else piece + term
        slab[2, 512 + 32 * k : 544 + 32 * k, 128:256] = piece
    poll()
    total = exchange_end(BACK + SLOW_A)
    poll()

    bias_sa, gain_sa = take(total, 0, 256), take(total, 256, 256)
    report(SLOW_A, bias_sa, gain_sa)
    vec_sa = back_vectors(SLOW_A, stats_sa, bias_sa, gain_sa, slow_count)
    def low_sa(i):
        at = rows_at(i, band)
        value = norm_grad(dbuf, sec_sa, at, vec_sa)
        gcs[at, 0:bs] = roll_frames(value, prev(256), -1, True).astype(BF16)
        gcs[at, bs : 2 * bs] = value.astype(BF16)
        gcs[at, 2 * bs :] = roll_frames(value, following(256), 1, True).astype(BF16)

    loop(bands, low_sa, unroll=2)
    poll()

    def narrow_gradient(k):
        ref, lane = pieces[SA + k].ref, pieces[SA + k].lane
        source = xs[:, 256 * k : 256 * (k + 1)] if k < 4 else jl[...]
        ref[0 : 3 * bs, lane : lane + 256] = dot(gcs[0:rows, :], source, TN)
        advance(SA + k)

    narrow_gradient(0)
    poll()

    def back_lateral(i):
        at = rows_at(i, half)
        dbuf[at, :] = dot(gcs[at, :], wsa[:, cs_n:], NN)

    loop(2, back_lateral)
    poll()
    bias_lat, gain_lat = slope_pass(sec_lat, stats_lat, dbuf)
    put(BACK + LAT, 0, bias_lat)
    put(BACK + LAT, 256, gain_lat)
    exchange_start(BACK + LAT)

    poll()

    for k in range(1, 4):
        narrow_gradient(k)
        poll()
    total = exchange_end(BACK + LAT)

    bias_lat, gain_lat = take(total, 0, 256), take(total, 256, 256)
    report(LAT, bias_lat, gain_lat)

    def pack(rows_ref, target):
        lanes = lax.broadcasted_iota(jnp.int32, (24, LANES), 1)
        stacked = rows_ref[...]
        turned = pltpu.roll(stacked, 64, 1)
        moved = jnp.where(lanes >= 64, turned, pltpu.roll(turned, 1, 0))[0:16, :]
        first = jnp.where(lane16[0:1, :] < 32, stacked[16:17, :], stacked[17:18, :])
        first = jnp.where(lane16[0:1, :] < 64, first, moved[0:1, :])
        target[...] = moved * factor
        target[0:1, :] = first * factor

    pack(gain_rows, dbuf_f.at[pl.ds(0, 16)])
    pack(bias_rows, dbuf_f.at[pl.ds(16, 16)])
    parameter_stores = [
        store(dbuf_f.at[pl.ds(0, 16)], dgains_h, 19), store(dbuf_f.at[pl.ds(16, 16)], dbiases_h, 20)
    ]
    vec_lat = back_vectors(LAT, stats_lat, bias_lat, gain_lat, slow_count)

    def low_lat(i):
        at = rows_at(i, band)
        hbs[at, :] = norm_grad(dbuf, sec_lat, at, vec_lat).astype(BF16)

    loop(bands, low_lat, unroll=2)
    value = dot(hbs[...], vx[:, 0:640], TN)
    for k in range(5):
        at, lane = 256 * (k % 3), 128 * (k // 3)
        slab[2, at : at + 256, lane : lane + 128] = value[:, 128 * k : 128 * (k + 1)]
    advance(LT)
    poll()
    narrow_gradient(4)
    poll()

    def slow_back(i):
        at = rows_at(i, half)
        for tile in range(cs_n // 256):
            lanes = slice(256 * tile, 256 * (tile + 1))
            value = gsum[at, lanes].astype(F32) + dot(gcs[at, :], wsa[:, lanes], NN)
            gsum[at, lanes] = value.astype(BF16)

    for part in range(2):
        slow_back(part)
        poll()

    fast_store.wait()

    def fast_back(i):
        at, fat = rows_at(i, 2 * band), rows_at(i, 2 * fband)
        conv = dot(hbf[at, :], wfa[...], NN)
        side_in = dot(hbs[at, :], wlat[...], NN)

        def lane(values, block):
            return values[:, 128 * block : 128 * (block + 1)]

        grads = [gsf[at, 128 * phase : 128 * (phase + 1)] + lane(conv, phase + 1) for phase in range(4)]
        grads[0] = grads[0] + roll_frames(lane(conv, 5), following(128), 1, True) + lane(side_in, 2)
        grads[1] = grads[1] + lane(side_in, 3)
        grads[2] = grads[2] + lane(side_in, 4) + roll_frames(lane(side_in, 0), prev(128), -1, True)
        grads[3] = grads[3] + roll_frames(lane(side_in, 1) + lane(conv, 0), prev(128), -1, True)
        for part in range(2):
            for phase in range(4):
                stage_a[pl.ds(phase, band, stride=4), :] = grads[phase][part * band : (part + 1) * band]
            xf[rows_at(2 * i + part, fband), :] = stage_a[...].astype(BF16)

    third = bands // 6
    loop(third, fast_back)
    poll()
    loop(third, lambda i: fast_back(i + third))
    poll()
    loop(bands // 2 - 2 * third, lambda i: fast_back(i + 2 * third))
    poll()

    poll()
    while not all(done(name) for name in order):
        for name in order:
            if not done(name):
                advance(name)
    for copy in stores + parameter_stores:
        copy.wait()


def hand_on(*refs):
    sources, targets, staged, small, sem = refs[0:11], refs[11:24], refs[24:31], refs[31:36], refs[36]
    held = staged[0:2] + sources[2:6] + staged[2:7]
    loads = {k: pltpu.make_async_copy(sources[k], held[k], sem.at[k]) for k in (8, 9, 10, 0, 1, 6, 7)}
    stores = {k: pltpu.make_async_copy(held[k], targets[k], sem.at[11 + k]) for k in (0, 1, 2, 3, 5, 6, 7)}
    for k in range(5):
        stores[8 + k] = pltpu.make_async_copy(small[k], targets[8 + k], sem.at[19 + k])
        stores[13 + k] = pltpu.make_async_copy(
            held[4].at[pl.ds(768 * k, 768)], targets[4].at[:, pl.ds(256 * k, 256)], sem.at[24 + k]
        )
    for copy in loads.values():
        copy.start()
    for k in (2, 3, 5, 13, 14, 15, 16, 17):
        stores[k].start()
    for k in (8, 9, 10):
        loads[k].wait()
    small[0][...] = held[8][0:96, :]
    for tap in range(9):
        at = 96 + 32 * (tap // 4)
        small[1][32 * tap : 32 * (tap + 1), :] = held[8][at : at + 32, 32 * (tap % 4) : 32 * (tap % 4 + 1)]
    small[2][...] = held[8][192:224, :]
    for source, target in ((held[9], small[3]), (held[10], small[4])):
        count = target.shape[0]
        for row in range(16):
            width = min(LANES, count - row * LANES)
            target[pl.ds(row * LANES, width)] = source[row : row + 1, 0:width].reshape(width)
    for k in range(8, 13):
        stores[k].start()
    for k in (0, 1, 6, 7):
        loads[k].wait()
        stores[k].start()
    for copy in stores.values():
        copy.wait()


def body(
    slow_input,
    fast_input,
    clip_ids,
    fast_narrow,
    fast_spatial,
    fast_widen,
    lateral_conv,
    slow_narrow,
    slow_spatial,
    slow_widen,
    norm_gains,
    norm_biases,
    slow_cotangent,
    fast_cotangent,
):
    n_dp, n_rep = lax.axis_size("dp"), lax.axis_size("rep")
    low = 2 if n_dp % 2 == 0 else 1
    high = n_dp // low
    frames, plane, channels = slow_input.shape
    fast_frames, _, fast_channels = fast_input.shape
    side = math.isqrt(plane)
    rows = frames * plane
    slow_count = rows * n_dp * n_rep
    fast_count = slow_count * (fast_frames // frames)

    def flat(values):
        return values.transpose(1, 0, 2).reshape(values.shape[0] * values.shape[1], values.shape[2])

    def unflat(values, count):
        return values.reshape(plane, count, values.shape[1]).transpose(1, 0, 2)

    widths = [
        fast_narrow.shape[1], fast_spatial.shape[1], fast_widen.shape[0], lateral_conv.shape[1],
        slow_narrow.shape[1], slow_spatial.shape[1], slow_widen.shape[0],
    ]

    cf = fast_channels
    bs = slow_spatial.shape[1]
    band = side * frames
    any_spec = pl.BlockSpec(memory_space=pl.ANY)
    vmem_spec = pl.BlockSpec(memory_space=pltpu.VMEM)
    near_low = n_dp if n_dp * n_rep <= 32 else low
    stages = 1 if near_low == n_dp else 2
    pad = rows + 2 * band

    def shape(dims, dtype):
        return jax.ShapeDtypeStruct(dims, dtype)

    out_shape = [
        shape((rows, channels), BF16), shape((4 * rows, cf), BF16),
        pltpu.VMEM((rows, channels), BF16), pltpu.VMEM((4 * rows, cf), BF16),
        pltpu.VMEM((15 * bs, bs), F32), pltpu.VMEM((9 * bs, bs), F32), shape((channels, bs), F32),
        shape((5 * bs, cf), F32), shape((256, cf), F32), shape((16, LANES), F32), shape((16, LANES), F32),
        shape((10, max(high // 4, 1), 32, 256), F32),
    ]
    scratch = [
        pltpu.VMEM((rows, channels), BF16), pltpu.VMEM((rows, channels), BF16),
        pltpu.VMEM((4 * rows, cf), BF16), pltpu.VMEM((rows, channels), F32),
        pltpu.VMEM((rows, 512), F32), pltpu.VMEM((rows, 512), F32),
        pltpu.VMEM((pad, 3 * bs), BF16), pltpu.VMEM((pad, 3 * bs), BF16),
        pltpu.VMEM((pad, 384), BF16), pltpu.VMEM((pad, 384), BF16),
        pltpu.VMEM((rows, bs), F32), pltpu.VMEM((rows, bs), F32),
        pltpu.VMEM((rows, 128), F32), pltpu.VMEM((rows, 128), F32), pltpu.VMEM((rows, 128), F32),
        pltpu.VMEM((rows, bs), BF16), pltpu.VMEM((rows, bs), BF16), pltpu.VMEM((rows, 128), BF16),
        pltpu.VMEM((rows, 896), BF16), pltpu.VMEM((3, 1512, 256), F32), pltpu.VMEM((2016, 256), F32),
        pltpu.VMEM((768, 256), F32),
        pltpu.VMEM((3 * bs, channels + bs), BF16), pltpu.VMEM((9 * bs, bs), BF16),
        pltpu.VMEM((channels, bs), BF16), pltpu.VMEM(norm_gains.shape, F32), pltpu.VMEM(norm_gains.shape, F32),
        pltpu.VMEM((9, 8, channels), F32), pltpu.VMEM((2, 8, 256), F32),
        pltpu.VMEM((96, cf), BF16), pltpu.VMEM((288, 32), BF16), pltpu.VMEM((32, cf), BF16),
        pltpu.VMEM((bs, 640), BF16), pltpu.VMEM((128, 768), BF16),
        pltpu.VMEM((3, 128, 384), BF16), pltpu.VMEM((3, 384, 128), BF16), pltpu.VMEM((512, 128), BF16),
        pltpu.VMEM((4 * band, cf), F32),
        pltpu.VMEM((24, LANES), F32), pltpu.VMEM((24, LANES), F32),
        pltpu.VMEM((near_low * n_rep, 1, sum(TURNS.values())), F32),
        pltpu.VMEM((max(n_dp // near_low, 1), 1, sum(TURNS.values())), F32),
        pltpu.SemaphoreType.DMA((stages, len(TURNS))), pltpu.SemaphoreType.DMA((stages, len(TURNS))),
        pltpu.SemaphoreType.DMA((32,)), pltpu.SemaphoreType.DMA((10, 2)),
        pltpu.SemaphoreType.DMA((10,)), pltpu.SemaphoreType.DMA((10, 10 if high == 4 else 11)),
    ]
    factor = 1.0 / math.sqrt(float(slow_count))
    results = pl.pallas_call(
        functools.partial(kernel, (n_dp, n_rep, low, frames, side, float(slow_count), float(fast_count), factor)),
        out_shape=out_shape,
        in_specs=[any_spec] * 4 + [pl.BlockSpec(memory_space=pltpu.SMEM)] + [any_spec] * 9,
        out_specs=[any_spec] * 2 + [vmem_spec] * 4 + [any_spec] * 6,
        scratch_shapes=scratch,
        compiler_params=pltpu.CompilerParams(
            collective_id=0, has_side_effects=True, vmem_limit_bytes=54528 * 2**10
        ),
    )(
        flat(slow_input), flat(fast_input), flat(slow_cotangent), flat(fast_cotangent), clip_ids,
        fast_narrow.reshape(-1, cf), fast_spatial.reshape(-1, 32), fast_widen.T,
        lateral_conv.reshape(-1, cf), slow_narrow.reshape(3 * bs, -1), slow_spatial.reshape(9 * bs, bs),
        slow_widen, norm_gains, norm_biases,
    )
    final = [shape((rows, channels), BF16), shape((4 * rows, cf), BF16)] * 2 + [
        shape((3 * bs, channels + bs), F32), shape((9 * bs, bs), F32), *out_shape[6:8],
        shape((96, cf), F32), shape((288, 32), F32), shape((32, cf), F32),
        shape(norm_gains.shape, F32), shape(norm_gains.shape, F32),
    ]
    handed = pl.pallas_call(
        hand_on,
        out_shape=final,
        in_specs=[any_spec] * 2 + [vmem_spec] * 4 + [any_spec] * 5,
        out_specs=[any_spec] * 13,
        scratch_shapes=[pltpu.VMEM(item.shape, item.dtype) for item in out_shape[0:2] + out_shape[6:11] + final[8:13]]
        + [pltpu.SemaphoreType.DMA((29,))],
        compiler_params=pltpu.CompilerParams(vmem_limit_bytes=54528 * 2**10),
    )(*results[0:2], *[pltpu.with_memory_space_constraint(r, pltpu.VMEM) for r in results[2:6]], *results[6:11])
    slow_out, fast_out, slow_grad, fast_grad, dsa, dsb, dsc, dl, dfa, dfb, dfc, dgains, dbiases = handed

    return (
        unflat(slow_out, frames),
        unflat(fast_out, fast_frames),
        unflat(slow_grad, frames),
        unflat(fast_grad, fast_frames),
        dfa.reshape(fast_narrow.shape),
        dfb.reshape(fast_spatial.shape),
        dfc.T,
        dl.reshape(lateral_conv.shape),
        dsa.reshape(slow_narrow.shape),
        dsb.reshape(slow_spatial.shape),
        dsc,
        dgains,
        dbiases,
    )


def solution(mesh):
    sharded = P(("dp", "rep"), None, None)
    return jax.shard_map(
        body,
        mesh=mesh,
        in_specs=(sharded, sharded, P(("dp", "rep"), None)) + (P(),) * 9 + (sharded, sharded),
        out_specs=(sharded,) * 4 + (P(),) * 9,
        check_vma=False,
    )
```

```python
import functools
import math

import jax
import jax.numpy as jnp
from jax import lax
from jax.experimental import pallas as pl
from jax.experimental.pallas import tpu as pltpu
from jax.sharding import PartitionSpec as P

EPS = 1e-05
F32 = jnp.float32
BF16 = jnp.bfloat16
MESH = pl.DeviceIdType.MESH
NN = ((1,), (0,))
NT = ((1,), (1,))
TN = ((0,), (0,))
LANES = 128
FA, FB, FC, LAT, SLOW_A, SLOW_B, SLOW_C = range(7)
FORWARD = {LAT: 512, FA: 128, SLOW_A: 512, FB: 128, SLOW_B: 512, FC: 256, SLOW_C: 768, SLOW_C + 1: 512}
BACKWARD = {SLOW_C: 1024, SLOW_C + 1: 1024, FC: 256, SLOW_B: 512, FB: 128, SLOW_A: 512, FA: 128, LAT: 512}
BACK = 8
TURNS = {**FORWARD, **{BACK + norm: lanes for norm, lanes in BACKWARD.items()}}


class Piece:
    pass


SC, SB, SA, LT = 0, 1, 4, 9
C, X, Y, Z, Z0, Z1 = range(6)
PLANE = ((C, X, Y, Z), (C, Y, X, Z))
HALVES = ((C, X, Y, Z0, Z1), (C, Y, X, Z0, Z1))
BETWEEN = ((C, X, Z0, Z1, Y), (C, Y, Z0, Z1, X))
LINE = ((C, Z0, Z1, X, Y), (C, Z0, Z1, Y, X))
ORDER_OF = (PLANE, HALVES, LINE, PLANE, BETWEEN, PLANE, HALVES, HALVES, PLANE, PLANE)
POLLS = (
    (),
    (0,),
    (),
    (),
    (),
    (),
    (),
    (0,),
    (),
    (1,),
    (2,),
    (0, 3),
    (),
    (),
    (),
    (1,),
    (4,),
    (3, 2),
    (1, 5),
    (4, 0, 6),
    (3, 7, 1),
    (5, 2, 9),
    (6, 4, 8),
    (7, 0),
    (5, 3, 2),
    (1,),
    (9,),
    (
        6, 5, 4, 7, 6, 3, 8, 1, 9, 5, 4, 7, 6, 2, 1, 3, 9, 5, 8, 7, 4, 6, 2, 1,
        3, 9, 5, 0, 8, 7, 6, 4, 1, 2, 9, 3, 5, 8, 0, 7, 6, 4, 1, 9, 2, 8, 0, 7,
        6, 4, 2, 9, 8, 4, 7, 6, 2, 8, 7,
    ),
)


def dot(left, right, dims):
    return lax.dot_general(left, right, (dims, ((), ())), preferred_element_type=F32)


def column_sums(values):
    return jnp.sum(values.reshape(values.shape[0] // 8, 8, values.shape[1]), axis=0)


def squash(partial):
    return jnp.sum(partial, axis=0, keepdims=True)


def fold_lanes(values):
    half = values + pltpu.roll(values, 64, 1)
    return half + pltpu.roll(half, 32, 1)


def loop(count, body, init=None, unroll=1):
    if init is None:

        def plain(index, carry):
            body(index)
            return carry

        lax.fori_loop(0, count, plain, 0, unroll=unroll)
        return None
    return lax.fori_loop(0, count, body, init, unroll=unroll)


def rows_at(index, size):
    return pl.ds(pl.multiple_of(index * size, 16), size)


def kernel(
    dims,
    xs_h, xf_h, cs_h, cf_h, clip, wfa_h, wfb_h, wfc_h, wl_h, wsa_h, wsb_h, wsc_h, gains_h, biases_h,
    slow_h, cf, gsum, xf, dsa, dsb, dsc_h, dl_h, small_h, dgains_h, dbiases_h, extra_h,
    xs, cs, big, sec_fc, gsf, hcs, gcs, hcf, gcf,
    sec_lat, dbuf, sec_fa, sec_fb, dbuf_f, jl, hbs, hbf, vx, slab, slab_sc, summed,
    wsa, wsb, wsc, gains_in, biases_in, vectors, masks, wfa_in, wfb_in, wfc_in, wlat, wfa, wfb, wfbk, wfc,
    stage_a, gain_rows, bias_rows, near, far, sum_send, sum_recv, io_sem, own_sem, big_send, big_recv,
):
    n_dp, n_rep, low, frames, side, slow_count, fast_count, factor = dims
    sec_sa, sec_sb = dsa, dsb
    rows = xs.shape[0]
    half = rows // 2
    band = side * frames
    bands = side
    fband = 4 * band
    cs_n = xs.shape[1]
    bs = wsb.shape[1]

    dp_i, rep_i = lax.axis_index("dp"), lax.axis_index("rep")
    dp_lo, dp_hi = lax.rem(dp_i, low), lax.div(dp_i, low)
    high = n_dp // low
    direct = n_dp * n_rep <= 32
    near_low = n_dp if direct else low
    near_dp, far_dp = lax.rem(dp_i, near_low), lax.div(dp_i, near_low)
    near_peers = [
        (far_dp * near_low + lax.rem(near_dp + a, near_low), lax.rem(rep_i + b, n_rep))
        for a in range(near_low)
        for b in range(n_rep)
        if a or b
    ]
    far_count = n_dp // near_low
    far_peers = [(lax.rem(far_dp + a, far_count) * near_low + near_dp, rep_i) for a in range(1, far_count)]
    stages = [(near, near_dp * n_rep + rep_i, near_peers)]
    if far_peers:
        stages.append((far, far_dp, far_peers))

    c, x = lax.rem(rep_i, 2), lax.div(rep_i, 2)
    y, z = dp_lo, lax.rem(dp_hi, 4)
    outer, outers = lax.div(dp_hi, 4), high // 4
    core_peer = (dp_i, 2 * x + 1 - c)
    x_peer = (dp_i, 2 * (1 - x) + c)
    y_peer = (dp_hi * low + 1 - y, rep_i)
    def z_peer(flip):
        return ((outer * 4 + z + flip - 2 * flip * lax.rem(lax.div(z, flip), 2)) * low + y, rep_i)

    z_peers = [((outer * 4 + lax.rem(z + k, 4)) * low + y, rep_i) for k in range(1, 4)]
    outer_peers = [((lax.rem(outer + k, outers) * 4 + z) * low + y, rep_i) for k in range(1, outers)]

    barrier = pltpu.get_barrier_semaphore()
    greeted = near_peers + far_peers
    for peer in greeted:
        pl.semaphore_signal(barrier, inc=1, device_id=peer, device_id_type=MESH)

    loads = {}
    for slot, (name, src, dst) in enumerate([
        ("xf", xf_h, xf), ("wfa", wfa_h, wfa_in), ("xs", xs_h, xs),
        ("wsa", wsa_h, wsa), ("wfb", wfb_h, wfb_in), ("wfc", wfc_h, wfc_in), ("wsb", wsb_h, wsb),
        ("wsc", wsc_h, wsc), ("cf", cf_h, cf), ("cs", cs_h, cs), ("gains", gains_h, gains_in), ("biases", biases_h, biases_in),
    ]):
        loads[name] = pltpu.make_async_copy(src, dst, io_sem.at[slot])
        loads[name].start()
        if name == "wfa":
            taps = [
                pltpu.make_async_copy(
                    wl_h.at[pl.ds(bs * k, bs)], wlat.at[:, pl.ds(LANES * k, LANES)], io_sem.at[27 + k]
                )
                for k in range(5)
            ]
            for tap in taps:
                tap.start()
    stores = []

    def store(src, dst, slot):
        copy = pltpu.make_async_copy(src, dst, io_sem.at[slot])
        copy.start()
        return copy

    turn_at, turn_index = {}, {}
    for index, (turn, width) in enumerate(TURNS.items()):
        turn_at[turn] = sum(list(TURNS.values())[:index])
        turn_index[turn] = index

    def put(turn, at, vector):
        near[stages[0][1], :, pl.ds(turn_at[turn] + at, vector.shape[1])] = vector

    def sum_copy(turn, stage, first, count, peer):
        buffer = stages[stage][0]
        block = buffer.at[pl.ds(first, count), :, pl.ds(turn_at[turn], TURNS[turn])]
        return pltpu.make_async_remote_copy(
            src_ref=block, dst_ref=block, send_sem=sum_send.at[stage, turn_index[turn]],
            recv_sem=sum_recv.at[stage, turn_index[turn]], device_id=peer, device_id_type=MESH,
        )

    def exchange_start(turn):
        for peer in near_peers:
            sum_copy(turn, 0, stages[0][1], 1, peer).start()

    def exchange_end(turn):
        lanes = pl.ds(turn_at[turn], TURNS[turn])
        for stage, (buffer, rank, peers) in enumerate(stages):
            if stage:
                buffer[rank, :, lanes] = total
                for peer in peers:
                    sum_copy(turn, stage, rank, 1, peer).start()
            copy = sum_copy(turn, stage, 0, len(peers), peers[0])
            copy.wait_recv()
            total = jnp.sum(buffer[:, :, lanes], axis=0)
            copy.wait_send()
        return total

    def take(total, at, width):
        return total[:, at : at + width]

    def pair32(first, second):
        group = lax.broadcasted_iota(jnp.int32, (8, LANES), 1) // 32
        rows8 = (8, LANES)
        first = fold_lanes(jnp.broadcast_to(first, rows8))
        second = fold_lanes(jnp.broadcast_to(second, rows8))
        return jnp.where(group == 0, first, jnp.where(group == 1, second, 0.0))[0:1, :]

    def unpair32(total):
        group = lax.broadcasted_iota(jnp.int32, (8, LANES), 1) // 32
        total = jnp.broadcast_to(total, (8, LANES))
        first = fold_lanes(jnp.where(group == 0, total, 0.0))
        second = fold_lanes(jnp.where(group == 1, total, 0.0))
        return first[0:1, :], second[0:1, :]

    pieces = {}

    bits = {C: (c, core_peer), X: (x, x_peer), Y: (y, y_peer),
            Z0: (lax.rem(z, 2), z_peer(1)), Z1: (lax.div(z, 2), z_peer(2))}

    def add_piece(name, ref, lane, size, index):
        axes = ORDER_OF[name]
        piece = Piece()
        piece.name, piece.ref, piece.lane, piece.size, piece.index = name, ref, lane, size, index
        piece.step, piece.axes, piece.steps = 0, axes, len(axes[0])
        starts, counts, arriving = [[0], [0]], [size], [size]
        for step, pair in enumerate(zip(*axes)):
            for side, axis in enumerate(pair):
                if axis == Z:
                    starts[side].append(starts[side][-1] + z * (counts[-1] // 4))
                else:
                    starts[side].append(starts[side][-1] + bits[axis][0] * (counts[-1] // 2))
            counts.append(counts[-1] // (4 if pair[0] == Z else 2))
            arriving.append(arriving[-1] + (3 if pair[0] == Z else 1) * counts[-1])
        piece.starts, piece.counts, piece.arriving = starts, counts, arriving
        pieces[name] = piece

    for k in range(2):
        add_piece(SB + k, sec_fc, 256 * k, 768, k)
    for k in range(4):
        add_piece(SA + k, big, 256 * k, 768, 2 + k)
    add_piece(SB + 2, slab.at[0], 0, 768, 6)
    add_piece(SA + 4, slab.at[1], 0, 768, 7)
    add_piece(LT, slab.at[2], 0, 768, 8)
    add_piece(SC, slab_sc, 0, 1024, 9)

    def span(piece, start, count, lane=0, width=256):
        return piece.ref.at[pl.ds(pl.multiple_of(start, 8), count), pl.ds(piece.lane + lane, width)]

    def send(piece, step, src, dst, peer):
        pltpu.make_async_remote_copy(
            src_ref=src, dst_ref=dst, send_sem=big_send.at[piece.index],
            recv_sem=big_recv.at[piece.index, step], device_id=peer, device_id_type=MESH,
        ).start()

    def result(piece, start, count, lane=0, width=256):
        name = piece.name
        start = pl.multiple_of(start, 8)
        if name == LT:
            return summed.at[pl.ds(start, count), pl.ds(lane, width)]
        if name == SC:
            return dsc_h.at[pl.ds(start, count), pl.ds(lane, width)]
        if name >= SA:
            return dsa.at[pl.ds(768 * (name - SA) + start, count), pl.ds(lane, width)]
        return dsb.at[pl.ds(768 * (name - SB) + start, count), pl.ds(lane, width)]

    def own_copies(piece):
        count, sem = piece.counts[-1], own_sem.at[piece.index]
        return [
            pltpu.make_async_copy(
                span(piece, start[-1], count, 128 * side, 128),
                result(piece, start[-1], count, 128 * side, 128),
                sem.at[side],
            )
            for side, start in enumerate(piece.starts)
        ]

    def arrived(piece, step, rows_in):
        block = span(piece, 0, rows_in) if step < piece.steps else result(piece, 0, rows_in)
        copy = pltpu.make_async_remote_copy(
            src_ref=block, dst_ref=block, send_sem=big_send.at[piece.index],
            recv_sem=big_recv.at[piece.index, step], device_id=core_peer, device_id_type=MESH,
        )
        copy.wait_recv()
        copy.wait_send()

    def add_rows(piece, target, source, count, lane, width):
        lanes = pl.ds(piece.lane + lane, width)
        chunk = piece.size // 32
        ref = piece.ref

        def step(i):
            into = pl.ds(pl.multiple_of(target + i * chunk, 8), chunk)
            ref[into, lanes] = ref[into, lanes] + ref[pl.ds(pl.multiple_of(source + i * chunk, 8), chunk), lanes]

        loop(count // chunk, step)

    order = range(10)

    def unpack_small():
        stores.append(store(summed.at[:, pl.ds(0, 128)], dl_h.at[pl.ds(0, 768)], 16))
        stores.append(store(summed.at[pl.ds(0, 512), pl.ds(128, 128)], dl_h.at[pl.ds(768, 512)], 17))
        stores.append(store(summed.at[pl.ds(512, 256), pl.ds(128, 128)], small_h, 18))

    polled = [0]

    def poll():
        polled[0] += 1
        for name in POLLS[polled[0] - 1]:
            advance(name)

    def done(name):
        return pieces[name].step > 2 * pieces[name].steps

    def advance(name):
        piece = pieces[name]
        step, steps, index = piece.step, piece.steps, piece.index
        piece.step = step + 1
        starts, counts, arriving, axes = piece.starts, piece.counts, piece.arriving, piece.axes
        ref, lane = piece.ref, piece.lane

        def received(last):
            fan = 3 if axes[0][last] == Z else 1
            return fan * counts[last + 1]

        if 0 < step < steps or (step == steps and axes[0][-1] != Z):
            arrived(piece, step - 1, received(step - 1))
            if step == 1:
                add_rows(piece, starts[0][1], arriving[0], counts[1], 0, 256)
            else:
                for side in range(2):
                    add_rows(piece, starts[side][step], arriving[step - 1], counts[step], 128 * side, 128)
        elif step == steps:
            arrived(piece, step - 1, received(step - 1))
        elif step > steps:
            arrived(piece, step - 1, received(2 * steps - step))

        if step < steps:
            held, keep = counts[step], counts[step + 1]
            if step == 0:
                at = starts[0][0] + (1 - c) * keep
                send(piece, 0, span(piece, at, keep), span(piece, arriving[0], keep), core_peer)
                return
            for side in range(2):
                axis, start = axes[side][step], starts[side][step]
                if axis == Z:
                    for k, peer in enumerate(z_peers):
                        at, into = start + lax.rem(z + k + 1, 4) * keep, arriving[step] + k * keep
                        send(
                            piece, step, span(piece, at, keep, 128 * side, 128),
                            span(piece, into, keep, 128 * side, 128), peer,
                        )
                else:
                    bit, peer = bits[axis]
                    at = start + (1 - bit) * keep
                    send(
                        piece, step, span(piece, at, keep, 128 * side, 128),
                        span(piece, arriving[step], keep, 128 * side, 128), peer,
                    )
        elif step == steps:
            last = counts[-1]
            own = [
                (pl.ds(pl.multiple_of(starts[side][-1], 8), last), pl.ds(lane + 128 * side, 128))
                for side in range(2)
            ]
            both = jnp.concatenate([ref[own[0]], ref[own[1]]], axis=1)
            if axes[0][-1] == Z:
                for k in range(3):
                    both = both + ref[pl.ds(arriving[steps - 1] + k * last, last), pl.ds(lane, 256)]
            if outers > 1:
                held = span(piece, arriving[steps - 1], last)
                ref[pl.ds(arriving[steps - 1], last), pl.ds(lane, 256)] = both
                for peer in outer_peers:
                    send(piece, 10, held, extra_h.at[index, outer, pl.ds(0, last)], peer)
                block = extra_h.at[index, pl.ds(0, outers - 1), pl.ds(0, last)]
                copy = pltpu.make_async_remote_copy(
                    src_ref=block, dst_ref=block, send_sem=big_send.at[index], recv_sem=big_recv.at[index, 10],
                    device_id=core_peer, device_id_type=MESH,
                )
                copy.wait_recv()
                copy.wait_send()
                local = [(held, extra_h.at[index, outer, pl.ds(0, last)])]
                for k in range(outers):
                    local.append((extra_h.at[index, k, pl.ds(0, last)], span(piece, arriving[0] + k * last, last)))
                for src, dst in local:
                    copy = pltpu.make_async_copy(src, dst, own_sem.at[index, 0])
                    copy.start()
                    copy.wait()
                both = ref[pl.ds(arriving[0], last), pl.ds(lane, 256)]
                for k in range(1, outers):
                    both = both + ref[pl.ds(arriving[0] + k * last, last), pl.ds(lane, 256)]
            both = both * factor
            for side in range(2):
                ref[own[side]] = both[:, 128 * side : 128 * (side + 1)]
        if steps <= step < 2 * steps:
            back = 2 * steps - 1 - step
            count = counts[back + 1]
            if step == steps + 1:
                for copy in own_copies(piece):
                    copy.wait()
            if back == 0:
                block = result(piece, starts[0][1], count)
                send(piece, step, block, block, core_peer)
                return
            for side in range(2):
                axis, start = axes[side][back], starts[side][back + 1]
                block = result(piece, start, count, 128 * side, 128)
                source = span(piece, start, count, 128 * side, 128) if step == steps else block
                for peer in z_peers if axis == Z else [bits[axis][1]]:
                    send(piece, step, source, block, peer)
            if step == steps:
                for copy in own_copies(piece):
                    copy.start()
        elif step == 2 * steps and name == LT:
            unpack_small()

    spots = {FC: 0, LAT: 1, SLOW_A: 3, SLOW_B: 5, SLOW_C: 7, FA: 16, FB: 17}

    lane16 = lax.broadcasted_iota(jnp.int32, (16, LANES), 1)

    def unpack(packed):
        fa = fold_lanes(jnp.where(lane16 // 32 == 0, packed, 0.0))[0:1, :]
        fb = fold_lanes(jnp.where(lane16 // 32 == 1, packed, 0.0))[0:1, :]
        turned = pltpu.roll(packed, 64, 1)
        moved = jnp.where(lane16 < 64, turned, pltpu.roll(turned, 15, 0))
        found = {FA: fa, FB: fb}
        at = 0
        for name, count in ((FC, 1), (LAT, 2), (SLOW_A, 2), (SLOW_B, 2), (SLOW_C, 8)):
            found[name] = jnp.concatenate([moved[at + k : at + k + 1, :] for k in range(count)], axis=1)
            at += count
        return found

    held = [0]

    def settle(vector):
        at, width = held[0], vector.shape[1]
        held[0] += 1
        line, row = at // 8, slice(at % 8, at % 8 + 1)
        vectors[line, row, 0:width] = vector

        def read(lanes=slice(0, width)):
            return vectors[line, row, lanes]

        return read

    gains, biases = {}, {}

    def read_parameters():
        for name, flat_in, target in (("gains", gains_in, gains), ("biases", biases_in, biases)):
            loads[name].wait()
            count = flat_in.shape[0]
            stage_a[0:16, :] = jnp.zeros((16, LANES), F32)
            for row in range(16):
                width = min(LANES, count - row * LANES)
                stage_a[row : row + 1, 0:width] = flat_in[pl.ds(row * LANES, width)].reshape(1, width)
            for key, vector in unpack(stage_a[0:16, :]).items():
                target[key] = settle(vector)

    def gain(name):
        return gains[name]()

    def bias(name):
        return biases[name]()

    def moments(name, total, squares, count, *lanes):
        mean = total * (1.0 / count)
        scale = lax.rsqrt(squares * (1.0 / count) - mean * mean + EPS)
        return settle(mean), settle(scale), settle(0.5 * gains[name](*lanes) * scale), settle(0.5 * biases[name](*lanes))

    def back_vectors(name, stats, bias_total, gain_total, count):
        mean, scale = stats[0](), stats[1]()
        lead = gain(name) * scale
        tilt = lead * scale * gain_total * (1.0 / count)
        level = lead * bias_total * (1.0 / count) - mean * tilt
        return settle(lead), settle(level), settle(tilt)

    def report(name, bias_total, gain_total, skip=0):
        at = spots[name] + skip
        for piece in range(bias_total.shape[1] // LANES):
            lanes = slice(piece * LANES, (piece + 1) * LANES)
            gain_rows[at + piece : at + piece + 1, :] = gain_total[:, lanes]
            bias_rows[at + piece : at + piece + 1, :] = bias_total[:, lanes]

    def silu_of(values, stats):
        h = (values - stats[0]()) * stats[2]() + stats[3]()
        return h + h * jnp.tanh(h)

    def slope_of(h):
        t = jnp.tanh(h)
        out, gate = h + h * t, 0.5 + 0.5 * t
        return out, gate + out * (1.0 - gate)

    def clip_masks(width):
        frame = lax.broadcasted_iota(jnp.int32, (1, 8, width), 1)
        with_prev = jnp.zeros((1, 8, width), F32)
        with_next = jnp.zeros((1, 8, width), F32)
        for t in range(1, frames):
            same = jnp.where(clip[0, t] == clip[0, t - 1], 1.0, 0.0)
            with_prev = jnp.where(frame == t, same, with_prev)
            with_next = jnp.where(frame == t - 1, same, with_next)
        return with_prev, with_next

    masks[0:1], masks[1:2] = clip_masks(256)

    def prev(width):
        return masks[0:1, :, 0:width]

    def following(width):
        return masks[1:2, :, 0:width]

    def roll_frames(values, mask, step, mask_first):
        grouped = values.reshape(values.shape[0] // 8, 8, values.shape[1])
        if mask_first:
            grouped = grouped * mask
        grouped = pltpu.roll(grouped, step % 8, 1)
        if not mask_first:
            grouped = grouped * mask
        return grouped.reshape(values.shape)

    def spread_columns(target, index, values):
        width = values.shape[1]
        nothing = jnp.zeros((frames, width), F32)
        at = pl.ds(pl.multiple_of((index + 1) * band, 16), band)
        target[at, 0:width] = jnp.concatenate([nothing, values[: band - frames]], axis=0).astype(BF16)
        target[at, width : 2 * width] = values.astype(BF16)
        target[at, 2 * width :] = jnp.concatenate([values[frames:], nothing], axis=0).astype(BF16)

    gain_rows[...] = jnp.zeros(gain_rows.shape, F32)
    bias_rows[...] = jnp.zeros(bias_rows.shape, F32)
    for target in (hcs, gcs, hcf, gcf):
        edge = jnp.zeros((band, target.shape[1]), BF16)
        target[0:band, :] = edge
        target[band + rows : rows + 2 * band, :] = edge

    def lane_groups(count=LANES):
        return lax.broadcasted_iota(jnp.int32, (count, LANES), 1) // 32

    def block_mask():
        row_group = lax.broadcasted_iota(jnp.int32, (LANES, LANES), 0) // 32
        return jnp.where(lane_groups() == row_group, 1.0, 0.0)

    repeat_lanes = jnp.where(
        lax.broadcasted_iota(jnp.int32, (32, LANES), 1) % 32 == lax.broadcasted_iota(jnp.int32, (32, LANES), 0),
        1.0, 0.0,
    ).astype(BF16)

    wfa[...] = jnp.zeros(wfa.shape, BF16)
    loads["wfa"].wait()
    for phase in range(4):
        for k in range(3):
            wfa[32 * phase : 32 * (phase + 1), LANES * (phase + k) : LANES * (phase + k + 1)] = wfa_in[
                32 * k : 32 * (k + 1), :
            ]
    loads["xf"].wait()

    def arrange(i):
        at = rows_at(i, band)
        stage_a[...] = xf[rows_at(i, fband), :].astype(F32)
        phases = [stage_a[pl.ds(phase, band, stride=4), :] for phase in range(4)]
        vx[at, 0:128] = roll_frames(phases[2], prev(128), 1, False).astype(BF16)
        vx[at, 128:256] = roll_frames(phases[3], prev(128), 1, False).astype(BF16)
        for phase in range(4):
            vx[at, 256 + 128 * phase : 384 + 128 * phase] = phases[phase].astype(BF16)
        vx[at, 768:896] = roll_frames(phases[0], following(128), -1, False).astype(BF16)

    loop(bands, arrange, unroll=2)
    for tap in taps:
        tap.wait()

    def zero2(width):
        return (jnp.zeros((8, width), F32), jnp.zeros((8, width), F32))

    def conv_fa(i, carry):
        at = rows_at(i, half)
        value = dot(vx[at, 128:896], wfa[...], NT)
        sec_fa[at, :] = value
        return carry[0] + column_sums(value), carry[1] + column_sums(value * value)

    def conv_lat(i, carry):
        at = rows_at(i, half)
        value = dot(vx[at, 0:640], wlat[...], NT)
        sec_lat[at, :] = value
        return carry[0] + column_sums(value), carry[1] + column_sums(value * value)

    sum_lat, sq_lat = loop(2, conv_lat, zero2(256))
    put(LAT, 0, squash(sum_lat))
    put(LAT, 256, squash(sq_lat))
    pl.semaphore_wait(barrier, len(greeted))
    exchange_start(LAT)

    sum_fa, sq_fa = loop(2, conv_fa, zero2(128))
    put(FA, 0, pair32(squash(sum_fa), squash(sq_fa)))
    exchange_start(FA)

    loads["xs"].wait()
    loads["wsa"].wait()

    def narrow_main(i):
        at = rows_at(i, half)
        for k in range(3):
            big[at, bs * k : bs * (k + 1)] = dot(xs[at, :], wsa[bs * k : bs * (k + 1), 0:cs_n], NT)

    loop(2, narrow_main)
    loads["wfb"].wait()
    loads["wfc"].wait()
    spread = dot(wfb_in[...], repeat_lanes, NN)
    for a in range(3):
        for b in range(3):
            piece = spread[32 * (3 * a + b) : 32 * (3 * a + b + 1), :]
            block = (jnp.concatenate([piece] * 4, axis=0) * block_mask()).astype(BF16)
            wfb[a, :, LANES * b : LANES * (b + 1)] = block
            wfbk[a, LANES * (2 - b) : LANES * (3 - b), :] = block
    widen = dot(wfc_in[...], repeat_lanes, TN)
    for phase in range(4):
        wfc[LANES * phase : LANES * (phase + 1), :] = jnp.where(lane_groups() == phase, widen, 0.0).astype(BF16)
    read_parameters()
    total = exchange_end(LAT)

    stats_lat = moments(LAT, take(total, 0, 256), take(total, 256, 256), slow_count)

    def act_fa(i):
        spread_columns(hcf, i, silu_of(sec_fa[rows_at(i, band), :], stats_fa))

    def act_lat(i):
        at = rows_at(i, 2 * band)
        jl[at, :] = silu_of(sec_lat[at, :], stats_lat).astype(BF16)

    loop(bands // 2, act_lat)

    def conv_fb(i, carry):
        value = None
        for a in range(3):
            at = pl.ds(pl.multiple_of(i * half + band * a, 16), half)
            term = dot(hcf[at, :], wfb[a], NT)
            value = term if value is None else value + term
        sec_fb[rows_at(i, half), :] = value
        return carry[0] + column_sums(value), carry[1] + column_sums(value * value)

    def narrow_lateral(i):
        at = rows_at(i, half)
        for k in range(3):
            big[at, bs * k : bs * (k + 1)] += dot(jl[at, :], wsa[bs * k : bs * (k + 1), cs_n:], NT)

    loop(2, narrow_lateral)

    def combine_sa(i, carry):
        at = rows_at(i, band)
        value = (
            big[at, bs : 2 * bs]
            + roll_frames(big[at, 0:bs], prev(256), 1, False)
            + roll_frames(big[at, 2 * bs : 3 * bs], following(256), -1, False)
        )
        sec_sa[at, :] = value
        return carry[0] + column_sums(value), carry[1] + column_sums(value * value)

    sum_sa, sq_sa = loop(bands, combine_sa, zero2(256))
    put(SLOW_A, 0, squash(sum_sa))
    put(SLOW_A, 256, squash(sq_sa))
    exchange_start(SLOW_A)

    total = exchange_end(FA)
    stats_fa = moments(FA, *unpair32(total), fast_count)
    loop(bands, act_fa, unroll=2)
    sum_fb, sq_fb = loop(2, conv_fb, zero2(128))
    put(FB, 0, pair32(squash(sum_fb), squash(sq_fb)))
    exchange_start(FB)
    total = exchange_end(SLOW_A)

    stats_sa = moments(SLOW_A, take(total, 0, 256), take(total, 256, 256), slow_count)

    def act_sa(i):
        spread_columns(hcs, i, silu_of(sec_sa[rows_at(i, band), :], stats_sa))

    def act_fb(i):
        at = rows_at(i, 2 * band)
        hbf[at, :] = silu_of(sec_fb[at, :], stats_fb).astype(BF16)

    loop(bands, act_sa, unroll=2)
    loads["wsb"].wait()

    def conv_sb(i, carry):
        value = None
        for a in range(3):
            at = pl.ds(pl.multiple_of(i * half + band * a, 16), half)
            for b in range(3):
                tap = 3 * a + b
                term = dot(hcs[at, bs * b : bs * (b + 1)], wsb[bs * tap : bs * (tap + 1), :], NT)
                value = term if value is None else value + term
        sec_sb[rows_at(i, half), :] = value
        return carry[0] + column_sums(value), carry[1] + column_sums(value * value)

    sum_sb, sq_sb = loop(2, conv_sb, zero2(256))
    put(SLOW_B, 0, squash(sum_sb))
    put(SLOW_B, 256, squash(sq_sb))
    exchange_start(SLOW_B)

    total = exchange_end(FB)
    stats_fb = moments(FB, *unpair32(total), fast_count)
    loop(bands // 2, act_fb)

    def widen_fast(i, carry):
        at = rows_at(i, half)
        value = dot(hbf[at, :], wfc[...], NT)
        sec_fc[at, :] = value
        return carry[0] + column_sums(value), carry[1] + column_sums(value * value)

    sum_fc, sq_fc = loop(2, widen_fast, zero2(512))

    def fold4(vector):
        return vector[:, 0:128] + vector[:, 128:256] + vector[:, 256:384] + vector[:, 384:512]

    put(FC, 0, squash(fold4(sum_fc)))
    put(FC, 128, squash(fold4(sq_fc)))
    exchange_start(FC)
    total = exchange_end(SLOW_B)

    stats_sb = moments(SLOW_B, take(total, 0, 256), take(total, 256, 256), slow_count)

    def act_sb(i, carry):
        at = rows_at(i, 2 * band)
        value = silu_of(sec_sb[at, :], stats_sb).astype(BF16)
        hbs[at, :] = value
        return carry + column_sums(value.astype(F32))

    sum_hbs = loop(bands // 2, act_sb, jnp.zeros((8, bs), F32))
    loads["wsc"].wait()
    mid = cs_n // 2

    def widen_slow(part):
        lanes = slice(part * mid, (part + 1) * mid)

        def step(i, carry):
            at = rows_at(i, half)
            value = dot(hbs[at, :], wsc[lanes, :], NT)
            big[at, lanes] = value
            return carry + column_sums(value * value)

        return loop(2, step, jnp.zeros((8, mid), F32))

    put(SLOW_C, 0, squash(sum_hbs))
    put(SLOW_C, 256, squash(widen_slow(0)))
    exchange_start(SLOW_C)
    put(SLOW_C + 1, 0, squash(widen_slow(1)))
    exchange_start(SLOW_C + 1)
    total = exchange_end(FC)
    stats_fc = moments(FC, take(total, 0, 128), take(total, 128, 128), fast_count)

    loads["cf"].wait()

    def finish_fast(i, carry):
        at, fat = rows_at(i, band), rows_at(i, fband)
        bias_sum, gain_sum = carry
        dbuf_f[0:fband, :] = cf[fat, :].astype(F32)
        for phase in range(4):
            lanes = slice(128 * phase, 128 * (phase + 1))
            centred = sec_fc[at, lanes] - stats_fc[0]()
            total_in = vx[at, 256 + 128 * phase : 384 + 128 * phase].astype(F32)
            out, slope = slope_of(0.5 * total_in + (centred * stats_fc[2]() + stats_fc[3]()))
            stage_a[pl.ds(phase, band, stride=4), :] = out
            grad = dbuf_f[pl.ds(phase, band, stride=4), :] * slope
            gsf[at, lanes] = grad
            bias_sum = bias_sum + column_sums(grad)
            gain_sum = gain_sum + column_sums(grad * centred)
        cf[fat, :] = stage_a[...].astype(BF16)
        return bias_sum, gain_sum

    bias_fc, gain_fc = loop(bands, finish_fast, zero2(128))
    put(BACK + FC, 0, squash(bias_fc))
    put(BACK + FC, 128, squash(gain_fc) * stats_fc[1]())
    exchange_start(BACK + FC)
    loads["cs"].wait()
    total = exchange_end(SLOW_C)
    squares = [take(total, 256, mid)]
    whole = settle(
        lax.dot_general(
            jnp.broadcast_to(take(total, 0, 256), (8, bs)), wsc[...].astype(F32), (NT, ((), ())),
            precision=lax.Precision.HIGHEST, preferred_element_type=F32,
        )[0:1, :]
    )
    stats_sc = []

    def finish_slow(part):
        lanes = slice(part * mid, (part + 1) * mid)
        def step(i, carry):
            at = rows_at(i, band)
            mean, lead, level = [stats_sc[part][k]() for k in (0, 2, 3)]
            centred = big[at, lanes] - mean
            out, slope = slope_of(0.5 * xs[at, lanes].astype(F32) + (centred * lead + level))
            grad = cs[at, lanes].astype(F32) * slope
            cs[at, lanes] = out.astype(BF16)
            gsum[at, lanes] = centred.astype(BF16)
            big[at, lanes] = grad
            return carry[0] + column_sums(grad), carry[1] + column_sums(grad * centred)

        bias_part, gain_part = loop(bands, step, zero2(mid))
        return squash(bias_part), squash(gain_part) * stats_sc[part][1]()

    for part in range(2):
        if part:
            squares.append(exchange_end(SLOW_C + 1))
        lanes = slice(part * mid, (part + 1) * mid)
        stats_sc.append(moments(SLOW_C, whole(lanes), squares[part], slow_count, lanes))
        bias_part, gain_part = finish_slow(part)
        put(BACK + SLOW_C + part, 0, bias_part)
        put(BACK + SLOW_C + part, mid, gain_part)
        exchange_start(BACK + SLOW_C + part)
    slow_store = store(cs, slow_h, 11)

    total = exchange_end(BACK + FC)
    bias_fc, gain_fc = take(total, 0, 128), take(total, 128, 128)
    report(FC, bias_fc, gain_fc)
    def slope_pass(section, stats, buffer):
        def step(i, carry):
            at = rows_at(i, 2 * band)
            centred = section[at, :] - stats[0]()
            grad = buffer[at, :] * slope_of(centred * stats[2]() + stats[3]())[1]
            buffer[at, :] = grad
            return carry[0] + column_sums(grad), carry[1] + column_sums(grad * centred)

        bias_sum, gain_sum = loop(bands // 2, step, zero2(section.shape[1]))
        return squash(bias_sum), squash(gain_sum) * stats[1]()

    lead_fc, level_fc, tilt_fc = back_vectors(FC, stats_fc, bias_fc, gain_fc, fast_count)

    def low_fc(i):
        at = rows_at(i, band)
        for phase in range(4):
            lanes = slice(128 * phase, 128 * (phase + 1))
            value = gsf[at, lanes] * lead_fc() - level_fc() - sec_fc[at, lanes] * tilt_fc()
            gcs[at, lanes] = value.astype(BF16)

    loop(bands, low_fc, unroll=2)

    def back_fc(i):
        at = rows_at(i, half)
        dbuf_f[at, :] = dot(gcs[at, 0:512], wfc[...], NN)

    loop(2, back_fc)
    bias_fb, gain_fb = slope_pass(sec_fb, stats_fb, dbuf_f)
    put(BACK + FB, 0, pair32(bias_fb, gain_fb))
    exchange_start(BACK + FB)
    slow_store.wait()

    def back_widen(part):
        lanes = slice(part * mid, (part + 1) * mid)
        total = exchange_end(BACK + SLOW_C + part)
        bias_sc, gain_sc = take(total, 0, mid), take(total, mid, mid)
        report(SLOW_C, bias_sc, gain_sc, part * (mid // LANES))
        scale = stats_sc[part][1]()
        lead = gains[SLOW_C](lanes) * scale
        tilt_sc = settle(lead * scale * gain_sc * (1.0 / slow_count))
        level_sc = settle(lead * bias_sc * (1.0 / slow_count))
        lead_sc = settle(lead)

        def low_sc(i):
            at = rows_at(i, 32)
            grad = big[at, lanes]
            cs[at, lanes] = (grad * lead_sc() - level_sc() - gsum[at, lanes].astype(F32) * tilt_sc()).astype(BF16)
            gsum[at, lanes] = grad.astype(BF16)

        loop(rows // 32, low_sc, unroll=7)

        def back_sc(i):
            at = rows_at(i, half)
            value = dot(cs[at, lanes], wsc[lanes, :], NN)
            dbuf[at, :] = dbuf[at, :] + value if part else value

        loop(2, back_sc)

    for part in range(2):
        back_widen(part)
    bias_sb, gain_sb = slope_pass(sec_sb, stats_sb, dbuf)

    put(BACK + SLOW_B, 0, bias_sb)
    put(BACK + SLOW_B, 256, gain_sb)
    exchange_start(BACK + SLOW_B)

    slab_sc[0:cs_n, :] = dot(cs[...], hbs[...], TN)
    advance(SC)
    widening = None
    for phase in range(4):
        term = dot(hbf[...], gcs[0:rows, 128 * phase : 128 * (phase + 1)], TN)[32 * phase : 32 * (phase + 1), :]
        widening = term if widening is None else widening + term
    slab[2, 704:736, 128:256] = widening
    slab[2, 736:768, 128:256] = jnp.zeros((32, LANES), F32)
    poll()

    bias_fb, gain_fb = unpair32(exchange_end(BACK + FB))
    report(FB, bias_fb, gain_fb)
    vec_fb = back_vectors(FB, stats_fb, bias_fb, gain_fb, fast_count)

    def norm_grad(buffer, section, at, vectors):
        lead, level, tilt = vectors
        return buffer[at, :] * lead() - level() - section[at, :] * tilt()

    def low_fb(i):
        spread_columns(gcf, i, norm_grad(dbuf_f, sec_fb, rows_at(i, band), vec_fb))

    loop(bands, low_fb, unroll=2)

    def back_fb(i):
        value = None
        for a in range(3):
            at = pl.ds(pl.multiple_of(i * half + band * (2 - a), 16), half)
            term = dot(gcf[at, :], wfbk[a], NN)
            value = term if value is None else value + term
        dbuf_f[rows_at(i, half), :] = value

    loop(2, back_fb)
    poll()
    bias_fa, gain_fa = slope_pass(sec_fa, stats_fa, dbuf_f)
    put(BACK + FA, 0, pair32(bias_fa, gain_fa))
    exchange_start(BACK + FA)
    poll()
    total = exchange_end(BACK + SLOW_B)

    bias_sb, gain_sb = take(total, 0, 256), take(total, 256, 256)
    report(SLOW_B, bias_sb, gain_sb)
    vec_sb = back_vectors(SLOW_B, stats_sb, bias_sb, gain_sb, slow_count)

    gcs[0:band, :] = jnp.zeros((band, gcs.shape[1]), BF16)

    def low_sb(i):
        spread_columns(gcs, i, norm_grad(dbuf, sec_sb, rows_at(i, band), vec_sb))

    loop(bands, low_sb, unroll=2)
    poll()

    def back_sb(i):
        value = None
        for a in range(3):
            at = pl.ds(pl.multiple_of(i * half + band * (2 - a), 16), half)
            for b in range(3):
                tap = 3 * a + b
                term = dot(gcs[at, bs * (2 - b) : bs * (3 - b)], wsb[bs * tap : bs * (tap + 1), :], NN)
                value = term if value is None else value + term
        dbuf[rows_at(i, half), :] = value

    for part in range(2):
        back_sb(part)
        poll()
    bias_sa, gain_sa = slope_pass(sec_sa, stats_sa, dbuf)

    put(BACK + SLOW_A, 0, bias_sa)
    put(BACK + SLOW_A, 256, gain_sa)
    exchange_start(BACK + SLOW_A)
    poll()

    for a in range(3):
        value = dot(gcs[band : band + rows, bs : 2 * bs], hcs[band * a : band * a + rows, :], TN)
        ref, lane = pieces[SB + a].ref, pieces[SB + a].lane
        for b in range(3):
            ref[bs * b : bs * (b + 1), lane : lane + bs] = value[:, bs * b : bs * (b + 1)]
        advance(SB + a)
        poll()
    for a in range(3):
        value = dot(gcf[band : band + rows, 128:256], hcf[band * a : band * a + rows, :], TN)
        for b in range(3):
            tap = 3 * a + b
            block = value[:, 128 * b : 128 * (b + 1)] * block_mask()
            folded = fold_lanes(block[0:32] + block[32:64] + block[64:96] + block[96:128])
            folded = jnp.where(lane_groups(32) == tap % 4, folded, 0.0)
            at = slice(608 + 32 * (tap // 4), 640 + 32 * (tap // 4))
            slab[2, at, 128:256] = folded if tap % 4 == 0 else slab[2, at, 128:256] + folded
    poll()
    bias_fa, gain_fa = unpair32(exchange_end(BACK + FA))
    report(FA, bias_fa, gain_fa)
    vec_fa = back_vectors(FA, stats_fa, bias_fa, gain_fa, fast_count)

    def low_fa(i):
        at = rows_at(i, band)
        hbf[at, :] = norm_grad(dbuf_f, sec_fa, at, vec_fa).astype(BF16)

    loop(bands, low_fa, unroll=2)
    value = dot(hbf[...], vx[:, 128:896], TN)
    for k in range(3):
        piece = None
        for phase in range(4):
            term = value[32 * phase : 32 * (phase + 1), 128 * (phase + k) : 128 * (phase + k + 1)]
            piece = term if piece is None else piece + term
        slab[2, 512 + 32 * k : 544 + 32 * k, 128:256] = piece
    poll()
    total = exchange_end(BACK + SLOW_A)
    poll()

    bias_sa, gain_sa = take(total, 0, 256), take(total, 256, 256)
    report(SLOW_A, bias_sa, gain_sa)
    vec_sa = back_vectors(SLOW_A, stats_sa, bias_sa, gain_sa, slow_count)
    def low_sa(i):
        at = rows_at(i, band)
        value = norm_grad(dbuf, sec_sa, at, vec_sa)
        gcs[at, 0:bs] = roll_frames(value, prev(256), -1, True).astype(BF16)
        gcs[at, bs : 2 * bs] = value.astype(BF16)
        gcs[at, 2 * bs :] = roll_frames(value, following(256), 1, True).astype(BF16)

    loop(bands, low_sa, unroll=2)
    poll()

    def narrow_gradient(k):
        ref, lane = pieces[SA + k].ref, pieces[SA + k].lane
        source = xs[:, 256 * k : 256 * (k + 1)] if k < 4 else jl[...]
        ref[0 : 3 * bs, lane : lane + 256] = dot(gcs[0:rows, :], source, TN)
        advance(SA + k)

    narrow_gradient(0)
    poll()

    def back_lateral(i):
        at = rows_at(i, half)
        dbuf[at, :] = dot(gcs[at, :], wsa[:, cs_n:], NN)

    loop(2, back_lateral)
    poll()
    bias_lat, gain_lat = slope_pass(sec_lat, stats_lat, dbuf)
    put(BACK + LAT, 0, bias_lat)
    put(BACK + LAT, 256, gain_lat)
    exchange_start(BACK + LAT)

    poll()

    for k in range(1, 4):
        narrow_gradient(k)
        poll()
    total = exchange_end(BACK + LAT)

    bias_lat, gain_lat = take(total, 0, 256), take(total, 256, 256)
    report(LAT, bias_lat, gain_lat)

    def pack(rows_ref, target):
        lanes = lax.broadcasted_iota(jnp.int32, (24, LANES), 1)
        stacked = rows_ref[...]
        turned = pltpu.roll(stacked, 64, 1)
        moved = jnp.where(lanes >= 64, turned, pltpu.roll(turned, 1, 0))[0:16, :]
        first = jnp.where(lane16[0:1, :] < 32, stacked[16:17, :], stacked[17:18, :])
        first = jnp.where(lane16[0:1, :] < 64, first, moved[0:1, :])
        target[...] = moved * factor
        target[0:1, :] = first * factor

    pack(gain_rows, dbuf_f.at[pl.ds(0, 16)])
    pack(bias_rows, dbuf_f.at[pl.ds(16, 16)])
    parameter_stores = [
        store(dbuf_f.at[pl.ds(0, 16)], dgains_h, 19), store(dbuf_f.at[pl.ds(16, 16)], dbiases_h, 20)
    ]
    vec_lat = back_vectors(LAT, stats_lat, bias_lat, gain_lat, slow_count)

    def low_lat(i):
        at = rows_at(i, band)
        hbs[at, :] = norm_grad(dbuf, sec_lat, at, vec_lat).astype(BF16)

    loop(bands, low_lat, unroll=2)
    value = dot(hbs[...], vx[:, 0:640], TN)
    for k in range(5):
        at, lane = 256 * (k % 3), 128 * (k // 3)
        slab[2, at : at + 256, lane : lane + 128] = value[:, 128 * k : 128 * (k + 1)]
    advance(LT)
    poll()
    narrow_gradient(4)
    poll()

    def slow_back(i):
        at = rows_at(i, half)
        for tile in range(cs_n // 256):
            lanes = slice(256 * tile, 256 * (tile + 1))
            value = gsum[at, lanes].astype(F32) + dot(gcs[at, :], wsa[:, lanes], NN)
            gsum[at, lanes] = value.astype(BF16)

    for part in range(2):
        slow_back(part)
        poll()


    def fast_back(i):
        at, fat = rows_at(i, 2 * band), rows_at(i, 2 * fband)
        conv = dot(hbf[at, :], wfa[...], NN)
        side_in = dot(hbs[at, :], wlat[...], NN)

        def lane(values, block):
            return values[:, 128 * block : 128 * (block + 1)]

        grads = [gsf[at, 128 * phase : 128 * (phase + 1)] + lane(conv, phase + 1) for phase in range(4)]
        grads[0] = grads[0] + roll_frames(lane(conv, 5), following(128), 1, True) + lane(side_in, 2)
        grads[1] = grads[1] + lane(side_in, 3)
        grads[2] = grads[2] + lane(side_in, 4) + roll_frames(lane(side_in, 0), prev(128), -1, True)
        grads[3] = grads[3] + roll_frames(lane(side_in, 1) + lane(conv, 0), prev(128), -1, True)
        for part in range(2):
            for phase in range(4):
                stage_a[pl.ds(phase, band, stride=4), :] = grads[phase][part * band : (part + 1) * band]
            xf[rows_at(2 * i + part, fband), :] = stage_a[...].astype(BF16)

    third = bands // 6
    loop(third, fast_back)
    poll()
    loop(third, lambda i: fast_back(i + third))
    poll()
    loop(bands // 2 - 2 * third, lambda i: fast_back(i + 2 * third))
    poll()

    poll()
    while not all(done(name) for name in order):
        for name in order:
            if not done(name):
                advance(name)
    for copy in stores + parameter_stores:
        copy.wait()


def hand_on(*refs):
    sources, targets, staged, small, sem = refs[0:11], refs[11:24], refs[24:30], refs[30:35], refs[35]
    held = staged[0:1] + sources[1:6] + staged[1:6]
    loads = {k: pltpu.make_async_copy(sources[k], held[k], sem.at[k]) for k in (8, 9, 10, 0, 6, 7)}
    stores = {k: pltpu.make_async_copy(held[k], targets[k], sem.at[11 + k]) for k in (0, 1, 2, 3, 5, 6, 7)}
    for k in range(5):
        stores[8 + k] = pltpu.make_async_copy(small[k], targets[8 + k], sem.at[19 + k])
        stores[13 + k] = pltpu.make_async_copy(
            held[4].at[pl.ds(768 * k, 768)], targets[4].at[:, pl.ds(256 * k, 256)], sem.at[24 + k]
        )
    for copy in loads.values():
        copy.start()
    for k in (1, 2, 3, 5, 13, 14, 15, 16, 17):
        stores[k].start()
    for k in (8, 9, 10):
        loads[k].wait()
    small[0][...] = held[8][0:96, :]
    for tap in range(9):
        at = 96 + 32 * (tap // 4)
        small[1][32 * tap : 32 * (tap + 1), :] = held[8][at : at + 32, 32 * (tap % 4) : 32 * (tap % 4 + 1)]
    small[2][...] = held[8][192:224, :]
    for source, target in ((held[9], small[3]), (held[10], small[4])):
        count = target.shape[0]
        for row in range(16):
            width = min(LANES, count - row * LANES)
            target[pl.ds(row * LANES, width)] = source[row : row + 1, 0:width].reshape(width)
    for k in range(8, 13):
        stores[k].start()
    for k in (0, 6, 7):
        loads[k].wait()
        stores[k].start()
    for copy in stores.values():
        copy.wait()


def body(
    slow_input,
    fast_input,
    clip_ids,
    fast_narrow,
    fast_spatial,
    fast_widen,
    lateral_conv,
    slow_narrow,
    slow_spatial,
    slow_widen,
    norm_gains,
    norm_biases,
    slow_cotangent,
    fast_cotangent,
):
    n_dp, n_rep = lax.axis_size("dp"), lax.axis_size("rep")
    low = 2 if n_dp % 2 == 0 else 1
    high = n_dp // low
    frames, plane, channels = slow_input.shape
    fast_frames, _, fast_channels = fast_input.shape
    side = math.isqrt(plane)
    rows = frames * plane
    slow_count = rows * n_dp * n_rep
    fast_count = slow_count * (fast_frames // frames)

    def flat(values):
        return values.transpose(1, 0, 2).reshape(values.shape[0] * values.shape[1], values.shape[2])

    def unflat(values, count):
        return values.reshape(plane, count, values.shape[1]).transpose(1, 0, 2)

    widths = [
        fast_narrow.shape[1], fast_spatial.shape[1], fast_widen.shape[0], lateral_conv.shape[1],
        slow_narrow.shape[1], slow_spatial.shape[1], slow_widen.shape[0],
    ]

    cf = fast_channels
    bs = slow_spatial.shape[1]
    band = side * frames
    any_spec = pl.BlockSpec(memory_space=pl.ANY)
    vmem_spec = pl.BlockSpec(memory_space=pltpu.VMEM)
    near_low = n_dp if n_dp * n_rep <= 32 else low
    stages = 1 if near_low == n_dp else 2
    pad = rows + 2 * band

    def shape(dims, dtype):
        return jax.ShapeDtypeStruct(dims, dtype)

    out_shape = [
        shape((rows, channels), BF16), pltpu.VMEM((4 * rows, cf), BF16),
        pltpu.VMEM((rows, channels), BF16), pltpu.VMEM((4 * rows, cf), BF16),
        pltpu.VMEM((15 * bs, bs), F32), pltpu.VMEM((9 * bs, bs), F32), shape((channels, bs), F32),
        shape((5 * bs, cf), F32), shape((256, cf), F32), shape((16, LANES), F32), shape((16, LANES), F32),
        shape((10, max(high // 4, 1), 32, 256), F32),
    ]
    scratch = [
        pltpu.VMEM((rows, channels), BF16), pltpu.VMEM((rows, channels), BF16),
        pltpu.VMEM((rows, channels), F32),
        pltpu.VMEM((rows, 512), F32), pltpu.VMEM((rows, 512), F32),
        pltpu.VMEM((pad, 3 * bs), BF16), pltpu.VMEM((pad, 3 * bs), BF16),
        pltpu.VMEM((pad, 384), BF16), pltpu.VMEM((pad, 384), BF16),
        pltpu.VMEM((rows, bs), F32), pltpu.VMEM((rows, bs), F32),
        pltpu.VMEM((rows, 128), F32), pltpu.VMEM((rows, 128), F32), pltpu.VMEM((rows, 128), F32),
        pltpu.VMEM((rows, bs), BF16), pltpu.VMEM((rows, bs), BF16), pltpu.VMEM((rows, 128), BF16),
        pltpu.VMEM((rows, 896), BF16), pltpu.VMEM((3, 1512, 256), F32), pltpu.VMEM((2016, 256), F32),
        pltpu.VMEM((768, 256), F32),
        pltpu.VMEM((3 * bs, channels + bs), BF16), pltpu.VMEM((9 * bs, bs), BF16),
        pltpu.VMEM((channels, bs), BF16), pltpu.VMEM(norm_gains.shape, F32), pltpu.VMEM(norm_gains.shape, F32),
        pltpu.VMEM((9, 8, channels), F32), pltpu.VMEM((2, 8, 256), F32),
        pltpu.VMEM((96, cf), BF16), pltpu.VMEM((288, 32), BF16), pltpu.VMEM((32, cf), BF16),
        pltpu.VMEM((bs, 640), BF16), pltpu.VMEM((128, 768), BF16),
        pltpu.VMEM((3, 128, 384), BF16), pltpu.VMEM((3, 384, 128), BF16), pltpu.VMEM((512, 128), BF16),
        pltpu.VMEM((4 * band, cf), F32),
        pltpu.VMEM((24, LANES), F32), pltpu.VMEM((24, LANES), F32),
        pltpu.VMEM((near_low * n_rep, 1, sum(TURNS.values())), F32),
        pltpu.VMEM((max(n_dp // near_low, 1), 1, sum(TURNS.values())), F32),
        pltpu.SemaphoreType.DMA((stages, len(TURNS))), pltpu.SemaphoreType.DMA((stages, len(TURNS))),
        pltpu.SemaphoreType.DMA((32,)), pltpu.SemaphoreType.DMA((10, 2)),
        pltpu.SemaphoreType.DMA((10,)), pltpu.SemaphoreType.DMA((10, 10 if high == 4 else 11)),
    ]
    factor = 1.0 / math.sqrt(float(slow_count))
    results = pl.pallas_call(
        functools.partial(kernel, (n_dp, n_rep, low, frames, side, float(slow_count), float(fast_count), factor)),
        out_shape=out_shape,
        in_specs=[any_spec] * 4 + [pl.BlockSpec(memory_space=pltpu.SMEM)] + [any_spec] * 9,
        out_specs=[any_spec] + [vmem_spec] * 5 + [any_spec] * 6,
        scratch_shapes=scratch,
        compiler_params=pltpu.CompilerParams(
            collective_id=0, has_side_effects=True, vmem_limit_bytes=52960 * 2**10
        ),
    )(
        flat(slow_input), flat(fast_input), flat(slow_cotangent), flat(fast_cotangent), clip_ids,
        fast_narrow.reshape(-1, cf), fast_spatial.reshape(-1, 32), fast_widen.T,
        lateral_conv.reshape(-1, cf), slow_narrow.reshape(3 * bs, -1), slow_spatial.reshape(9 * bs, bs),
        slow_widen, norm_gains, norm_biases,
    )
    final = [shape((rows, channels), BF16), shape((4 * rows, cf), BF16)] * 2 + [
        shape((3 * bs, channels + bs), F32), shape((9 * bs, bs), F32), *out_shape[6:8],
        shape((96, cf), F32), shape((288, 32), F32), shape((32, cf), F32),
        shape(norm_gains.shape, F32), shape(norm_gains.shape, F32),
    ]
    handed = pl.pallas_call(
        hand_on,
        out_shape=final,
        in_specs=[any_spec] + [vmem_spec] * 5 + [any_spec] * 5,
        out_specs=[any_spec] * 13,
        scratch_shapes=[pltpu.VMEM(item.shape, item.dtype) for item in out_shape[0:1] + out_shape[6:11] + final[8:13]]
        + [pltpu.SemaphoreType.DMA((29,))],
        compiler_params=pltpu.CompilerParams(vmem_limit_bytes=52960 * 2**10),
    )(results[0], *[pltpu.with_memory_space_constraint(r, pltpu.VMEM) for r in results[1:6]], *results[6:11])
    slow_out, fast_out, slow_grad, fast_grad, dsa, dsb, dsc, dl, dfa, dfb, dfc, dgains, dbiases = handed

    return (
        unflat(slow_out, frames),
        unflat(fast_out, fast_frames),
        unflat(slow_grad, frames),
        unflat(fast_grad, fast_frames),
        dfa.reshape(fast_narrow.shape),
        dfb.reshape(fast_spatial.shape),
        dfc.T,
        dl.reshape(lateral_conv.shape),
        dsa.reshape(slow_narrow.shape),
        dsb.reshape(slow_spatial.shape),
        dsc,
        dgains,
        dbiases,
    )


def solution(mesh):
    sharded = P(("dp", "rep"), None, None)
    return jax.shard_map(
        body,
        mesh=mesh,
        in_specs=(sharded, sharded, P(("dp", "rep"), None)) + (P(),) * 9 + (sharded, sharded),
        out_specs=(sharded,) * 4 + (P(),) * 9,
        check_vma=False,
    )
```

```python
import functools
import math

import jax
import jax.numpy as jnp
from jax import lax
from jax.experimental import pallas as pl
from jax.experimental.pallas import tpu as pltpu
from jax.sharding import PartitionSpec as P

EPS = 1e-05
F32 = jnp.float32
BF16 = jnp.bfloat16
MESH = pl.DeviceIdType.MESH
NN = ((1,), (0,))
NT = ((1,), (1,))
TN = ((0,), (0,))
LANES = 128
FA, FB, FC, LAT, SLOW_A, SLOW_B, SLOW_C = range(7)
FORWARD = {LAT: 512, FA: 128, SLOW_A: 512, FB: 128, SLOW_B: 512, FC: 256, SLOW_C: 768, SLOW_C + 1: 512}
BACKWARD = {SLOW_C: 1024, SLOW_C + 1: 1024, FC: 256, SLOW_B: 512, FB: 128, SLOW_A: 512, FA: 128, LAT: 512}
BACK = 8
TURNS = {**FORWARD, **{BACK + norm: lanes for norm, lanes in BACKWARD.items()}}


class Piece:
    pass


SC, SB, SA, LT = 0, 1, 4, 9
C, X, Y, Z, Z0, Z1 = range(6)
PLANE = ((C, X, Y, Z), (C, Y, X, Z))
HALVES = ((C, X, Y, Z0, Z1), (C, Y, X, Z0, Z1))
BETWEEN = ((C, X, Z0, Z1, Y), (C, Y, Z0, Z1, X))
LINE = ((C, Z0, Z1, X, Y), (C, Z0, Z1, Y, X))
ORDER_OF = (PLANE, HALVES, LINE, PLANE, BETWEEN, PLANE, HALVES, HALVES, PLANE, PLANE)
POLLS = (
    (),
    (0,),
    (),
    (),
    (),
    (),
    (),
    (0,),
    (),
    (1,),
    (2,),
    (0, 3),
    (),
    (),
    (),
    (1,),
    (4,),
    (3, 2),
    (1, 5),
    (4, 0, 6),
    (3, 7, 1),
    (5, 2, 9),
    (6, 4, 8),
    (7, 0),
    (5, 3, 2),
    (1,),
    (9,),
    (
        6, 5, 4, 7, 6, 3, 8, 1, 9, 5, 4, 7, 6, 2, 1, 3, 9, 5, 8, 7, 4, 6, 2, 1,
        3, 9, 5, 0, 8, 7, 6, 4, 1, 2, 9, 3, 5, 8, 0, 7, 6, 4, 1, 9, 2, 8, 0, 7,
        6, 4, 2, 9, 8, 4, 7, 6, 2, 8, 7,
    ),
)


def dot(left, right, dims):
    return lax.dot_general(left, right, (dims, ((), ())), preferred_element_type=F32)


def column_sums(values):
    return jnp.sum(values.reshape(values.shape[0] // 8, 8, values.shape[1]), axis=0)


def squash(partial):
    return jnp.sum(partial, axis=0, keepdims=True)


def fold_lanes(values):
    half = values + pltpu.roll(values, 64, 1)
    return half + pltpu.roll(half, 32, 1)


def loop(count, body, init=None, unroll=1):
    if init is None:

        def plain(index, carry):
            body(index)
            return carry

        lax.fori_loop(0, count, plain, 0, unroll=unroll)
        return None
    return lax.fori_loop(0, count, body, init, unroll=unroll)


def rows_at(index, size):
    return pl.ds(pl.multiple_of(index * size, 16), size)


def kernel(
    dims,
    xs_h, xf_h, cs_h, cf_h, clip, wfa_h, wfb_h, wfc_h, wl_h, wsa_h, wsb_h, wsc_h, gains_h, biases_h,
    slow_h, cf, gsum, xf, dsa, dsb, dsc_h, dl_h, small_h, dgains_h, dbiases_h, extra_h,
    xs, cs, big, sec_fc, gsf, hcs, gcs, hcf, gcf,
    sec_lat, dbuf, sec_fa, sec_fb, dbuf_f, jl, hbs, hbf, vx, slab, slab_sc, summed,
    wsa, wsb, wsc, gains_in, biases_in, vectors, masks, wfa_in, wfb_in, wfc_in, wlat, wfa, wfb, wfbk, wfc,
    stage_a, gain_rows, bias_rows, near, far, sum_send, sum_recv, io_sem, own_sem, big_send, big_recv,
):
    n_dp, n_rep, low, frames, side, slow_count, fast_count, factor = dims
    sec_sa, sec_sb = dsa, dsb
    rows = xs.shape[0]
    half = rows // 2
    band = side * frames
    bands = side
    fband = 4 * band
    cs_n = xs.shape[1]
    bs = wsb.shape[1]

    dp_i, rep_i = lax.axis_index("dp"), lax.axis_index("rep")
    dp_lo, dp_hi = lax.rem(dp_i, low), lax.div(dp_i, low)
    high = n_dp // low
    direct = n_dp * n_rep <= 32
    near_low = n_dp if direct else low
    near_dp, far_dp = lax.rem(dp_i, near_low), lax.div(dp_i, near_low)
    near_peers = [
        (far_dp * near_low + lax.rem(near_dp + a, near_low), lax.rem(rep_i + b, n_rep))
        for a in range(near_low)
        for b in range(n_rep)
        if a or b
    ]
    far_count = n_dp // near_low
    far_peers = [(lax.rem(far_dp + a, far_count) * near_low + near_dp, rep_i) for a in range(1, far_count)]
    stages = [(near, near_dp * n_rep + rep_i, near_peers)]
    if far_peers:
        stages.append((far, far_dp, far_peers))

    c, x = lax.rem(rep_i, 2), lax.div(rep_i, 2)
    y, z = dp_lo, lax.rem(dp_hi, 4)
    outer, outers = lax.div(dp_hi, 4), high // 4
    core_peer = (dp_i, 2 * x + 1 - c)
    x_peer = (dp_i, 2 * (1 - x) + c)
    y_peer = (dp_hi * low + 1 - y, rep_i)
    def z_peer(flip):
        return ((outer * 4 + z + flip - 2 * flip * lax.rem(lax.div(z, flip), 2)) * low + y, rep_i)

    z_peers = [((outer * 4 + lax.rem(z + k, 4)) * low + y, rep_i) for k in range(1, 4)]
    outer_peers = [((lax.rem(outer + k, outers) * 4 + z) * low + y, rep_i) for k in range(1, outers)]

    barrier = pltpu.get_barrier_semaphore()
    greeted = near_peers + far_peers
    for peer in greeted:
        pl.semaphore_signal(barrier, inc=1, device_id=peer, device_id_type=MESH)

    loads = {}
    for slot, (name, src, dst) in enumerate([
        ("xf", xf_h, xf), ("wfa", wfa_h, wfa_in), ("xs", xs_h, xs),
        ("wsa", wsa_h, wsa), ("wfb", wfb_h, wfb_in), ("wfc", wfc_h, wfc_in), ("wsb", wsb_h, wsb),
        ("wsc", wsc_h, wsc), ("cf", cf_h, cf), ("cs", cs_h, cs), ("gains", gains_h, gains_in), ("biases", biases_h, biases_in),
    ]):
        loads[name] = pltpu.make_async_copy(src, dst, io_sem.at[slot])
        loads[name].start()
        if name == "wfa":
            taps = [
                pltpu.make_async_copy(
                    wl_h.at[pl.ds(bs * k, bs)], wlat.at[:, pl.ds(LANES * k, LANES)], io_sem.at[27 + k]
                )
                for k in range(5)
            ]
            for tap in taps:
                tap.start()
    stores = []

    def store(src, dst, slot):
        copy = pltpu.make_async_copy(src, dst, io_sem.at[slot])
        copy.start()
        return copy

    turn_at, turn_index = {}, {}
    for index, (turn, width) in enumerate(TURNS.items()):
        turn_at[turn] = sum(list(TURNS.values())[:index])
        turn_index[turn] = index

    def put(turn, at, vector):
        near[stages[0][1], :, pl.ds(turn_at[turn] + at, vector.shape[1])] = vector

    def sum_copy(turn, stage, first, count, peer):
        buffer = stages[stage][0]
        block = buffer.at[pl.ds(first, count), :, pl.ds(turn_at[turn], TURNS[turn])]
        return pltpu.make_async_remote_copy(
            src_ref=block, dst_ref=block, send_sem=sum_send.at[stage, turn_index[turn]],
            recv_sem=sum_recv.at[stage, turn_index[turn]], device_id=peer, device_id_type=MESH,
        )

    def exchange_start(turn):
        for peer in near_peers:
            sum_copy(turn, 0, stages[0][1], 1, peer).start()

    def exchange_end(turn):
        lanes = pl.ds(turn_at[turn], TURNS[turn])
        for stage, (buffer, rank, peers) in enumerate(stages):
            if stage:
                buffer[rank, :, lanes] = total
                for peer in peers:
                    sum_copy(turn, stage, rank, 1, peer).start()
            copy = sum_copy(turn, stage, 0, len(peers), peers[0])
            copy.wait_recv()
            total = jnp.sum(buffer[:, :, lanes], axis=0)
            copy.wait_send()
        return total

    def take(total, at, width):
        return total[:, at : at + width]

    def pair32(first, second):
        group = lax.broadcasted_iota(jnp.int32, (8, LANES), 1) // 32
        rows8 = (8, LANES)
        first = fold_lanes(jnp.broadcast_to(first, rows8))
        second = fold_lanes(jnp.broadcast_to(second, rows8))
        return jnp.where(group == 0, first, jnp.where(group == 1, second, 0.0))[0:1, :]

    def unpair32(total):
        group = lax.broadcasted_iota(jnp.int32, (8, LANES), 1) // 32
        total = jnp.broadcast_to(total, (8, LANES))
        first = fold_lanes(jnp.where(group == 0, total, 0.0))
        second = fold_lanes(jnp.where(group == 1, total, 0.0))
        return first[0:1, :], second[0:1, :]

    pieces = {}

    bits = {C: (c, core_peer), X: (x, x_peer), Y: (y, y_peer),
            Z0: (lax.rem(z, 2), z_peer(1)), Z1: (lax.div(z, 2), z_peer(2))}

    def add_piece(name, ref, lane, size, index):
        axes = ORDER_OF[name]
        piece = Piece()
        piece.name, piece.ref, piece.lane, piece.size, piece.index = name, ref, lane, size, index
        piece.step, piece.axes, piece.steps = 0, axes, len(axes[0])
        starts, counts, arriving = [[0], [0]], [size], [size]
        for step, pair in enumerate(zip(*axes)):
            for side, axis in enumerate(pair):
                if axis == Z:
                    starts[side].append(starts[side][-1] + z * (counts[-1] // 4))
                else:
                    starts[side].append(starts[side][-1] + bits[axis][0] * (counts[-1] // 2))
            counts.append(counts[-1] // (4 if pair[0] == Z else 2))
            arriving.append(arriving[-1] + (3 if pair[0] == Z else 1) * counts[-1])
        piece.starts, piece.counts, piece.arriving = starts, counts, arriving
        pieces[name] = piece

    for k in range(2):
        add_piece(SB + k, sec_fc, 256 * k, 768, k)
    for k in range(4):
        add_piece(SA + k, big, 256 * k, 768, 2 + k)
    add_piece(SB + 2, slab.at[0], 0, 768, 6)
    add_piece(SA + 4, slab.at[1], 0, 768, 7)
    add_piece(LT, slab.at[2], 0, 768, 8)
    add_piece(SC, slab_sc, 0, 1024, 9)

    def span(piece, start, count, lane=0, width=256):
        return piece.ref.at[pl.ds(pl.multiple_of(start, 8), count), pl.ds(piece.lane + lane, width)]

    def send(piece, step, src, dst, peer):
        pltpu.make_async_remote_copy(
            src_ref=src, dst_ref=dst, send_sem=big_send.at[piece.index],
            recv_sem=big_recv.at[piece.index, step], device_id=peer, device_id_type=MESH,
        ).start()

    def result(piece, start, count, lane=0, width=256):
        name = piece.name
        start = pl.multiple_of(start, 8)
        if name == LT:
            return summed.at[pl.ds(start, count), pl.ds(lane, width)]
        if name == SC:
            return dsc_h.at[pl.ds(start, count), pl.ds(lane, width)]
        if name >= SA:
            return dsa.at[pl.ds(768 * (name - SA) + start, count), pl.ds(lane, width)]
        return dsb.at[pl.ds(768 * (name - SB) + start, count), pl.ds(lane, width)]

    def own_copies(piece):
        count, sem = piece.counts[-1], own_sem.at[piece.index]
        return [
            pltpu.make_async_copy(
                span(piece, start[-1], count, 128 * side, 128),
                result(piece, start[-1], count, 128 * side, 128),
                sem.at[side],
            )
            for side, start in enumerate(piece.starts)
        ]

    def arrived(piece, step, rows_in):
        block = span(piece, 0, rows_in) if step < piece.steps else result(piece, 0, rows_in)
        copy = pltpu.make_async_remote_copy(
            src_ref=block, dst_ref=block, send_sem=big_send.at[piece.index],
            recv_sem=big_recv.at[piece.index, step], device_id=core_peer, device_id_type=MESH,
        )
        copy.wait_recv()
        copy.wait_send()

    def add_rows(piece, target, source, count, lane, width):
        lanes = pl.ds(piece.lane + lane, width)
        chunk = piece.size // 32
        ref = piece.ref

        def step(i):
            into = pl.ds(pl.multiple_of(target + i * chunk, 8), chunk)
            ref[into, lanes] = ref[into, lanes] + ref[pl.ds(pl.multiple_of(source + i * chunk, 8), chunk), lanes]

        loop(count // chunk, step)

    order = range(10)

    def unpack_small():
        stores.append(store(summed.at[:, pl.ds(0, 128)], dl_h.at[pl.ds(0, 768)], 16))
        stores.append(store(summed.at[pl.ds(0, 512), pl.ds(128, 128)], dl_h.at[pl.ds(768, 512)], 17))
        stores.append(store(summed.at[pl.ds(512, 256), pl.ds(128, 128)], small_h, 18))

    polled = [0]

    def poll():
        polled[0] += 1
        for name in POLLS[polled[0] - 1]:
            advance(name)

    def done(name):
        return pieces[name].step > 2 * pieces[name].steps

    def advance(name):
        piece = pieces[name]
        step, steps, index = piece.step, piece.steps, piece.index
        piece.step = step + 1
        starts, counts, arriving, axes = piece.starts, piece.counts, piece.arriving, piece.axes
        ref, lane = piece.ref, piece.lane

        def received(last):
            fan = 3 if axes[0][last] == Z else 1
            return fan * counts[last + 1]

        if 0 < step < steps or (step == steps and axes[0][-1] != Z):
            arrived(piece, step - 1, received(step - 1))
            if step == 1:
                add_rows(piece, starts[0][1], arriving[0], counts[1], 0, 256)
            else:
                for side in range(2):
                    add_rows(piece, starts[side][step], arriving[step - 1], counts[step], 128 * side, 128)
        elif step == steps:
            arrived(piece, step - 1, received(step - 1))
        elif step > steps:
            arrived(piece, step - 1, received(2 * steps - step))

        if step < steps:
            held, keep = counts[step], counts[step + 1]
            if step == 0:
                at = starts[0][0] + (1 - c) * keep
                send(piece, 0, span(piece, at, keep), span(piece, arriving[0], keep), core_peer)
                return
            for side in range(2):
                axis, start = axes[side][step], starts[side][step]
                if axis == Z:
                    for k, peer in enumerate(z_peers):
                        at, into = start + lax.rem(z + k + 1, 4) * keep, arriving[step] + k * keep
                        send(
                            piece, step, span(piece, at, keep, 128 * side, 128),
                            span(piece, into, keep, 128 * side, 128), peer,
                        )
                else:
                    bit, peer = bits[axis]
                    at = start + (1 - bit) * keep
                    send(
                        piece, step, span(piece, at, keep, 128 * side, 128),
                        span(piece, arriving[step], keep, 128 * side, 128), peer,
                    )
        elif step == steps:
            last = counts[-1]
            own = [
                (pl.ds(pl.multiple_of(starts[side][-1], 8), last), pl.ds(lane + 128 * side, 128))
                for side in range(2)
            ]
            both = jnp.concatenate([ref[own[0]], ref[own[1]]], axis=1)
            if axes[0][-1] == Z:
                for k in range(3):
                    both = both + ref[pl.ds(arriving[steps - 1] + k * last, last), pl.ds(lane, 256)]
            if outers > 1:
                held = span(piece, arriving[steps - 1], last)
                ref[pl.ds(arriving[steps - 1], last), pl.ds(lane, 256)] = both
                for peer in outer_peers:
                    send(piece, 10, held, extra_h.at[index, outer, pl.ds(0, last)], peer)
                block = extra_h.at[index, pl.ds(0, outers - 1), pl.ds(0, last)]
                copy = pltpu.make_async_remote_copy(
                    src_ref=block, dst_ref=block, send_sem=big_send.at[index], recv_sem=big_recv.at[index, 10],
                    device_id=core_peer, device_id_type=MESH,
                )
                copy.wait_recv()
                copy.wait_send()
                local = [(held, extra_h.at[index, outer, pl.ds(0, last)])]
                for k in range(outers):
                    local.append((extra_h.at[index, k, pl.ds(0, last)], span(piece, arriving[0] + k * last, last)))
                for src, dst in local:
                    copy = pltpu.make_async_copy(src, dst, own_sem.at[index, 0])
                    copy.start()
                    copy.wait()
                both = ref[pl.ds(arriving[0], last), pl.ds(lane, 256)]
                for k in range(1, outers):
                    both = both + ref[pl.ds(arriving[0] + k * last, last), pl.ds(lane, 256)]
            both = both * factor
            for side in range(2):
                ref[own[side]] = both[:, 128 * side : 128 * (side + 1)]
        if steps <= step < 2 * steps:
            back = 2 * steps - 1 - step
            count = counts[back + 1]
            if step == steps + 1:
                for copy in own_copies(piece):
                    copy.wait()
            if back == 0:
                block = result(piece, starts[0][1], count)
                send(piece, step, block, block, core_peer)
                return
            for side in range(2):
                axis, start = axes[side][back], starts[side][back + 1]
                block = result(piece, start, count, 128 * side, 128)
                source = span(piece, start, count, 128 * side, 128) if step == steps else block
                for peer in z_peers if axis == Z else [bits[axis][1]]:
                    send(piece, step, source, block, peer)
            if step == steps:
                for copy in own_copies(piece):
                    copy.start()
        elif step == 2 * steps and name == LT:
            unpack_small()

    spots = {FC: 0, LAT: 1, SLOW_A: 3, SLOW_B: 5, SLOW_C: 7, FA: 16, FB: 17}

    lane16 = lax.broadcasted_iota(jnp.int32, (16, LANES), 1)

    def unpack(packed):
        fa = fold_lanes(jnp.where(lane16 // 32 == 0, packed, 0.0))[0:1, :]
        fb = fold_lanes(jnp.where(lane16 // 32 == 1, packed, 0.0))[0:1, :]
        turned = pltpu.roll(packed, 64, 1)
        moved = jnp.where(lane16 < 64, turned, pltpu.roll(turned, 15, 0))
        found = {FA: fa, FB: fb}
        at = 0
        for name, count in ((FC, 1), (LAT, 2), (SLOW_A, 2), (SLOW_B, 2), (SLOW_C, 8)):
            found[name] = jnp.concatenate([moved[at + k : at + k + 1, :] for k in range(count)], axis=1)
            at += count
        return found

    held = [0]

    def settle(vector):
        at, width = held[0], vector.shape[1]
        held[0] += 1
        line, row = at // 8, slice(at % 8, at % 8 + 1)
        vectors[line, row, 0:width] = vector

        def read(lanes=slice(0, width)):
            return vectors[line, row, lanes]

        return read

    gains, biases = {}, {}

    def read_parameters():
        for name, flat_in, target in (("gains", gains_in, gains), ("biases", biases_in, biases)):
            loads[name].wait()
            count = flat_in.shape[0]
            stage_a[0:16, :] = jnp.zeros((16, LANES), F32)
            for row in range(16):
                width = min(LANES, count - row * LANES)
                stage_a[row : row + 1, 0:width] = flat_in[pl.ds(row * LANES, width)].reshape(1, width)
            for key, vector in unpack(stage_a[0:16, :]).items():
                target[key] = settle(vector)

    def gain(name):
        return gains[name]()

    def bias(name):
        return biases[name]()

    def moments(name, total, squares, count, *lanes):
        mean = total * (1.0 / count)
        scale = lax.rsqrt(squares * (1.0 / count) - mean * mean + EPS)
        return settle(mean), settle(scale), settle(0.5 * gains[name](*lanes) * scale), settle(0.5 * biases[name](*lanes))

    def back_vectors(name, stats, bias_total, gain_total, count):
        mean, scale = stats[0](), stats[1]()
        lead = gain(name) * scale
        tilt = lead * scale * gain_total * (1.0 / count)
        level = lead * bias_total * (1.0 / count) - mean * tilt
        return settle(lead), settle(level), settle(tilt)

    def report(name, bias_total, gain_total, skip=0):
        at = spots[name] + skip
        for piece in range(bias_total.shape[1] // LANES):
            lanes = slice(piece * LANES, (piece + 1) * LANES)
            gain_rows[at + piece : at + piece + 1, :] = gain_total[:, lanes]
            bias_rows[at + piece : at + piece + 1, :] = bias_total[:, lanes]

    def silu_of(values, stats):
        h = (values - stats[0]()) * stats[2]() + stats[3]()
        return h + h * jnp.tanh(h)

    def slope_of(h):
        t = jnp.tanh(h)
        out, gate = h + h * t, 0.5 + 0.5 * t
        return out, gate + out * (1.0 - gate)

    def clip_masks(width):
        frame = lax.broadcasted_iota(jnp.int32, (1, 8, width), 1)
        with_prev = jnp.zeros((1, 8, width), F32)
        with_next = jnp.zeros((1, 8, width), F32)
        for t in range(1, frames):
            same = jnp.where(clip[0, t] == clip[0, t - 1], 1.0, 0.0)
            with_prev = jnp.where(frame == t, same, with_prev)
            with_next = jnp.where(frame == t - 1, same, with_next)
        return with_prev, with_next

    masks[0:1], masks[1:2] = clip_masks(256)

    def prev(width):
        return masks[0:1, :, 0:width]

    def following(width):
        return masks[1:2, :, 0:width]

    def roll_frames(values, mask, step, mask_first):
        grouped = values.reshape(values.shape[0] // 8, 8, values.shape[1])
        if mask_first:
            grouped = grouped * mask
        grouped = pltpu.roll(grouped, step % 8, 1)
        if not mask_first:
            grouped = grouped * mask
        return grouped.reshape(values.shape)

    def spread_columns(target, index, values):
        width = values.shape[1]
        nothing = jnp.zeros((frames, width), F32)
        at = pl.ds(pl.multiple_of((index + 1) * band, 16), band)
        target[at, 0:width] = jnp.concatenate([nothing, values[: band - frames]], axis=0).astype(BF16)
        target[at, width : 2 * width] = values.astype(BF16)
        target[at, 2 * width :] = jnp.concatenate([values[frames:], nothing], axis=0).astype(BF16)

    gain_rows[...] = jnp.zeros(gain_rows.shape, F32)
    bias_rows[...] = jnp.zeros(bias_rows.shape, F32)
    for target in (hcs, gcs, hcf, gcf):
        edge = jnp.zeros((band, target.shape[1]), BF16)
        target[0:band, :] = edge
        target[band + rows : rows + 2 * band, :] = edge

    def lane_groups(count=LANES):
        return lax.broadcasted_iota(jnp.int32, (count, LANES), 1) // 32

    def block_mask():
        row_group = lax.broadcasted_iota(jnp.int32, (LANES, LANES), 0) // 32
        return jnp.where(lane_groups() == row_group, 1.0, 0.0)

    repeat_lanes = jnp.where(
        lax.broadcasted_iota(jnp.int32, (32, LANES), 1) % 32 == lax.broadcasted_iota(jnp.int32, (32, LANES), 0),
        1.0, 0.0,
    ).astype(BF16)

    wfa[...] = jnp.zeros(wfa.shape, BF16)
    loads["wfa"].wait()
    for phase in range(4):
        for k in range(3):
            wfa[32 * phase : 32 * (phase + 1), LANES * (phase + k) : LANES * (phase + k + 1)] = wfa_in[
                32 * k : 32 * (k + 1), :
            ]
    loads["xf"].wait()

    def arrange(i):
        at = rows_at(i, band)
        stage_a[...] = xf[rows_at(i, fband), :].astype(F32)
        phases = [stage_a[pl.ds(phase, band, stride=4), :] for phase in range(4)]
        vx[at, 0:128] = roll_frames(phases[2], prev(128), 1, False).astype(BF16)
        vx[at, 128:256] = roll_frames(phases[3], prev(128), 1, False).astype(BF16)
        for phase in range(4):
            vx[at, 256 + 128 * phase : 384 + 128 * phase] = phases[phase].astype(BF16)
        vx[at, 768:896] = roll_frames(phases[0], following(128), -1, False).astype(BF16)

    loop(bands, arrange, unroll=2)
    for tap in taps:
        tap.wait()

    def zero2(width):
        return (jnp.zeros((8, width), F32), jnp.zeros((8, width), F32))

    def conv_fa(i, carry):
        at = rows_at(i, half)
        value = dot(vx[at, 128:896], wfa[...], NT)
        sec_fa[at, :] = value
        return carry[0] + column_sums(value), carry[1] + column_sums(value * value)

    def conv_lat(i, carry):
        at = rows_at(i, half)
        value = dot(vx[at, 0:640], wlat[...], NT)
        sec_lat[at, :] = value
        return carry[0] + column_sums(value), carry[1] + column_sums(value * value)

    sum_lat, sq_lat = loop(2, conv_lat, zero2(256))
    put(LAT, 0, squash(sum_lat))
    put(LAT, 256, squash(sq_lat))
    pl.semaphore_wait(barrier, len(greeted))
    exchange_start(LAT)

    sum_fa, sq_fa = loop(2, conv_fa, zero2(128))
    put(FA, 0, pair32(squash(sum_fa), squash(sq_fa)))
    exchange_start(FA)

    loads["xs"].wait()
    loads["wsa"].wait()

    def narrow_main(i):
        at = rows_at(i, half)
        for k in range(3):
            big[at, bs * k : bs * (k + 1)] = dot(xs[at, :], wsa[bs * k : bs * (k + 1), 0:cs_n], NT)

    loop(2, narrow_main)
    loads["wfb"].wait()
    loads["wfc"].wait()
    spread = dot(wfb_in[...], repeat_lanes, NN)
    for a in range(3):
        for b in range(3):
            piece = spread[32 * (3 * a + b) : 32 * (3 * a + b + 1), :]
            block = (jnp.concatenate([piece] * 4, axis=0) * block_mask()).astype(BF16)
            wfb[a, :, LANES * b : LANES * (b + 1)] = block
            wfbk[a, LANES * (2 - b) : LANES * (3 - b), :] = block
    widen = dot(wfc_in[...], repeat_lanes, TN)
    for phase in range(4):
        wfc[LANES * phase : LANES * (phase + 1), :] = jnp.where(lane_groups() == phase, widen, 0.0).astype(BF16)
    read_parameters()
    total = exchange_end(LAT)

    stats_lat = moments(LAT, take(total, 0, 256), take(total, 256, 256), slow_count)

    def act_fa(i):
        spread_columns(hcf, i, silu_of(sec_fa[rows_at(i, band), :], stats_fa))

    def act_lat(i):
        at = rows_at(i, 2 * band)
        jl[at, :] = silu_of(sec_lat[at, :], stats_lat).astype(BF16)

    loop(bands // 2, act_lat)

    def conv_fb(i, carry):
        value = None
        for a in range(3):
            at = pl.ds(pl.multiple_of(i * half + band * a, 16), half)
            term = dot(hcf[at, :], wfb[a], NT)
            value = term if value is None else value + term
        sec_fb[rows_at(i, half), :] = value
        return carry[0] + column_sums(value), carry[1] + column_sums(value * value)

    def narrow_lateral(i):
        at = rows_at(i, half)
        for k in range(3):
            big[at, bs * k : bs * (k + 1)] += dot(jl[at, :], wsa[bs * k : bs * (k + 1), cs_n:], NT)

    loop(2, narrow_lateral)

    def combine_sa(i, carry):
        at = rows_at(i, band)
        value = (
            big[at, bs : 2 * bs]
            + roll_frames(big[at, 0:bs], prev(256), 1, False)
            + roll_frames(big[at, 2 * bs : 3 * bs], following(256), -1, False)
        )
        sec_sa[at, :] = value
        return carry[0] + column_sums(value), carry[1] + column_sums(value * value)

    sum_sa, sq_sa = loop(bands, combine_sa, zero2(256))
    put(SLOW_A, 0, squash(sum_sa))
    put(SLOW_A, 256, squash(sq_sa))
    exchange_start(SLOW_A)

    total = exchange_end(FA)
    stats_fa = moments(FA, *unpair32(total), fast_count)
    loop(bands, act_fa, unroll=2)
    sum_fb, sq_fb = loop(2, conv_fb, zero2(128))
    put(FB, 0, pair32(squash(sum_fb), squash(sq_fb)))
    exchange_start(FB)
    total = exchange_end(SLOW_A)

    stats_sa = moments(SLOW_A, take(total, 0, 256), take(total, 256, 256), slow_count)

    def act_sa(i):
        spread_columns(hcs, i, silu_of(sec_sa[rows_at(i, band), :], stats_sa))

    def act_fb(i):
        at = rows_at(i, 2 * band)
        hbf[at, :] = silu_of(sec_fb[at, :], stats_fb).astype(BF16)

    loop(bands, act_sa, unroll=2)
    loads["wsb"].wait()

    def conv_sb(i, carry):
        value = None
        for a in range(3):
            at = pl.ds(pl.multiple_of(i * half + band * a, 16), half)
            for b in range(3):
                tap = 3 * a + b
                term = dot(hcs[at, bs * b : bs * (b + 1)], wsb[bs * tap : bs * (tap + 1), :], NT)
                value = term if value is None else value + term
        sec_sb[rows_at(i, half), :] = value
        return carry[0] + column_sums(value), carry[1] + column_sums(value * value)

    sum_sb, sq_sb = loop(2, conv_sb, zero2(256))
    put(SLOW_B, 0, squash(sum_sb))
    put(SLOW_B, 256, squash(sq_sb))
    exchange_start(SLOW_B)

    total = exchange_end(FB)
    stats_fb = moments(FB, *unpair32(total), fast_count)
    loop(bands // 2, act_fb)

    def widen_fast(i, carry):
        at = rows_at(i, half)
        value = dot(hbf[at, :], wfc[...], NT)
        sec_fc[at, :] = value
        return carry[0] + column_sums(value), carry[1] + column_sums(value * value)

    sum_fc, sq_fc = loop(2, widen_fast, zero2(512))

    def fold4(vector):
        return vector[:, 0:128] + vector[:, 128:256] + vector[:, 256:384] + vector[:, 384:512]

    put(FC, 0, squash(fold4(sum_fc)))
    put(FC, 128, squash(fold4(sq_fc)))
    exchange_start(FC)
    total = exchange_end(SLOW_B)

    stats_sb = moments(SLOW_B, take(total, 0, 256), take(total, 256, 256), slow_count)

    def act_sb(i, carry):
        at = rows_at(i, 2 * band)
        value = silu_of(sec_sb[at, :], stats_sb).astype(BF16)
        hbs[at, :] = value
        return carry + column_sums(value.astype(F32))

    sum_hbs = loop(bands // 2, act_sb, jnp.zeros((8, bs), F32))
    loads["wsc"].wait()
    mid = cs_n // 2

    def widen_slow(part):
        lanes = slice(part * mid, (part + 1) * mid)

        def step(i, carry):
            at = rows_at(i, half)
            value = dot(hbs[at, :], wsc[lanes, :], NT)
            big[at, lanes] = value
            return carry + column_sums(value * value)

        return loop(2, step, jnp.zeros((8, mid), F32))

    put(SLOW_C, 0, squash(sum_hbs))
    put(SLOW_C, 256, squash(widen_slow(0)))
    exchange_start(SLOW_C)
    put(SLOW_C + 1, 0, squash(widen_slow(1)))
    exchange_start(SLOW_C + 1)
    total = exchange_end(FC)
    stats_fc = moments(FC, take(total, 0, 128), take(total, 128, 128), fast_count)

    loads["cf"].wait()

    def finish_fast(i, carry):
        at, fat = rows_at(i, band), rows_at(i, fband)
        bias_sum, gain_sum = carry
        dbuf_f[0:fband, :] = cf[fat, :].astype(F32)
        for phase in range(4):
            lanes = slice(128 * phase, 128 * (phase + 1))
            centred = sec_fc[at, lanes] - stats_fc[0]()
            total_in = vx[at, 256 + 128 * phase : 384 + 128 * phase].astype(F32)
            out, slope = slope_of(0.5 * total_in + (centred * stats_fc[2]() + stats_fc[3]()))
            stage_a[pl.ds(phase, band, stride=4), :] = out
            grad = dbuf_f[pl.ds(phase, band, stride=4), :] * slope
            gsf[at, lanes] = grad
            bias_sum = bias_sum + column_sums(grad)
            gain_sum = gain_sum + column_sums(grad * centred)
        cf[fat, :] = stage_a[...].astype(BF16)
        return bias_sum, gain_sum

    bias_fc, gain_fc = loop(bands, finish_fast, zero2(128))
    put(BACK + FC, 0, squash(bias_fc))
    put(BACK + FC, 128, squash(gain_fc) * stats_fc[1]())
    exchange_start(BACK + FC)
    loads["cs"].wait()
    total = exchange_end(SLOW_C)
    squares = [take(total, 256, mid)]
    rest, row = take(total, 0, 256), lax.broadcasted_iota(jnp.int32, (16, bs), 0)
    parts = jnp.zeros((16, bs), F32)
    for k in range(3):
        part_k = rest.astype(BF16).astype(F32)
        parts = jnp.where(row == k, part_k, parts)
        rest = rest - part_k
    whole = settle(squash(dot(parts.astype(BF16), wsc[...], NT)))
    stats_sc = []

    def finish_slow(part):
        lanes = slice(part * mid, (part + 1) * mid)
        def step(i, carry):
            at = rows_at(i, band)
            mean, lead, level = [stats_sc[part][k]() for k in (0, 2, 3)]
            centred = big[at, lanes] - mean
            out, slope = slope_of(0.5 * xs[at, lanes].astype(F32) + (centred * lead + level))
            grad = cs[at, lanes].astype(F32) * slope
            cs[at, lanes] = out.astype(BF16)
            gsum[at, lanes] = centred.astype(BF16)
            big[at, lanes] = grad
            return carry[0] + column_sums(grad), carry[1] + column_sums(grad * centred)

        bias_part, gain_part = loop(bands, step, zero2(mid))
        return squash(bias_part), squash(gain_part) * stats_sc[part][1]()

    for part in range(2):
        if part:
            squares.append(exchange_end(SLOW_C + 1))
        lanes = slice(part * mid, (part + 1) * mid)
        stats_sc.append(moments(SLOW_C, whole(lanes), squares[part], slow_count, lanes))
        bias_part, gain_part = finish_slow(part)
        put(BACK + SLOW_C + part, 0, bias_part)
        put(BACK + SLOW_C + part, mid, gain_part)
        exchange_start(BACK + SLOW_C + part)
    slow_store = store(cs, slow_h, 11)

    total = exchange_end(BACK + FC)
    bias_fc, gain_fc = take(total, 0, 128), take(total, 128, 128)
    report(FC, bias_fc, gain_fc)
    def slope_pass(section, stats, buffer):
        def step(i, carry):
            at = rows_at(i, 2 * band)
            centred = section[at, :] - stats[0]()
            grad = buffer[at, :] * slope_of(centred * stats[2]() + stats[3]())[1]
            buffer[at, :] = grad
            return carry[0] + column_sums(grad), carry[1] + column_sums(grad * centred)

        bias_sum, gain_sum = loop(bands // 2, step, zero2(section.shape[1]))
        return squash(bias_sum), squash(gain_sum) * stats[1]()

    lead_fc, level_fc, tilt_fc = back_vectors(FC, stats_fc, bias_fc, gain_fc, fast_count)

    def low_fc(i):
        at = rows_at(i, band)
        for phase in range(4):
            lanes = slice(128 * phase, 128 * (phase + 1))
            value = gsf[at, lanes] * lead_fc() - level_fc() - sec_fc[at, lanes] * tilt_fc()
            gcs[at, lanes] = value.astype(BF16)

    loop(bands, low_fc, unroll=2)

    def back_fc(i):
        at = rows_at(i, half)
        dbuf_f[at, :] = dot(gcs[at, 0:512], wfc[...], NN)

    loop(2, back_fc)
    bias_fb, gain_fb = slope_pass(sec_fb, stats_fb, dbuf_f)
    put(BACK + FB, 0, pair32(bias_fb, gain_fb))
    exchange_start(BACK + FB)
    slow_store.wait()

    def back_widen(part):
        lanes = slice(part * mid, (part + 1) * mid)
        total = exchange_end(BACK + SLOW_C + part)
        bias_sc, gain_sc = take(total, 0, mid), take(total, mid, mid)
        report(SLOW_C, bias_sc, gain_sc, part * (mid // LANES))
        scale = stats_sc[part][1]()
        lead = gains[SLOW_C](lanes) * scale
        tilt_sc = settle(lead * scale * gain_sc * (1.0 / slow_count))
        level_sc = settle(lead * bias_sc * (1.0 / slow_count))
        lead_sc = settle(lead)

        def low_sc(i):
            at = rows_at(i, 32)
            grad = big[at, lanes]
            cs[at, lanes] = (grad * lead_sc() - level_sc() - gsum[at, lanes].astype(F32) * tilt_sc()).astype(BF16)
            gsum[at, lanes] = grad.astype(BF16)

        loop(rows // 32, low_sc, unroll=7)

        def back_sc(i):
            at = rows_at(i, half)
            value = dot(cs[at, lanes], wsc[lanes, :], NN)
            dbuf[at, :] = dbuf[at, :] + value if part else value

        loop(2, back_sc)

    for part in range(2):
        back_widen(part)
    bias_sb, gain_sb = slope_pass(sec_sb, stats_sb, dbuf)

    put(BACK + SLOW_B, 0, bias_sb)
    put(BACK + SLOW_B, 256, gain_sb)
    exchange_start(BACK + SLOW_B)

    slab_sc[0:cs_n, :] = dot(cs[...], hbs[...], TN)
    advance(SC)
    widening = None
    for phase in range(4):
        term = dot(hbf[...], gcs[0:rows, 128 * phase : 128 * (phase + 1)], TN)[32 * phase : 32 * (phase + 1), :]
        widening = term if widening is None else widening + term
    slab[2, 704:736, 128:256] = widening
    slab[2, 736:768, 128:256] = jnp.zeros((32, LANES), F32)
    poll()

    bias_fb, gain_fb = unpair32(exchange_end(BACK + FB))
    report(FB, bias_fb, gain_fb)
    vec_fb = back_vectors(FB, stats_fb, bias_fb, gain_fb, fast_count)

    def norm_grad(buffer, section, at, vectors):
        lead, level, tilt = vectors
        return buffer[at, :] * lead() - level() - section[at, :] * tilt()

    def low_fb(i):
        spread_columns(gcf, i, norm_grad(dbuf_f, sec_fb, rows_at(i, band), vec_fb))

    loop(bands, low_fb, unroll=2)

    def back_fb(i):
        value = None
        for a in range(3):
            at = pl.ds(pl.multiple_of(i * half + band * (2 - a), 16), half)
            term = dot(gcf[at, :], wfbk[a], NN)
            value = term if value is None else value + term
        dbuf_f[rows_at(i, half), :] = value

    loop(2, back_fb)
    poll()
    bias_fa, gain_fa = slope_pass(sec_fa, stats_fa, dbuf_f)
    put(BACK + FA, 0, pair32(bias_fa, gain_fa))
    exchange_start(BACK + FA)
    poll()
    total = exchange_end(BACK + SLOW_B)

    bias_sb, gain_sb = take(total, 0, 256), take(total, 256, 256)
    report(SLOW_B, bias_sb, gain_sb)
    vec_sb = back_vectors(SLOW_B, stats_sb, bias_sb, gain_sb, slow_count)

    gcs[0:band, :] = jnp.zeros((band, gcs.shape[1]), BF16)

    def low_sb(i):
        spread_columns(gcs, i, norm_grad(dbuf, sec_sb, rows_at(i, band), vec_sb))

    loop(bands, low_sb, unroll=2)
    poll()

    def back_sb(i):
        value = None
        for a in range(3):
            at = pl.ds(pl.multiple_of(i * half + band * (2 - a), 16), half)
            for b in range(3):
                tap = 3 * a + b
                term = dot(gcs[at, bs * (2 - b) : bs * (3 - b)], wsb[bs * tap : bs * (tap + 1), :], NN)
                value = term if value is None else value + term
        dbuf[rows_at(i, half), :] = value

    for part in range(2):
        back_sb(part)
        poll()
    bias_sa, gain_sa = slope_pass(sec_sa, stats_sa, dbuf)

    put(BACK + SLOW_A, 0, bias_sa)
    put(BACK + SLOW_A, 256, gain_sa)
    exchange_start(BACK + SLOW_A)
    poll()

    for a in range(3):
        value = dot(gcs[band : band + rows, bs : 2 * bs], hcs[band * a : band * a + rows, :], TN)
        ref, lane = pieces[SB + a].ref, pieces[SB + a].lane
        for b in range(3):
            ref[bs * b : bs * (b + 1), lane : lane + bs] = value[:, bs * b : bs * (b + 1)]
        advance(SB + a)
        poll()
    for a in range(3):
        value = dot(gcf[band : band + rows, 128:256], hcf[band * a : band * a + rows, :], TN)
        for b in range(3):
            tap = 3 * a + b
            block = value[:, 128 * b : 128 * (b + 1)] * block_mask()
            folded = fold_lanes(block[0:32] + block[32:64] + block[64:96] + block[96:128])
            folded = jnp.where(lane_groups(32) == tap % 4, folded, 0.0)
            at = slice(608 + 32 * (tap // 4), 640 + 32 * (tap // 4))
            slab[2, at, 128:256] = folded if tap % 4 == 0 else slab[2, at, 128:256] + folded
    poll()
    poll()
    total = exchange_end(BACK + SLOW_A)
    poll()

    bias_sa, gain_sa = take(total, 0, 256), take(total, 256, 256)
    report(SLOW_A, bias_sa, gain_sa)
    vec_sa = back_vectors(SLOW_A, stats_sa, bias_sa, gain_sa, slow_count)
    def low_sa(i):
        at = rows_at(i, band)
        value = norm_grad(dbuf, sec_sa, at, vec_sa)
        gcs[at, 0:bs] = roll_frames(value, prev(256), -1, True).astype(BF16)
        gcs[at, bs : 2 * bs] = value.astype(BF16)
        gcs[at, 2 * bs :] = roll_frames(value, following(256), 1, True).astype(BF16)

    loop(bands, low_sa, unroll=2)
    poll()

    def narrow_gradient(k):
        ref, lane = pieces[SA + k].ref, pieces[SA + k].lane
        source = xs[:, 256 * k : 256 * (k + 1)] if k < 4 else jl[...]
        ref[0 : 3 * bs, lane : lane + 256] = dot(gcs[0:rows, :], source, TN)
        advance(SA + k)

    narrow_gradient(0)
    poll()

    def back_lateral(i):
        at = rows_at(i, half)
        dbuf[at, :] = dot(gcs[at, :], wsa[:, cs_n:], NN)

    loop(2, back_lateral)
    poll()
    bias_lat, gain_lat = slope_pass(sec_lat, stats_lat, dbuf)
    put(BACK + LAT, 0, bias_lat)
    put(BACK + LAT, 256, gain_lat)
    exchange_start(BACK + LAT)
    bias_fa, gain_fa = unpair32(exchange_end(BACK + FA))
    report(FA, bias_fa, gain_fa)
    vec_fa = back_vectors(FA, stats_fa, bias_fa, gain_fa, fast_count)

    def low_fa(i):
        at = rows_at(i, band)
        hbf[at, :] = norm_grad(dbuf_f, sec_fa, at, vec_fa).astype(BF16)

    loop(bands, low_fa, unroll=2)
    value = dot(hbf[...], vx[:, 128:896], TN)
    for k in range(3):
        piece = None
        for phase in range(4):
            term = value[32 * phase : 32 * (phase + 1), 128 * (phase + k) : 128 * (phase + k + 1)]
            piece = term if piece is None else piece + term
        slab[2, 512 + 32 * k : 544 + 32 * k, 128:256] = piece

    poll()

    for k in range(1, 4):
        narrow_gradient(k)
        poll()
    total = exchange_end(BACK + LAT)

    bias_lat, gain_lat = take(total, 0, 256), take(total, 256, 256)
    report(LAT, bias_lat, gain_lat)

    def pack(rows_ref, target):
        lanes = lax.broadcasted_iota(jnp.int32, (24, LANES), 1)
        stacked = rows_ref[...]
        turned = pltpu.roll(stacked, 64, 1)
        moved = jnp.where(lanes >= 64, turned, pltpu.roll(turned, 1, 0))[0:16, :]
        first = jnp.where(lane16[0:1, :] < 32, stacked[16:17, :], stacked[17:18, :])
        first = jnp.where(lane16[0:1, :] < 64, first, moved[0:1, :])
        target[...] = moved * factor
        target[0:1, :] = first * factor

    pack(gain_rows, dbuf_f.at[pl.ds(0, 16)])
    pack(bias_rows, dbuf_f.at[pl.ds(16, 16)])
    parameter_stores = [
        store(dbuf_f.at[pl.ds(0, 16)], dgains_h, 19), store(dbuf_f.at[pl.ds(16, 16)], dbiases_h, 20)
    ]
    vec_lat = back_vectors(LAT, stats_lat, bias_lat, gain_lat, slow_count)

    def low_lat(i):
        at = rows_at(i, band)
        hbs[at, :] = norm_grad(dbuf, sec_lat, at, vec_lat).astype(BF16)

    loop(bands, low_lat, unroll=2)
    value = dot(hbs[...], vx[:, 0:640], TN)
    for k in range(5):
        at, lane = 256 * (k % 3), 128 * (k // 3)
        slab[2, at : at + 256, lane : lane + 128] = value[:, 128 * k : 128 * (k + 1)]
    advance(LT)
    poll()
    narrow_gradient(4)
    poll()

    def slow_back(i):
        at = rows_at(i, half)
        for tile in range(cs_n // 256):
            lanes = slice(256 * tile, 256 * (tile + 1))
            value = gsum[at, lanes].astype(F32) + dot(gcs[at, :], wsa[:, lanes], NN)
            gsum[at, lanes] = value.astype(BF16)

    for part in range(2):
        slow_back(part)
        poll()


    def fast_back(i):
        at, fat = rows_at(i, 2 * band), rows_at(i, 2 * fband)
        conv = dot(hbf[at, :], wfa[...], NN)
        side_in = dot(hbs[at, :], wlat[...], NN)

        def lane(values, block):
            return values[:, 128 * block : 128 * (block + 1)]

        grads = [gsf[at, 128 * phase : 128 * (phase + 1)] + lane(conv, phase + 1) for phase in range(4)]
        grads[0] = grads[0] + roll_frames(lane(conv, 5), following(128), 1, True) + lane(side_in, 2)
        grads[1] = grads[1] + lane(side_in, 3)
        grads[2] = grads[2] + lane(side_in, 4) + roll_frames(lane(side_in, 0), prev(128), -1, True)
        grads[3] = grads[3] + roll_frames(lane(side_in, 1) + lane(conv, 0), prev(128), -1, True)
        for part in range(2):
            for phase in range(4):
                stage_a[pl.ds(phase, band, stride=4), :] = grads[phase][part * band : (part + 1) * band]
            xf[rows_at(2 * i + part, fband), :] = stage_a[...].astype(BF16)

    third = bands // 6
    loop(third, fast_back)
    poll()
    loop(third, lambda i: fast_back(i + third))
    poll()
    loop(bands // 2 - 2 * third, lambda i: fast_back(i + 2 * third))
    poll()

    poll()
    while not all(done(name) for name in order):
        for name in order:
            if not done(name):
                advance(name)
    for copy in stores + parameter_stores:
        copy.wait()


def hand_on(*refs):
    sources, targets, staged, small, sem = refs[0:11], refs[11:24], refs[24:30], refs[30:35], refs[35]
    held = staged[0:1] + sources[1:6] + staged[1:6]
    loads = {k: pltpu.make_async_copy(sources[k], held[k], sem.at[k]) for k in (8, 9, 10, 0, 6, 7)}
    stores = {k: pltpu.make_async_copy(held[k], targets[k], sem.at[11 + k]) for k in (0, 1, 2, 3, 5, 6, 7)}
    for k in range(5):
        stores[8 + k] = pltpu.make_async_copy(small[k], targets[8 + k], sem.at[19 + k])
        stores[13 + k] = pltpu.make_async_copy(
            held[4].at[pl.ds(768 * k, 768)], targets[4].at[:, pl.ds(256 * k, 256)], sem.at[24 + k]
        )
    for copy in loads.values():
        copy.start()
    for k in (1, 2, 3, 5, 13, 14, 15, 16, 17):
        stores[k].start()
    for k in (8, 9, 10):
        loads[k].wait()
    small[0][...] = held[8][0:96, :]
    for tap in range(9):
        at = 96 + 32 * (tap // 4)
        small[1][32 * tap : 32 * (tap + 1), :] = held[8][at : at + 32, 32 * (tap % 4) : 32 * (tap % 4 + 1)]
    small[2][...] = held[8][192:224, :]
    for source, target in ((held[9], small[3]), (held[10], small[4])):
        count = target.shape[0]
        for row in range(16):
            width = min(LANES, count - row * LANES)
            target[pl.ds(row * LANES, width)] = source[row : row + 1, 0:width].reshape(width)
    for k in range(8, 13):
        stores[k].start()
    for k in (0, 6, 7):
        loads[k].wait()
        stores[k].start()
    for copy in stores.values():
        copy.wait()


def body(
    slow_input,
    fast_input,
    clip_ids,
    fast_narrow,
    fast_spatial,
    fast_widen,
    lateral_conv,
    slow_narrow,
    slow_spatial,
    slow_widen,
    norm_gains,
    norm_biases,
    slow_cotangent,
    fast_cotangent,
):
    n_dp, n_rep = lax.axis_size("dp"), lax.axis_size("rep")
    low = 2 if n_dp % 2 == 0 else 1
    high = n_dp // low
    frames, plane, channels = slow_input.shape
    fast_frames, _, fast_channels = fast_input.shape
    side = math.isqrt(plane)
    rows = frames * plane
    slow_count = rows * n_dp * n_rep
    fast_count = slow_count * (fast_frames // frames)

    def flat(values):
        return values.transpose(1, 0, 2).reshape(values.shape[0] * values.shape[1], values.shape[2])

    def unflat(values, count):
        return values.reshape(plane, count, values.shape[1]).transpose(1, 0, 2)

    widths = [
        fast_narrow.shape[1], fast_spatial.shape[1], fast_widen.shape[0], lateral_conv.shape[1],
        slow_narrow.shape[1], slow_spatial.shape[1], slow_widen.shape[0],
    ]

    cf = fast_channels
    bs = slow_spatial.shape[1]
    band = side * frames
    any_spec = pl.BlockSpec(memory_space=pl.ANY)
    vmem_spec = pl.BlockSpec(memory_space=pltpu.VMEM)
    near_low = n_dp if n_dp * n_rep <= 32 else low
    stages = 1 if near_low == n_dp else 2
    pad = rows + 2 * band

    def shape(dims, dtype):
        return jax.ShapeDtypeStruct(dims, dtype)

    out_shape = [
        shape((rows, channels), BF16), pltpu.VMEM((4 * rows, cf), BF16),
        pltpu.VMEM((rows, channels), BF16), pltpu.VMEM((4 * rows, cf), BF16),
        pltpu.VMEM((15 * bs, bs), F32), pltpu.VMEM((9 * bs, bs), F32), shape((channels, bs), F32),
        shape((5 * bs, cf), F32), shape((256, cf), F32), shape((16, LANES), F32), shape((16, LANES), F32),
        shape((10, max(high // 4, 1), 32, 256), F32),
    ]
    scratch = [
        pltpu.VMEM((rows, channels), BF16), pltpu.VMEM((rows, channels), BF16),
        pltpu.VMEM((rows, channels), F32),
        pltpu.VMEM((rows, 512), F32), pltpu.VMEM((rows, 512), F32),
        pltpu.VMEM((pad, 3 * bs), BF16), pltpu.VMEM((pad, 3 * bs), BF16),
        pltpu.VMEM((pad, 384), BF16), pltpu.VMEM((pad, 384), BF16),
        pltpu.VMEM((rows, bs), F32), pltpu.VMEM((rows, bs), F32),
        pltpu.VMEM((rows, 128), F32), pltpu.VMEM((rows, 128), F32), pltpu.VMEM((rows, 128), F32),
        pltpu.VMEM((rows, bs), BF16), pltpu.VMEM((rows, bs), BF16), pltpu.VMEM((rows, 128), BF16),
        pltpu.VMEM((rows, 896), BF16), pltpu.VMEM((3, 1512, 256), F32), pltpu.VMEM((2016, 256), F32),
        pltpu.VMEM((768, 256), F32),
        pltpu.VMEM((3 * bs, channels + bs), BF16), pltpu.VMEM((9 * bs, bs), BF16),
        pltpu.VMEM((channels, bs), BF16), pltpu.VMEM(norm_gains.shape, F32), pltpu.VMEM(norm_gains.shape, F32),
        pltpu.VMEM((9, 8, channels), F32), pltpu.VMEM((2, 8, 256), F32),
        pltpu.VMEM((96, cf), BF16), pltpu.VMEM((288, 32), BF16), pltpu.VMEM((32, cf), BF16),
        pltpu.VMEM((bs, 640), BF16), pltpu.VMEM((128, 768), BF16),
        pltpu.VMEM((3, 128, 384), BF16), pltpu.VMEM((3, 384, 128), BF16), pltpu.VMEM((512, 128), BF16),
        pltpu.VMEM((4 * band, cf), F32),
        pltpu.VMEM((24, LANES), F32), pltpu.VMEM((24, LANES), F32),
        pltpu.VMEM((near_low * n_rep, 1, sum(TURNS.values())), F32),
        pltpu.VMEM((max(n_dp // near_low, 1), 1, sum(TURNS.values())), F32),
        pltpu.SemaphoreType.DMA((stages, len(TURNS))), pltpu.SemaphoreType.DMA((stages, len(TURNS))),
        pltpu.SemaphoreType.DMA((32,)), pltpu.SemaphoreType.DMA((10, 2)),
        pltpu.SemaphoreType.DMA((10,)), pltpu.SemaphoreType.DMA((10, 10 if high == 4 else 11)),
    ]
    factor = 1.0 / math.sqrt(float(slow_count))
    results = pl.pallas_call(
        functools.partial(kernel, (n_dp, n_rep, low, frames, side, float(slow_count), float(fast_count), factor)),
        out_shape=out_shape,
        in_specs=[any_spec] * 4 + [pl.BlockSpec(memory_space=pltpu.SMEM)] + [any_spec] * 9,
        out_specs=[any_spec] + [vmem_spec] * 5 + [any_spec] * 6,
        scratch_shapes=scratch,
        compiler_params=pltpu.CompilerParams(
            collective_id=0, has_side_effects=True, vmem_limit_bytes=52960 * 2**10
        ),
    )(
        flat(slow_input), flat(fast_input), flat(slow_cotangent), flat(fast_cotangent), clip_ids,
        fast_narrow.reshape(-1, cf), fast_spatial.reshape(-1, 32), fast_widen.T,
        lateral_conv.reshape(-1, cf), slow_narrow.reshape(3 * bs, -1), slow_spatial.reshape(9 * bs, bs),
        slow_widen, norm_gains, norm_biases,
    )
    final = [shape((rows, channels), BF16), shape((4 * rows, cf), BF16)] * 2 + [
        shape((3 * bs, channels + bs), F32), shape((9 * bs, bs), F32), *out_shape[6:8],
        shape((96, cf), F32), shape((288, 32), F32), shape((32, cf), F32),
        shape(norm_gains.shape, F32), shape(norm_gains.shape, F32),
    ]
    handed = pl.pallas_call(
        hand_on,
        out_shape=final,
        in_specs=[any_spec] + [vmem_spec] * 5 + [any_spec] * 5,
        out_specs=[any_spec] * 13,
        scratch_shapes=[pltpu.VMEM(item.shape, item.dtype) for item in out_shape[0:1] + out_shape[6:11] + final[8:13]]
        + [pltpu.SemaphoreType.DMA((29,))],
        compiler_params=pltpu.CompilerParams(vmem_limit_bytes=52960 * 2**10),
    )(results[0], *[pltpu.with_memory_space_constraint(r, pltpu.VMEM) for r in results[1:6]], *results[6:11])
    slow_out, fast_out, slow_grad, fast_grad, dsa, dsb, dsc, dl, dfa, dfb, dfc, dgains, dbiases = handed

    return (
        unflat(slow_out, frames),
        unflat(fast_out, fast_frames),
        unflat(slow_grad, frames),
        unflat(fast_grad, fast_frames),
        dfa.reshape(fast_narrow.shape),
        dfb.reshape(fast_spatial.shape),
        dfc.T,
        dl.reshape(lateral_conv.shape),
        dsa.reshape(slow_narrow.shape),
        dsb.reshape(slow_spatial.shape),
        dsc,
        dgains,
        dbiases,
    )


def solution(mesh):
    sharded = P(("dp", "rep"), None, None)
    return jax.shard_map(
        body,
        mesh=mesh,
        in_specs=(sharded, sharded, P(("dp", "rep"), None)) + (P(),) * 9 + (sharded, sharded),
        out_specs=(sharded,) * 4 + (P(),) * 9,
        check_vma=False,
    )
```

```python
import functools
import math

import jax
import jax.numpy as jnp
from jax import lax
from jax.experimental import pallas as pl
from jax.experimental.pallas import tpu as pltpu
from jax.sharding import PartitionSpec as P

EPS = 1e-05
F32 = jnp.float32
BF16 = jnp.bfloat16
MESH = pl.DeviceIdType.MESH
NN = ((1,), (0,))
NT = ((1,), (1,))
TN = ((0,), (0,))
LANES = 128
FA, FB, FC, LAT, SLOW_A, SLOW_B, SLOW_C = range(7)
FORWARD = {LAT: 512, FA: 128, SLOW_A: 512, FB: 128, SLOW_B: 512, FC: 256, SLOW_C: 768, SLOW_C + 1: 512}
BACKWARD = {SLOW_C: 1024, SLOW_C + 1: 1024, FC: 256, SLOW_B: 512, FB: 128, SLOW_A: 512, FA: 128, LAT: 512}
BACK = 8
TURNS = {**FORWARD, **{BACK + norm: lanes for norm, lanes in BACKWARD.items()}}


class Piece:
    pass


SC, SB, SA, LT = 0, 1, 4, 9
C, X, Y, Z, Z0, Z1 = range(6)
PLANE = ((C, X, Y, Z), (C, Y, X, Z))
HALVES = ((C, X, Y, Z0, Z1), (C, Y, X, Z0, Z1))
BETWEEN = ((C, X, Z0, Z1, Y), (C, Y, Z0, Z1, X))
LINE = ((C, Z0, Z1, X, Y), (C, Z0, Z1, Y, X))
ORDER_OF = (PLANE, HALVES, LINE, PLANE, BETWEEN, PLANE, HALVES, HALVES, PLANE, PLANE)
POLLS = (
    (),
    (0,),
    (),
    (),
    (),
    (),
    (),
    (0,),
    (),
    (1,),
    (2,),
    (0, 3),
    (),
    (),
    (),
    (1,),
    (4,),
    (3, 2),
    (1, 5),
    (4, 0, 6),
    (3, 7, 1),
    (5, 2, 9),
    (6, 4, 8),
    (7, 0),
    (5, 3, 2),
    (1,),
    (9,),
    (
        6, 5, 4, 7, 6, 3, 8, 1, 9, 5, 4, 7, 6, 2, 1, 3, 9, 5, 8, 7, 4, 6, 2, 1,
        3, 9, 5, 0, 8, 7, 6, 4, 1, 2, 9, 3, 5, 8, 0, 7, 6, 4, 1, 9, 2, 8, 0, 7,
        6, 4, 2, 9, 8, 4, 7, 6, 2, 8, 7,
    ),
)


def dot(left, right, dims):
    return lax.dot_general(left, right, (dims, ((), ())), preferred_element_type=F32)


def column_sums(values):
    return jnp.sum(values.reshape(values.shape[0] // 8, 8, values.shape[1]), axis=0)


def squash(partial):
    return jnp.sum(partial, axis=0, keepdims=True)


def fold_lanes(values):
    half = values + pltpu.roll(values, 64, 1)
    return half + pltpu.roll(half, 32, 1)


def loop(count, body, init=None, unroll=1):
    if init is None:

        def plain(index, carry):
            body(index)
            return carry

        lax.fori_loop(0, count, plain, 0, unroll=unroll)
        return None
    return lax.fori_loop(0, count, body, init, unroll=unroll)


def rows_at(index, size):
    return pl.ds(pl.multiple_of(index * size, 16), size)


def kernel(
    dims,
    xs_h, xf_h, cs_h, cf_h, clip, wfa_h, wfb_h, wfc_h, wl_h, wsa_h, wsb_h, wsc_h, gains_h, biases_h,
    slow_h, cf, gsum, xf, dsa, dsb, dsc_h, dl_h, small_h, dgains_h, dbiases_h, extra_h,
    xs, cs, big, sec_fc, gsf, hcs, gcs, hcf, gcf,
    sec_lat, dbuf, sec_fa, sec_fb, dbuf_f, jl, hbs, hbf, vx, slab, slab_sc, summed,
    wsa, wsb, wsc, gains_in, biases_in, vectors, masks, wfa_in, wfb_in, wfc_in, wlat, wfa, wfb, wfbk, wfc,
    stage_a, gain_rows, bias_rows, near, far, sum_send, sum_recv, io_sem, own_sem, big_send, big_recv,
):
    n_dp, n_rep, low, frames, side, slow_count, fast_count, factor = dims
    sec_sa, sec_sb = dsa, dsb
    rows = xs.shape[0]
    half = rows // 2
    band = side * frames
    bands = side
    fband = 4 * band
    cs_n = xs.shape[1]
    bs = wsb.shape[1]

    dp_i, rep_i = lax.axis_index("dp"), lax.axis_index("rep")
    dp_lo, dp_hi = lax.rem(dp_i, low), lax.div(dp_i, low)
    high = n_dp // low
    direct = n_dp * n_rep <= 32
    near_low = n_dp if direct else low
    near_dp, far_dp = lax.rem(dp_i, near_low), lax.div(dp_i, near_low)
    near_peers = [
        (far_dp * near_low + lax.rem(near_dp + a, near_low), lax.rem(rep_i + b, n_rep))
        for a in range(near_low)
        for b in range(n_rep)
        if a or b
    ]
    far_count = n_dp // near_low
    far_peers = [(lax.rem(far_dp + a, far_count) * near_low + near_dp, rep_i) for a in range(1, far_count)]
    stages = [(near, near_dp * n_rep + rep_i, near_peers)]
    if far_peers:
        stages.append((far, far_dp, far_peers))

    c, x = lax.rem(rep_i, 2), lax.div(rep_i, 2)
    y, z = dp_lo, lax.rem(dp_hi, 4)
    outer, outers = lax.div(dp_hi, 4), high // 4
    core_peer = (dp_i, 2 * x + 1 - c)
    x_peer = (dp_i, 2 * (1 - x) + c)
    y_peer = (dp_hi * low + 1 - y, rep_i)
    def z_peer(flip):
        return ((outer * 4 + z + flip - 2 * flip * lax.rem(lax.div(z, flip), 2)) * low + y, rep_i)

    z_peers = [((outer * 4 + lax.rem(z + k, 4)) * low + y, rep_i) for k in range(1, 4)]
    outer_peers = [((lax.rem(outer + k, outers) * 4 + z) * low + y, rep_i) for k in range(1, outers)]

    barrier = pltpu.get_barrier_semaphore()
    greeted = near_peers + far_peers
    for peer in greeted:
        pl.semaphore_signal(barrier, inc=1, device_id=peer, device_id_type=MESH)

    loads = {}
    for slot, (name, src, dst) in enumerate([
        ("xf", xf_h, xf), ("wfa", wfa_h, wfa_in), ("xs", xs_h, xs),
        ("wsa", wsa_h, wsa), ("wfb", wfb_h, wfb_in), ("wfc", wfc_h, wfc_in), ("wsb", wsb_h, wsb),
        ("wsc", wsc_h, wsc), ("cf", cf_h, cf), ("cs", cs_h, cs), ("gains", gains_h, gains_in), ("biases", biases_h, biases_in),
    ]):
        loads[name] = pltpu.make_async_copy(src, dst, io_sem.at[slot])
        loads[name].start()
        if name == "wfa":
            taps = [
                pltpu.make_async_copy(
                    wl_h.at[pl.ds(bs * k, bs)], wlat.at[:, pl.ds(LANES * k, LANES)], io_sem.at[27 + k]
                )
                for k in range(5)
            ]
            for tap in taps:
                tap.start()
    stores = []

    def store(src, dst, slot):
        copy = pltpu.make_async_copy(src, dst, io_sem.at[slot])
        copy.start()
        return copy

    turn_at, turn_index = {}, {}
    for index, (turn, width) in enumerate(TURNS.items()):
        turn_at[turn] = sum(list(TURNS.values())[:index])
        turn_index[turn] = index

    def put(turn, at, vector):
        near[stages[0][1], :, pl.ds(turn_at[turn] + at, vector.shape[1])] = vector

    def sum_copy(turn, stage, first, count, peer):
        buffer = stages[stage][0]
        block = buffer.at[pl.ds(first, count), :, pl.ds(turn_at[turn], TURNS[turn])]
        return pltpu.make_async_remote_copy(
            src_ref=block, dst_ref=block, send_sem=sum_send.at[stage, turn_index[turn]],
            recv_sem=sum_recv.at[stage, turn_index[turn]], device_id=peer, device_id_type=MESH,
        )

    def exchange_start(turn):
        for peer in near_peers:
            sum_copy(turn, 0, stages[0][1], 1, peer).start()

    def exchange_end(turn):
        lanes = pl.ds(turn_at[turn], TURNS[turn])
        for stage, (buffer, rank, peers) in enumerate(stages):
            if stage:
                buffer[rank, :, lanes] = total
                for peer in peers:
                    sum_copy(turn, stage, rank, 1, peer).start()
            copy = sum_copy(turn, stage, 0, len(peers), peers[0])
            copy.wait_recv()
            total = jnp.sum(buffer[:, :, lanes], axis=0)
            copy.wait_send()
        return total

    def take(total, at, width):
        return total[:, at : at + width]

    def pair32(first, second):
        group = lax.broadcasted_iota(jnp.int32, (8, LANES), 1) // 32
        rows8 = (8, LANES)
        first = fold_lanes(jnp.broadcast_to(first, rows8))
        second = fold_lanes(jnp.broadcast_to(second, rows8))
        return jnp.where(group == 0, first, jnp.where(group == 1, second, 0.0))[0:1, :]

    def unpair32(total):
        group = lax.broadcasted_iota(jnp.int32, (8, LANES), 1) // 32
        total = jnp.broadcast_to(total, (8, LANES))
        first = fold_lanes(jnp.where(group == 0, total, 0.0))
        second = fold_lanes(jnp.where(group == 1, total, 0.0))
        return first[0:1, :], second[0:1, :]

    pieces = {}

    bits = {C: (c, core_peer), X: (x, x_peer), Y: (y, y_peer),
            Z0: (lax.rem(z, 2), z_peer(1)), Z1: (lax.div(z, 2), z_peer(2))}

    def add_piece(name, ref, lane, size, index):
        axes = ORDER_OF[name]
        piece = Piece()
        piece.name, piece.ref, piece.lane, piece.size, piece.index = name, ref, lane, size, index
        piece.step, piece.axes, piece.steps = 0, axes, len(axes[0])
        starts, counts, arriving = [[0], [0]], [size], [size]
        for step, pair in enumerate(zip(*axes)):
            for side, axis in enumerate(pair):
                if axis == Z:
                    starts[side].append(starts[side][-1] + z * (counts[-1] // 4))
                else:
                    starts[side].append(starts[side][-1] + bits[axis][0] * (counts[-1] // 2))
            counts.append(counts[-1] // (4 if pair[0] == Z else 2))
            arriving.append(arriving[-1] + (3 if pair[0] == Z else 1) * counts[-1])
        piece.starts, piece.counts, piece.arriving = starts, counts, arriving
        pieces[name] = piece

    for k in range(2):
        add_piece(SB + k, sec_fc, 256 * k, 768, k)
    for k in range(4):
        add_piece(SA + k, big, 256 * k, 768, 2 + k)
    add_piece(SB + 2, slab.at[0], 0, 768, 6)
    add_piece(SA + 4, slab.at[1], 0, 768, 7)
    add_piece(LT, slab.at[2], 0, 768, 8)
    add_piece(SC, slab_sc, 0, 1024, 9)

    def span(piece, start, count, lane=0, width=256):
        return piece.ref.at[pl.ds(pl.multiple_of(start, 8), count), pl.ds(piece.lane + lane, width)]

    def send(piece, step, src, dst, peer):
        pltpu.make_async_remote_copy(
            src_ref=src, dst_ref=dst, send_sem=big_send.at[piece.index],
            recv_sem=big_recv.at[piece.index, step], device_id=peer, device_id_type=MESH,
        ).start()

    def result(piece, start, count, lane=0, width=256):
        name = piece.name
        start = pl.multiple_of(start, 8)
        if name == LT:
            return summed.at[pl.ds(start, count), pl.ds(lane, width)]
        if name == SC:
            return dsc_h.at[pl.ds(start, count), pl.ds(lane, width)]
        if name >= SA:
            return dsa.at[pl.ds(768 * (name - SA) + start, count), pl.ds(lane, width)]
        return dsb.at[pl.ds(768 * (name - SB) + start, count), pl.ds(lane, width)]

    def own_copies(piece):
        count, sem = piece.counts[-1], own_sem.at[piece.index]
        return [
            pltpu.make_async_copy(
                span(piece, start[-1], count, 128 * side, 128),
                result(piece, start[-1], count, 128 * side, 128),
                sem.at[side],
            )
            for side, start in enumerate(piece.starts)
        ]

    def arrived(piece, step, rows_in):
        block = span(piece, 0, rows_in) if step < piece.steps else result(piece, 0, rows_in)
        copy = pltpu.make_async_remote_copy(
            src_ref=block, dst_ref=block, send_sem=big_send.at[piece.index],
            recv_sem=big_recv.at[piece.index, step], device_id=core_peer, device_id_type=MESH,
        )
        copy.wait_recv()
        copy.wait_send()

    def add_rows(piece, target, source, count, lane, width):
        lanes = pl.ds(piece.lane + lane, width)
        chunk = piece.size // 32
        ref = piece.ref

        def step(i):
            into = pl.ds(pl.multiple_of(target + i * chunk, 8), chunk)
            ref[into, lanes] = ref[into, lanes] + ref[pl.ds(pl.multiple_of(source + i * chunk, 8), chunk), lanes]

        loop(count // chunk, step)

    order = range(10)

    def unpack_small():
        stores.append(store(summed.at[:, pl.ds(0, 128)], dl_h.at[pl.ds(0, 768)], 16))
        stores.append(store(summed.at[pl.ds(0, 512), pl.ds(128, 128)], dl_h.at[pl.ds(768, 512)], 17))
        stores.append(store(summed.at[pl.ds(512, 256), pl.ds(128, 128)], small_h, 18))

    polled = [0]

    def poll():
        polled[0] += 1
        for name in POLLS[polled[0] - 1]:
            advance(name)

    def done(name):
        return pieces[name].step > 2 * pieces[name].steps

    def advance(name):
        piece = pieces[name]
        step, steps, index = piece.step, piece.steps, piece.index
        piece.step = step + 1
        starts, counts, arriving, axes = piece.starts, piece.counts, piece.arriving, piece.axes
        ref, lane = piece.ref, piece.lane

        def received(last):
            fan = 3 if axes[0][last] == Z else 1
            return fan * counts[last + 1]

        if 0 < step < steps or (step == steps and axes[0][-1] != Z):
            arrived(piece, step - 1, received(step - 1))
            if step == 1:
                add_rows(piece, starts[0][1], arriving[0], counts[1], 0, 256)
            else:
                for side in range(2):
                    add_rows(piece, starts[side][step], arriving[step - 1], counts[step], 128 * side, 128)
        elif step == steps:
            arrived(piece, step - 1, received(step - 1))
        elif step > steps:
            arrived(piece, step - 1, received(2 * steps - step))

        if step < steps:
            held, keep = counts[step], counts[step + 1]
            if step == 0:
                at = starts[0][0] + (1 - c) * keep
                send(piece, 0, span(piece, at, keep), span(piece, arriving[0], keep), core_peer)
                return
            for side in range(2):
                axis, start = axes[side][step], starts[side][step]
                if axis == Z:
                    for k, peer in enumerate(z_peers):
                        at, into = start + lax.rem(z + k + 1, 4) * keep, arriving[step] + k * keep
                        send(
                            piece, step, span(piece, at, keep, 128 * side, 128),
                            span(piece, into, keep, 128 * side, 128), peer,
                        )
                else:
                    bit, peer = bits[axis]
                    at = start + (1 - bit) * keep
                    send(
                        piece, step, span(piece, at, keep, 128 * side, 128),
                        span(piece, arriving[step], keep, 128 * side, 128), peer,
                    )
        elif step == steps:
            last = counts[-1]
            own = [
                (pl.ds(pl.multiple_of(starts[side][-1], 8), last), pl.ds(lane + 128 * side, 128))
                for side in range(2)
            ]
            both = jnp.concatenate([ref[own[0]], ref[own[1]]], axis=1)
            if axes[0][-1] == Z:
                for k in range(3):
                    both = both + ref[pl.ds(arriving[steps - 1] + k * last, last), pl.ds(lane, 256)]
            if outers > 1:
                held = span(piece, arriving[steps - 1], last)
                ref[pl.ds(arriving[steps - 1], last), pl.ds(lane, 256)] = both
                for peer in outer_peers:
                    send(piece, 10, held, extra_h.at[index, outer, pl.ds(0, last)], peer)
                block = extra_h.at[index, pl.ds(0, outers - 1), pl.ds(0, last)]
                copy = pltpu.make_async_remote_copy(
                    src_ref=block, dst_ref=block, send_sem=big_send.at[index], recv_sem=big_recv.at[index, 10],
                    device_id=core_peer, device_id_type=MESH,
                )
                copy.wait_recv()
                copy.wait_send()
                local = [(held, extra_h.at[index, outer, pl.ds(0, last)])]
                for k in range(outers):
                    local.append((extra_h.at[index, k, pl.ds(0, last)], span(piece, arriving[0] + k * last, last)))
                for src, dst in local:
                    copy = pltpu.make_async_copy(src, dst, own_sem.at[index, 0])
                    copy.start()
                    copy.wait()
                both = ref[pl.ds(arriving[0], last), pl.ds(lane, 256)]
                for k in range(1, outers):
                    both = both + ref[pl.ds(arriving[0] + k * last, last), pl.ds(lane, 256)]
            both = both * factor
            for side in range(2):
                ref[own[side]] = both[:, 128 * side : 128 * (side + 1)]
        if steps <= step < 2 * steps:
            back = 2 * steps - 1 - step
            count = counts[back + 1]
            if step == steps + 1:
                for copy in own_copies(piece):
                    copy.wait()
            if back == 0:
                block = result(piece, starts[0][1], count)
                send(piece, step, block, block, core_peer)
                return
            for side in range(2):
                axis, start = axes[side][back], starts[side][back + 1]
                block = result(piece, start, count, 128 * side, 128)
                source = span(piece, start, count, 128 * side, 128) if step == steps else block
                for peer in z_peers if axis == Z else [bits[axis][1]]:
                    send(piece, step, source, block, peer)
            if step == steps:
                for copy in own_copies(piece):
                    copy.start()
        elif step == 2 * steps and name == LT:
            unpack_small()

    spots = {FC: 0, LAT: 1, SLOW_A: 3, SLOW_B: 5, SLOW_C: 7, FA: 16, FB: 17}

    lane16 = lax.broadcasted_iota(jnp.int32, (16, LANES), 1)

    def unpack(packed):
        fa = fold_lanes(jnp.where(lane16 // 32 == 0, packed, 0.0))[0:1, :]
        fb = fold_lanes(jnp.where(lane16 // 32 == 1, packed, 0.0))[0:1, :]
        turned = pltpu.roll(packed, 64, 1)
        moved = jnp.where(lane16 < 64, turned, pltpu.roll(turned, 15, 0))
        found = {FA: fa, FB: fb}
        at = 0
        for name, count in ((FC, 1), (LAT, 2), (SLOW_A, 2), (SLOW_B, 2), (SLOW_C, 8)):
            found[name] = jnp.concatenate([moved[at + k : at + k + 1, :] for k in range(count)], axis=1)
            at += count
        return found

    held = [0]

    def settle(vector):
        at, width = held[0], vector.shape[1]
        held[0] += 1
        line, row = at // 8, slice(at % 8, at % 8 + 1)
        vectors[line, row, 0:width] = vector

        def read(lanes=slice(0, width)):
            return vectors[line, row, lanes]

        return read

    gains, biases = {}, {}

    def read_parameters():
        for name, flat_in, target in (("gains", gains_in, gains), ("biases", biases_in, biases)):
            loads[name].wait()
            count = flat_in.shape[0]
            stage_a[0:16, :] = jnp.zeros((16, LANES), F32)
            for row in range(16):
                width = min(LANES, count - row * LANES)
                stage_a[row : row + 1, 0:width] = flat_in[pl.ds(row * LANES, width)].reshape(1, width)
            for key, vector in unpack(stage_a[0:16, :]).items():
                target[key] = settle(vector)

    def gain(name):
        return gains[name]()

    def bias(name):
        return biases[name]()

    def moments(name, total, squares, count, *lanes):
        mean = total * (1.0 / count)
        scale = lax.rsqrt(squares * (1.0 / count) - mean * mean + EPS)
        return settle(mean), settle(scale), settle(0.5 * gains[name](*lanes) * scale), settle(0.5 * biases[name](*lanes))

    def back_vectors(name, stats, bias_total, gain_total, count):
        mean, scale = stats[0](), stats[1]()
        lead = gain(name) * scale
        tilt = lead * scale * gain_total * (1.0 / count)
        level = lead * bias_total * (1.0 / count) - mean * tilt
        return settle(lead), settle(level), settle(tilt)

    def report(name, bias_total, gain_total, skip=0):
        at = spots[name] + skip
        for piece in range(bias_total.shape[1] // LANES):
            lanes = slice(piece * LANES, (piece + 1) * LANES)
            gain_rows[at + piece : at + piece + 1, :] = gain_total[:, lanes]
            bias_rows[at + piece : at + piece + 1, :] = bias_total[:, lanes]

    def silu_of(values, stats):
        h = (values - stats[0]()) * stats[2]() + stats[3]()
        return h + h * jnp.tanh(h)

    def slope_of(h):
        t = jnp.tanh(h)
        out, gate = h + h * t, 0.5 + 0.5 * t
        return out, gate + out * (1.0 - gate)

    def clip_masks(width):
        frame = lax.broadcasted_iota(jnp.int32, (1, 8, width), 1)
        with_prev = jnp.zeros((1, 8, width), F32)
        with_next = jnp.zeros((1, 8, width), F32)
        for t in range(1, frames):
            same = jnp.where(clip[0, t] == clip[0, t - 1], 1.0, 0.0)
            with_prev = jnp.where(frame == t, same, with_prev)
            with_next = jnp.where(frame == t - 1, same, with_next)
        return with_prev, with_next

    masks[0:1], masks[1:2] = clip_masks(256)

    def prev(width):
        return masks[0:1, :, 0:width]

    def following(width):
        return masks[1:2, :, 0:width]

    def roll_frames(values, mask, step, mask_first):
        grouped = values.reshape(values.shape[0] // 8, 8, values.shape[1])
        if mask_first:
            grouped = grouped * mask
        grouped = pltpu.roll(grouped, step % 8, 1)
        if not mask_first:
            grouped = grouped * mask
        return grouped.reshape(values.shape)

    def spread_columns(target, index, values):
        width = values.shape[1]
        nothing = jnp.zeros((frames, width), F32)
        at = pl.ds(pl.multiple_of((index + 1) * band, 16), band)
        target[at, 0:width] = jnp.concatenate([nothing, values[: band - frames]], axis=0).astype(BF16)
        target[at, width : 2 * width] = values.astype(BF16)
        target[at, 2 * width :] = jnp.concatenate([values[frames:], nothing], axis=0).astype(BF16)

    gain_rows[...] = jnp.zeros(gain_rows.shape, F32)
    bias_rows[...] = jnp.zeros(bias_rows.shape, F32)
    for target in (hcs, gcs, hcf, gcf):
        edge = jnp.zeros((band, target.shape[1]), BF16)
        target[0:band, :] = edge
        target[band + rows : rows + 2 * band, :] = edge

    def lane_groups(count=LANES):
        return lax.broadcasted_iota(jnp.int32, (count, LANES), 1) // 32

    def block_mask():
        row_group = lax.broadcasted_iota(jnp.int32, (LANES, LANES), 0) // 32
        return jnp.where(lane_groups() == row_group, 1.0, 0.0)

    repeat_lanes = jnp.where(
        lax.broadcasted_iota(jnp.int32, (32, LANES), 1) % 32 == lax.broadcasted_iota(jnp.int32, (32, LANES), 0),
        1.0, 0.0,
    ).astype(BF16)

    wfa[...] = jnp.zeros(wfa.shape, BF16)
    loads["wfa"].wait()
    for phase in range(4):
        for k in range(3):
            wfa[32 * phase : 32 * (phase + 1), LANES * (phase + k) : LANES * (phase + k + 1)] = wfa_in[
                32 * k : 32 * (k + 1), :
            ]
    loads["xf"].wait()

    def arrange(i):
        at = rows_at(i, band)
        stage_a[...] = xf[rows_at(i, fband), :].astype(F32)
        phases = [stage_a[pl.ds(phase, band, stride=4), :] for phase in range(4)]
        vx[at, 0:128] = roll_frames(phases[2], prev(128), 1, False).astype(BF16)
        vx[at, 128:256] = roll_frames(phases[3], prev(128), 1, False).astype(BF16)
        for phase in range(4):
            vx[at, 256 + 128 * phase : 384 + 128 * phase] = phases[phase].astype(BF16)
        vx[at, 768:896] = roll_frames(phases[0], following(128), -1, False).astype(BF16)

    loop(bands, arrange, unroll=2)
    for tap in taps:
        tap.wait()

    def zero2(width):
        return (jnp.zeros((8, width), F32), jnp.zeros((8, width), F32))

    def conv_fa(i, carry):
        at = rows_at(i, half)
        value = dot(vx[at, 128:896], wfa[...], NT)
        sec_fa[at, :] = value
        return carry[0] + column_sums(value), carry[1] + column_sums(value * value)

    def conv_lat(i, carry):
        at = rows_at(i, half)
        value = dot(vx[at, 0:640], wlat[...], NT)
        sec_lat[at, :] = value
        return carry[0] + column_sums(value), carry[1] + column_sums(value * value)

    sum_lat, sq_lat = loop(2, conv_lat, zero2(256))
    put(LAT, 0, squash(sum_lat))
    put(LAT, 256, squash(sq_lat))
    pl.semaphore_wait(barrier, len(greeted))
    exchange_start(LAT)

    sum_fa, sq_fa = loop(2, conv_fa, zero2(128))
    put(FA, 0, pair32(squash(sum_fa), squash(sq_fa)))
    exchange_start(FA)

    loads["xs"].wait()
    loads["wsa"].wait()

    def narrow_main(i):
        at = rows_at(i, half)
        for k in range(3):
            big[at, bs * k : bs * (k + 1)] = dot(xs[at, :], wsa[bs * k : bs * (k + 1), 0:cs_n], NT)

    loop(2, narrow_main)
    loads["wfb"].wait()
    loads["wfc"].wait()
    spread = dot(wfb_in[...], repeat_lanes, NN)
    for a in range(3):
        for b in range(3):
            piece = spread[32 * (3 * a + b) : 32 * (3 * a + b + 1), :]
            block = (jnp.concatenate([piece] * 4, axis=0) * block_mask()).astype(BF16)
            wfb[a, :, LANES * b : LANES * (b + 1)] = block
            wfbk[a, LANES * (2 - b) : LANES * (3 - b), :] = block
    widen = dot(wfc_in[...], repeat_lanes, TN)
    for phase in range(4):
        wfc[LANES * phase : LANES * (phase + 1), :] = jnp.where(lane_groups() == phase, widen, 0.0).astype(BF16)
    read_parameters()
    total = exchange_end(LAT)

    stats_lat = moments(LAT, take(total, 0, 256), take(total, 256, 256), slow_count)

    def act_fa(i):
        spread_columns(hcf, i, silu_of(sec_fa[rows_at(i, band), :], stats_fa))

    def act_lat(i):
        at = rows_at(i, 2 * band)
        jl[at, :] = silu_of(sec_lat[at, :], stats_lat).astype(BF16)

    loop(bands // 2, act_lat)

    def conv_fb(i, carry):
        value = None
        for a in range(3):
            at = pl.ds(pl.multiple_of(i * half + band * a, 16), half)
            term = dot(hcf[at, :], wfb[a], NT)
            value = term if value is None else value + term
        sec_fb[rows_at(i, half), :] = value
        return carry[0] + column_sums(value), carry[1] + column_sums(value * value)

    def combine_sa(i, carry):
        at = rows_at(i, half)

        def tap(k):
            lanes = slice(bs * k, bs * (k + 1))
            return big[at, lanes] + dot(jl[at, :], wsa[lanes, cs_n:], NT)

        value = roll_frames(tap(0), prev(256), 1, False)
        value = value + tap(1)
        value = value + roll_frames(tap(2), following(256), -1, False)
        sec_sa[at, :] = value
        return carry[0] + column_sums(value), carry[1] + column_sums(value * value)

    sum_sa, sq_sa = loop(2, combine_sa, zero2(256))
    put(SLOW_A, 0, squash(sum_sa))
    put(SLOW_A, 256, squash(sq_sa))
    exchange_start(SLOW_A)

    total = exchange_end(FA)
    stats_fa = moments(FA, *unpair32(total), fast_count)
    loop(bands, act_fa, unroll=2)
    sum_fb, sq_fb = loop(2, conv_fb, zero2(128))
    put(FB, 0, pair32(squash(sum_fb), squash(sq_fb)))
    exchange_start(FB)
    total = exchange_end(SLOW_A)

    stats_sa = moments(SLOW_A, take(total, 0, 256), take(total, 256, 256), slow_count)

    def act_sa(i):
        spread_columns(hcs, i, silu_of(sec_sa[rows_at(i, band), :], stats_sa))

    def act_fb(i):
        at = rows_at(i, 2 * band)
        hbf[at, :] = silu_of(sec_fb[at, :], stats_fb).astype(BF16)

    loop(bands, act_sa, unroll=2)
    loads["wsb"].wait()

    def conv_sb(i, carry):
        value = None
        for a in range(3):
            at = pl.ds(pl.multiple_of(i * half + band * a, 16), half)
            for b in range(3):
                tap = 3 * a + b
                term = dot(hcs[at, bs * b : bs * (b + 1)], wsb[bs * tap : bs * (tap + 1), :], NT)
                value = term if value is None else value + term
        sec_sb[rows_at(i, half), :] = value
        return carry[0] + column_sums(value), carry[1] + column_sums(value * value)

    sum_sb, sq_sb = loop(2, conv_sb, zero2(256))
    put(SLOW_B, 0, squash(sum_sb))
    put(SLOW_B, 256, squash(sq_sb))
    exchange_start(SLOW_B)

    total = exchange_end(FB)
    stats_fb = moments(FB, *unpair32(total), fast_count)
    loop(bands // 2, act_fb)

    def widen_fast(i, carry):
        at = rows_at(i, half)
        value = dot(hbf[at, :], wfc[...], NT)
        sec_fc[at, :] = value
        return carry[0] + column_sums(value), carry[1] + column_sums(value * value)

    sum_fc, sq_fc = loop(2, widen_fast, zero2(512))

    def fold4(vector):
        return vector[:, 0:128] + vector[:, 128:256] + vector[:, 256:384] + vector[:, 384:512]

    put(FC, 0, squash(fold4(sum_fc)))
    put(FC, 128, squash(fold4(sq_fc)))
    exchange_start(FC)
    total = exchange_end(SLOW_B)

    stats_sb = moments(SLOW_B, take(total, 0, 256), take(total, 256, 256), slow_count)

    def act_sb(i, carry):
        at = rows_at(i, 2 * band)
        value = silu_of(sec_sb[at, :], stats_sb).astype(BF16)
        hbs[at, :] = value
        return carry + column_sums(value.astype(F32))

    sum_hbs = loop(bands // 2, act_sb, jnp.zeros((8, bs), F32))
    loads["wsc"].wait()
    mid = cs_n // 2

    def widen_slow(part):
        lanes = slice(part * mid, (part + 1) * mid)

        def step(i, carry):
            at = rows_at(i, half)
            value = dot(hbs[at, :], wsc[lanes, :], NT)
            big[at, lanes] = value
            return carry + column_sums(value * value)

        return loop(2, step, jnp.zeros((8, mid), F32))

    put(SLOW_C, 0, squash(sum_hbs))
    put(SLOW_C, 256, squash(widen_slow(0)))
    exchange_start(SLOW_C)
    put(SLOW_C + 1, 0, squash(widen_slow(1)))
    exchange_start(SLOW_C + 1)
    total = exchange_end(FC)
    stats_fc = moments(FC, take(total, 0, 128), take(total, 128, 128), fast_count)

    loads["cf"].wait()

    def finish_fast(i, carry):
        at, fat = rows_at(i, band), rows_at(i, fband)
        bias_sum, gain_sum = carry
        dbuf_f[0:fband, :] = cf[fat, :].astype(F32)
        for phase in range(4):
            lanes = slice(128 * phase, 128 * (phase + 1))
            centred = sec_fc[at, lanes] - stats_fc[0]()
            total_in = vx[at, 256 + 128 * phase : 384 + 128 * phase].astype(F32)
            out, slope = slope_of(0.5 * total_in + (centred * stats_fc[2]() + stats_fc[3]()))
            stage_a[pl.ds(phase, band, stride=4), :] = out
            grad = dbuf_f[pl.ds(phase, band, stride=4), :] * slope
            gsf[at, lanes] = grad
            bias_sum = bias_sum + column_sums(grad)
            gain_sum = gain_sum + column_sums(grad * centred)
        cf[fat, :] = stage_a[...].astype(BF16)
        return bias_sum, gain_sum

    bias_fc, gain_fc = loop(bands, finish_fast, zero2(128))
    put(BACK + FC, 0, squash(bias_fc))
    put(BACK + FC, 128, squash(gain_fc) * stats_fc[1]())
    exchange_start(BACK + FC)
    loads["cs"].wait()
    total = exchange_end(SLOW_C)
    squares = [take(total, 256, mid)]
    rest, row = take(total, 0, 256), lax.broadcasted_iota(jnp.int32, (16, bs), 0)
    parts = jnp.zeros((16, bs), F32)
    for k in range(3):
        part_k = rest.astype(BF16).astype(F32)
        parts = jnp.where(row == k, part_k, parts)
        rest = rest - part_k
    whole = settle(squash(dot(parts.astype(BF16), wsc[...], NT)))
    stats_sc = []

    def finish_slow(part):
        lanes = slice(part * mid, (part + 1) * mid)
        def step(i, carry):
            at = rows_at(i, band)
            mean, lead, level = [stats_sc[part][k]() for k in (0, 2, 3)]
            centred = big[at, lanes] - mean
            out, slope = slope_of(0.5 * xs[at, lanes].astype(F32) + (centred * lead + level))
            grad = cs[at, lanes].astype(F32) * slope
            cs[at, lanes] = out.astype(BF16)
            gsum[at, lanes] = centred.astype(BF16)
            big[at, lanes] = grad
            return carry[0] + column_sums(grad), carry[1] + column_sums(grad * centred)

        bias_part, gain_part = loop(bands, step, zero2(mid))
        return squash(bias_part), squash(gain_part) * stats_sc[part][1]()

    for part in range(2):
        if part:
            squares.append(exchange_end(SLOW_C + 1))
        lanes = slice(part * mid, (part + 1) * mid)
        stats_sc.append(moments(SLOW_C, whole(lanes), squares[part], slow_count, lanes))
        bias_part, gain_part = finish_slow(part)
        put(BACK + SLOW_C + part, 0, bias_part)
        put(BACK + SLOW_C + part, mid, gain_part)
        exchange_start(BACK + SLOW_C + part)
    slow_store = store(cs, slow_h, 11)

    total = exchange_end(BACK + FC)
    bias_fc, gain_fc = take(total, 0, 128), take(total, 128, 128)
    report(FC, bias_fc, gain_fc)
    def slope_pass(section, stats, buffer):
        def step(i, carry):
            at = rows_at(i, 2 * band)
            centred = section[at, :] - stats[0]()
            grad = buffer[at, :] * slope_of(centred * stats[2]() + stats[3]())[1]
            buffer[at, :] = grad
            return carry[0] + column_sums(grad), carry[1] + column_sums(grad * centred)

        bias_sum, gain_sum = loop(bands // 2, step, zero2(section.shape[1]))
        return squash(bias_sum), squash(gain_sum) * stats[1]()

    lead_fc, level_fc, tilt_fc = back_vectors(FC, stats_fc, bias_fc, gain_fc, fast_count)

    def low_fc(i):
        at = rows_at(i, band)
        for phase in range(4):
            lanes = slice(128 * phase, 128 * (phase + 1))
            value = gsf[at, lanes] * lead_fc() - level_fc() - sec_fc[at, lanes] * tilt_fc()
            gcs[at, lanes] = value.astype(BF16)

    loop(bands, low_fc, unroll=2)

    def back_fc(i):
        at = rows_at(i, half)
        dbuf_f[at, :] = dot(gcs[at, 0:512], wfc[...], NN)

    loop(2, back_fc)
    bias_fb, gain_fb = slope_pass(sec_fb, stats_fb, dbuf_f)
    put(BACK + FB, 0, pair32(bias_fb, gain_fb))
    exchange_start(BACK + FB)
    slow_store.wait()

    def back_widen(part):
        lanes = slice(part * mid, (part + 1) * mid)
        total = exchange_end(BACK + SLOW_C + part)
        bias_sc, gain_sc = take(total, 0, mid), take(total, mid, mid)
        report(SLOW_C, bias_sc, gain_sc, part * (mid // LANES))
        scale = stats_sc[part][1]()
        lead = gains[SLOW_C](lanes) * scale
        tilt_sc = settle(lead * scale * gain_sc * (1.0 / slow_count))
        level_sc = settle(lead * bias_sc * (1.0 / slow_count))
        lead_sc = settle(lead)

        def low_sc(i):
            at = rows_at(i, 32)
            grad = big[at, lanes]
            cs[at, lanes] = (grad * lead_sc() - level_sc() - gsum[at, lanes].astype(F32) * tilt_sc()).astype(BF16)
            gsum[at, lanes] = grad.astype(BF16)

        loop(rows // 32, low_sc, unroll=7)

        def back_sc(i):
            at = rows_at(i, half)
            value = dot(cs[at, lanes], wsc[lanes, :], NN)
            dbuf[at, :] = dbuf[at, :] + value if part else value

        loop(2, back_sc)

    for part in range(2):
        back_widen(part)
    bias_sb, gain_sb = slope_pass(sec_sb, stats_sb, dbuf)

    put(BACK + SLOW_B, 0, bias_sb)
    put(BACK + SLOW_B, 256, gain_sb)
    exchange_start(BACK + SLOW_B)

    slab_sc[0:cs_n, :] = dot(cs[...], hbs[...], TN)
    advance(SC)
    widening = None
    for phase in range(4):
        term = dot(hbf[...], gcs[0:rows, 128 * phase : 128 * (phase + 1)], TN)[32 * phase : 32 * (phase + 1), :]
        widening = term if widening is None else widening + term
    slab[2, 704:736, 128:256] = widening
    slab[2, 736:768, 128:256] = jnp.zeros((32, LANES), F32)
    poll()

    bias_fb, gain_fb = unpair32(exchange_end(BACK + FB))
    report(FB, bias_fb, gain_fb)
    vec_fb = back_vectors(FB, stats_fb, bias_fb, gain_fb, fast_count)

    def norm_grad(buffer, section, at, vectors):
        lead, level, tilt = vectors
        return buffer[at, :] * lead() - level() - section[at, :] * tilt()

    def low_fb(i):
        spread_columns(gcf, i, norm_grad(dbuf_f, sec_fb, rows_at(i, band), vec_fb))

    loop(bands, low_fb, unroll=2)

    def back_fb(i):
        value = None
        for a in range(3):
            at = pl.ds(pl.multiple_of(i * half + band * (2 - a), 16), half)
            term = dot(gcf[at, :], wfbk[a], NN)
            value = term if value is None else value + term
        dbuf_f[rows_at(i, half), :] = value

    loop(2, back_fb)
    poll()
    bias_fa, gain_fa = slope_pass(sec_fa, stats_fa, dbuf_f)
    put(BACK + FA, 0, pair32(bias_fa, gain_fa))
    exchange_start(BACK + FA)
    poll()
    total = exchange_end(BACK + SLOW_B)

    bias_sb, gain_sb = take(total, 0, 256), take(total, 256, 256)
    report(SLOW_B, bias_sb, gain_sb)
    vec_sb = back_vectors(SLOW_B, stats_sb, bias_sb, gain_sb, slow_count)

    gcs[0:band, :] = jnp.zeros((band, gcs.shape[1]), BF16)

    def low_sb(i):
        spread_columns(gcs, i, norm_grad(dbuf, sec_sb, rows_at(i, band), vec_sb))

    loop(bands, low_sb, unroll=2)
    poll()

    def back_sb(i):
        value = None
        for a in range(3):
            at = pl.ds(pl.multiple_of(i * half + band * (2 - a), 16), half)
            for b in range(3):
                tap = 3 * a + b
                term = dot(gcs[at, bs * (2 - b) : bs * (3 - b)], wsb[bs * tap : bs * (tap + 1), :], NN)
                value = term if value is None else value + term
        dbuf[rows_at(i, half), :] = value

    for part in range(2):
        back_sb(part)
        poll()
    bias_sa, gain_sa = slope_pass(sec_sa, stats_sa, dbuf)

    put(BACK + SLOW_A, 0, bias_sa)
    put(BACK + SLOW_A, 256, gain_sa)
    exchange_start(BACK + SLOW_A)
    poll()

    for a in range(3):
        value = dot(gcs[band : band + rows, bs : 2 * bs], hcs[band * a : band * a + rows, :], TN)
        ref, lane = pieces[SB + a].ref, pieces[SB + a].lane
        for b in range(3):
            ref[bs * b : bs * (b + 1), lane : lane + bs] = value[:, bs * b : bs * (b + 1)]
        advance(SB + a)
        poll()
    for a in range(3):
        value = dot(gcf[band : band + rows, 128:256], hcf[band * a : band * a + rows, :], TN)
        for b in range(3):
            tap = 3 * a + b
            block = value[:, 128 * b : 128 * (b + 1)] * block_mask()
            folded = fold_lanes(block[0:32] + block[32:64] + block[64:96] + block[96:128])
            folded = jnp.where(lane_groups(32) == tap % 4, folded, 0.0)
            at = slice(608 + 32 * (tap // 4), 640 + 32 * (tap // 4))
            slab[2, at, 128:256] = folded if tap % 4 == 0 else slab[2, at, 128:256] + folded
    poll()
    poll()
    total = exchange_end(BACK + SLOW_A)
    poll()

    bias_sa, gain_sa = take(total, 0, 256), take(total, 256, 256)
    report(SLOW_A, bias_sa, gain_sa)
    vec_sa = back_vectors(SLOW_A, stats_sa, bias_sa, gain_sa, slow_count)
    def low_sa(i):
        at = rows_at(i, band)
        value = norm_grad(dbuf, sec_sa, at, vec_sa)
        gcs[at, 0:bs] = roll_frames(value, prev(256), -1, True).astype(BF16)
        gcs[at, bs : 2 * bs] = value.astype(BF16)
        gcs[at, 2 * bs :] = roll_frames(value, following(256), 1, True).astype(BF16)

    loop(bands, low_sa, unroll=2)
    poll()

    def narrow_gradient(k):
        ref, lane = pieces[SA + k].ref, pieces[SA + k].lane
        source = xs[:, 256 * k : 256 * (k + 1)] if k < 4 else jl[...]
        ref[0 : 3 * bs, lane : lane + 256] = dot(gcs[0:rows, :], source, TN)
        advance(SA + k)

    narrow_gradient(0)
    poll()

    def back_lateral(i):
        at = rows_at(i, half)
        dbuf[at, :] = dot(gcs[at, :], wsa[:, cs_n:], NN)

    loop(2, back_lateral)
    poll()
    bias_lat, gain_lat = slope_pass(sec_lat, stats_lat, dbuf)
    put(BACK + LAT, 0, bias_lat)
    put(BACK + LAT, 256, gain_lat)
    exchange_start(BACK + LAT)
    bias_fa, gain_fa = unpair32(exchange_end(BACK + FA))
    report(FA, bias_fa, gain_fa)
    vec_fa = back_vectors(FA, stats_fa, bias_fa, gain_fa, fast_count)

    def low_fa(i):
        at = rows_at(i, band)
        hbf[at, :] = norm_grad(dbuf_f, sec_fa, at, vec_fa).astype(BF16)

    loop(bands, low_fa, unroll=2)
    value = dot(hbf[...], vx[:, 128:896], TN)
    for k in range(3):
        piece = None
        for phase in range(4):
            term = value[32 * phase : 32 * (phase + 1), 128 * (phase + k) : 128 * (phase + k + 1)]
            piece = term if piece is None else piece + term
        slab[2, 512 + 32 * k : 544 + 32 * k, 128:256] = piece

    poll()

    for k in range(1, 4):
        narrow_gradient(k)
        poll()
    total = exchange_end(BACK + LAT)

    bias_lat, gain_lat = take(total, 0, 256), take(total, 256, 256)
    report(LAT, bias_lat, gain_lat)

    def pack(rows_ref, target):
        lanes = lax.broadcasted_iota(jnp.int32, (24, LANES), 1)
        stacked = rows_ref[...]
        turned = pltpu.roll(stacked, 64, 1)
        moved = jnp.where(lanes >= 64, turned, pltpu.roll(turned, 1, 0))[0:16, :]
        first = jnp.where(lane16[0:1, :] < 32, stacked[16:17, :], stacked[17:18, :])
        first = jnp.where(lane16[0:1, :] < 64, first, moved[0:1, :])
        target[...] = moved * factor
        target[0:1, :] = first * factor

    pack(gain_rows, dbuf_f.at[pl.ds(0, 16)])
    pack(bias_rows, dbuf_f.at[pl.ds(16, 16)])
    parameter_stores = [
        store(dbuf_f.at[pl.ds(0, 16)], dgains_h, 19), store(dbuf_f.at[pl.ds(16, 16)], dbiases_h, 20)
    ]
    vec_lat = back_vectors(LAT, stats_lat, bias_lat, gain_lat, slow_count)

    def low_lat(i):
        at = rows_at(i, band)
        hbs[at, :] = norm_grad(dbuf, sec_lat, at, vec_lat).astype(BF16)

    loop(bands, low_lat, unroll=2)
    value = dot(hbs[...], vx[:, 0:640], TN)
    for k in range(5):
        at, lane = 256 * (k % 3), 128 * (k // 3)
        slab[2, at : at + 256, lane : lane + 128] = value[:, 128 * k : 128 * (k + 1)]
    advance(LT)
    poll()
    narrow_gradient(4)
    poll()

    def slow_back(i):
        at = rows_at(i, half)
        for tile in range(cs_n // 256):
            lanes = slice(256 * tile, 256 * (tile + 1))
            value = gsum[at, lanes].astype(F32) + dot(gcs[at, :], wsa[:, lanes], NN)
            gsum[at, lanes] = value.astype(BF16)

    for part in range(2):
        slow_back(part)
        poll()


    def fast_back(i):
        at, fat = rows_at(i, 2 * band), rows_at(i, 2 * fband)
        conv = dot(hbf[at, :], wfa[...], NN)
        side_in = dot(hbs[at, :], wlat[...], NN)

        def lane(values, block):
            return values[:, 128 * block : 128 * (block + 1)]

        grads = [gsf[at, 128 * phase : 128 * (phase + 1)] + lane(conv, phase + 1) for phase in range(4)]
        grads[0] = grads[0] + roll_frames(lane(conv, 5), following(128), 1, True) + lane(side_in, 2)
        grads[1] = grads[1] + lane(side_in, 3)
        grads[2] = grads[2] + lane(side_in, 4) + roll_frames(lane(side_in, 0), prev(128), -1, True)
        grads[3] = grads[3] + roll_frames(lane(side_in, 1) + lane(conv, 0), prev(128), -1, True)
        for part in range(2):
            for phase in range(4):
                stage_a[pl.ds(phase, band, stride=4), :] = grads[phase][part * band : (part + 1) * band]
            xf[rows_at(2 * i + part, fband), :] = stage_a[...].astype(BF16)

    third = bands // 6
    loop(third, fast_back)
    poll()
    loop(third, lambda i: fast_back(i + third))
    poll()
    loop(bands // 2 - 2 * third, lambda i: fast_back(i + 2 * third))
    poll()

    poll()
    while not all(done(name) for name in order):
        for name in order:
            if not done(name):
                advance(name)
    for copy in stores + parameter_stores:
        copy.wait()


def hand_on(*refs):
    sources, targets, staged, small, sem = refs[0:11], refs[11:24], refs[24:30], refs[30:35], refs[35]
    held = staged[0:1] + sources[1:6] + staged[1:6]
    loads = {k: pltpu.make_async_copy(sources[k], held[k], sem.at[k]) for k in (8, 9, 10, 0, 6, 7)}
    stores = {k: pltpu.make_async_copy(held[k], targets[k], sem.at[11 + k]) for k in (0, 1, 2, 3, 5, 6, 7)}
    for k in range(5):
        stores[8 + k] = pltpu.make_async_copy(small[k], targets[8 + k], sem.at[19 + k])
        stores[13 + k] = pltpu.make_async_copy(
            held[4].at[pl.ds(768 * k, 768)], targets[4].at[:, pl.ds(256 * k, 256)], sem.at[24 + k]
        )
    for copy in loads.values():
        copy.start()
    for k in (1, 2, 3, 5, 13, 14, 15, 16, 17):
        stores[k].start()
    for k in (8, 9, 10):
        loads[k].wait()
    small[0][...] = held[8][0:96, :]
    for tap in range(9):
        at = 96 + 32 * (tap // 4)
        small[1][32 * tap : 32 * (tap + 1), :] = held[8][at : at + 32, 32 * (tap % 4) : 32 * (tap % 4 + 1)]
    small[2][...] = held[8][192:224, :]
    for source, target in ((held[9], small[3]), (held[10], small[4])):
        count = target.shape[0]
        for row in range(16):
            width = min(LANES, count - row * LANES)
            target[pl.ds(row * LANES, width)] = source[row : row + 1, 0:width].reshape(width)
    for k in range(8, 13):
        stores[k].start()
    for k in (0, 6, 7):
        loads[k].wait()
        stores[k].start()
    for copy in stores.values():
        copy.wait()


def body(
    slow_input,
    fast_input,
    clip_ids,
    fast_narrow,
    fast_spatial,
    fast_widen,
    lateral_conv,
    slow_narrow,
    slow_spatial,
    slow_widen,
    norm_gains,
    norm_biases,
    slow_cotangent,
    fast_cotangent,
):
    n_dp, n_rep = lax.axis_size("dp"), lax.axis_size("rep")
    low = 2 if n_dp % 2 == 0 else 1
    high = n_dp // low
    frames, plane, channels = slow_input.shape
    fast_frames, _, fast_channels = fast_input.shape
    side = math.isqrt(plane)
    rows = frames * plane
    slow_count = rows * n_dp * n_rep
    fast_count = slow_count * (fast_frames // frames)

    def flat(values):
        return values.transpose(1, 0, 2).reshape(values.shape[0] * values.shape[1], values.shape[2])

    def unflat(values, count):
        return values.reshape(plane, count, values.shape[1]).transpose(1, 0, 2)

    widths = [
        fast_narrow.shape[1], fast_spatial.shape[1], fast_widen.shape[0], lateral_conv.shape[1],
        slow_narrow.shape[1], slow_spatial.shape[1], slow_widen.shape[0],
    ]

    cf = fast_channels
    bs = slow_spatial.shape[1]
    band = side * frames
    any_spec = pl.BlockSpec(memory_space=pl.ANY)
    vmem_spec = pl.BlockSpec(memory_space=pltpu.VMEM)
    near_low = n_dp if n_dp * n_rep <= 32 else low
    stages = 1 if near_low == n_dp else 2
    pad = rows + 2 * band

    def shape(dims, dtype):
        return jax.ShapeDtypeStruct(dims, dtype)

    out_shape = [
        shape((rows, channels), BF16), pltpu.VMEM((4 * rows, cf), BF16),
        pltpu.VMEM((rows, channels), BF16), pltpu.VMEM((4 * rows, cf), BF16),
        pltpu.VMEM((15 * bs, bs), F32), pltpu.VMEM((9 * bs, bs), F32), shape((channels, bs), F32),
        shape((5 * bs, cf), F32), shape((256, cf), F32), shape((16, LANES), F32), shape((16, LANES), F32),
        shape((10, max(high // 4, 1), 32, 256), F32),
    ]
    scratch = [
        pltpu.VMEM((rows, channels), BF16), pltpu.VMEM((rows, channels), BF16),
        pltpu.VMEM((rows, channels), F32),
        pltpu.VMEM((rows, 512), F32), pltpu.VMEM((rows, 512), F32),
        pltpu.VMEM((pad, 3 * bs), BF16), pltpu.VMEM((pad, 3 * bs), BF16),
        pltpu.VMEM((pad, 384), BF16), pltpu.VMEM((pad, 384), BF16),
        pltpu.VMEM((rows, bs), F32), pltpu.VMEM((rows, bs), F32),
        pltpu.VMEM((rows, 128), F32), pltpu.VMEM((rows, 128), F32), pltpu.VMEM((rows, 128), F32),
        pltpu.VMEM((rows, bs), BF16), pltpu.VMEM((rows, bs), BF16), pltpu.VMEM((rows, 128), BF16),
        pltpu.VMEM((rows, 896), BF16), pltpu.VMEM((3, 1512, 256), F32), pltpu.VMEM((2016, 256), F32),
        pltpu.VMEM((768, 256), F32),
        pltpu.VMEM((3 * bs, channels + bs), BF16), pltpu.VMEM((9 * bs, bs), BF16),
        pltpu.VMEM((channels, bs), BF16), pltpu.VMEM(norm_gains.shape, F32), pltpu.VMEM(norm_gains.shape, F32),
        pltpu.VMEM((9, 8, channels), F32), pltpu.VMEM((2, 8, 256), F32),
        pltpu.VMEM((96, cf), BF16), pltpu.VMEM((288, 32), BF16), pltpu.VMEM((32, cf), BF16),
        pltpu.VMEM((bs, 640), BF16), pltpu.VMEM((128, 768), BF16),
        pltpu.VMEM((3, 128, 384), BF16), pltpu.VMEM((3, 384, 128), BF16), pltpu.VMEM((512, 128), BF16),
        pltpu.VMEM((4 * band, cf), F32),
        pltpu.VMEM((24, LANES), F32), pltpu.VMEM((24, LANES), F32),
        pltpu.VMEM((near_low * n_rep, 1, sum(TURNS.values())), F32),
        pltpu.VMEM((max(n_dp // near_low, 1), 1, sum(TURNS.values())), F32),
        pltpu.SemaphoreType.DMA((stages, len(TURNS))), pltpu.SemaphoreType.DMA((stages, len(TURNS))),
        pltpu.SemaphoreType.DMA((32,)), pltpu.SemaphoreType.DMA((10, 2)),
        pltpu.SemaphoreType.DMA((10,)), pltpu.SemaphoreType.DMA((10, 10 if high == 4 else 11)),
    ]
    factor = 1.0 / math.sqrt(float(slow_count))
    results = pl.pallas_call(
        functools.partial(kernel, (n_dp, n_rep, low, frames, side, float(slow_count), float(fast_count), factor)),
        out_shape=out_shape,
        in_specs=[any_spec] * 4 + [pl.BlockSpec(memory_space=pltpu.SMEM)] + [any_spec] * 9,
        out_specs=[any_spec] + [vmem_spec] * 5 + [any_spec] * 6,
        scratch_shapes=scratch,
        compiler_params=pltpu.CompilerParams(
            collective_id=0, has_side_effects=True, vmem_limit_bytes=52960 * 2**10
        ),
    )(
        flat(slow_input), flat(fast_input), flat(slow_cotangent), flat(fast_cotangent), clip_ids,
        fast_narrow.reshape(-1, cf), fast_spatial.reshape(-1, 32), fast_widen.T,
        lateral_conv.reshape(-1, cf), slow_narrow.reshape(3 * bs, -1), slow_spatial.reshape(9 * bs, bs),
        slow_widen, norm_gains, norm_biases,
    )
    final = [shape((rows, channels), BF16), shape((4 * rows, cf), BF16)] * 2 + [
        shape((3 * bs, channels + bs), F32), shape((9 * bs, bs), F32), *out_shape[6:8],
        shape((96, cf), F32), shape((288, 32), F32), shape((32, cf), F32),
        shape(norm_gains.shape, F32), shape(norm_gains.shape, F32),
    ]
    handed = pl.pallas_call(
        hand_on,
        out_shape=final,
        in_specs=[any_spec] + [vmem_spec] * 5 + [any_spec] * 5,
        out_specs=[any_spec] * 13,
        scratch_shapes=[pltpu.VMEM(item.shape, item.dtype) for item in out_shape[0:1] + out_shape[6:11] + final[8:13]]
        + [pltpu.SemaphoreType.DMA((29,))],
        compiler_params=pltpu.CompilerParams(vmem_limit_bytes=52960 * 2**10),
    )(results[0], *[pltpu.with_memory_space_constraint(r, pltpu.VMEM) for r in results[1:6]], *results[6:11])
    slow_out, fast_out, slow_grad, fast_grad, dsa, dsb, dsc, dl, dfa, dfb, dfc, dgains, dbiases = handed

    return (
        unflat(slow_out, frames),
        unflat(fast_out, fast_frames),
        unflat(slow_grad, frames),
        unflat(fast_grad, fast_frames),
        dfa.reshape(fast_narrow.shape),
        dfb.reshape(fast_spatial.shape),
        dfc.T,
        dl.reshape(lateral_conv.shape),
        dsa.reshape(slow_narrow.shape),
        dsb.reshape(slow_spatial.shape),
        dsc,
        dgains,
        dbiases,
    )


def solution(mesh):
    sharded = P(("dp", "rep"), None, None)
    return jax.shard_map(
        body,
        mesh=mesh,
        in_specs=(sharded, sharded, P(("dp", "rep"), None)) + (P(),) * 9 + (sharded, sharded),
        out_specs=(sharded,) * 4 + (P(),) * 9,
        check_vma=False,
    )
```
